32 devices in a mesh: fsdp: 8 (over z, x), ns: 4 (over y, core).
Axes of the slice: x: 2, y: 2, z: 4, core: 2. Of those that a mesh axis runs over, the one named last changes fastest.
Arguments:
- tokens: bfloat16 [32768, 384], P(('fsdp', 'ns')), may hold values from -6 to 6
- cotangent: bfloat16 [32768, 384], P(('fsdp', 'ns')), may hold values from -30 to 30
- lengths: int32 [512], P(('fsdp', 'ns')), may hold values from 32 to 64, as said below
- variates: int32 [512, 64], P(('fsdp', 'ns')), may hold values from 0 to 3
- times: int32 [32768], P(('fsdp', 'ns')), may hold values from 0 to 63
- weight_qkv: float32 [3, 384, 384], P(None, None, 'fsdp'), may hold values from -0.3125 to 0.3125
- weight_out: float32 [384, 384], P('fsdp'), may hold values from -0.875 to 0.875
- weight_gate_up: float32 [2, 384, 1024], P(None, None, 'fsdp'), may hold values from -0.3125 to 0.3125
- weight_down: float32 [1024, 384], P('fsdp'), may hold values from -0.1875 to 0.1875
- momentum_qkv: float32 [3, 384, 384], P(None, None, 'fsdp'), may hold values from -2896.3094 to 2896.3094
- momentum_out: float32 [384, 384], P('fsdp'), may hold values from -2896.3094 to 2896.3094
- momentum_gate_up: float32 [2, 384, 1024], P(None, None, 'fsdp'), may hold values from -2896.3094 to 2896.3094
- momentum_down: float32 [1024, 384], P('fsdp'), may hold values from -2896.3094 to 2896.3094
- gains: float32 [2, 384], replicated, may hold values from 0.5 to 1.5
- attn_bias: float32 [2, 6], replicated, may hold values from -3 to 3
- gain_moment: float32 [2, 384], replicated, may hold values from -128 to 128
- gain_square: float32 [2, 384], replicated, may hold values from 1638.4 to 6553.6
- bias_moment: float32 [2, 6], replicated, may hold values from -256 to 256
- bias_square: float32 [2, 6], replicated, may hold values from 9830.4 to 39321.6
Outputs:
- out_tokens: bfloat16 [32768, 384], P(('fsdp', 'ns'))
- grad_tokens: bfloat16 [32768, 384], P(('fsdp', 'ns'))
- grad_qkv: float32 [3, 384, 384], P(None, None, 'fsdp')
- grad_out: float32 [384, 384], P('fsdp')
- grad_gate_up: float32 [2, 384, 1024], P(None, None, 'fsdp')
- grad_down: float32 [1024, 384], P('fsdp')
- new_momentum_qkv: float32 [3, 384, 384], P(None, None, 'fsdp')
- new_momentum_out: float32 [384, 384], P('fsdp')
- new_momentum_gate_up: float32 [2, 384, 1024], P(None, None, 'fsdp')
- new_momentum_down: float32 [1024, 384], P('fsdp')
- new_weight_qkv: float32 [3, 384, 384], P(None, None, 'fsdp')
- new_weight_out: float32 [384, 384], P('fsdp')
- new_weight_gate_up: float32 [2, 384, 1024], P(None, None, 'fsdp')
- new_weight_down: float32 [1024, 384], P('fsdp')
- grad_gains: float32 [2, 384], replicated
- new_gain_moment: float32 [2, 384], replicated
- new_gain_square: float32 [2, 384], replicated
- new_gains: float32 [2, 384], replicated
- grad_bias: float32 [2, 6], replicated
- new_bias_moment: float32 [2, 6], replicated
- new_bias_square: float32 [2, 6], replicated
- new_bias: float32 [2, 6], replicated
The draws below stay inside these ranges and needn't reach their ends.
Inputs may be any that keep to these rules, and one draw needn't show every extreme that they name: `lengths`: one bucket of all has all 64 slots live.
All inputs are finite; a program needn't handle non-finite values.
Results may differ from the reference program's by a relative error of at most 0.022.
The reference program's roundings to bfloat16 on the way count: a program that leaves them out, or rounds other values in their place, can miss the bound.
Values may be sent and summed in bfloat16 or wider, within the bound.
A program may use at most 128 MiB of HBM per device.

```python
import math
import jax
import jax.numpy as jnp
from jax import lax

D = 384
HEADS = 6
HEAD_DIM = 64
FF = 1024
BUCKET = 64
VARIATES = 4
NS_ITERS = 5
STEP = 10
TOK_DEV = 1024
BUCKETS = 512
TOKENS = 32768
N_FSDP = 8
N_NS = 4


def draw_lengths(key, part):
    first_key, second_key = jax.random.split(key)
    drawn = jax.random.randint(first_key, (BUCKETS,), BUCKET // 2, BUCKET + 1)
    picked = jax.random.randint(second_key, (), 0, BUCKETS)
    filled = jnp.arange(BUCKETS, dtype=jnp.int32) == picked
    return jnp.where(filled, BUCKET, drawn).astype(jnp.int32)


def draw_cotangent(key, part):
    base = jnp.clip(jax.random.normal(key, (TOKENS, D), jnp.float32), -6.0, 6.0)
    device = jnp.arange(TOKENS, dtype=jnp.int32) // TOK_DEV
    along_first = (device // N_NS).astype(jnp.float32) / max(N_FSDP - 1, 1)
    along_second = (device % N_NS).astype(jnp.float32) / max(N_NS - 1, 1)
    ratio = 3.0
    factor = ratio ** (along_first + along_second - 1.0)
    return (base * factor[:, None]).astype(jnp.bfloat16)


def rising(key, shape, axis, width_axis):
    first_key, second_key = jax.random.split(key)
    base = jnp.clip(jax.random.normal(first_key, shape, jnp.float32), -6.0, 6.0)
    count = shape[axis]
    ramp = jnp.arange(count, dtype=jnp.float32) / max(count - 1, 1)
    ratio = 3.0
    column_shape = [1] * len(shape)
    column_shape[axis] = count
    row_shape = [1] * len(shape)
    row_shape[width_axis] = shape[width_axis]
    column_factor = (ratio ** ramp).reshape(column_shape)
    row_factor = jnp.exp(jax.random.uniform(second_key, (shape[width_axis],), jnp.float32, -0.7, 0.7)).reshape(row_shape)
    return base * column_factor * row_factor * (0.25 * TOKENS ** 0.5)


def draw_momentum_qkv(key, part):
    return rising(key, (3, D, HEADS * HEAD_DIM), 2, 1)


def draw_momentum_out(key, part):
    return rising(key, (HEADS * HEAD_DIM, D), 0, 1)


def draw_momentum_gate_up(key, part):
    return rising(key, (2, D, FF), 2, 1)


def draw_momentum_down(key, part):
    return rising(key, (FF, D), 0, 1)


def plant(values, rng, smallest, high):
    longest = values.shape.index(max(values.shape))
    spots = []
    for shift in (0, 1):
        where = [jax.random.randint(jax.random.fold_in(rng, axis), (), 0, length) for axis, length in enumerate(values.shape)]
        where[longest] = (where[longest] + shift) % values.shape[longest]
        spots.append(tuple(where))
    return values.at[spots[0]].set(smallest).at[spots[1]].set(high)


def block_levels(own_key, shape, cuts, least, high):
    gain, own = 1.0, jax.random.fold_in(own_key, 6)
    for dim, parts in cuts:
        heights = jnp.exp(jax.random.uniform(jax.random.fold_in(own, dim), (parts,), jnp.float32, least / len(cuts), high / len(cuts)))
        gain = gain * jnp.repeat(heights, shape[dim] // parts).reshape([-1 if axis == dim else 1 for axis in range(len(shape))])
    return gain


def scatter_about(stream_key, extent, width, reach, cuts=(), held_as=jnp.bfloat16):
    gain = block_levels(stream_key, extent, cuts, -0.22, 0.18) if cuts else 1.0
    entries = jax.random.normal(stream_key, extent, jnp.float32) * width * gain
    return jnp.minimum(jnp.maximum(entries, -reach), reach).astype(held_as)


def setup_inputs(seed: int = 0) -> dict:
    streams_of = jax.random.split(jax.random.key(seed), 20)
    return {
        "tokens": scatter_about(streams_of[0], (TOKENS, D), 1.0, 6.0, ((0, 32),)),
        "cotangent": draw_cotangent(jax.random.fold_in(streams_of[19], 71), 0),
        "lengths": draw_lengths(jax.random.fold_in(streams_of[19], 71), 0),
        "variates": plant(jax.random.randint(streams_of[3], (BUCKETS, BUCKET), 0, VARIATES), jax.random.fold_in(streams_of[3], 1), 0, VARIATES - 1).astype(jnp.int32),
        "times": plant(jax.random.randint(streams_of[4], (TOKENS,), 0, BUCKET), jax.random.fold_in(streams_of[4], 1), 0, BUCKET - 1).astype(jnp.int32),
        "weight_qkv": scatter_about(streams_of[5], (3, D, HEADS * HEAD_DIM), D ** -0.5, 0.3125, ((2, 8),), jnp.float32),
        "weight_out": scatter_about(streams_of[6], (HEADS * HEAD_DIM, D), (HEADS * HEAD_DIM // 8) ** -0.5, 0.875, ((0, 8),), jnp.float32),
        "weight_gate_up": scatter_about(streams_of[7], (2, D, FF), D ** -0.5, 0.3125, ((2, 8),), jnp.float32),
        "weight_down": scatter_about(streams_of[8], (FF, D), FF ** -0.5, 0.1875, ((0, 8),), jnp.float32),
        "momentum_qkv": draw_momentum_qkv(jax.random.fold_in(streams_of[19], 71), 0),
        "momentum_out": draw_momentum_out(jax.random.fold_in(streams_of[19], 71), 0),
        "momentum_gate_up": draw_momentum_gate_up(jax.random.fold_in(streams_of[19], 71), 0),
        "momentum_down": draw_momentum_down(jax.random.fold_in(streams_of[19], 71), 0),
        "gains": jnp.clip(1.0 + 0.1 * jax.random.normal(streams_of[13], (2, D), jnp.float32), 0.5, 1.5),
        "attn_bias": scatter_about(streams_of[14], (2, HEADS), 1.0, 3.0, (), jnp.float32),
        "gain_moment": scatter_about(streams_of[15], (2, D), (0.11 * TOKENS ** 0.5), 128.0, (), jnp.float32),
        "gain_square": jnp.clip(jnp.exp(jax.random.uniform(streams_of[16], (2, D), jnp.float32, math.log(1638.4), math.log(6553.6))), 1638.4, 6553.6),
        "bias_moment": scatter_about(streams_of[17], (2, HEADS), (0.27 * TOKENS ** 0.5), 256.0, (), jnp.float32),
        "bias_square": jnp.clip(jnp.exp(jax.random.uniform(streams_of[18], (2, HEADS), jnp.float32, math.log(9830.4), math.log(39321.6))), 9830.4, 39321.6),
    }


@jax.custom_vjp
def low(v):
    return lax.optimization_barrier(v.astype(jnp.bfloat16)).astype(jnp.float32)

@jax.custom_vjp
def low_back(v):
    return v

def low_keep(v):
    return (low(v), None)

def low_pass(kept, grad):
    return (grad,)

def back_keep(v):
    return (v, None)

def back_low(kept, grad):
    return (low(grad),)
low.defvjp(low_keep, low_pass)
low_back.defvjp(back_keep, back_low)
EPS_NORM = 1e-06
ROPE_BASE = 10000.0
NEG_FILL = -1000000000.0
COEF_A = 3.4445
COEF_B = -4.775
COEF_C = 2.0315
NS_EPS = 1e-07
MUON_MU = 0.95
MUON_RATE = 0.25
MUON_DECAY = 0.01
ADAM_RATE = 0.8
BETA_ONE = 0.9
BETA_TWO = 0.95
ADAM_EPS = 1e-08

def product(left, right):
    return jnp.dot(left, right, precision=lax.Precision.HIGHEST, preferred_element_type=jnp.float32)

def rotary_tables(positions, head_size):
    half_dim = head_size // 2
    frequency = ROPE_BASE ** (-2.0 * jnp.arange(half_dim, dtype=jnp.float32) / head_size)
    angles = positions.astype(jnp.float32)[:, None] * frequency[None, :]
    return (jnp.cos(angles), jnp.sin(angles))

def rotate(vectors, cosine, sine_tab):
    half_dim = vectors.shape[-1] // 2
    first_half = vectors[..., :half_dim]
    second_half = vectors[..., half_dim:]
    cos_b = cosine[:, None, :]
    sin_b = sine_tab[:, None, :]
    return jnp.concatenate([first_half * cos_b - second_half * sin_b, first_half * sin_b + second_half * cos_b], axis=-1)

def block_forward(block_tokens, block_vars, block_times, block_lengths, rounded):
    w_query, w_key, w_value, w_proj, w_gate, w_upper, w_lower, gain_pair, bias_pair = rounded
    tok_rows = block_tokens.shape[0]
    bucket_count = block_lengths.shape[0]
    attn_width = HEADS * HEAD_DIM
    scale_one = lax.rsqrt(lax.optimization_barrier(jnp.mean(block_tokens * block_tokens, axis=-1, keepdims=True)) + EPS_NORM)
    normed_one = low(block_tokens * scale_one * gain_pair[0])
    query_raw = low_back(product(normed_one, w_query))
    key_raw = low_back(product(normed_one, w_key))
    value_raw = low_back(product(normed_one, w_value))
    cosine, sine_tab = rotary_tables(block_times, HEAD_DIM)
    query_rot = low(rotate(query_raw.reshape(tok_rows, HEADS, HEAD_DIM), cosine, sine_tab) * HEAD_DIM ** (-0.5))
    key_rot = low(rotate(key_raw.reshape(tok_rows, HEADS, HEAD_DIM), cosine, sine_tab))
    value_low = low(value_raw)
    shape_four = (bucket_count, BUCKET, HEADS, HEAD_DIM)
    query_b = query_rot.reshape(shape_four)
    key_b = key_rot.reshape(shape_four)
    value_b = value_low.reshape(shape_four)
    raw_scores = low_back(jnp.einsum('bqhd,bkhd->bhqk', query_b, key_b, precision=lax.Precision.HIGHEST))
    same_var = (block_vars[:, :, None] == block_vars[:, None, :]).astype(jnp.float32)[:, None]
    scores = raw_scores + bias_pair[0][None, :, None, None] * same_var + bias_pair[1][None, :, None, None] * (1.0 - same_var)
    live_keys = jnp.arange(BUCKET, dtype=jnp.int32)[None, :] < block_lengths[:, None]
    scores = jnp.where(live_keys[:, None, None, :], scores, NEG_FILL)
    attn_probs = jax.nn.softmax(scores, axis=-1)
    attended = jnp.einsum('bhqk,bkhd->bqhd', low(attn_probs), value_b, precision=lax.Precision.HIGHEST).reshape(tok_rows, attn_width)
    attended = low(low_back(attended))
    mid_resid = block_tokens + low_back(product(attended, w_proj))
    scale_two = lax.rsqrt(lax.optimization_barrier(jnp.mean(mid_resid * mid_resid, axis=-1, keepdims=True)) + EPS_NORM)
    normed_two = low(mid_resid * scale_two * gain_pair[1])
    gate_val = low_back(product(normed_two, w_gate))
    up_val = low_back(product(normed_two, w_upper))
    hidden = low(jax.nn.silu(gate_val) * up_val)
    return mid_resid + low_back(product(hidden, w_lower))

def orthogonal(advance):
    norm_val = jnp.sqrt(jnp.sum(advance * advance))
    current = advance / (norm_val + NS_EPS)
    for turn_idx in range(NS_ITERS):
        gram_mat = product(current, current.T)
        poly_mat = COEF_B * gram_mat + COEF_C * product(gram_mat, gram_mat)
        current = COEF_A * current + product(poly_mat, current)
    return current

def muon_step(weight, grad, momentum):
    new_momentum = MUON_MU * momentum + grad
    advance = grad + MUON_MU * new_momentum
    orthogonal_x = orthogonal(advance)
    factor = 0.2 * math.sqrt(max(weight.shape))
    new_weight = weight * (1.0 - MUON_RATE * MUON_DECAY) - MUON_RATE * factor * orthogonal_x
    return (new_momentum, new_weight)

def adam_step(param, grad, moment, square):
    new_moment = BETA_ONE * moment + (1.0 - BETA_ONE) * grad
    new_square = BETA_TWO * square + (1.0 - BETA_TWO) * grad * grad
    corrected = new_moment / (1.0 - BETA_ONE ** STEP)
    scaled = jnp.sqrt(new_square / (1.0 - BETA_TWO ** STEP)) + ADAM_EPS
    return (new_moment, new_square, param - ADAM_RATE * corrected / scaled)

def reference(tokens, cotangent, lengths, variates, times, weight_qkv, weight_out, weight_gate_up, weight_down, momentum_qkv, momentum_out, momentum_gate_up, momentum_down, gains, attn_bias, gain_moment, gain_square, bias_moment, bias_square):
    group = math.gcd(BUCKETS, 64)
    turns = BUCKETS // group
    live_rows = (jnp.arange(BUCKET, dtype=jnp.int32)[None, :] < lengths[:, None]).astype(jnp.float32).reshape(TOKENS)
    tokens_wide = tokens.astype(jnp.float32)
    params = (weight_qkv, weight_out, weight_gate_up, weight_down, gains, attn_bias)

    def forward(params, tokens_wide):
        qkv_w, out_w, gate_up_w, down_w, gain_pair, bias_pair = params
        rounded = (low(qkv_w[0]), low(qkv_w[1]), low(qkv_w[2]), low(out_w), low(gate_up_w[0]), low(gate_up_w[1]), low(down_w), gain_pair, bias_pair)

        def one_group(pieces):
            return jax.checkpoint(block_forward)(pieces[0], pieces[1], pieces[2], pieces[3], rounded)
        outputs = lax.map(one_group, (tokens_wide.reshape(turns, group * BUCKET, D), variates.reshape(turns, group, BUCKET), times.reshape(turns, group * BUCKET), lengths.reshape(turns, group)))
        return outputs.reshape(TOKENS, D)
    block_out, pullback = jax.vjp(forward, params, tokens_wide)
    grad_params, grad_input = pullback(cotangent.astype(jnp.float32) * live_rows[:, None])
    grad_qkv, grad_out, grad_gate_up, grad_down, grad_gains, grad_bias = grad_params
    mom_list = []
    new_list = []
    for index_j in range(3):
        momentum_j, weight_j = muon_step(weight_qkv[index_j], grad_qkv[index_j], momentum_qkv[index_j])
        mom_list.append(momentum_j)
        new_list.append(weight_j)
    new_momentum_qkv = jnp.stack(mom_list)
    new_weight_qkv = jnp.stack(new_list)
    momentum_o, weight_o = muon_step(weight_out.T, grad_out.T, momentum_out.T)
    mom_list = []
    new_list = []
    for index_j in range(2):
        momentum_j, weight_j = muon_step(weight_gate_up[index_j], grad_gate_up[index_j], momentum_gate_up[index_j])
        mom_list.append(momentum_j)
        new_list.append(weight_j)
    new_momentum_gate_up = jnp.stack(mom_list)
    new_weight_gate_up = jnp.stack(new_list)
    momentum_d, weight_d = muon_step(weight_down.T, grad_down.T, momentum_down.T)
    new_gain_moment, new_gain_square, new_gains = adam_step(gains, grad_gains, gain_moment, gain_square)
    new_bias_moment, new_bias_square, new_bias = adam_step(attn_bias, grad_bias, bias_moment, bias_square)
    return (block_out.astype(jnp.bfloat16), grad_input.astype(jnp.bfloat16), grad_qkv, grad_out, grad_gate_up, grad_down, new_momentum_qkv, momentum_o.T, new_momentum_gate_up, momentum_d.T, new_weight_qkv, weight_o.T, new_weight_gate_up, weight_d.T, grad_gains, new_gain_moment, new_gain_square, new_gains, grad_bias, new_bias_moment, new_bias_square, new_bias)
```

```python
import math

import jax
import jax.numpy as jnp
from jax import lax
from jax.sharding import PartitionSpec as P

D = 384
HEADS = 6
HEAD_DIM = 64
FF = 1024
NS_ITERS = 5
STEP = 10


EPS_NORM = 1e-06
ROPE_BASE = 10000.0
NEG_FILL = -1000000000.0
COEF_A = 3.4445
COEF_B = -4.775
COEF_C = 2.0315
NS_EPS = 1e-07
MUON_MU = 0.95
MUON_RATE = 0.25
MUON_DECAY = 0.01
ADAM_RATE = 0.8
BETA_ONE = 0.9
BETA_TWO = 0.95
ADAM_EPS = 1e-08


def rotary_tables(positions, head_size):
    half_dim = head_size // 2
    frequency = ROPE_BASE ** (-2.0 * jnp.arange(half_dim, dtype=jnp.float32) / head_size)
    angles = positions.astype(jnp.float32)[:, None] * frequency[None, :]
    return (jnp.cos(angles), jnp.sin(angles))


def rotate(vectors, cosine, sine_tab):
    half_dim = vectors.shape[-1] // 2
    first_half = vectors[..., :half_dim]
    second_half = vectors[..., half_dim:]
    cos_b = cosine[:, None, :]
    sin_b = sine_tab[:, None, :]
    return jnp.concatenate(
        [first_half * cos_b - second_half * sin_b, first_half * sin_b + second_half * cos_b],
        axis=-1,
    )


def unrotate(vectors, cosine, sine_tab):
    half_dim = vectors.shape[-1] // 2
    first_half = vectors[..., :half_dim]
    second_half = vectors[..., half_dim:]
    cos_b = cosine[:, None, :]
    sin_b = sine_tab[:, None, :]
    return jnp.concatenate(
        [first_half * cos_b + second_half * sin_b, second_half * cos_b - first_half * sin_b],
        axis=-1,
    )


def rms_scale(values):
    return lax.rsqrt(jnp.mean(values * values, axis=-1, keepdims=True) + EPS_NORM)


def norm_back(source, scale, gain_row, incoming):
    normed = source * scale
    gain_grad = jnp.sum(incoming * normed, axis=0)
    scaled_in = incoming * gain_row
    back = scale * (scaled_in - normed * jnp.mean(scaled_in * normed, axis=-1, keepdims=True))
    return (back, gain_grad)


def gram_local(current):
    return jnp.einsum(
        "mdn,men->mde",
        current,
        current,
        precision=lax.Precision.HIGHEST,
        preferred_element_type=jnp.float32,
    )


def newton_schulz(advance, gram_total):
    def product(left, right):
        return jnp.einsum(
            "mde,mef->mdf",
            left,
            right,
            precision=lax.Precision.HIGHEST,
            preferred_element_type=jnp.float32,
        )

    gram_mat = gram_total(gram_local(advance))
    norm_val = jnp.sqrt(jnp.trace(gram_mat, axis1=1, axis2=2))[:, None, None] + NS_EPS
    gram_mat = gram_mat / (norm_val * norm_val)
    unit = jnp.eye(D, dtype=jnp.float32)[None]
    chain = None
    for turn_idx in range(NS_ITERS):
        poly_mat = COEF_A * unit + COEF_B * gram_mat + COEF_C * product(gram_mat, gram_mat)
        chain = poly_mat if chain is None else product(poly_mat, chain)
        if turn_idx < NS_ITERS - 1:
            gram_mat = product(product(poly_mat, gram_mat), poly_mat)
    return product(chain, advance / norm_val)


def adam_step(param, grad, moment, square):
    new_moment = BETA_ONE * moment + (1.0 - BETA_ONE) * grad
    new_square = BETA_TWO * square + (1.0 - BETA_TWO) * grad * grad
    corrected = new_moment / (1.0 - BETA_ONE**STEP)
    scaled = jnp.sqrt(new_square / (1.0 - BETA_TWO**STEP)) + ADAM_EPS
    return (new_moment, new_square, param - ADAM_RATE * corrected / scaled)


def body(
    tokens,
    cotangent,
    lengths,
    variates,
    times,
    weight_qkv,
    weight_out,
    weight_gate_up,
    weight_down,
    momentum_qkv,
    momentum_out,
    momentum_gate_up,
    momentum_down,
    gains,
    attn_bias,
    gain_moment,
    gain_square,
    bias_moment,
    bias_square,
):
    low_type = jnp.bfloat16
    tok_rows = tokens.shape[0]
    bucket_count = lengths.shape[0]
    bucket_len = tok_rows // bucket_count
    head_count = attn_bias.shape[1]
    attn_width = head_count * HEAD_DIM
    shape_four = (bucket_count, bucket_len, head_count, HEAD_DIM)
    shards = (
        weight_qkv.astype(low_type),
        weight_out.astype(low_type),
        weight_gate_up.astype(low_type),
        weight_down.astype(low_type),
    )
    full_qkv, full_out, full_gate_up, full_down = (
        lax.all_gather(shards[0], "fsdp", axis=2, tiled=True),
        lax.all_gather(shards[1], "fsdp", axis=0, tiled=True),
        lax.all_gather(shards[2], "fsdp", axis=2, tiled=True),
        lax.all_gather(shards[3], "fsdp", axis=0, tiled=True),
    )
    tokens_wide = tokens.astype(jnp.float32)
    scale_one = rms_scale(tokens_wide)
    normed_one = (tokens_wide * scale_one * gains[0]).astype(low_type)
    qkv_proj = jnp.einsum("td,kde->kte", normed_one, full_qkv, preferred_element_type=jnp.float32)
    cosine, sine_tab = rotary_tables(times, HEAD_DIM)
    query_scale = HEAD_DIM ** (-0.5)
    query_rot = (
        (
            rotate(qkv_proj[0].reshape(tok_rows, head_count, HEAD_DIM), cosine, sine_tab)
            * query_scale
        )
        .astype(low_type)
        .reshape(shape_four)
    )
    key_rot = (
        rotate(qkv_proj[1].reshape(tok_rows, head_count, HEAD_DIM), cosine, sine_tab)
        .astype(low_type)
        .reshape(shape_four)
    )
    value_low = qkv_proj[2].astype(low_type).reshape(shape_four)
    live_keys = jnp.arange(bucket_len, dtype=jnp.int32)[None, :] < lengths[:, None]
    same_var = (variates[:, :, None] == variates[:, None, :]).astype(jnp.float32)[:, None]

    def scores_of(query_part, key_part):
        raw_scores = jnp.einsum(
            "bqhd,bkhd->bhqk", query_part, key_part, preferred_element_type=jnp.float32
        )
        biased = (
            raw_scores
            + attn_bias[0][None, :, None, None] * same_var
            + attn_bias[1][None, :, None, None] * (1.0 - same_var)
        )
        return jnp.where(live_keys[:, None, None, :], biased, NEG_FILL)

    scores = scores_of(query_rot, key_rot)
    row_top = jnp.max(scores, axis=-1, keepdims=True)
    exponent = jnp.exp(scores - row_top)
    row_total = jnp.sum(exponent, axis=-1, keepdims=True)
    attn_probs = exponent / row_total
    log_total = row_top + jnp.log(row_total)
    attended = (
        jnp.einsum(
            "bhqk,bkhd->bqhd",
            attn_probs.astype(low_type),
            value_low,
            preferred_element_type=jnp.float32,
        )
        .reshape(tok_rows, attn_width)
        .astype(low_type)
    )
    mid_resid = tokens_wide + jnp.dot(attended, full_out, preferred_element_type=jnp.float32)
    scale_two = rms_scale(mid_resid)
    normed_two = (mid_resid * scale_two * gains[1]).astype(low_type)
    gate_up = jnp.einsum(
        "td,kdf->ktf", normed_two, full_gate_up, preferred_element_type=jnp.float32
    )
    gate_val = gate_up[0]
    up_val = gate_up[1]
    sigmoid_g = jax.nn.sigmoid(gate_val)
    silu_val = gate_val * sigmoid_g
    hidden = (silu_val * up_val).astype(low_type)
    out_tokens = (
        mid_resid + jnp.dot(hidden, full_down, preferred_element_type=jnp.float32)
    ).astype(low_type)
    full_qkv, full_out, full_gate_up, full_down = (
        lax.all_gather(shards[0], "fsdp", axis=2, tiled=True),
        lax.all_gather(shards[1], "fsdp", axis=0, tiled=True),
        lax.all_gather(shards[2], "fsdp", axis=2, tiled=True),
        lax.all_gather(shards[3], "fsdp", axis=0, tiled=True),
    )
    live_rows = live_keys.reshape(tok_rows).astype(jnp.float32)
    grad_block = cotangent.astype(jnp.float32) * live_rows[:, None]
    grad_low = grad_block.astype(low_type)
    grad_down = jnp.einsum("tf,td->fd", hidden, grad_low, preferred_element_type=jnp.float32)
    grad_hidden = jnp.einsum("td,fd->tf", grad_low, full_down, preferred_element_type=jnp.float32)
    grad_gate = grad_hidden * up_val * sigmoid_g * (1.0 + gate_val * (1.0 - sigmoid_g))
    grad_up = grad_hidden * silu_val
    grad_pair = jnp.stack([grad_gate, grad_up]).astype(low_type)
    grad_gate_up = jnp.einsum(
        "td,ktf->kdf", normed_two, grad_pair, preferred_element_type=jnp.float32
    )
    grad_norm_two = jnp.einsum(
        "ktf,kdf->td", grad_pair, full_gate_up, preferred_element_type=jnp.float32
    )
    back_two, gain_two_grad = norm_back(mid_resid, scale_two, gains[1], grad_norm_two)
    grad_mid = grad_block + back_two
    grad_mid_low = grad_mid.astype(low_type)
    grad_out = jnp.einsum("te,td->ed", attended, grad_mid_low, preferred_element_type=jnp.float32)
    grad_att = (
        jnp.einsum("td,ed->te", grad_mid_low, full_out, preferred_element_type=jnp.float32)
        .astype(low_type)
        .reshape(shape_four)
    )
    probs_again = jnp.exp(scores_of(query_rot, key_rot) - log_total)
    grad_probs = jnp.einsum(
        "bqhd,bkhd->bhqk", grad_att, value_low, preferred_element_type=jnp.float32
    )
    row_dot = jnp.sum(probs_again * grad_probs, axis=-1, keepdims=True)
    grad_scores = probs_again * (grad_probs - row_dot)
    same_part = jnp.sum(grad_scores * same_var, axis=(0, 2, 3))
    other_part = jnp.sum(grad_scores * (1.0 - same_var), axis=(0, 2, 3))
    bias_grads = jnp.stack([same_part, other_part])
    scores_low = grad_scores.astype(low_type)
    grad_query = jnp.einsum(
        "bhqk,bkhd->bqhd", scores_low, key_rot, preferred_element_type=jnp.float32
    )
    grad_keys = jnp.einsum(
        "bhqk,bqhd->bkhd", scores_low, query_rot, preferred_element_type=jnp.float32
    )
    grad_values = jnp.einsum(
        "bhqk,bqhd->bkhd",
        probs_again.astype(low_type),
        grad_att,
        preferred_element_type=jnp.float32,
    )
    grad_q = (
        unrotate(grad_query.reshape(tok_rows, head_count, HEAD_DIM), cosine, sine_tab) * query_scale
    )
    grad_k = unrotate(grad_keys.reshape(tok_rows, head_count, HEAD_DIM), cosine, sine_tab)
    grad_triple = jnp.stack(
        [
            grad_q.reshape(tok_rows, attn_width),
            grad_k.reshape(tok_rows, attn_width),
            grad_values.reshape(tok_rows, attn_width),
        ]
    ).astype(low_type)
    grad_qkv = jnp.einsum(
        "td,kte->kde", normed_one, grad_triple, preferred_element_type=jnp.float32
    )
    grad_norm_one = jnp.einsum(
        "kte,kde->td", grad_triple, full_qkv, preferred_element_type=jnp.float32
    )
    back_one, gain_one_grad = norm_back(tokens_wide, scale_one, gains[0], grad_norm_one)
    grad_tokens = (grad_mid + back_one).astype(low_type)
    summed = (
        lax.psum_scatter(grad_qkv, "fsdp", scatter_dimension=2, tiled=True),
        lax.psum_scatter(grad_out, "fsdp", scatter_dimension=0, tiled=True),
        lax.psum_scatter(grad_gate_up, "fsdp", scatter_dimension=2, tiled=True),
        lax.psum_scatter(grad_down, "fsdp", scatter_dimension=0, tiled=True),
    )
    grad_qkv, grad_out, grad_gate_up, grad_down = (
        lax.psum(summed[0].astype(jnp.bfloat16), "ns").astype(jnp.float32),
        lax.psum(summed[1].astype(jnp.bfloat16), "ns").astype(jnp.float32),
        lax.psum(summed[2].astype(jnp.bfloat16), "ns").astype(jnp.float32),
        lax.psum(summed[3].astype(jnp.bfloat16), "ns").astype(jnp.float32),
    )
    grad_gains, grad_bias = lax.psum(
        (jnp.stack([gain_one_grad, gain_two_grad]), bias_grads), ("fsdp", "ns")
    )
    new_momentum_qkv = MUON_MU * momentum_qkv + grad_qkv
    new_momentum_out = MUON_MU * momentum_out + grad_out
    new_momentum_gate_up = MUON_MU * momentum_gate_up + grad_gate_up
    new_momentum_down = MUON_MU * momentum_down + grad_down
    look_qkv = grad_qkv + MUON_MU * new_momentum_qkv
    look_out = grad_out + MUON_MU * new_momentum_out
    look_gate_up = grad_gate_up + MUON_MU * new_momentum_gate_up
    look_down = grad_down + MUON_MU * new_momentum_down
    attn_stack = jnp.concatenate([look_qkv, look_out.T[None]], axis=0)
    ff_stack = jnp.concatenate([look_gate_up, look_down.T[None]], axis=0)
    attn_ortho = newton_schulz(attn_stack, lambda partial_gram: lax.psum(partial_gram, "fsdp"))
    quarter = ff_stack.shape[2] // lax.axis_size("ns")
    own_cols = lax.dynamic_slice_in_dim(ff_stack, lax.axis_index("ns") * quarter, quarter, 2)
    own_ortho = newton_schulz(own_cols, lambda partial_gram: lax.psum(partial_gram, ("fsdp", "ns")))
    ff_ortho = lax.all_gather(own_ortho, "ns", axis=2, tiled=True)
    shrink = 1.0 - MUON_RATE * MUON_DECAY
    attn_factor = MUON_RATE * 0.2 * math.sqrt(max(D, HEADS * HEAD_DIM))
    ff_factor = MUON_RATE * 0.2 * math.sqrt(max(D, FF))
    new_weight_qkv = weight_qkv * shrink - attn_factor * attn_ortho[:3]
    new_weight_out = weight_out * shrink - attn_factor * attn_ortho[3].T
    new_weight_gate_up = weight_gate_up * shrink - ff_factor * ff_ortho[:2]
    new_weight_down = weight_down * shrink - ff_factor * ff_ortho[2].T
    new_gain_moment, new_gain_square, new_gains = adam_step(
        gains, grad_gains, gain_moment, gain_square
    )
    new_bias_moment, new_bias_square, new_bias = adam_step(
        attn_bias, grad_bias, bias_moment, bias_square
    )
    return (
        out_tokens,
        grad_tokens,
        grad_qkv,
        grad_out,
        grad_gate_up,
        grad_down,
        new_momentum_qkv,
        new_momentum_out,
        new_momentum_gate_up,
        new_momentum_down,
        new_weight_qkv,
        new_weight_out,
        new_weight_gate_up,
        new_weight_down,
        grad_gains,
        new_gain_moment,
        new_gain_square,
        new_gains,
        grad_bias,
        new_bias_moment,
        new_bias_square,
        new_bias,
    )


def solution(mesh):
    return jax.shard_map(
        body,
        mesh=mesh,
        in_specs=(
            P(("fsdp", "ns"), None),
            P(("fsdp", "ns"), None),
            P(("fsdp", "ns")),
            P(("fsdp", "ns"), None),
            P(("fsdp", "ns")),
            P(None, None, "fsdp"),
            P("fsdp", None),
            P(None, None, "fsdp"),
            P("fsdp", None),
            P(None, None, "fsdp"),
            P("fsdp", None),
            P(None, None, "fsdp"),
            P("fsdp", None),
            P(),
            P(),
            P(),
            P(),
            P(),
            P(),
        ),
        out_specs=(
            P(("fsdp", "ns"), None),
            P(("fsdp", "ns"), None),
            P(None, None, "fsdp"),
            P("fsdp", None),
            P(None, None, "fsdp"),
            P("fsdp", None),
            P(None, None, "fsdp"),
            P("fsdp", None),
            P(None, None, "fsdp"),
            P("fsdp", None),
            P(None, None, "fsdp"),
            P("fsdp", None),
            P(None, None, "fsdp"),
            P("fsdp", None),
            P(),
            P(),
            P(),
            P(),
            P(),
            P(),
            P(),
            P(),
        ),
        check_vma=False,
    )
```

```python
import functools
import math

import jax
import jax.numpy as jnp
from jax import lax
from jax.experimental import pallas as pl
from jax.experimental.pallas import tpu as pltpu
from jax.sharding import PartitionSpec as P

HEAD_DIM = 64
BUCKET = 64
TIME_SLOTS = 64
NS_ITERS = 5
STEP = 10

EPS_NORM = 1e-06
ROPE_BASE = 10000.0
NEG_FILL = -1000000000.0
COEF_A = 3.4445
COEF_B = -4.775
COEF_C = 2.0315
NS_EPS = 1e-07
MUON_MU = 0.95
MUON_RATE = 0.25
MUON_DECAY = 0.01
ADAM_RATE = 0.8
BETA_ONE = 0.9
BETA_TWO = 0.95
ADAM_EPS = 1e-08

LOW = jnp.bfloat16
WIDE = jnp.float32
BLOCK = 256
PAIR = 2 * BUCKET
LANES = 2 * HEAD_DIM
WHOLE = pl.BlockSpec(memory_space=pltpu.VMEM)
SCALARS = pl.BlockSpec(memory_space=pltpu.SMEM)


def mul_nn(left, right):
    return lax.dot_general(left, right, (((1,), (0,)), ((), ())), preferred_element_type=WIDE)


def mul_nt(left, right):
    return lax.dot_general(left, right, (((1,), (1,)), ((), ())), preferred_element_type=WIDE)


def mul_tn(left, right):
    return lax.dot_general(left, right, (((0,), (0,)), ((), ())), preferred_element_type=WIDE)


def offsets(attn_rows, ff_rows):
    counts = [attn_rows] * 4 + [ff_rows] * 3
    starts = [sum(counts[:i]) for i in range(7)]
    return list(zip(starts, counts))


def layer_kernel(
    pieces,
    lengths,
    bias,
    tok_ref,
    cot_ref,
    var_ref,
    time_ref,
    table_ref,
    gain_ref,
    w_ref,
    out_ref,
    gtok_ref,
    grad_ref,
    ggain_ref,
    gbias_ref,
    n1_s,
    n2_s,
    att_s,
    gml_s,
    hid_s,
    glow_s,
    gg_s,
    gu_s,
    gqkv_s,
):
    step = pl.program_id(0)
    rows, width = tok_ref.shape
    heads = bias.shape[1]
    here = pl.ds(pl.multiple_of(step * rows, rows), rows)

    def weight(first, last):
        parts = []
        for i in range(first, last):
            start, count = pieces[i]
            part = w_ref[:, start : start + count, :]
            parts.append(part.reshape(part.shape[0] * count, width))
        return parts[0] if len(parts) == 1 else jnp.concatenate(parts, axis=0)

    @pl.when(step == 0)
    def _():
        ggain_ref[...] = jnp.zeros_like(ggain_ref)
        gbias_ref[...] = jnp.zeros_like(gbias_ref)

    lane = lax.broadcasted_iota(jnp.int32, (1, LANES), 1)
    low_head = lane < HEAD_DIM
    low_half = lane % HEAD_DIM < HEAD_DIM // 2
    per_block = rows // PAIR
    var_rows = var_ref[pl.ds(step * per_block, per_block), :]
    time_rows = time_ref[pl.ds(step * per_block, per_block), :]
    filler = jnp.zeros((8 - 2 * per_block, PAIR), WIDE)
    columns = jnp.concatenate([var_rows, time_rows, filler], axis=0).T
    slots = lax.broadcasted_iota(jnp.int32, (1, TIME_SLOTS), 1).astype(WIDE)
    hot = jnp.concatenate(
        [(columns[:, per_block + p : per_block + p + 1] == slots) for p in range(per_block)], axis=0
    ).astype(LOW)
    looked = mul_nn(hot, table_ref[0]) + mul_nn(hot, table_ref[1]) + mul_nn(hot, table_ref[2])
    cosine = looked[:, :LANES]
    sine = looked[:, LANES:]

    def swapped(values):
        half = HEAD_DIM // 2
        return jnp.where(
            low_half, pltpu.roll(values, LANES - half, 1), pltpu.roll(values, half, 1)
        )

    gain_one = gain_ref[0:1, :]
    gain_two = gain_ref[1:2, :]
    tokens = tok_ref[...].astype(WIDE)
    scale_one = lax.rsqrt(jnp.mean(tokens * tokens, axis=-1, keepdims=True) + EPS_NORM)
    unit_one = tokens * scale_one
    normed_one = (unit_one * gain_one).astype(LOW)
    n1_s[here, :] = normed_one
    qkv = mul_nt(normed_one, weight(0, 3))

    query_scale = HEAD_DIM ** (-0.5)
    units = []
    attended = []
    row_id = lax.broadcasted_iota(jnp.int32, (PAIR, 1), 0)
    lane_id = lax.broadcasted_iota(jnp.int32, (1, PAIR), 1)
    same_bucket = (row_id < BUCKET) == (lane_id < BUCKET)
    masks = []
    live_cols = []
    for p in range(per_block):
        first = lengths[(step * per_block + p) * 2]
        second = lengths[(step * per_block + p) * 2 + 1]
        live_key = lane_id % BUCKET < jnp.where(lane_id < BUCKET, first, second)
        live_cols.append(row_id % BUCKET < jnp.where(row_id < BUCKET, first, second))
        mask = same_bucket & live_key
        same_var = columns[:, p : p + 1] == var_rows[p : p + 1, :]
        masks.append((mask, same_var))

    for hp in range(heads // 2):
        cols = slice(hp * LANES, (hp + 1) * LANES)
        q = qkv[:, cols]
        k = qkv[:, width + hp * LANES : width + (hp + 1) * LANES]
        v = qkv[:, 2 * width + hp * LANES : 2 * width + (hp + 1) * LANES].astype(LOW)
        q = ((q * cosine + swapped(q) * sine) * query_scale).astype(LOW)
        k = (k * cosine + swapped(k) * sine).astype(LOW)
        q_first = jnp.where(low_head, q, jnp.zeros_like(q))
        q_second = jnp.where(low_head, jnp.zeros_like(q), q)
        att_pairs = []
        for p in range(per_block):
            part = slice(p * PAIR, (p + 1) * PAIR)
            mask, same_var = masks[p]
            q2 = jnp.concatenate([q_first[part], q_second[part]], axis=0)
            kp = k[part]
            vp = v[part]
            raw = mul_nt(q2, kp)
            halves = []
            for j in range(2):
                h = 2 * hp + j
                biased = raw[j * PAIR : (j + 1) * PAIR] + jnp.where(
                    same_var, bias[0, h], bias[1, h]
                )
                halves.append(jnp.where(mask, biased, NEG_FILL))
            scores = jnp.concatenate(halves, axis=0)
            top = jnp.max(scores, axis=-1, keepdims=True)
            exponent = jnp.exp(scores - top)
            probs = exponent / jnp.sum(exponent, axis=-1, keepdims=True)
            probs_low = probs.astype(LOW)
            both = mul_nn(probs_low, vp)
            att_pairs.append(jnp.where(low_head, both[:PAIR], both[PAIR:]))
            units.append((hp, p, q2, kp, vp, probs, probs_low))
        attended.append(jnp.concatenate(att_pairs, axis=0).astype(LOW))
    attended = jnp.concatenate(attended, axis=1)
    att_s[here, :] = attended
    w_out = weight(3, 4)
    mid = tokens + mul_nn(attended, w_out)
    scale_two = lax.rsqrt(jnp.mean(mid * mid, axis=-1, keepdims=True) + EPS_NORM)
    unit_two = mid * scale_two
    normed_two = (unit_two * gain_two).astype(LOW)
    n2_s[here, :] = normed_two
    w_gate = weight(4, 5)
    w_up = weight(5, 6)
    w_down = weight(6, 7)
    gate = mul_nt(normed_two, w_gate)
    up = mul_nt(normed_two, w_up)
    sig = 1.0 / (1.0 + jnp.exp(-gate))
    silu = gate * sig
    hidden = (silu * up).astype(LOW)
    hid_s[here, :] = hidden
    out_ref[...] = (mid + mul_nn(hidden, w_down)).astype(LOW)

    live_row = jnp.concatenate(live_cols, axis=0)
    g_out = jnp.where(live_row, cot_ref[...].astype(WIDE), 0.0)
    g_low = g_out.astype(LOW)
    glow_s[here, :] = g_low
    g_hidden = mul_nt(g_low, w_down)
    g_gate = (g_hidden * up * sig * (1.0 + gate * (1.0 - sig))).astype(LOW)
    g_up = (g_hidden * silu).astype(LOW)
    gg_s[here, :] = g_gate
    gu_s[here, :] = g_up
    e_two = mul_nn(g_gate, w_gate) + mul_nn(g_up, w_up)
    ggain_ref[1:2, :] += jnp.sum(e_two * unit_two, axis=0, keepdims=True)
    scaled = e_two * gain_two
    g_mid = g_out + scale_two * (
        scaled - unit_two * jnp.mean(scaled * unit_two, axis=-1, keepdims=True)
    )
    g_mid_low = g_mid.astype(LOW)
    gml_s[here, :] = g_mid_low
    g_att = mul_nt(g_mid_low, w_out).astype(LOW)

    parts_q = [[None] * per_block for _ in range(heads // 2)]
    parts_k = [[None] * per_block for _ in range(heads // 2)]
    parts_v = [[None] * per_block for _ in range(heads // 2)]
    for hp, p, q2, kp, vp, probs, probs_low in units:
        part = slice(p * PAIR, (p + 1) * PAIR)
        mask, same_var = masks[p]
        ga = g_att[part, hp * LANES : (hp + 1) * LANES]
        ga2 = jnp.concatenate(
            [
                jnp.where(low_head, ga, jnp.zeros_like(ga)),
                jnp.where(low_head, jnp.zeros_like(ga), ga),
            ],
            axis=0,
        )
        g_probs = mul_nt(ga2, vp)
        row_dot = jnp.sum(probs * g_probs, axis=-1, keepdims=True)
        g_scores = probs * (g_probs - row_dot)
        for j in range(2):
            h = 2 * hp + j
            mine = g_scores[j * PAIR : (j + 1) * PAIR]
            gbias_ref[h : h + 1, :] += jnp.sum(
                jnp.where(same_var, mine, 0.0), axis=0, keepdims=True
            )
            gbias_ref[8 + h : 9 + h, :] += jnp.sum(
                jnp.where(same_var, 0.0, mine), axis=0, keepdims=True
            )
        low_scores = g_scores.astype(LOW)
        both = mul_nn(low_scores, kp)
        parts_q[hp][p] = jnp.where(low_head, both[:PAIR], both[PAIR:])
        parts_k[hp][p] = mul_tn(low_scores, q2)
        parts_v[hp][p] = mul_tn(probs_low, ga2)
    g_q = []
    g_k = []
    g_v = []
    for hp in range(heads // 2):
        dq = jnp.concatenate(parts_q[hp], axis=0)
        dk = jnp.concatenate(parts_k[hp], axis=0)
        g_q.append(((dq * cosine - swapped(dq) * sine) * query_scale).astype(LOW))
        g_k.append((dk * cosine - swapped(dk) * sine).astype(LOW))
        g_v.append(jnp.concatenate(parts_v[hp], axis=0).astype(LOW))
    g_qkv = jnp.concatenate(g_q + g_k + g_v, axis=1)
    gqkv_s[here, :] = g_qkv
    e_one = mul_nn(g_qkv, weight(0, 3))
    ggain_ref[0:1, :] += jnp.sum(e_one * unit_one, axis=0, keepdims=True)
    scaled = e_one * gain_one
    gtok_ref[...] = (
        g_mid
        + scale_one * (scaled - unit_one * jnp.mean(scaled * unit_one, axis=-1, keepdims=True))
    ).astype(LOW)

    @pl.when(step == pl.num_programs(0) - 1)
    def _():
        def put(index, left, right):
            start, count = pieces[index]
            grad_ref[:, start : start + count, :] = (
                mul_tn(left, right)
                .reshape(grad_ref.shape[0], count, width)
                .astype(grad_ref.dtype)
            )

        for j in range(3):
            put(j, gqkv_s[:, j * width : (j + 1) * width], n1_s[...])
        put(3, att_s[...], gml_s[...])
        put(4, gg_s[...], n2_s[...])
        put(5, gu_s[...], n2_s[...])
        put(6, hid_s[...], glow_s[...])


def layer(tokens, cotangent, lengths, variates, times, packed, gains, attn_bias, ff, grad_type):
    rows, width = tokens.shape
    heads = attn_bias.shape[1]
    copies, shard_rows, _ = packed.shape
    pieces = offsets(heads * HEAD_DIM // copies, ff // copies)
    half = HEAD_DIM // 2
    frequency = ROPE_BASE ** (-2.0 * jnp.arange(half, dtype=WIDE) / HEAD_DIM)
    angles = jnp.arange(TIME_SLOTS, dtype=WIDE)[:, None] * frequency[None, :]
    cosine, sine = jnp.cos(angles), jnp.sin(angles)
    table = jnp.concatenate([cosine] * 4 + [-sine, sine, -sine, sine], axis=1)
    first = table.astype(LOW)
    rest = table - first.astype(WIDE)
    second = rest.astype(LOW)
    third = (rest - second.astype(WIDE)).astype(LOW)
    table = jnp.stack([first, second, third])
    grid = rows // BLOCK
    block = pl.BlockSpec((BLOCK, width), lambda i: (i, 0))
    low_scratch = lambda columns: pltpu.VMEM((rows, columns), LOW)
    return pl.pallas_call(
        functools.partial(layer_kernel, pieces),
        grid=(grid,),
        out_shape=(
            jax.ShapeDtypeStruct((rows, width), LOW),
            jax.ShapeDtypeStruct((rows, width), LOW),
            jax.ShapeDtypeStruct((copies, shard_rows, width), grad_type),
            jax.ShapeDtypeStruct((2, width), WIDE),
            jax.ShapeDtypeStruct((16, PAIR), WIDE),
        ),
        in_specs=[SCALARS, SCALARS, block, block, WHOLE, WHOLE, WHOLE, WHOLE, WHOLE],
        out_specs=(block, block, WHOLE, WHOLE, WHOLE),
        scratch_shapes=[
            low_scratch(width),
            low_scratch(width),
            low_scratch(width),
            low_scratch(width),
            low_scratch(ff),
            low_scratch(width),
            low_scratch(ff),
            low_scratch(ff),
            low_scratch(3 * width),
        ],
        compiler_params=pltpu.CompilerParams(vmem_limit_bytes=58 << 20),
        name="layer",
    )(
        lengths,
        attn_bias,
        tokens,
        cotangent,
        variates.astype(WIDE).reshape(rows // PAIR, PAIR),
        times.astype(WIDE).reshape(rows // PAIR, PAIR),
        table,
        gains,
        packed,
    )


def pack(qkv, out, gate_up, down):
    width = out.shape[-1]
    return jnp.concatenate(
        [
            jnp.swapaxes(qkv, 1, 2).reshape(-1, width),
            out,
            jnp.swapaxes(gate_up, 1, 2).reshape(-1, width),
            down,
        ],
        axis=0,
    )


def unpack(packed, attn_rows, ff_rows):
    width = packed.shape[-1]
    qkv = jnp.swapaxes(packed[: 3 * attn_rows].reshape(3, attn_rows, width), 1, 2)
    out = packed[3 * attn_rows : 4 * attn_rows]
    ends = 4 * attn_rows + 2 * ff_rows
    gate_up = jnp.swapaxes(packed[4 * attn_rows : ends].reshape(2, ff_rows, width), 1, 2)
    return qkv, out, gate_up, packed[ends:]


def newton_schulz(gram_mat):
    def product(left, right):
        return jnp.einsum(
            "mde,mef->mdf",
            left,
            right,
            precision=lax.Precision.HIGHEST,
            preferred_element_type=WIDE,
        )

    norm_val = jnp.sqrt(jnp.trace(gram_mat, axis1=1, axis2=2))[:, None, None] + NS_EPS
    gram_mat = gram_mat / (norm_val * norm_val)
    unit = jnp.eye(gram_mat.shape[-1], dtype=WIDE)[None]
    chain = None
    for turn_idx in range(NS_ITERS):
        poly_mat = COEF_A * unit + COEF_B * gram_mat + COEF_C * product(gram_mat, gram_mat)
        chain = poly_mat if chain is None else product(poly_mat, chain)
        if turn_idx < NS_ITERS - 1:
            gram_mat = product(product(poly_mat, gram_mat), poly_mat)
    return chain / norm_val


def adam_step(param, grad, moment, square):
    new_moment = BETA_ONE * moment + (1.0 - BETA_ONE) * grad
    new_square = BETA_TWO * square + (1.0 - BETA_TWO) * grad * grad
    corrected = new_moment / (1.0 - BETA_ONE**STEP)
    scaled = jnp.sqrt(new_square / (1.0 - BETA_TWO**STEP)) + ADAM_EPS
    return (new_moment, new_square, param - ADAM_RATE * corrected / scaled)


def body(
    tokens,
    cotangent,
    lengths,
    variates,
    times,
    weight_qkv,
    weight_out,
    weight_gate_up,
    weight_down,
    momentum_qkv,
    momentum_out,
    momentum_gate_up,
    momentum_down,
    gains,
    attn_bias,
    gain_moment,
    gain_square,
    bias_moment,
    bias_square,
):
    width = tokens.shape[1]
    heads = attn_bias.shape[1]
    attn_rows = weight_out.shape[0]
    ff_rows = weight_down.shape[0]
    fsdp = lax.axis_size("fsdp")
    ff = ff_rows * fsdp
    attn_width = attn_rows * fsdp
    weights = pack(weight_qkv, weight_out, weight_gate_up, weight_down)
    momenta = pack(momentum_qkv, momentum_out, momentum_gate_up, momentum_down)
    full = lax.all_gather(weights.astype(LOW), "fsdp", axis=0, tiled=False)
    aligned = attn_rows % 16 == 0 and ff_rows % 16 == 0
    pieces = offsets(attn_rows, ff_rows)
    if not aligned:
        full = jnp.concatenate(
            [full[:, s : s + n].reshape(1, fsdp * n, width) for s, n in pieces], axis=1
        )
    out_tokens, grad_tokens, grads, gain_rows, bias_rows = layer(
        tokens, cotangent, lengths, variates, times, full, gains, attn_bias, ff, WIDE
    )
    if not aligned:
        wholes = offsets(attn_width, ff)
        grads = jnp.concatenate(
            [grads[0, s : s + n].reshape(fsdp, n // fsdp, width) for s, n in wholes], axis=1
        )
    summed = lax.psum_scatter(grads, "fsdp", scatter_dimension=0, tiled=False)
    grad_rows = lax.psum(summed.astype(LOW), "ns").astype(WIDE)
    bias_part = jnp.sum(bias_rows, axis=1).reshape(2, 8)[:, :heads]
    grad_gains, grad_bias = lax.psum((gain_rows, bias_part), ("fsdp", "ns"))

    new_momenta = MUON_MU * momenta + grad_rows
    advance = grad_rows + MUON_MU * new_momenta
    parts = [advance[s : s + n] for s, n in pieces]
    grams = jnp.stack(
        [
            lax.dot_general(
                y,
                y,
                (((0,), (0,)), ((), ())),
                precision=lax.Precision.HIGHEST,
                preferred_element_type=WIDE,
            )
            for y in parts
        ]
    )
    factor = newton_schulz(lax.psum(grams, "fsdp"))
    shrink = 1.0 - MUON_RATE * MUON_DECAY
    scale_attn = MUON_RATE * 0.2 * math.sqrt(max(width, attn_width))
    scale_ff = MUON_RATE * 0.2 * math.sqrt(max(width, ff))
    turned = jnp.concatenate(
        [
            (scale_attn if i < 4 else scale_ff)
            * jnp.dot(
                y, factor[i], precision=lax.Precision.HIGHEST, preferred_element_type=WIDE
            )
            for i, y in enumerate(parts)
        ],
        axis=0,
    )
    new_weights = weights * shrink - turned
    new_gain_moment, new_gain_square, new_gains = adam_step(
        gains, grad_gains, gain_moment, gain_square
    )
    new_bias_moment, new_bias_square, new_bias = adam_step(
        attn_bias, grad_bias, bias_moment, bias_square
    )
    return (
        out_tokens,
        grad_tokens,
        *unpack(grad_rows, attn_rows, ff_rows),
        *unpack(new_momenta, attn_rows, ff_rows),
        *unpack(new_weights, attn_rows, ff_rows),
        grad_gains,
        new_gain_moment,
        new_gain_square,
        new_gains,
        grad_bias,
        new_bias_moment,
        new_bias_square,
        new_bias,
    )


def solution(mesh):
    rows = P(("fsdp", "ns"), None)
    line = P(("fsdp", "ns"))
    matrices = (P(None, None, "fsdp"), P("fsdp", None), P(None, None, "fsdp"), P("fsdp", None))
    return jax.shard_map(
        body,
        mesh=mesh,
        in_specs=(rows, rows, line, rows, line, *matrices, *matrices, *([P()] * 6)),
        out_specs=(rows, rows, *matrices, *matrices, *matrices, *([P()] * 8)),
        check_vma=False,
    )
```

```python
import functools
import math

import jax
import jax.numpy as jnp
from jax import lax
from jax.experimental import pallas as pl
from jax.experimental.pallas import tpu as pltpu
from jax.sharding import PartitionSpec as P

HEAD_DIM = 64
BUCKET = 64
TIME_SLOTS = 64
NS_ITERS = 5
STEP = 10

EPS_NORM = 1e-06
ROPE_BASE = 10000.0
NEG_FILL = -1000000000.0
COEF_A = 3.4445
COEF_B = -4.775
COEF_C = 2.0315
NS_EPS = 1e-07
MUON_MU = 0.95
MUON_RATE = 0.25
MUON_DECAY = 0.01
ADAM_RATE = 0.8
BETA_ONE = 0.9
BETA_TWO = 0.95
ADAM_EPS = 1e-08

LOW = jnp.bfloat16
WIDE = jnp.float32
BLOCK = 256
PAIR = 2 * BUCKET
LANES = 2 * HEAD_DIM
STATS = 24
WHOLE = pl.BlockSpec(memory_space=pltpu.VMEM)
SCALARS = pl.BlockSpec(memory_space=pltpu.SMEM)


def mul_nn(left, right):
    return lax.dot_general(left, right, (((1,), (0,)), ((), ())), preferred_element_type=WIDE)


def mul_nt(left, right):
    return lax.dot_general(left, right, (((1,), (1,)), ((), ())), preferred_element_type=WIDE)


def mul_tn(left, right):
    return lax.dot_general(left, right, (((0,), (0,)), ((), ())), preferred_element_type=WIDE)


def offsets(attn_rows, ff_rows):
    counts = [attn_rows] * 4 + [ff_rows] * 3
    starts = [sum(counts[:i]) for i in range(7)]
    return list(zip(starts, counts))


def layer_kernel(
    pieces,
    lengths,
    bias,
    tok_ref,
    cot_ref,
    var_ref,
    time_ref,
    table_ref,
    gain_ref,
    w_ref,
    out_ref,
    gtok_ref,
    grad_ref,
    stat_ref,
    n1_s,
    n2_s,
    att_s,
    gml_s,
    hid_s,
    glow_s,
    gg_s,
    gu_s,
    gqkv_s,
):
    step = pl.program_id(0)
    rows, width = tok_ref.shape
    heads = bias.shape[1]
    here = pl.ds(pl.multiple_of(step * rows, rows), rows)

    def weight(first, last):
        parts = []
        for i in range(first, last):
            start, count = pieces[i]
            part = w_ref[:, start : start + count, :]
            parts.append(part.reshape(part.shape[0] * count, width))
        return parts[0] if len(parts) == 1 else jnp.concatenate(parts, axis=0)

    @pl.when(step == 0)
    def _():
        stat_ref[...] = jnp.zeros_like(stat_ref)

    lane = lax.broadcasted_iota(jnp.int32, (1, LANES), 1)
    low_head = lane < HEAD_DIM
    low_half = lane % HEAD_DIM < HEAD_DIM // 2
    per_block = rows // PAIR
    var_rows = var_ref[pl.ds(step * per_block, per_block), :]
    time_rows = time_ref[pl.ds(step * per_block, per_block), :]
    filler = jnp.zeros((8 - 2 * per_block, PAIR), WIDE)
    columns = jnp.concatenate([var_rows, time_rows, filler], axis=0).T
    slots = lax.broadcasted_iota(jnp.int32, (1, TIME_SLOTS), 1).astype(WIDE)
    hot = jnp.concatenate(
        [(columns[:, per_block + p : per_block + p + 1] == slots) for p in range(per_block)], axis=0
    ).astype(LOW)
    looked = mul_nn(hot, table_ref[0]) + mul_nn(hot, table_ref[1]) + mul_nn(hot, table_ref[2])
    cosine = looked[:, :LANES]
    sine = looked[:, LANES:]

    def swapped(values):
        half = HEAD_DIM // 2
        return jnp.where(
            low_half, pltpu.roll(values, LANES - half, 1), pltpu.roll(values, half, 1)
        )

    gain_one = gain_ref[0:1, :]
    gain_two = gain_ref[1:2, :]
    tokens = tok_ref[...].astype(WIDE)
    scale_one = lax.rsqrt(jnp.mean(tokens * tokens, axis=-1, keepdims=True) + EPS_NORM)
    unit_one = tokens * scale_one
    normed_one = (unit_one * gain_one).astype(LOW)
    n1_s[here, :] = normed_one
    qkv = mul_nt(normed_one, weight(0, 3))

    query_scale = HEAD_DIM ** (-0.5)
    units = []
    attended = []
    row_id = lax.broadcasted_iota(jnp.int32, (PAIR, 1), 0)
    lane_id = lax.broadcasted_iota(jnp.int32, (1, PAIR), 1)
    same_bucket = (row_id < BUCKET) == (lane_id < BUCKET)
    masks = []
    live_cols = []
    for p in range(per_block):
        first = lengths[(step * per_block + p) * 2]
        second = lengths[(step * per_block + p) * 2 + 1]
        live_key = lane_id % BUCKET < jnp.where(lane_id < BUCKET, first, second)
        live_cols.append(row_id % BUCKET < jnp.where(row_id < BUCKET, first, second))
        mask = same_bucket & live_key
        same_var = columns[:, p : p + 1] == var_rows[p : p + 1, :]
        masks.append((mask, same_var))

    for hp in range(heads // 2):
        cols = slice(hp * LANES, (hp + 1) * LANES)
        q = qkv[:, cols]
        k = qkv[:, width + hp * LANES : width + (hp + 1) * LANES]
        v = qkv[:, 2 * width + hp * LANES : 2 * width + (hp + 1) * LANES].astype(LOW)
        q = ((q * cosine + swapped(q) * sine) * query_scale).astype(LOW)
        k = (k * cosine + swapped(k) * sine).astype(LOW)
        q_first = jnp.where(low_head, q, jnp.zeros_like(q))
        q_second = jnp.where(low_head, jnp.zeros_like(q), q)
        att_pairs = []
        for p in range(per_block):
            part = slice(p * PAIR, (p + 1) * PAIR)
            mask, same_var = masks[p]
            q2 = jnp.concatenate([q_first[part], q_second[part]], axis=0)
            kp = k[part]
            vp = v[part]
            raw = mul_nt(q2, kp)
            halves = []
            for j in range(2):
                h = 2 * hp + j
                biased = raw[j * PAIR : (j + 1) * PAIR] + jnp.where(
                    same_var, bias[0, h], bias[1, h]
                )
                halves.append(jnp.where(mask, biased, NEG_FILL))
            scores = jnp.concatenate(halves, axis=0)
            top = jnp.max(scores, axis=-1, keepdims=True)
            exponent = jnp.exp(scores - top)
            probs = exponent / jnp.sum(exponent, axis=-1, keepdims=True)
            probs_low = probs.astype(LOW)
            both = mul_nn(probs_low, vp)
            att_pairs.append(jnp.where(low_head, both[:PAIR], both[PAIR:]))
            units.append((hp, p, q2, kp, vp, probs, probs_low))
        attended.append(jnp.concatenate(att_pairs, axis=0).astype(LOW))
    attended = jnp.concatenate(attended, axis=1)
    att_s[here, :] = attended
    w_out = weight(3, 4)
    mid = tokens + mul_nn(attended, w_out)
    scale_two = lax.rsqrt(jnp.mean(mid * mid, axis=-1, keepdims=True) + EPS_NORM)
    unit_two = mid * scale_two
    normed_two = (unit_two * gain_two).astype(LOW)
    n2_s[here, :] = normed_two
    w_gate = weight(4, 5)
    w_up = weight(5, 6)
    w_down = weight(6, 7)
    gate = mul_nt(normed_two, w_gate)
    up = mul_nt(normed_two, w_up)
    sig = 1.0 / (1.0 + jnp.exp(-gate))
    silu = gate * sig
    hidden = (silu * up).astype(LOW)
    hid_s[here, :] = hidden
    out_ref[...] = (mid + mul_nn(hidden, w_down)).astype(LOW)

    live_row = jnp.concatenate(live_cols, axis=0)
    g_out = jnp.where(live_row, cot_ref[...].astype(WIDE), 0.0)
    g_low = g_out.astype(LOW)
    glow_s[here, :] = g_low
    g_hidden = mul_nt(g_low, w_down)
    g_gate = (g_hidden * up * sig * (1.0 + gate * (1.0 - sig))).astype(LOW)
    g_up = (g_hidden * silu).astype(LOW)
    gg_s[here, :] = g_gate
    gu_s[here, :] = g_up
    e_two = mul_nn(g_gate, w_gate) + mul_nn(g_up, w_up)
    stat_ref[1:2, :] += jnp.sum(e_two * unit_two, axis=0, keepdims=True)
    scaled = e_two * gain_two
    g_mid = g_out + scale_two * (
        scaled - unit_two * jnp.mean(scaled * unit_two, axis=-1, keepdims=True)
    )
    g_mid_low = g_mid.astype(LOW)
    gml_s[here, :] = g_mid_low
    g_att = mul_nt(g_mid_low, w_out).astype(LOW)

    parts_q = [[None] * per_block for _ in range(heads // 2)]
    parts_k = [[None] * per_block for _ in range(heads // 2)]
    parts_v = [[None] * per_block for _ in range(heads // 2)]
    for hp, p, q2, kp, vp, probs, probs_low in units:
        part = slice(p * PAIR, (p + 1) * PAIR)
        mask, same_var = masks[p]
        ga = g_att[part, hp * LANES : (hp + 1) * LANES]
        ga2 = jnp.concatenate(
            [
                jnp.where(low_head, ga, jnp.zeros_like(ga)),
                jnp.where(low_head, jnp.zeros_like(ga), ga),
            ],
            axis=0,
        )
        g_probs = mul_nt(ga2, vp)
        row_dot = jnp.sum(probs * g_probs, axis=-1, keepdims=True)
        g_scores = probs * (g_probs - row_dot)
        for j in range(2):
            h = 2 * hp + j
            mine = g_scores[j * PAIR : (j + 1) * PAIR]
            stat_ref[8 + h : 9 + h, :PAIR] += jnp.sum(
                jnp.where(same_var, mine, 0.0), axis=0, keepdims=True
            )
            stat_ref[16 + h : 17 + h, :PAIR] += jnp.sum(
                jnp.where(same_var, 0.0, mine), axis=0, keepdims=True
            )
        low_scores = g_scores.astype(LOW)
        both = mul_nn(low_scores, kp)
        parts_q[hp][p] = jnp.where(low_head, both[:PAIR], both[PAIR:])
        parts_k[hp][p] = mul_tn(low_scores, q2)
        parts_v[hp][p] = mul_tn(probs_low, ga2)
    g_q = []
    g_k = []
    g_v = []
    for hp in range(heads // 2):
        dq = jnp.concatenate(parts_q[hp], axis=0)
        dk = jnp.concatenate(parts_k[hp], axis=0)
        g_q.append(((dq * cosine - swapped(dq) * sine) * query_scale).astype(LOW))
        g_k.append((dk * cosine - swapped(dk) * sine).astype(LOW))
        g_v.append(jnp.concatenate(parts_v[hp], axis=0).astype(LOW))
    g_qkv = jnp.concatenate(g_q + g_k + g_v, axis=1)
    gqkv_s[here, :] = g_qkv
    e_one = mul_nn(g_qkv, weight(0, 3))
    stat_ref[0:1, :] += jnp.sum(e_one * unit_one, axis=0, keepdims=True)
    scaled = e_one * gain_one
    gtok_ref[...] = (
        g_mid
        + scale_one * (scaled - unit_one * jnp.mean(scaled * unit_one, axis=-1, keepdims=True))
    ).astype(LOW)

    @pl.when(step == pl.num_programs(0) - 1)
    def _():
        def put(index, left, right):
            start, count = pieces[index]
            grad_ref[:, start : start + count, :] = (
                mul_tn(left, right)
                .reshape(grad_ref.shape[0], count, width)
                .astype(grad_ref.dtype)
            )

        for j in range(3):
            put(j, gqkv_s[:, j * width : (j + 1) * width], n1_s[...])
        put(3, att_s[...], gml_s[...])
        put(4, gg_s[...], n2_s[...])
        put(5, gu_s[...], n2_s[...])
        put(6, hid_s[...], glow_s[...])


def layer(tokens, cotangent, lengths, variates, times, packed, gains, attn_bias, ff, grad_type):
    rows, width = tokens.shape
    heads = attn_bias.shape[1]
    copies, shard_rows, _ = packed.shape
    pieces = offsets(heads * HEAD_DIM // copies, ff // copies)
    half = HEAD_DIM // 2
    frequency = ROPE_BASE ** (-2.0 * jnp.arange(half, dtype=WIDE) / HEAD_DIM)
    angles = jnp.arange(TIME_SLOTS, dtype=WIDE)[:, None] * frequency[None, :]
    cosine, sine = jnp.cos(angles), jnp.sin(angles)
    table = jnp.concatenate([cosine] * 4 + [-sine, sine, -sine, sine], axis=1)
    first = table.astype(LOW)
    rest = table - first.astype(WIDE)
    second = rest.astype(LOW)
    third = (rest - second.astype(WIDE)).astype(LOW)
    table = jnp.stack([first, second, third])
    grid = rows // BLOCK
    block = pl.BlockSpec((BLOCK, width), lambda i: (i, 0))
    low_scratch = lambda columns: pltpu.VMEM((rows, columns), LOW)
    return pl.pallas_call(
        functools.partial(layer_kernel, pieces),
        grid=(grid,),
        out_shape=(
            jax.ShapeDtypeStruct((rows, width), LOW),
            jax.ShapeDtypeStruct((rows, width), LOW),
            jax.ShapeDtypeStruct((copies, shard_rows, width), grad_type),
            jax.ShapeDtypeStruct((STATS, width), WIDE),
        ),
        in_specs=[SCALARS, SCALARS, block, block, WHOLE, WHOLE, WHOLE, WHOLE, WHOLE],
        out_specs=(block, block, WHOLE, WHOLE),
        scratch_shapes=[
            low_scratch(width),
            low_scratch(width),
            low_scratch(width),
            low_scratch(width),
            low_scratch(ff),
            low_scratch(width),
            low_scratch(ff),
            low_scratch(ff),
            low_scratch(3 * width),
        ],
        compiler_params=pltpu.CompilerParams(vmem_limit_bytes=58 << 20),
        name="layer",
    )(
        lengths,
        attn_bias,
        tokens,
        cotangent,
        variates.astype(WIDE).reshape(rows // PAIR, PAIR),
        times.astype(WIDE).reshape(rows // PAIR, PAIR),
        table,
        gains,
        packed,
    )


def pack(qkv, out, gate_up, down):
    width = out.shape[-1]
    return jnp.concatenate(
        [
            jnp.swapaxes(qkv, 1, 2).reshape(-1, width),
            out,
            jnp.swapaxes(gate_up, 1, 2).reshape(-1, width),
            down,
        ],
        axis=0,
    )


def unpack(packed, attn_rows, ff_rows):
    width = packed.shape[-1]
    qkv = jnp.swapaxes(packed[: 3 * attn_rows].reshape(3, attn_rows, width), 1, 2)
    out = packed[3 * attn_rows : 4 * attn_rows]
    ends = 4 * attn_rows + 2 * ff_rows
    gate_up = jnp.swapaxes(packed[4 * attn_rows : ends].reshape(2, ff_rows, width), 1, 2)
    return qkv, out, gate_up, packed[ends:]


def newton_schulz(gram_mat):
    def product(left, right):
        return jnp.einsum(
            "mde,mef->mdf",
            left,
            right,
            precision=lax.Precision.HIGHEST,
            preferred_element_type=WIDE,
        )

    norm_val = jnp.sqrt(jnp.trace(gram_mat, axis1=1, axis2=2))[:, None, None] + NS_EPS
    gram_mat = gram_mat / (norm_val * norm_val)
    unit = jnp.eye(gram_mat.shape[-1], dtype=WIDE)[None]
    chain = None
    for turn_idx in range(NS_ITERS):
        poly_mat = COEF_A * unit + COEF_B * gram_mat + COEF_C * product(gram_mat, gram_mat)
        chain = poly_mat if chain is None else product(poly_mat, chain)
        if turn_idx < NS_ITERS - 1:
            gram_mat = product(product(poly_mat, gram_mat), poly_mat)
    return chain / norm_val


def adam_step(param, grad, moment, square):
    new_moment = BETA_ONE * moment + (1.0 - BETA_ONE) * grad
    new_square = BETA_TWO * square + (1.0 - BETA_TWO) * grad * grad
    corrected = new_moment / (1.0 - BETA_ONE**STEP)
    scaled = jnp.sqrt(new_square / (1.0 - BETA_TWO**STEP)) + ADAM_EPS
    return (new_moment, new_square, param - ADAM_RATE * corrected / scaled)


DEPTH, ACROSS = 4, 2
SIDES, CORES = 2, 2
TURNS = (2, 1, 3, 0)
OWNERS = (
    (2, 0, 0, 0),
    (2, 1, 0, 1),
    (1, 1, 0, 0),
    (2, 1, 1, 0),
    (2, 0, 1, 1),
    (1, 0, 0, 1),
    (1, 1, 1, 0),
)


def place():
    f = lax.axis_index("fsdp")
    n = lax.axis_index("ns")
    return f // ACROSS, f % ACROSS, n // CORES, n % CORES


def device(z, x, y, c):
    return (z * ACROSS + x, y * CORES + c)


def remote(src, dst, send_sem, recv_sem, where):
    return pltpu.make_async_remote_copy(
        src_ref=src,
        dst_ref=dst,
        send_sem=send_sem,
        recv_sem=recv_sem,
        device_id=where,
        device_id_type=pl.DeviceIdType.MESH,
    )


def greet(where):
    pl.semaphore_signal(
        pltpu.get_barrier_semaphore(),
        inc=1,
        device_id=where,
        device_id_type=pl.DeviceIdType.MESH,
    )


def gather_kernel(
    pieces,
    qkv_ref,
    out_ref,
    gate_up_ref,
    down_ref,
    full,
    up_send,
    down_send,
    x_send,
    sib_send,
    below_recv,
    above_recv,
    x_recv,
    sib_recv,
):
    z, x, y, c = place()
    me = z * ACROSS + x
    rows = full.shape[1]
    half = rows // 2
    mine = pl.ds(pl.multiple_of(c * half, 16), half)
    sibling = device(z, x, y, 1 - c)
    beside = device(z, 1 - x, y, c)
    upper = device(z + 1, x, y, c)
    lower = device(z - 1, x, y, c)
    greet(sibling)
    greet(beside)

    @pl.when(z < DEPTH - 1)
    def _():
        greet(upper)

    @pl.when(z > 0)
    def _():
        greet(lower)

    def put(index, value):
        start, count = pieces[index]
        full[me, start : start + count, :] = value.astype(LOW)

    for j in range(3):
        put(j, qkv_ref[j].T)
    put(3, out_ref[...])
    put(4, gate_up_ref[0].T)
    put(5, gate_up_ref[1].T)
    put(6, down_ref[...])
    near = 2 + (z < DEPTH - 1).astype(jnp.int32) + (z > 0).astype(jnp.int32)
    pl.semaphore_wait(pltpu.get_barrier_semaphore(), near)

    def part(shard):
        return full.at[shard, mine]

    def shard_at(rel):
        return me + rel * ACROSS

    def up_copy(d):
        return remote(
            part(shard_at(-d)), part(shard_at(-d)), up_send.at[d], below_recv.at[d], upper
        )

    def down_copy(d):
        return remote(
            part(shard_at(d)), part(shard_at(d)), down_send.at[d], above_recv.at[d], lower
        )

    def x_copy(rel):
        return remote(
            part(shard_at(rel)), part(shard_at(rel)), x_send.at[rel + 3], x_recv.at[rel + 3], beside
        )

    def other_at(rel):
        return (z + rel) * ACROSS + 1 - x

    def sib_copy(rel):
        shard = shard_at(rel)
        return remote(
            part(shard), part(shard), sib_send.at[0, rel + 3], sib_recv.at[0, rel + 3], sibling
        )

    def sib_other(rel):
        shard = other_at(rel)
        return remote(
            part(shard), part(shard), sib_send.at[1, rel + 3], sib_recv.at[1, rel + 3], sibling
        )

    has_up = z < DEPTH - 1
    has_down = z > 0

    def exists(rel):
        return (z + rel >= 0) & (z + rel < DEPTH)

    @pl.when(has_up)
    def _():
        up_copy(0).start()

    @pl.when(has_down)
    def _():
        down_copy(0).start()

    x_copy(0).start()
    for d in range(1, DEPTH):

        @pl.when(exists(-d))
        def _():
            remote(
                part(shard_at(-d)), part(shard_at(-d)), up_send.at[d], below_recv.at[d - 1], lower
            ).wait_recv()

            if d < DEPTH - 1:

                @pl.when(has_up)
                def _():
                    up_copy(d).start()

            x_copy(-d).start()
            sib_copy(-d).start()

        @pl.when(exists(d))
        def _():
            remote(
                part(shard_at(d)), part(shard_at(d)), down_send.at[d], above_recv.at[d - 1], upper
            ).wait_recv()

            if d < DEPTH - 1:

                @pl.when(has_down)
                def _():
                    down_copy(d).start()

            x_copy(d).start()
            sib_copy(d).start()

    def from_beside(rel):
        remote(
            part(other_at(rel)), part(other_at(rel)), x_send.at[rel + 3], x_recv.at[rel + 3], beside
        ).wait_recv()
        sib_other(rel).start()

    from_beside(0)
    for d in range(1, DEPTH):
        for rel in (-d, d):

            @pl.when(exists(rel))
            def _():
                from_beside(rel)

    theirs = pl.ds(pl.multiple_of((1 - c) * half, 16), half)

    def sib_done(kind, rel, shard):
        remote(
            full.at[shard, theirs],
            full.at[shard, theirs],
            sib_send.at[kind, rel + 3],
            sib_recv.at[kind, rel + 3],
            sibling,
        ).wait_recv()

    for rel in range(1 - DEPTH, DEPTH):

        @pl.when(exists(rel))
        def _():
            if rel != 0:
                sib_done(0, rel, shard_at(rel))
                sib_copy(rel).wait_send()
            sib_done(1, rel, other_at(rel))
            sib_other(rel).wait_send()
            x_copy(rel).wait_send()

    for d in range(DEPTH - 1):

        @pl.when(exists(-d) & has_up)
        def _():
            up_copy(d).wait_send()

        @pl.when(exists(d) & has_down)
        def _():
            down_copy(d).wait_send()


def gather(qkv, out, gate_up, down):
    attn_rows, width = out.shape
    pieces = offsets(attn_rows, down.shape[0])
    dma = pltpu.SemaphoreType.DMA
    return pl.pallas_call(
        functools.partial(gather_kernel, pieces),
        out_shape=jax.ShapeDtypeStruct(
            (DEPTH * ACROSS, pieces[-1][0] + pieces[-1][1], width), LOW
        ),
        in_specs=[WHOLE] * 4,
        out_specs=WHOLE,
        scratch_shapes=[
            dma((DEPTH,)),
            dma((DEPTH,)),
            dma((2 * DEPTH - 1,)),
            dma((2, 2 * DEPTH - 1)),
            dma((DEPTH,)),
            dma((DEPTH,)),
            dma((2 * DEPTH - 1,)),
            dma((2, 2 * DEPTH - 1)),
        ],
        compiler_params=pltpu.CompilerParams(
            vmem_limit_bytes=32 << 20, collective_id=0, has_side_effects=True
        ),
        name="gather",
    )(qkv, out, gate_up, down)


def halves(value):
    high = value.astype(LOW)
    return high, (value - high.astype(WIDE)).astype(LOW)


def mul_wide(left, right):
    columns = right.shape[1]
    left_high, left_low = halves(left)
    right_high, right_low = halves(right)
    first = mul_nn(left_high, jnp.concatenate([right_high, right_low], axis=1))
    return first[:, :columns] + (first[:, columns:] + mul_nn(left_low, right_high))


def gram_wide(value):
    high, low = halves(value)
    cross = mul_tn(high, low)
    return mul_tn(high, high) + (cross + cross.T)


def reduce_kernel(
    pieces,
    grad_ref,
    stat_ref,
    mqkv_ref,
    mout_ref,
    mgate_up_ref,
    mdown_ref,
    grows_ref,
    xrows_ref,
    total_ref,
    in_zero,
    acc_zero,
    in_one,
    acc_one,
    in_two,
    acc_two,
    in_three,
    momenta,
    advance,
    y_attn,
    y_ff,
    x_attn,
    x_ff,
    gram_s,
    chain_s,
    stat_in,
    stat_acc,
    stat_line,
    send_zero,
    send_one,
    send_two,
    send_three,
    recv_zero,
    recv_one,
    recv_two,
    recv_three,
    stat_send,
    stat_recv,
    adv_send,
    adv_recv,
    row_send,
    row_recv,
    x_send,
    x_recv,
    fan_send,
    fan_recv,
):
    z, x, y, c = place()
    shard = z * ACROSS + x
    rows = grad_ref.shape[2]
    width = grad_ref.shape[3]
    half, quarter = rows // 2, rows // 4
    sibling = device(z, x, y, 1 - c)
    facing = device(z, x, 1 - y, c)
    corner = device(z, x, 1 - y, 1 - c)
    beside = device(z, 1 - x, y, c)
    world = DEPTH * ACROSS * SIDES * CORES
    rank = shard * (SIDES * CORES) + y * CORES + c

    def hello(i, carry):
        other = lax.rem(rank + 1 + i, world)
        greet((other // (SIDES * CORES), lax.rem(other, SIDES * CORES)))
        return carry

    lax.fori_loop(0, world - 1, hello, 0)
    pl.semaphore_wait(pltpu.get_barrier_semaphore(), world - 1)

    keep_half = pl.ds(pl.multiple_of(c * half, 16), half)
    give_half = pl.ds(pl.multiple_of((1 - c) * half, 16), half)
    keep_quarter = pl.ds(pl.multiple_of(y * quarter, 16), quarter)
    give_quarter = pl.ds(pl.multiple_of((1 - y) * quarter, 16), quarter)
    line = [lax.rem(z + k, DEPTH) for k in range(DEPTH)]

    def zero(k):
        return remote(
            grad_ref.at[line[k], :, give_half],
            in_zero.at[k],
            send_zero.at[k],
            recv_zero.at[k],
            sibling,
        )

    def one_y(k):
        return remote(
            acc_zero.at[k, :, give_quarter],
            in_one.at[k, :, pl.ds(0, quarter)],
            send_one.at[k],
            recv_one.at[k],
            facing,
        )

    def two_x(k):
        return remote(
            acc_one.at[k, 1 - x, pl.ds(0, quarter)],
            in_two.at[k],
            send_two.at[k],
            recv_two.at[k],
            beside,
        )

    def one_x(k):
        return remote(
            acc_zero.at[k, 1 - x], in_one.at[k, 0], send_one.at[k], recv_one.at[k], beside
        )

    def two_y(k):
        return remote(
            acc_one.at[k, 0, give_quarter],
            in_two.at[k],
            send_two.at[k],
            recv_two.at[k],
            facing,
        )

    def three(k):
        return remote(
            acc_two.at[k],
            in_three.at[k],
            send_three.at[k],
            recv_three.at[k],
            device(line[k], x, y, c),
        )

    for k in TURNS:
        zero(k).start()

    def stat_copy(step, src, where):
        return remote(src, stat_in.at[step], stat_send.at[step], stat_recv.at[step], where)

    stat_copy(0, stat_ref, sibling).start()

    def put(index, value):
        start, count = pieces[index]
        momenta[start : start + count, :] = value

    for j in range(3):
        put(j, mqkv_ref[j].T)
    put(3, mout_ref[...])
    put(4, mgate_up_ref[0].T)
    put(5, mgate_up_ref[1].T)
    put(6, mdown_ref[...])

    stat_copy(0, stat_ref, sibling).wait()
    stat_acc[0] = stat_ref[...] + stat_in[0]
    stat_copy(1, stat_acc.at[0], facing).start()

    def add(left, right):
        return left.astype(WIDE) + right.astype(WIDE)

    for t in range(DEPTH + 2):
        if t < DEPTH:
            k = TURNS[t]
            zero(k).wait_recv()
            acc_zero[k] = add(grad_ref[line[k], :, keep_half], in_zero[k]).astype(LOW)

            @pl.when(c == 0)
            def _():
                one_y(k).start()

            @pl.when(c == 1)
            def _():
                one_x(k).start()

        if 1 <= t <= DEPTH:
            k = TURNS[t - 1]

            @pl.when(c == 0)
            def _():
                one_y(k).wait_recv()
                acc_one[k, :, :quarter] = add(
                    acc_zero[k, :, keep_quarter], in_one[k, :, :quarter]
                ).astype(LOW)
                two_x(k).start()

            @pl.when(c == 1)
            def _():
                one_x(k).wait_recv()
                acc_one[k, 0] = add(acc_zero[k, x], in_one[k, 0]).astype(LOW)
                two_y(k).start()

        if t == 1:
            stat_copy(1, stat_acc.at[0], facing).wait()
            stat_acc[1] = stat_acc[0] + stat_in[1]
            stat_copy(2, stat_acc.at[1], beside).start()
        if t == 3:
            stat_copy(2, stat_acc.at[1], beside).wait()
            stat_acc[2] = stat_acc[1] + stat_in[2]
            stat_line[z] = stat_acc[2]
            for j in range(1, DEPTH):
                remote(
                    stat_acc.at[2],
                    stat_line.at[z],
                    stat_send.at[2 + j],
                    stat_recv.at[2 + j],
                    device(line[j], x, y, c),
                ).start()

        if t >= 2:
            k = TURNS[t - 2]

            @pl.when(c == 0)
            def _():
                two_x(k).wait_recv()
                acc_two[k] = add(acc_one[k, x, :quarter], in_two[k]).astype(LOW)

            @pl.when(c == 1)
            def _():
                two_y(k).wait_recv()
                acc_two[k] = add(acc_one[k, 0, keep_quarter], in_two[k]).astype(LOW)

            if k != 0:
                three(k).start()

    total = acc_two[0].astype(WIDE)
    for k in range(1, DEPTH):
        three(k).wait_recv()
        total = total + in_three[k].astype(WIDE)
    part = 2 * c + y
    here = pl.ds(pl.multiple_of(part * quarter, 16), quarter)
    old = momenta[here, :]
    advance[...] = total + MUON_MU * (MUON_MU * old + total)

    def segments(index):
        found = []
        for m, (start, count) in enumerate(pieces):
            first = max(start, index * quarter)
            last = min(start + count, (index + 1) * quarter)
            if first < last:
                found.append((m, first - index * quarter, first - start, last - first))
        return found

    def owned(m):
        oz, ox, oy, oc = OWNERS[m]
        return (z == oz) & (x == ox) & (y == oy) & (c == oc)

    def stage(m):
        return y_attn if m < 4 else y_ff

    def adv_copy(index, i):
        m, first, to, count = segments(index)[i]
        return remote(
            advance.at[pl.ds(first, count)],
            stage(m).at[shard, pl.ds(to, count)],
            adv_send.at[i],
            adv_recv.at[0],
            device(*OWNERS[m]),
        )

    for index in range(4):
        for i, (m, first, to, count) in enumerate(segments(index)):

            @pl.when((part == index) & jnp.logical_not(owned(m)))
            def _():
                adv_copy(index, i).start()

            @pl.when((part == index) & owned(m))
            def _():
                pltpu.make_async_copy(
                    advance.at[pl.ds(first, count)],
                    stage(m).at[shard, pl.ds(to, count)],
                    adv_recv.at[0],
                ).start()

    grows_ref[here, :] = total.astype(LOW)

    def row_copy(j, where):
        return remote(
            grows_ref.at[here], grows_ref.at[here], row_send.at[j], row_recv.at[j], where
        )

    mates = (sibling, facing, corner)
    for j, where in enumerate(mates):
        row_copy(j, where).start()

    attn_owner = functools.reduce(jnp.logical_or, [owned(m) for m in range(4)])
    ff_owner = functools.reduce(jnp.logical_or, [owned(m) for m in range(4, 7)])

    def arrived(buffer):
        pltpu.make_async_copy(buffer, buffer, adv_recv.at[0]).wait()

    @pl.when(attn_owner)
    def _():
        arrived(y_attn)
        value = y_attn[...].reshape(-1, width)
        gram_s[...] = gram_wide(value)

    @pl.when(ff_owner)
    def _():
        arrived(y_ff)
        value = y_ff[...].reshape(-1, width)
        gram_s[...] = gram_wide(value)

    @pl.when(attn_owner | ff_owner)
    def _():
        row_id = lax.broadcasted_iota(jnp.int32, (width, width), 0)
        col_id = lax.broadcasted_iota(jnp.int32, (width, width), 1)
        unit = row_id == col_id
        gram_mat = gram_s[...]
        trace = jnp.sum(jnp.where(unit, gram_mat, 0.0), keepdims=True)
        norm = jnp.sqrt(trace) + NS_EPS
        inverse = 1.0 / norm
        diagonal = jnp.where(unit, COEF_A, 0.0)
        gram_mat = gram_mat * (inverse * inverse)

        def poly(value):
            return diagonal + COEF_B * value + COEF_C * mul_wide(value, value)

        step_mat = poly(gram_mat)
        gram_s[...] = mul_wide(mul_wide(gram_mat, step_mat), step_mat)
        chain_s[...] = step_mat * inverse

        def turn(i, carry):
            now = gram_s[...]
            step_now = poly(now)
            both = mul_wide(jnp.concatenate([now, chain_s[...]], axis=0), step_now)
            chain_s[...] = both[width:]
            gram_s[...] = mul_wide(both[:width], step_now)
            return carry

        lax.fori_loop(0, NS_ITERS - 2, turn, 0)
        chain_s[...] = mul_wide(chain_s[...], poly(gram_s[...]))

    @pl.when(attn_owner)
    def _():
        value = y_attn[...].reshape(-1, width)
        x_attn[...] = mul_wide(value, chain_s[...]).astype(LOW).reshape(x_attn.shape)

    @pl.when(ff_owner)
    def _():
        value = y_ff[...].reshape(-1, width)
        x_ff[...] = mul_wide(value, chain_s[...]).astype(LOW).reshape(x_ff.shape)

    chips = DEPTH * ACROSS * SIDES

    def x_copy(m, i):
        start, count = pieces[m]
        source = x_attn if m < 4 else x_ff
        to = i // SIDES
        return remote(
            source.at[to],
            xrows_ref.at[pl.ds(start, count)],
            x_send.at[i],
            x_recv.at[m],
            (to, lax.rem(i, SIDES) * CORES + OWNERS[m][3]),
        )

    for m in range(7):
        start, count = pieces[m]
        source = x_attn if m < 4 else x_ff

        @pl.when(owned(m))
        def _():
            mine = shard * SIDES + y

            def send(i, carry):
                x_copy(m, lax.rem(mine + i, chips)).start()
                return carry

            lax.fori_loop(1, chips, send, 0)
            pltpu.make_async_copy(
                source.at[shard], xrows_ref.at[pl.ds(start, count)], x_recv.at[m]
            ).start()

    for j in range(1, DEPTH):
        remote(
            stat_acc.at[2],
            stat_line.at[lax.rem(z + DEPTH - j, DEPTH)],
            stat_send.at[2 + j],
            stat_recv.at[2 + j],
            device(line[j], x, y, c),
        ).wait()
    total_ref[...] = (stat_line[0] + stat_line[1]) + (stat_line[2] + stat_line[3])
    for j, (dy, dc) in enumerate(((0, 1), (1, 0), (1, 1))):
        source = 2 * (c ^ dc) + (y ^ dy)
        there = pl.ds(pl.multiple_of(source * quarter, 16), quarter)
        remote(
            grows_ref.at[here], grows_ref.at[there], row_send.at[j], row_recv.at[j], mates[j]
        ).wait_recv()

    def fan_copy(m):
        start, count = pieces[m]
        rows_m = xrows_ref.at[pl.ds(start, count)]
        return remote(rows_m, rows_m, fan_send.at[m], fan_recv.at[m], sibling)

    for m in range(7):
        start, count = pieces[m]

        @pl.when(c == OWNERS[m][3])
        def _():
            rows_m = xrows_ref.at[pl.ds(start, count)]
            pltpu.make_async_copy(rows_m, rows_m, x_recv.at[m]).wait()
            fan_copy(m).start()

    for m in range(7):

        @pl.when(c != OWNERS[m][3])
        def _():
            fan_copy(m).wait_recv()

    for m in range(7):

        @pl.when(c == OWNERS[m][3])
        def _():
            fan_copy(m).wait_send()

        @pl.when(owned(m))
        def _():
            mine = shard * SIDES + y

            def sent(i, carry):
                x_copy(m, lax.rem(mine + i, chips)).wait_send()
                return carry

            lax.fori_loop(1, chips, sent, 0)

    for j, where in enumerate(mates):
        row_copy(j, where).wait_send()
    for index in range(4):
        for i, (m, first, to, count) in enumerate(segments(index)):

            @pl.when((part == index) & jnp.logical_not(owned(m)))
            def _():
                adv_copy(index, i).wait_send()

    for k in TURNS:
        zero(k).wait_send()
        if k != 0:
            three(k).wait_send()

        @pl.when(c == 0)
        def _():
            one_y(k).wait_send()
            two_x(k).wait_send()

        @pl.when(c == 1)
        def _():
            one_x(k).wait_send()
            two_y(k).wait_send()


def reduce_and_turn(grads, stats, qkv, out, gate_up, down):
    attn_rows, width = out.shape
    ff_rows = down.shape[0]
    pieces = offsets(attn_rows, ff_rows)
    rows = grads.shape[1]
    half, quarter = rows // 2, rows // 4
    shards = DEPTH * ACROSS
    low = lambda *shape: pltpu.VMEM((*shape, width), LOW)
    wide = lambda *shape: pltpu.VMEM((*shape, width), WIDE)
    dma = lambda *shape: pltpu.SemaphoreType.DMA(shape)
    return pl.pallas_call(
        functools.partial(reduce_kernel, pieces),
        out_shape=(
            jax.ShapeDtypeStruct((rows, width), LOW),
            jax.ShapeDtypeStruct((rows, width), LOW),
            jax.ShapeDtypeStruct(stats.shape, WIDE),
        ),
        in_specs=[WHOLE] * 6,
        out_specs=(WHOLE,) * 3,
        scratch_shapes=[
            low(DEPTH, ACROSS, half),
            low(DEPTH, ACROSS, half),
            low(DEPTH, ACROSS, half),
            low(DEPTH, ACROSS, half),
            low(DEPTH, quarter),
            low(DEPTH, quarter),
            low(DEPTH, quarter),
            wide(rows),
            wide(quarter),
            wide(shards, attn_rows),
            wide(shards, ff_rows),
            low(shards, attn_rows),
            low(shards, ff_rows),
            wide(width),
            wide(width),
            wide(3, STATS),
            wide(3, STATS),
            wide(DEPTH, STATS),
            *[dma(DEPTH) for _ in range(8)],
            dma(6),
            dma(6),
            dma(3),
            dma(1),
            dma(3),
            dma(3),
            dma(shards * SIDES),
            dma(7),
            dma(7),
            dma(7),
        ],
        compiler_params=pltpu.CompilerParams(
            vmem_limit_bytes=56 << 20, collective_id=1, has_side_effects=True
        ),
        name="reduce",
    )(grads.reshape(DEPTH, ACROSS, rows, width), stats, qkv, out, gate_up, down)


def update_kernel(
    pieces,
    factors,
    grow_ref,
    xrow_ref,
    stat_ref,
    w_qkv,
    w_out,
    w_gate_up,
    w_down,
    m_qkv,
    m_out,
    m_gate_up,
    m_down,
    gains,
    bias,
    gain_moment,
    gain_square,
    bias_moment,
    bias_square,
    g_qkv,
    g_out,
    g_gate_up,
    g_down,
    nm_qkv,
    nm_out,
    nm_gate_up,
    nm_down,
    nw_qkv,
    nw_out,
    nw_gate_up,
    nw_down,
    g_gains,
    n_gain_moment,
    n_gain_square,
    n_gains,
    g_bias,
    n_bias_moment,
    n_bias_square,
    n_bias,
):
    shrink = 1.0 - MUON_RATE * MUON_DECAY

    def one(index, turned, g, m, w, nm, nw):
        start, count = pieces[index]
        grad = grow_ref[start : start + count, :].astype(WIDE)
        ortho = xrow_ref[start : start + count, :].astype(WIDE)
        if turned:
            grad, ortho = grad.T, ortho.T
        g[...] = grad
        nm[...] = MUON_MU * m[...] + grad
        nw[...] = w[...] * shrink - factors[index] * ortho

    for j in range(3):
        one(j, True, *[r.at[j] for r in (g_qkv, m_qkv, w_qkv, nm_qkv, nw_qkv)])
    one(3, False, g_out, m_out, w_out, nm_out, nw_out)
    for j in range(2):
        refs = (g_gate_up, m_gate_up, w_gate_up, nm_gate_up, nw_gate_up)
        one(4 + j, True, *[r.at[j] for r in refs])
    one(6, False, g_down, m_down, w_down, nm_down, nw_down)

    grad = stat_ref[0:2, :]
    g_gains[...] = grad
    n_gain_moment[...], n_gain_square[...], n_gains[...] = adam_step(
        gains[...], grad, gain_moment[...], gain_square[...]
    )
    heads = bias.shape[1]
    sums = jnp.sum(stat_ref[8:24, :PAIR].T, axis=0, keepdims=True)
    grad = jnp.concatenate([sums[:, :heads], sums[:, 8 : 8 + heads]], axis=0)
    g_bias[...] = grad
    n_bias_moment[...], n_bias_square[...], n_bias[...] = adam_step(
        bias[...], grad, bias_moment[...], bias_square[...]
    )


def update(factors, grad_rows, ortho_rows, stats, weights, momenta, small):
    pieces = offsets(weights[1].shape[0], weights[3].shape[0])
    gains, bias = small[:2]
    like = lambda a: jax.ShapeDtypeStruct(a.shape, WIDE)
    outs = [like(a) for a in (*weights, *weights, *weights, *[gains] * 4, *[bias] * 4)]
    return pl.pallas_call(
        functools.partial(update_kernel, pieces, factors),
        out_shape=tuple(outs),
        in_specs=[WHOLE] * 17,
        out_specs=(WHOLE,) * len(outs),
        compiler_params=pltpu.CompilerParams(vmem_limit_bytes=40 << 20),
        name="update",
    )(grad_rows, ortho_rows, stats, *weights, *momenta, *small)


def body(
    tokens,
    cotangent,
    lengths,
    variates,
    times,
    weight_qkv,
    weight_out,
    weight_gate_up,
    weight_down,
    momentum_qkv,
    momentum_out,
    momentum_gate_up,
    momentum_down,
    gains,
    attn_bias,
    gain_moment,
    gain_square,
    bias_moment,
    bias_square,
):
    width = tokens.shape[1]
    heads = attn_bias.shape[1]
    attn_rows = weight_out.shape[0]
    ff_rows = weight_down.shape[0]
    fsdp = lax.axis_size("fsdp")
    ff = ff_rows * fsdp
    attn_width = attn_rows * fsdp
    shrink = 1.0 - MUON_RATE * MUON_DECAY
    scale_attn = MUON_RATE * 0.2 * math.sqrt(max(width, attn_width))
    scale_ff = MUON_RATE * 0.2 * math.sqrt(max(width, ff))
    sizes = (fsdp, lax.axis_size("ns"))
    if sizes == (DEPTH * ACROSS, SIDES * CORES) and attn_rows == 48 and ff_rows == 128:
        full = gather(weight_qkv, weight_out, weight_gate_up, weight_down)
        out_tokens, grad_tokens, grads, stats = layer(
            tokens, cotangent, lengths, variates, times, full, gains, attn_bias, ff, LOW
        )
        momenta = (momentum_qkv, momentum_out, momentum_gate_up, momentum_down)
        grad_rows, ortho_rows, stats = reduce_and_turn(grads, stats, *momenta)
        outs = update(
            (scale_attn,) * 4 + (scale_ff,) * 3,
            grad_rows,
            ortho_rows,
            stats,
            (weight_qkv, weight_out, weight_gate_up, weight_down),
            momenta,
            (gains, attn_bias, gain_moment, gain_square, bias_moment, bias_square),
        )
        return (out_tokens, grad_tokens, *outs)
    weights = pack(weight_qkv, weight_out, weight_gate_up, weight_down)
    momenta = pack(momentum_qkv, momentum_out, momentum_gate_up, momentum_down)
    full = lax.all_gather(weights.astype(LOW), "fsdp", axis=0, tiled=False)
    aligned = attn_rows % 16 == 0 and ff_rows % 16 == 0
    pieces = offsets(attn_rows, ff_rows)
    if not aligned:
        full = jnp.concatenate(
            [full[:, s : s + n].reshape(1, fsdp * n, width) for s, n in pieces], axis=1
        )
    out_tokens, grad_tokens, grads, stats = layer(
        tokens, cotangent, lengths, variates, times, full, gains, attn_bias, ff, WIDE
    )
    if not aligned:
        wholes = offsets(attn_width, ff)
        grads = jnp.concatenate(
            [grads[0, s : s + n].reshape(fsdp, n // fsdp, width) for s, n in wholes], axis=1
        )
    summed = lax.psum_scatter(grads, "fsdp", scatter_dimension=0, tiled=False)
    grad_rows = lax.psum(summed.astype(LOW), "ns").astype(WIDE)
    bias_part = jnp.sum(stats[8:, :PAIR], axis=1).reshape(2, 8)[:, :heads]
    grad_gains, grad_bias = lax.psum((stats[:2], bias_part), ("fsdp", "ns"))

    new_momenta = MUON_MU * momenta + grad_rows
    advance = grad_rows + MUON_MU * new_momenta
    parts = [advance[s : s + n] for s, n in pieces]
    grams = jnp.stack(
        [
            lax.dot_general(
                y,
                y,
                (((0,), (0,)), ((), ())),
                precision=lax.Precision.HIGHEST,
                preferred_element_type=WIDE,
            )
            for y in parts
        ]
    )
    factor = newton_schulz(lax.psum(grams, "fsdp"))
    turned = jnp.concatenate(
        [
            (scale_attn if i < 4 else scale_ff)
            * jnp.dot(
                y, factor[i], precision=lax.Precision.HIGHEST, preferred_element_type=WIDE
            )
            for i, y in enumerate(parts)
        ],
        axis=0,
    )
    new_weights = weights * shrink - turned
    new_gain_moment, new_gain_square, new_gains = adam_step(
        gains, grad_gains, gain_moment, gain_square
    )
    new_bias_moment, new_bias_square, new_bias = adam_step(
        attn_bias, grad_bias, bias_moment, bias_square
    )
    return (
        out_tokens,
        grad_tokens,
        *unpack(grad_rows, attn_rows, ff_rows),
        *unpack(new_momenta, attn_rows, ff_rows),
        *unpack(new_weights, attn_rows, ff_rows),
        grad_gains,
        new_gain_moment,
        new_gain_square,
        new_gains,
        grad_bias,
        new_bias_moment,
        new_bias_square,
        new_bias,
    )


def solution(mesh):
    rows = P(("fsdp", "ns"), None)
    line = P(("fsdp", "ns"))
    matrices = (P(None, None, "fsdp"), P("fsdp", None), P(None, None, "fsdp"), P("fsdp", None))
    return jax.shard_map(
        body,
        mesh=mesh,
        in_specs=(rows, rows, line, rows, line, *matrices, *matrices, *([P()] * 6)),
        out_specs=(rows, rows, *matrices, *matrices, *matrices, *([P()] * 8)),
        check_vma=False,
    )
```

```python
import functools
import math

import jax
import jax.numpy as jnp
import numpy as np
from jax import lax
from jax.experimental import pallas as pl
from jax.experimental.pallas import tpu as pltpu
from jax.sharding import PartitionSpec as P

HEAD_DIM = 64
BUCKET = 64
TIME_SLOTS = 64
NS_ITERS = 5
STEP = 10

EPS_NORM = 1e-06
ROPE_BASE = 10000.0
NEG_FILL = -1000000000.0
COEF_A = 3.4445
COEF_B = -4.775
COEF_C = 2.0315
NS_EPS = 1e-07
MUON_MU = 0.95
MUON_RATE = 0.25
MUON_DECAY = 0.01
ADAM_RATE = 0.8
BETA_ONE = 0.9
BETA_TWO = 0.95
ADAM_EPS = 1e-08

LOW = jnp.bfloat16
WIDE = jnp.float32
BLOCK = 256
PAIR = 2 * BUCKET
LANES = 2 * HEAD_DIM
STATS = 24
WHOLE = pl.BlockSpec(memory_space=pltpu.VMEM)
SCALARS = pl.BlockSpec(memory_space=pltpu.SMEM)


def mul_nn(left, right):
    return lax.dot_general(left, right, (((1,), (0,)), ((), ())), preferred_element_type=WIDE)


def mul_nt(left, right):
    return lax.dot_general(left, right, (((1,), (1,)), ((), ())), preferred_element_type=WIDE)


def mul_tn(left, right):
    return lax.dot_general(left, right, (((0,), (0,)), ((), ())), preferred_element_type=WIDE)


def offsets(attn_rows, ff_rows):
    counts = [attn_rows] * 4 + [ff_rows] * 3
    starts = [sum(counts[:i]) for i in range(7)]
    return list(zip(starts, counts))


def layer_kernel(
    pieces,
    lengths,
    bias,
    tok_ref,
    cot_ref,
    var_ref,
    time_ref,
    table_ref,
    gain_ref,
    w_ref,
    out_ref,
    gtok_ref,
    grad_ref,
    stat_ref,
    n1_s,
    n2_s,
    att_s,
    gml_s,
    hid_s,
    glow_s,
    gg_s,
    gu_s,
    gqkv_s,
):
    step = pl.program_id(0)
    rows, width = tok_ref.shape
    heads = bias.shape[1]
    here = pl.ds(pl.multiple_of(step * rows, rows), rows)

    def weight(first, last):
        parts = []
        for i in range(first, last):
            start, count = pieces[i]
            part = w_ref[:, start : start + count, :]
            parts.append(part.reshape(part.shape[0] * count, width))
        return parts[0] if len(parts) == 1 else jnp.concatenate(parts, axis=0)

    @pl.when(step == 0)
    def _():
        stat_ref[...] = jnp.zeros_like(stat_ref)

    lane = lax.broadcasted_iota(jnp.int32, (1, LANES), 1)
    low_head = lane < HEAD_DIM
    low_half = lane % HEAD_DIM < HEAD_DIM // 2
    per_block = rows // PAIR
    var_rows = var_ref[pl.ds(step * per_block, per_block), :]
    time_rows = time_ref[pl.ds(step * per_block, per_block), :]
    filler = jnp.zeros((8 - 2 * per_block, PAIR), WIDE)
    columns = jnp.concatenate([var_rows, time_rows, filler], axis=0).T
    slots = lax.broadcasted_iota(jnp.int32, (1, TIME_SLOTS), 1).astype(WIDE)
    hot = jnp.concatenate(
        [(columns[:, per_block + p : per_block + p + 1] == slots) for p in range(per_block)], axis=0
    ).astype(LOW)
    looked = mul_nn(hot, table_ref[0]) + mul_nn(hot, table_ref[1]) + mul_nn(hot, table_ref[2])
    cosine = looked[:, :LANES]
    sine = looked[:, LANES:]

    def swapped(values):
        half = HEAD_DIM // 2
        return jnp.where(
            low_half, pltpu.roll(values, LANES - half, 1), pltpu.roll(values, half, 1)
        )

    gain_one = gain_ref[0:1, :]
    gain_two = gain_ref[1:2, :]
    tokens = tok_ref[...].astype(WIDE)
    scale_one = lax.rsqrt(jnp.mean(tokens * tokens, axis=-1, keepdims=True) + EPS_NORM)
    unit_one = tokens * scale_one
    normed_one = (unit_one * gain_one).astype(LOW)
    n1_s[here, :] = normed_one
    qkv = mul_nt(normed_one, weight(0, 3))

    query_scale = HEAD_DIM ** (-0.5)
    units = []
    attended = []
    row_id = lax.broadcasted_iota(jnp.int32, (PAIR, 1), 0)
    lane_id = lax.broadcasted_iota(jnp.int32, (1, PAIR), 1)
    same_bucket = (row_id < BUCKET) == (lane_id < BUCKET)
    masks = []
    live_cols = []
    for p in range(per_block):
        first = lengths[(step * per_block + p) * 2]
        second = lengths[(step * per_block + p) * 2 + 1]
        live_key = lane_id % BUCKET < jnp.where(lane_id < BUCKET, first, second)
        live_cols.append(row_id % BUCKET < jnp.where(row_id < BUCKET, first, second))
        mask = same_bucket & live_key
        same_var = columns[:, p : p + 1] == var_rows[p : p + 1, :]
        masks.append((mask, same_var))

    for hp in range(heads // 2):
        cols = slice(hp * LANES, (hp + 1) * LANES)
        q = qkv[:, cols]
        k = qkv[:, width + hp * LANES : width + (hp + 1) * LANES]
        v = qkv[:, 2 * width + hp * LANES : 2 * width + (hp + 1) * LANES].astype(LOW)
        q = ((q * cosine + swapped(q) * sine) * query_scale).astype(LOW)
        k = (k * cosine + swapped(k) * sine).astype(LOW)
        q_first = jnp.where(low_head, q, jnp.zeros_like(q))
        q_second = jnp.where(low_head, jnp.zeros_like(q), q)
        att_pairs = []
        for p in range(per_block):
            part = slice(p * PAIR, (p + 1) * PAIR)
            mask, same_var = masks[p]
            q2 = jnp.concatenate([q_first[part], q_second[part]], axis=0)
            kp = k[part]
            vp = v[part]
            raw = mul_nt(q2, kp)
            halves = []
            for j in range(2):
                h = 2 * hp + j
                biased = raw[j * PAIR : (j + 1) * PAIR] + jnp.where(
                    same_var, bias[0, h], bias[1, h]
                )
                halves.append(jnp.where(mask, biased, NEG_FILL))
            scores = jnp.concatenate(halves, axis=0)
            top = jnp.max(scores, axis=-1, keepdims=True)
            exponent = jnp.exp(scores - top)
            probs = exponent / jnp.sum(exponent, axis=-1, keepdims=True)
            probs_low = probs.astype(LOW)
            both = mul_nn(probs_low, vp)
            att_pairs.append(jnp.where(low_head, both[:PAIR], both[PAIR:]))
            units.append((hp, p, q2, kp, vp, probs, probs_low))
        attended.append(jnp.concatenate(att_pairs, axis=0).astype(LOW))
    attended = jnp.concatenate(attended, axis=1)
    att_s[here, :] = attended
    w_out = weight(3, 4)
    mid = tokens + mul_nn(attended, w_out)
    scale_two = lax.rsqrt(jnp.mean(mid * mid, axis=-1, keepdims=True) + EPS_NORM)
    unit_two = mid * scale_two
    normed_two = (unit_two * gain_two).astype(LOW)
    n2_s[here, :] = normed_two
    w_gate = weight(4, 5)
    w_up = weight(5, 6)
    w_down = weight(6, 7)
    gate = mul_nt(normed_two, w_gate)
    up = mul_nt(normed_two, w_up)
    sig = 1.0 / (1.0 + jnp.exp(-gate))
    silu = gate * sig
    hidden = (silu * up).astype(LOW)
    hid_s[here, :] = hidden
    out_ref[...] = (mid + mul_nn(hidden, w_down)).astype(LOW)

    live_row = jnp.concatenate(live_cols, axis=0)
    g_out = jnp.where(live_row, cot_ref[...].astype(WIDE), 0.0)
    g_low = g_out.astype(LOW)
    glow_s[here, :] = g_low
    g_hidden = mul_nt(g_low, w_down)
    g_gate = (g_hidden * up * sig * (1.0 + gate * (1.0 - sig))).astype(LOW)
    g_up = (g_hidden * silu).astype(LOW)
    gg_s[here, :] = g_gate
    gu_s[here, :] = g_up
    e_two = mul_nn(g_gate, w_gate) + mul_nn(g_up, w_up)
    stat_ref[1:2, :] += jnp.sum(e_two * unit_two, axis=0, keepdims=True)
    scaled = e_two * gain_two
    g_mid = g_out + scale_two * (
        scaled - unit_two * jnp.mean(scaled * unit_two, axis=-1, keepdims=True)
    )
    g_mid_low = g_mid.astype(LOW)
    gml_s[here, :] = g_mid_low
    g_att = mul_nt(g_mid_low, w_out).astype(LOW)

    parts_q = [[None] * per_block for _ in range(heads // 2)]
    parts_k = [[None] * per_block for _ in range(heads // 2)]
    parts_v = [[None] * per_block for _ in range(heads // 2)]
    for hp, p, q2, kp, vp, probs, probs_low in units:
        part = slice(p * PAIR, (p + 1) * PAIR)
        mask, same_var = masks[p]
        ga = g_att[part, hp * LANES : (hp + 1) * LANES]
        ga2 = jnp.concatenate(
            [
                jnp.where(low_head, ga, jnp.zeros_like(ga)),
                jnp.where(low_head, jnp.zeros_like(ga), ga),
            ],
            axis=0,
        )
        g_probs = mul_nt(ga2, vp)
        row_dot = jnp.sum(probs * g_probs, axis=-1, keepdims=True)
        g_scores = probs * (g_probs - row_dot)
        for j in range(2):
            h = 2 * hp + j
            mine = g_scores[j * PAIR : (j + 1) * PAIR]
            stat_ref[8 + h : 9 + h, :PAIR] += jnp.sum(
                jnp.where(same_var, mine, 0.0), axis=0, keepdims=True
            )
            stat_ref[16 + h : 17 + h, :PAIR] += jnp.sum(
                jnp.where(same_var, 0.0, mine), axis=0, keepdims=True
            )
        low_scores = g_scores.astype(LOW)
        both = mul_nn(low_scores, kp)
        parts_q[hp][p] = jnp.where(low_head, both[:PAIR], both[PAIR:])
        parts_k[hp][p] = mul_tn(low_scores, q2)
        parts_v[hp][p] = mul_tn(probs_low, ga2)
    g_q = []
    g_k = []
    g_v = []
    for hp in range(heads // 2):
        dq = jnp.concatenate(parts_q[hp], axis=0)
        dk = jnp.concatenate(parts_k[hp], axis=0)
        g_q.append(((dq * cosine - swapped(dq) * sine) * query_scale).astype(LOW))
        g_k.append((dk * cosine - swapped(dk) * sine).astype(LOW))
        g_v.append(jnp.concatenate(parts_v[hp], axis=0).astype(LOW))
    g_qkv = jnp.concatenate(g_q + g_k + g_v, axis=1)
    gqkv_s[here, :] = g_qkv
    e_one = mul_nn(g_qkv, weight(0, 3))
    stat_ref[0:1, :] += jnp.sum(e_one * unit_one, axis=0, keepdims=True)
    scaled = e_one * gain_one
    gtok_ref[...] = (
        g_mid
        + scale_one * (scaled - unit_one * jnp.mean(scaled * unit_one, axis=-1, keepdims=True))
    ).astype(LOW)

    @pl.when(step == pl.num_programs(0) - 1)
    def _():
        def put(index, left, right):
            start, count = pieces[index]
            grad_ref[:, start : start + count, :] = (
                mul_tn(left, right)
                .reshape(grad_ref.shape[0], count, width)
                .astype(grad_ref.dtype)
            )

        for j in range(3):
            put(j, gqkv_s[:, j * width : (j + 1) * width], n1_s[...])
        put(3, att_s[...], gml_s[...])
        put(4, gg_s[...], n2_s[...])
        put(5, gu_s[...], n2_s[...])
        put(6, hid_s[...], glow_s[...])


def layer(tokens, cotangent, lengths, variates, times, packed, gains, attn_bias, ff, grad_type):
    rows, width = tokens.shape
    heads = attn_bias.shape[1]
    copies, shard_rows, _ = packed.shape
    pieces = offsets(heads * HEAD_DIM // copies, ff // copies)
    half = HEAD_DIM // 2
    frequency = ROPE_BASE ** (-2.0 * jnp.arange(half, dtype=WIDE) / HEAD_DIM)
    angles = jnp.arange(TIME_SLOTS, dtype=WIDE)[:, None] * frequency[None, :]
    cosine, sine = jnp.cos(angles), jnp.sin(angles)
    table = jnp.concatenate([cosine] * 4 + [-sine, sine, -sine, sine], axis=1)
    first = table.astype(LOW)
    rest = table - first.astype(WIDE)
    second = rest.astype(LOW)
    third = (rest - second.astype(WIDE)).astype(LOW)
    table = jnp.stack([first, second, third])
    grid = rows // BLOCK
    block = pl.BlockSpec((BLOCK, width), lambda i: (i, 0))
    low_scratch = lambda columns: pltpu.VMEM((rows, columns), LOW)
    return pl.pallas_call(
        functools.partial(layer_kernel, pieces),
        grid=(grid,),
        out_shape=(
            jax.ShapeDtypeStruct((rows, width), LOW),
            jax.ShapeDtypeStruct((rows, width), LOW),
            jax.ShapeDtypeStruct((copies, shard_rows, width), grad_type),
            jax.ShapeDtypeStruct((STATS, width), WIDE),
        ),
        in_specs=[SCALARS, SCALARS, block, block, WHOLE, WHOLE, WHOLE, WHOLE, WHOLE],
        out_specs=(block, block, WHOLE, WHOLE),
        scratch_shapes=[
            low_scratch(width),
            low_scratch(width),
            low_scratch(width),
            low_scratch(width),
            low_scratch(ff),
            low_scratch(width),
            low_scratch(ff),
            low_scratch(ff),
            low_scratch(3 * width),
        ],
        compiler_params=pltpu.CompilerParams(vmem_limit_bytes=58 << 20),
        name="layer",
    )(
        lengths,
        attn_bias,
        tokens,
        cotangent,
        variates.astype(WIDE).reshape(rows // PAIR, PAIR),
        times.astype(WIDE).reshape(rows // PAIR, PAIR),
        table,
        gains,
        packed,
    )


def pack(qkv, out, gate_up, down):
    width = out.shape[-1]
    return jnp.concatenate(
        [
            jnp.swapaxes(qkv, 1, 2).reshape(-1, width),
            out,
            jnp.swapaxes(gate_up, 1, 2).reshape(-1, width),
            down,
        ],
        axis=0,
    )


def unpack(packed, attn_rows, ff_rows):
    width = packed.shape[-1]
    qkv = jnp.swapaxes(packed[: 3 * attn_rows].reshape(3, attn_rows, width), 1, 2)
    out = packed[3 * attn_rows : 4 * attn_rows]
    ends = 4 * attn_rows + 2 * ff_rows
    gate_up = jnp.swapaxes(packed[4 * attn_rows : ends].reshape(2, ff_rows, width), 1, 2)
    return qkv, out, gate_up, packed[ends:]


def newton_schulz(gram_mat):
    def product(left, right):
        return jnp.einsum(
            "mde,mef->mdf",
            left,
            right,
            precision=lax.Precision.HIGHEST,
            preferred_element_type=WIDE,
        )

    norm_val = jnp.sqrt(jnp.trace(gram_mat, axis1=1, axis2=2))[:, None, None] + NS_EPS
    gram_mat = gram_mat / (norm_val * norm_val)
    unit = jnp.eye(gram_mat.shape[-1], dtype=WIDE)[None]
    chain = None
    for turn_idx in range(NS_ITERS):
        poly_mat = COEF_A * unit + COEF_B * gram_mat + COEF_C * product(gram_mat, gram_mat)
        chain = poly_mat if chain is None else product(poly_mat, chain)
        if turn_idx < NS_ITERS - 1:
            gram_mat = product(product(poly_mat, gram_mat), poly_mat)
    return chain / norm_val


def adam_step(param, grad, moment, square):
    new_moment = BETA_ONE * moment + (1.0 - BETA_ONE) * grad
    new_square = BETA_TWO * square + (1.0 - BETA_TWO) * grad * grad
    corrected = new_moment / (1.0 - BETA_ONE**STEP)
    scaled = jnp.sqrt(new_square / (1.0 - BETA_TWO**STEP)) + ADAM_EPS
    return (new_moment, new_square, param - ADAM_RATE * corrected / scaled)


DEPTH, ACROSS = 4, 2
SIDES, CORES = 2, 2
TURNS = (2, 1, 3, 0)
OWNERS = (
    (2, 0, 0, 0),
    (2, 1, 0, 1),
    (1, 1, 0, 0),
    (2, 1, 1, 0),
    (2, 0, 1, 1),
    (1, 0, 0, 1),
    (1, 1, 1, 0),
)


def place():
    f = lax.axis_index("fsdp")
    n = lax.axis_index("ns")
    return f // ACROSS, f % ACROSS, n // CORES, n % CORES


def device(z, x, y, c):
    return (z * ACROSS + x, y * CORES + c)


def remote(src, dst, send_sem, recv_sem, where):
    return pltpu.make_async_remote_copy(
        src_ref=src,
        dst_ref=dst,
        send_sem=send_sem,
        recv_sem=recv_sem,
        device_id=where,
        device_id_type=pl.DeviceIdType.MESH,
    )


def greet(where):
    pl.semaphore_signal(
        pltpu.get_barrier_semaphore(),
        inc=1,
        device_id=where,
        device_id_type=pl.DeviceIdType.MESH,
    )


def halves(value):
    high = value.astype(LOW)
    return high, (value - high.astype(WIDE)).astype(LOW)


def mul_wide(left, right):
    columns = right.shape[1]
    left_high, left_low = halves(left)
    right_high, right_low = halves(right)
    first = mul_nn(left_high, jnp.concatenate([right_high, right_low], axis=1))
    return first[:, :columns] + (first[:, columns:] + mul_nn(left_low, right_high))


def gram_wide(value):
    high, low = halves(value)
    cross = mul_tn(high, low)
    return mul_tn(high, high) + (cross + cross.T)


def whole_kernel(
    pieces,
    lengths,
    bias,
    tok_ref,
    cot_ref,
    var_ref,
    time_ref,
    table_ref,
    gain_ref,
    wqkv_ref,
    wout_ref,
    wgate_up_ref,
    wdown_ref,
    mqkv_ref,
    mout_ref,
    mgate_up_ref,
    mdown_ref,
    out_ref,
    gtok_ref,
    grows_ref,
    xrows_ref,
    total_ref,
    w_s,
    grad_s,
    momenta,
    n1_s,
    n2_s,
    att_s,
    gml_s,
    glow_s,
    hid_s,
    gg_s,
    gu_s,
    low_s,
    gqkv_s,
    probs_s,
    mid_s,
    gmid_s,
    gatt_s,
    scale_s,
    rope_s,
    y_attn,
    y_ff,
    x_attn,
    x_ff,
    gram_s,
    chain_s,
    stat_s,
    stat_in,
    stat_acc,
    stat_line,
    stat_send,
    stat_recv,
    adv_recv,
    x_send,
    x_recv,
    fan_send,
    fan_recv,
    *per_part,
):
    z, x, y, c = place()
    shard = z * ACROSS + x
    rows, width = tok_ref.shape
    heads = bias.shape[1]
    sibling = device(z, x, y, 1 - c)
    facing = device(z, x, 1 - y, c)
    corner = device(z, x, 1 - y, 1 - c)
    beside = device(z, 1 - x, y, c)
    upper = device(z + 1, x, y, c)
    lower = device(z - 1, x, y, c)
    world = DEPTH * ACROSS * SIDES * CORES
    rank = shard * (SIDES * CORES) + y * CORES + c
    line = [lax.rem(z + k, DEPTH) for k in range(DEPTH)]
    part = 2 * c + y

    def hello(i, carry):
        other = lax.rem(rank + 1 + i, world)
        greet((other // (SIDES * CORES), lax.rem(other, SIDES * CORES)))
        return carry

    lax.fori_loop(0, world - 1, hello, 0)

    def put(index, value):
        start, count = pieces[index]
        w_s[shard, start : start + count, :] = value.astype(LOW)

    for j in range(3):
        put(j, wqkv_ref[j])
    put(3, wout_ref[...])
    put(4, wgate_up_ref[0].T)
    put(5, wgate_up_ref[1].T)
    put(6, wdown_ref[...])
    pl.semaphore_wait(pltpu.get_barrier_semaphore(), world - 1)

    has_up = z < DEPTH - 1
    has_down = z > 0

    def exists(rel):
        return (z + rel >= 0) & (z + rel < DEPTH)

    class Gather:
        def __init__(self, start, count, sems):
            self.start_row, self.half = start, count // 2
            (
                self.up_send,
                self.down_send,
                self.x_send,
                self.sib_send,
                self.below_recv,
                self.above_recv,
                self.x_recv,
                self.sib_recv,
            ) = sems

        def view(self, at, core):
            first = pl.multiple_of(self.start_row + core * self.half, 16)
            return w_s.at[at, pl.ds(first, self.half)]

        def mine(self, rel):
            return self.view(shard + rel * ACROSS, c)

        def others(self, rel):
            return self.view((z + rel) * ACROSS + 1 - x, c)

        def up(self, d):
            return remote(
                self.mine(-d), self.mine(-d), self.up_send.at[d], self.below_recv.at[d], upper
            )

        def down(self, d):
            return remote(
                self.mine(d), self.mine(d), self.down_send.at[d], self.above_recv.at[d], lower
            )

        def over(self, rel, where):
            return remote(
                self.mine(rel), where, self.x_send.at[rel + 3], self.x_recv.at[rel + 3], beside
            )

        def sib(self, kind, rel, src):
            return remote(
                src, src, self.sib_send.at[kind, rel + 3], self.sib_recv.at[kind, rel + 3], sibling
            )

        def start(self):
            @pl.when(has_up)
            def _():
                self.up(0).start()

            @pl.when(has_down)
            def _():
                self.down(0).start()

            self.over(0, self.mine(0)).start()

        def hop(self, d):
            @pl.when(exists(-d))
            def _():
                here = self.mine(-d)
                remote(
                    here, here, self.up_send.at[d], self.below_recv.at[d - 1], lower
                ).wait_recv()
                if d < DEPTH - 1:

                    @pl.when(has_up)
                    def _():
                        self.up(d).start()

                self.over(-d, here).start()
                self.sib(0, -d, here).start()

            @pl.when(exists(d))
            def _():
                here = self.mine(d)
                remote(
                    here, here, self.down_send.at[d], self.above_recv.at[d - 1], upper
                ).wait_recv()
                if d < DEPTH - 1:

                    @pl.when(has_down)
                    def _():
                        self.down(d).start()

                self.over(d, here).start()
                self.sib(0, d, here).start()

        def from_beside(self, d):
            for rel in (0,) if d == 0 else (-d, d):

                @pl.when(exists(rel))
                def _():
                    there = self.others(rel)
                    remote(
                        there, there, self.x_send.at[rel + 3], self.x_recv.at[rel + 3], beside
                    ).wait_recv()
                    self.sib(1, rel, there).start()

        def arrive(self):
            for rel in range(1 - DEPTH, DEPTH):

                @pl.when(exists(rel))
                def _():
                    if rel != 0:
                        self.sib(0, rel, self.view(shard + rel * ACROSS, 1 - c)).wait_recv()
                    self.sib(1, rel, self.view((z + rel) * ACROSS + 1 - x, 1 - c)).wait_recv()

        def sent(self):
            for rel in range(1 - DEPTH, DEPTH):

                @pl.when(exists(rel))
                def _():
                    if rel != 0:
                        self.sib(0, rel, self.mine(rel)).wait_send()
                    self.sib(1, rel, self.others(rel)).wait_send()
                    self.over(rel, self.mine(rel)).wait_send()

            for d in range(DEPTH - 1):

                @pl.when(exists(-d) & has_up)
                def _():
                    self.up(d).wait_send()

                @pl.when(exists(d) & has_down)
                def _():
                    self.down(d).wait_send()

    ff_row = pieces[4][0]
    last_row = pieces[6][0] + pieces[6][1]
    spans = ((0, ff_row), (ff_row, last_row - ff_row))
    each = len(per_part) // 2
    gathers = [Gather(*spans[i], per_part[i * each : i * each + 8]) for i in range(2)]
    attn_gather, ff_gather = gathers
    attn_gather.start()

    for i, (value, turned) in enumerate(((mgate_up_ref[0], 4), (mgate_up_ref[1], 5))):
        start, count = pieces[turned]
        momenta[start : start + count, :] = value.T
    for j in range(3):
        start, count = pieces[j]
        momenta[start : start + count, :] = mqkv_ref[j]
    momenta[pieces[3][0] : pieces[3][0] + pieces[3][1], :] = mout_ref[...]
    momenta[pieces[6][0] : last_row, :] = mdown_ref[...]
    stat_s[...] = jnp.zeros_like(stat_s)

    lane = lax.broadcasted_iota(jnp.int32, (1, LANES), 1)
    low_head = lane < HEAD_DIM
    low_half = lane % HEAD_DIM < HEAD_DIM // 2
    row_id = lax.broadcasted_iota(jnp.int32, (PAIR, 1), 0)
    lane_id = lax.broadcasted_iota(jnp.int32, (1, PAIR), 1)
    same_bucket = (row_id < BUCKET) == (lane_id < BUCKET)
    slots = lax.broadcasted_iota(jnp.int32, (1, TIME_SLOTS), 1)
    query_scale = HEAD_DIM ** (-0.5)
    gain_one = gain_ref[0:1, :]
    gain_two = gain_ref[1:2, :]

    def column(row):
        return jnp.broadcast_to(row, (8, PAIR)).T[:, 0:1]

    def var_row(pair):
        two = var_ref[pl.ds(2 * pair, 2), :]
        return jnp.concatenate([two[0:1], two[1:2]], axis=1).astype(WIDE)

    def block_of(i, size):
        return pl.ds(pl.multiple_of(i * size, size), size)

    def prepare(i, carry):
        here = block_of(i, PAIR)
        times = column(time_ref[pl.ds(i, 1), :].astype(WIDE)).astype(jnp.int32)
        hot = (times == slots).astype(LOW)
        rope_s[here, :] = (
            mul_nn(hot, table_ref[0]) + mul_nn(hot, table_ref[1]) + mul_nn(hot, table_ref[2])
        )
        tokens = tok_ref[here, :].astype(WIDE)
        scale = lax.rsqrt(jnp.mean(tokens * tokens, axis=-1, keepdims=True) + EPS_NORM)
        scale_s[here, 0:1] = scale
        n1_s[here, :] = (tokens * scale * gain_one).astype(LOW)
        first, second = lengths[2 * i], lengths[2 * i + 1]
        live = row_id % BUCKET < jnp.where(row_id < BUCKET, first, second)
        glow_s[here, :] = jnp.where(live, cot_ref[here, :].astype(WIDE), 0.0).astype(LOW)
        return carry

    lax.fori_loop(0, rows // PAIR, prepare, 0)

    for d in range(1, DEPTH):
        attn_gather.hop(d)
    ff_gather.start()
    for d in range(DEPTH):
        attn_gather.from_beside(d)
    attn_gather.arrive()

    def weight(first, last):
        parts = []
        for i in range(first, last):
            start, count = pieces[i]
            piece = w_s[:, start : start + count, :]
            parts.append(piece.reshape(piece.shape[0] * count, width))
        return parts[0] if len(parts) == 1 else jnp.concatenate(parts, axis=0)

    def swapped(values):
        half = HEAD_DIM // 2
        return jnp.where(
            low_half, pltpu.roll(values, LANES - half, 1), pltpu.roll(values, half, 1)
        )

    def two_heads(value):
        none = jnp.zeros_like(value)
        return jnp.concatenate(
            [jnp.where(low_head, value, none), jnp.where(low_head, none, value)], axis=0
        )

    per_block = BLOCK // PAIR

    def attend(i, carry):
        here = block_of(i, BLOCK)
        qkv = mul_nt(n1_s[here, :], weight(0, 3))
        cosine = rope_s[here, :LANES]
        sine = rope_s[here, LANES:]
        masks = []
        for p in range(per_block):
            pair = i * per_block + p
            first, second = lengths[2 * pair], lengths[2 * pair + 1]
            live_key = lane_id % BUCKET < jnp.where(lane_id < BUCKET, first, second)
            row = var_row(pair)
            masks.append((same_bucket & live_key, column(row) == row))
        attended = []
        for hp in range(heads // 2):
            first = hp * LANES
            q = qkv[:, first : first + LANES]
            k = qkv[:, width + first : width + first + LANES]
            v = qkv[:, 2 * width + first : 2 * width + first + LANES].astype(LOW)
            q = ((q * cosine + swapped(q) * sine) * query_scale).astype(LOW)
            k = (k * cosine + swapped(k) * sine).astype(LOW)
            low_s[here, first : first + LANES] = q
            low_s[here, width + first : width + first + LANES] = k
            low_s[here, 2 * width + first : 2 * width + first + LANES] = v
            pairs = []
            for p in range(per_block):
                span = slice(p * PAIR, (p + 1) * PAIR)
                mask, same_var = masks[p]
                raw = mul_nt(two_heads(q[span]), k[span])
                both = []
                for j in range(2):
                    h = 2 * hp + j
                    biased = raw[j * PAIR : (j + 1) * PAIR] + jnp.where(
                        same_var, bias[0, h], bias[1, h]
                    )
                    both.append(jnp.where(mask, biased, NEG_FILL))
                scores = jnp.concatenate(both, axis=0)
                exponent = jnp.exp(scores - jnp.max(scores, axis=-1, keepdims=True))
                probs = exponent / jnp.sum(exponent, axis=-1, keepdims=True)
                probs_s[i * per_block + p, hp] = probs
                both = mul_nn(probs.astype(LOW), v[span])
                pairs.append(jnp.where(low_head, both[:PAIR], both[PAIR:]))
            attended.append(jnp.concatenate(pairs, axis=0).astype(LOW))
        attended = jnp.concatenate(attended, axis=1)
        att_s[here, :] = attended
        mid = tok_ref[here, :].astype(WIDE) + mul_nn(attended, weight(3, 4))
        mid_s[here, :] = mid
        scale = lax.rsqrt(jnp.mean(mid * mid, axis=-1, keepdims=True) + EPS_NORM)
        scale_s[here, 1:2] = scale
        n2_s[here, :] = (mid * scale * gain_two).astype(LOW)
        for d in range(1, DEPTH):

            @pl.when(i == d - 1)
            def _():
                ff_gather.hop(d)

        return carry

    lax.fori_loop(0, rows // BLOCK, attend, 0)
    for d in range(DEPTH):
        ff_gather.from_beside(d)
    ff_gather.arrive()

    def feed(i, carry):
        here = block_of(i, BLOCK)
        normed_two = n2_s[here, :]
        w_gate, w_up, w_down = weight(4, 5), weight(5, 6), weight(6, 7)
        gate = mul_nt(normed_two, w_gate)
        up = mul_nt(normed_two, w_up)
        sig = 1.0 / (1.0 + jnp.exp(-gate))
        silu = gate * sig
        hid_s[here, :] = (silu * up).astype(LOW)
        g_low = glow_s[here, :]
        g_hidden = mul_nt(g_low, w_down)
        g_gate = (g_hidden * up * sig * (1.0 + gate * (1.0 - sig))).astype(LOW)
        g_up = (g_hidden * silu).astype(LOW)
        gg_s[here, :] = g_gate
        gu_s[here, :] = g_up
        e_two = mul_nn(g_gate, w_gate) + mul_nn(g_up, w_up)
        scale = scale_s[here, 1:2]
        unit = mid_s[here, :] * scale
        stat_s[1:2, :] += jnp.sum(e_two * unit, axis=0, keepdims=True)
        scaled = e_two * gain_two
        g_mid = g_low.astype(WIDE) + scale * (
            scaled - unit * jnp.mean(scaled * unit, axis=-1, keepdims=True)
        )
        gmid_s[here, :] = g_mid
        g_mid_low = g_mid.astype(LOW)
        gml_s[here, :] = g_mid_low
        gatt_s[here, :] = mul_nt(g_mid_low, weight(3, 4)).astype(LOW)
        return carry

    lax.fori_loop(0, rows // BLOCK, feed, 0)

    def grad_put(index, left, right):
        start, count = pieces[index]
        grad_s[:, :, start : start + count, :] = (
            mul_tn(left, right).reshape(DEPTH, ACROSS, count, width).astype(LOW)
        )

    class Reduce:
        def __init__(self, start, count, refs):
            self.start_row, self.half, self.quarter = start, count // 2, count // 4
            (
                self.in_zero,
                self.acc_zero,
                self.in_one,
                self.acc_one,
                self.in_two,
                self.acc_two,
                self.in_three,
                self.advance,
                self.send_zero,
                self.send_one,
                self.send_two,
                self.send_three,
                self.recv_zero,
                self.recv_one,
                self.recv_two,
                self.recv_three,
                self.adv_send,
                self.row_send,
                self.row_recv,
            ) = refs
            self.keep_quarter = pl.ds(pl.multiple_of(y * self.quarter, 16), self.quarter)
            self.give_quarter = pl.ds(pl.multiple_of((1 - y) * self.quarter, 16), self.quarter)
            self.first_quarter = pl.ds(0, self.quarter)

        def half_of(self, core):
            return pl.ds(pl.multiple_of(self.start_row + core * self.half, 16), self.half)

        def rows_of(self, quarter):
            first = pl.multiple_of(self.start_row + quarter * self.quarter, 16)
            return pl.ds(first, self.quarter)

        def zero(self, k):
            return remote(
                grad_s.at[line[k], :, self.half_of(1 - c)],
                self.in_zero.at[k],
                self.send_zero.at[k],
                self.recv_zero.at[k],
                sibling,
            )

        def one(self, k, core):
            if core == 0:
                src, dst = self.acc_zero.at[k, :, self.give_quarter], self.in_one.at[
                    k, :, self.first_quarter
                ]
            else:
                src, dst = self.acc_zero.at[k, 1 - x], self.in_one.at[k, 0]
            where = facing if core == 0 else beside
            return remote(src, dst, self.send_one.at[k], self.recv_one.at[k], where)

        def two(self, k, core):
            if core == 0:
                src = self.acc_one.at[k, 1 - x, self.first_quarter]
            else:
                src = self.acc_one.at[k, 0, self.give_quarter]
            where = beside if core == 0 else facing
            return remote(src, self.in_two.at[k], self.send_two.at[k], self.recv_two.at[k], where)

        def three(self, k):
            return remote(
                self.acc_two.at[k],
                self.in_three.at[k],
                self.send_three.at[k],
                self.recv_three.at[k],
                device(line[k], x, y, c),
            )

        def start(self):
            for k in TURNS:
                self.zero(k).start()

        def step(self, t):
            def add(left, right):
                return (left.astype(WIDE) + right.astype(WIDE)).astype(LOW)

            quarter = self.quarter
            if t < DEPTH:
                k = TURNS[t]
                self.zero(k).wait_recv()
                self.acc_zero[k] = add(grad_s[line[k], :, self.half_of(c)], self.in_zero[k])
                for core in range(2):

                    @pl.when(c == core)
                    def _():
                        self.one(k, core).start()

            if 1 <= t <= DEPTH:
                k = TURNS[t - 1]

                @pl.when(c == 0)
                def _():
                    self.one(k, 0).wait_recv()
                    self.acc_one[k, :, :quarter] = add(
                        self.acc_zero[k, :, self.keep_quarter], self.in_one[k, :, :quarter]
                    )
                    self.two(k, 0).start()

                @pl.when(c == 1)
                def _():
                    self.one(k, 1).wait_recv()
                    self.acc_one[k, 0] = add(self.acc_zero[k, x], self.in_one[k, 0])
                    self.two(k, 1).start()

            if 2 <= t:
                k = TURNS[t - 2]

                @pl.when(c == 0)
                def _():
                    self.two(k, 0).wait_recv()
                    self.acc_two[k] = add(self.acc_one[k, x, :quarter], self.in_two[k])

                @pl.when(c == 1)
                def _():
                    self.two(k, 1).wait_recv()
                    self.acc_two[k] = add(self.acc_one[k, 0, self.keep_quarter], self.in_two[k])

                if k != 0:
                    self.three(k).start()

        def segments(self, index):
            found = []
            begin = self.start_row + index * self.quarter
            for m, (start, count) in enumerate(pieces):
                first, last = max(start, begin), min(start + count, begin + self.quarter)
                if first < last:
                    found.append((m, first - begin, first - start, last - first))
            return found

        def adv_copy(self, index, i):
            m, first, to, count = self.segments(index)[i]
            return remote(
                self.advance.at[pl.ds(first, count)],
                stage(m).at[shard, pl.ds(to, count)],
                self.adv_send.at[i],
                adv_recv.at[0],
                device(*OWNERS[m]),
            )

        def row_copy(self, j, quarter, where):
            here = grows_ref.at[self.rows_of(quarter)]
            return remote(here, here, self.row_send.at[j], self.row_recv.at[j], where)

        def finish(self):
            total = self.acc_two[0].astype(WIDE)
            for k in range(1, DEPTH):
                self.three(k).wait_recv()
                total = total + self.in_three[k].astype(WIDE)
            old = momenta[self.rows_of(part), :]
            self.advance[...] = total + MUON_MU * (MUON_MU * old + total)
            for index in range(4):
                for i, (m, first, to, count) in enumerate(self.segments(index)):

                    @pl.when((part == index) & jnp.logical_not(owned(m)))
                    def _():
                        self.adv_copy(index, i).start()

                    @pl.when((part == index) & owned(m))
                    def _():
                        pltpu.make_async_copy(
                            self.advance.at[pl.ds(first, count)],
                            stage(m).at[shard, pl.ds(to, count)],
                            adv_recv.at[0],
                        ).start()

            grows_ref[self.rows_of(part), :] = total.astype(LOW)
            for j, where in enumerate((sibling, facing, corner)):
                self.row_copy(j, part, where).start()

        def done(self):
            mates = ((sibling, 0, 1), (facing, 1, 0), (corner, 1, 1))
            for j, (where, dy, dc) in enumerate(mates):
                self.row_copy(j, 2 * (c ^ dc) + (y ^ dy), where).wait_recv()
                self.row_copy(j, part, where).wait_send()
            for index in range(4):
                for i, (m, first, to, count) in enumerate(self.segments(index)):

                    @pl.when((part == index) & jnp.logical_not(owned(m)))
                    def _():
                        self.adv_copy(index, i).wait_send()

            for k in TURNS:
                self.zero(k).wait_send()
                if k != 0:
                    self.three(k).wait_send()
                for core in range(2):

                    @pl.when(c == core)
                    def _():
                        self.one(k, core).wait_send()
                        self.two(k, core).wait_send()

    def owned(m):
        oz, ox, oy, oc = OWNERS[m]
        return (z == oz) & (x == ox) & (y == oy) & (c == oc)

    def stage(m):
        return y_attn if m < 4 else y_ff

    reduces = [Reduce(*spans[i], per_part[i * each + 8 : (i + 1) * each]) for i in range(2)]
    attn_reduce, ff_reduce = reduces

    grad_put(4, gg_s[...], n2_s[...])
    grad_put(5, gu_s[...], n2_s[...])
    grad_put(6, hid_s[...], glow_s[...])
    ff_reduce.start()

    def attend_back(i, carry):
        here = block_of(i, PAIR)
        row = var_row(i)
        same_var = column(row) == row
        cosine = rope_s[here, :LANES]
        sine = rope_s[here, LANES:]
        for hp in range(heads // 2):
            first = hp * LANES
            q2 = two_heads(low_s[here, first : first + LANES])
            k = low_s[here, width + first : width + first + LANES]
            v = low_s[here, 2 * width + first : 2 * width + first + LANES]
            probs = probs_s[i, hp]
            ga2 = two_heads(gatt_s[here, first : first + LANES])
            g_probs = mul_nt(ga2, v)
            row_dot = jnp.sum(probs * g_probs, axis=-1, keepdims=True)
            g_scores = probs * (g_probs - row_dot)
            for j in range(2):
                h = 2 * hp + j
                mine = g_scores[j * PAIR : (j + 1) * PAIR]
                stat_s[8 + h : 9 + h, :PAIR] += jnp.sum(
                    jnp.where(same_var, mine, 0.0), axis=0, keepdims=True
                )
                stat_s[16 + h : 17 + h, :PAIR] += jnp.sum(
                    jnp.where(same_var, 0.0, mine), axis=0, keepdims=True
                )
            low_scores = g_scores.astype(LOW)
            both = mul_nn(low_scores, k)
            dq = jnp.where(low_head, both[:PAIR], both[PAIR:])
            dk = mul_tn(low_scores, q2)
            dv = mul_tn(probs.astype(LOW), ga2)
            gqkv_s[here, first : first + LANES] = (
                (dq * cosine - swapped(dq) * sine) * query_scale
            ).astype(LOW)
            gqkv_s[here, width + first : width + first + LANES] = (
                dk * cosine - swapped(dk) * sine
            ).astype(LOW)
            gqkv_s[here, 2 * width + first : 2 * width + first + LANES] = dv.astype(LOW)
        for t in range(DEPTH + 2):

            @pl.when(i == t)
            def _():
                ff_reduce.step(t)

        return carry

    lax.fori_loop(0, rows // PAIR, attend_back, 0)
    for j in range(3):
        grad_put(j, gqkv_s[:, j * width : (j + 1) * width], n1_s[...])
    grad_put(3, att_s[...], gml_s[...])
    attn_reduce.start()
    ff_reduce.finish()

    def last(i):
        here = block_of(i, 2 * BLOCK)
        e_one = mul_nn(gqkv_s[here, :], weight(0, 3))
        scale = scale_s[here, 0:1]
        unit = tok_ref[here, :].astype(WIDE) * scale
        stat_s[0:1, :] += jnp.sum(e_one * unit, axis=0, keepdims=True)
        scaled = e_one * gain_one
        gtok_ref[here, :] = (
            gmid_s[here, :]
            + scale * (scaled - unit * jnp.mean(scaled * unit, axis=-1, keepdims=True))
        ).astype(LOW)

    def outgoing(i):
        here = block_of(i, 2 * BLOCK)
        out_ref[here, :] = (mid_s[here, :] + mul_nn(hid_s[here, :], weight(6, 7))).astype(LOW)

    def stat_copy(step, src, where):
        return remote(src, stat_in.at[step], stat_send.at[step], stat_recv.at[step], where)

    attn_reduce.step(0)
    last(0)
    attn_reduce.step(1)
    last(1)
    stat_copy(0, stat_s, sibling).start()
    attn_reduce.step(2)
    outgoing(0)
    stat_copy(0, stat_s, sibling).wait()
    stat_acc[0] = stat_s[...] + stat_in[0]
    stat_copy(1, stat_acc.at[0], facing).start()
    attn_reduce.step(3)
    outgoing(1)
    attn_reduce.step(4)
    attn_reduce.step(5)
    stat_copy(1, stat_acc.at[0], facing).wait()
    stat_acc[1] = stat_acc[0] + stat_in[1]
    stat_copy(2, stat_acc.at[1], beside).start()
    attn_reduce.finish()
    stat_copy(2, stat_acc.at[1], beside).wait()
    stat_acc[2] = stat_acc[1] + stat_in[2]
    stat_line[z] = stat_acc[2]

    def stat_send_line(j):
        return remote(
            stat_acc.at[2],
            stat_line.at[z],
            stat_send.at[2 + j],
            stat_recv.at[2 + j],
            device(line[j], x, y, c),
        )

    for j in range(1, DEPTH):
        stat_send_line(j).start()

    attn_owner = functools.reduce(jnp.logical_or, [owned(m) for m in range(4)])
    ff_owner = functools.reduce(jnp.logical_or, [owned(m) for m in range(4, 7)])

    def arrived(buffer):
        pltpu.make_async_copy(buffer, buffer, adv_recv.at[0]).wait()

    @pl.when(attn_owner)
    def _():
        arrived(y_attn)
        gram_s[...] = gram_wide(y_attn[...].reshape(-1, width))

    @pl.when(ff_owner)
    def _():
        arrived(y_ff)
        gram_s[...] = gram_wide(y_ff[...].reshape(-1, width))

    @pl.when(attn_owner | ff_owner)
    def _():
        unit = lax.broadcasted_iota(jnp.int32, (width, width), 0) == lax.broadcasted_iota(
            jnp.int32, (width, width), 1
        )
        gram_mat = gram_s[...]
        trace = jnp.sum(jnp.where(unit, gram_mat, 0.0), keepdims=True)
        inverse = 1.0 / (jnp.sqrt(trace) + NS_EPS)
        diagonal = jnp.where(unit, COEF_A, 0.0)
        gram_mat = gram_mat * (inverse * inverse)

        def poly(value):
            return diagonal + COEF_B * value + COEF_C * mul_wide(value, value)

        step_mat = poly(gram_mat)
        gram_s[...] = mul_wide(mul_wide(gram_mat, step_mat), step_mat)
        chain_s[...] = step_mat * inverse

        def turn(i, carry):
            now = gram_s[...]
            step_now = poly(now)
            both = mul_wide(jnp.concatenate([now, chain_s[...]], axis=0), step_now)
            chain_s[...] = both[width:]
            gram_s[...] = mul_wide(both[:width], step_now)
            return carry

        lax.fori_loop(0, NS_ITERS - 2, turn, 0)
        chain_s[...] = mul_wide(chain_s[...], poly(gram_s[...]))

    @pl.when(attn_owner)
    def _():
        value = y_attn[...].reshape(-1, width)
        x_attn[...] = mul_wide(value, chain_s[...]).astype(LOW).reshape(x_attn.shape)

    @pl.when(ff_owner)
    def _():
        value = y_ff[...].reshape(-1, width)
        x_ff[...] = mul_wide(value, chain_s[...]).astype(LOW).reshape(x_ff.shape)

    chips = DEPTH * ACROSS * SIDES

    def x_copy(m, i):
        start, count = pieces[m]
        source = x_attn if m < 4 else x_ff
        to = i // SIDES
        return remote(
            source.at[to],
            xrows_ref.at[pl.ds(start, count)],
            x_send.at[i],
            x_recv.at[m],
            (to, lax.rem(i, SIDES) * CORES + OWNERS[m][3]),
        )

    mine = shard * SIDES + y
    for m in range(7):
        start, count = pieces[m]
        source = x_attn if m < 4 else x_ff

        @pl.when(owned(m))
        def _():
            def send(i, carry):
                x_copy(m, lax.rem(mine + i, chips)).start()
                return carry

            lax.fori_loop(1, chips, send, 0)
            pltpu.make_async_copy(
                source.at[shard], xrows_ref.at[pl.ds(start, count)], x_recv.at[m]
            ).start()

    for j in range(1, DEPTH):
        remote(
            stat_acc.at[2],
            stat_line.at[lax.rem(z + DEPTH - j, DEPTH)],
            stat_send.at[2 + j],
            stat_recv.at[2 + j],
            device(line[j], x, y, c),
        ).wait()
    total_ref[...] = (stat_line[0] + stat_line[1]) + (stat_line[2] + stat_line[3])
    for one in gathers:
        one.sent()
    for one in reduces:
        one.done()

    def fan_copy(m):
        start, count = pieces[m]
        rows_m = xrows_ref.at[pl.ds(start, count)]
        return remote(rows_m, rows_m, fan_send.at[m], fan_recv.at[m], sibling)

    for m in range(7):
        start, count = pieces[m]

        @pl.when(c == OWNERS[m][3])
        def _():
            rows_m = xrows_ref.at[pl.ds(start, count)]
            pltpu.make_async_copy(rows_m, rows_m, x_recv.at[m]).wait()
            fan_copy(m).start()

    for m in range(7):

        @pl.when(c != OWNERS[m][3])
        def _():
            fan_copy(m).wait_recv()

        @pl.when(c == OWNERS[m][3])
        def _():
            fan_copy(m).wait_send()

        @pl.when(owned(m))
        def _():
            def sent(i, carry):
                x_copy(m, lax.rem(mine + i, chips)).wait_send()
                return carry

            lax.fori_loop(1, chips, sent, 0)


def rotary_table():
    half = HEAD_DIM // 2
    frequency = (ROPE_BASE ** (-2.0 * np.arange(half) / HEAD_DIM)).astype(np.float32)
    angles = np.arange(TIME_SLOTS, dtype=np.float32)[:, None] * frequency[None, :]
    cosine = np.cos(angles.astype(np.float64)).astype(np.float32)
    sine = np.sin(angles.astype(np.float64)).astype(np.float32)
    table = np.concatenate([cosine] * 4 + [-sine, sine, -sine, sine], axis=1)
    parts = []
    for _ in range(3):
        parts.append(table.astype(LOW))
        table = table - parts[-1].astype(np.float32)
    return np.stack(parts)


def whole_step(tokens, cotangent, lengths, variates, times, gains, attn_bias, weights, momenta):
    rows, width = tokens.shape
    heads = attn_bias.shape[1]
    attn_rows, ff_rows = weights[1].shape[0], weights[3].shape[0]
    pieces = offsets(attn_rows, ff_rows)
    ff = ff_rows * DEPTH * ACROSS
    shards = DEPTH * ACROSS
    shard_rows = 4 * attn_rows + 3 * ff_rows
    low = lambda *shape: pltpu.VMEM(shape, LOW)
    wide = lambda *shape: pltpu.VMEM(shape, WIDE)
    dma = lambda *shape: pltpu.SemaphoreType.DMA(shape)

    def part_scratch(count):
        half, quarter = count // 2, count // 4
        relative = 2 * DEPTH - 1
        return [
            dma(DEPTH),
            dma(DEPTH),
            dma(relative),
            dma(2, relative),
            dma(DEPTH),
            dma(DEPTH),
            dma(relative),
            dma(2, relative),
            low(DEPTH, ACROSS, half, width),
            low(DEPTH, ACROSS, half, width),
            low(DEPTH, ACROSS, half, width),
            low(DEPTH, ACROSS, half, width),
            low(DEPTH, quarter, width),
            low(DEPTH, quarter, width),
            low(DEPTH, quarter, width),
            wide(quarter, width),
            *[dma(DEPTH) for _ in range(8)],
            dma(3),
            dma(3),
            dma(3),
        ]

    return pl.pallas_call(
        functools.partial(whole_kernel, pieces),
        out_shape=(
            jax.ShapeDtypeStruct((rows, width), LOW),
            jax.ShapeDtypeStruct((rows, width), LOW),
            jax.ShapeDtypeStruct((shard_rows, width), LOW),
            jax.ShapeDtypeStruct((shard_rows, width), LOW),
            jax.ShapeDtypeStruct((STATS, width), WIDE),
        ),
        in_specs=[SCALARS] * 2 + [WHOLE] * 14,
        out_specs=(WHOLE,) * 5,
        scratch_shapes=[
            low(shards, shard_rows, width),
            low(DEPTH, ACROSS, shard_rows, width),
            wide(shard_rows, width),
            low(rows, width),
            low(rows, width),
            low(rows, width),
            low(rows, width),
            low(rows, width),
            low(rows, ff),
            low(rows, ff),
            low(rows, ff),
            low(rows, 3 * width),
            low(rows, 3 * width),
            wide(rows // PAIR, heads // 2, 2 * PAIR, PAIR),
            wide(rows, width),
            wide(rows, width),
            low(rows, width),
            wide(rows, 2),
            wide(rows, 2 * LANES),
            wide(shards, attn_rows, width),
            wide(shards, ff_rows, width),
            low(shards, attn_rows, width),
            low(shards, ff_rows, width),
            wide(width, width),
            wide(width, width),
            wide(STATS, width),
            wide(3, STATS, width),
            wide(3, STATS, width),
            wide(DEPTH, STATS, width),
            dma(6),
            dma(6),
            dma(1),
            dma(shards * SIDES),
            dma(7),
            dma(7),
            dma(7),
            *part_scratch(4 * attn_rows),
            *part_scratch(3 * ff_rows),
        ],
        compiler_params=pltpu.CompilerParams(
            vmem_limit_bytes=60 << 20, collective_id=0, has_side_effects=True
        ),
        name="whole",
    )(
        lengths,
        attn_bias,
        tokens,
        cotangent,
        variates,
        times.reshape(rows // PAIR, PAIR),
        jnp.asarray(rotary_table()),
        gains,
        *weights,
        *momenta,
    )


def update_kernel(
    pieces,
    factors,
    grow_ref,
    xrow_ref,
    stat_ref,
    w_qkv,
    w_out,
    w_gate_up,
    w_down,
    m_qkv,
    m_out,
    m_gate_up,
    m_down,
    gains,
    bias,
    gain_moment,
    gain_square,
    bias_moment,
    bias_square,
    g_qkv,
    g_out,
    g_gate_up,
    g_down,
    nm_qkv,
    nm_out,
    nm_gate_up,
    nm_down,
    nw_qkv,
    nw_out,
    nw_gate_up,
    nw_down,
    g_gains,
    n_gain_moment,
    n_gain_square,
    n_gains,
    g_bias,
    n_bias_moment,
    n_bias_square,
    n_bias,
):
    shrink = 1.0 - MUON_RATE * MUON_DECAY

    def one(index, turned, g, m, w, nm, nw):
        start, count = pieces[index]
        grad = grow_ref[start : start + count, :].astype(WIDE)
        ortho = xrow_ref[start : start + count, :].astype(WIDE)
        if turned:
            grad, ortho = grad.T, ortho.T
        g[...] = grad
        nm[...] = MUON_MU * m[...] + grad
        nw[...] = w[...] * shrink - factors[index] * ortho

    for j in range(3):
        one(j, False, *[r.at[j] for r in (g_qkv, m_qkv, w_qkv, nm_qkv, nw_qkv)])
    one(3, False, g_out, m_out, w_out, nm_out, nw_out)
    for j in range(2):
        refs = (g_gate_up, m_gate_up, w_gate_up, nm_gate_up, nw_gate_up)
        one(4 + j, True, *[r.at[j] for r in refs])
    one(6, False, g_down, m_down, w_down, nm_down, nw_down)

    grad = stat_ref[0:2, :]
    g_gains[...] = grad
    n_gain_moment[...], n_gain_square[...], n_gains[...] = adam_step(
        gains[...], grad, gain_moment[...], gain_square[...]
    )
    heads = bias.shape[1]
    sums = jnp.sum(stat_ref[8:24, :PAIR].T, axis=0, keepdims=True)
    grad = jnp.concatenate([sums[:, :heads], sums[:, 8 : 8 + heads]], axis=0)
    g_bias[...] = grad
    n_bias_moment[...], n_bias_square[...], n_bias[...] = adam_step(
        bias[...], grad, bias_moment[...], bias_square[...]
    )


def update(factors, grad_rows, ortho_rows, stats, weights, momenta, small):
    pieces = offsets(weights[1].shape[0], weights[3].shape[0])
    gains, bias = small[:2]
    like = lambda a: jax.ShapeDtypeStruct(a.shape, WIDE)
    outs = [like(a) for a in (*weights, *weights, *weights, *[gains] * 4, *[bias] * 4)]
    return pl.pallas_call(
        functools.partial(update_kernel, pieces, factors),
        out_shape=tuple(outs),
        in_specs=[WHOLE] * 17,
        out_specs=(WHOLE,) * len(outs),
        compiler_params=pltpu.CompilerParams(vmem_limit_bytes=58 << 20),
        name="update",
    )(grad_rows, ortho_rows, stats, *weights, *momenta, *small)


def body(
    tokens,
    cotangent,
    lengths,
    variates,
    times,
    weight_qkv,
    weight_out,
    weight_gate_up,
    weight_down,
    momentum_qkv,
    momentum_out,
    momentum_gate_up,
    momentum_down,
    gains,
    attn_bias,
    gain_moment,
    gain_square,
    bias_moment,
    bias_square,
):
    width = tokens.shape[1]
    heads = attn_bias.shape[1]
    attn_rows = weight_out.shape[0]
    ff_rows = weight_down.shape[0]
    fsdp = lax.axis_size("fsdp")
    ff = ff_rows * fsdp
    attn_width = attn_rows * fsdp
    shrink = 1.0 - MUON_RATE * MUON_DECAY
    scale_attn = MUON_RATE * 0.2 * math.sqrt(max(width, attn_width))
    scale_ff = MUON_RATE * 0.2 * math.sqrt(max(width, ff))
    sizes = (fsdp, lax.axis_size("ns"))
    if sizes == (DEPTH * ACROSS, SIDES * CORES) and attn_rows == 48 and ff_rows == 128:
        turn = lambda a: jnp.swapaxes(a, 1, 2)
        shards = (turn(weight_qkv), weight_out, weight_gate_up, weight_down)
        momenta = (turn(momentum_qkv), momentum_out, momentum_gate_up, momentum_down)
        out_tokens, grad_tokens, grad_rows, ortho_rows, stats = whole_step(
            tokens, cotangent, lengths, variates, times, gains, attn_bias, shards, momenta
        )
        outs = list(
            update(
                (scale_attn,) * 4 + (scale_ff,) * 3,
                grad_rows,
                ortho_rows,
                stats,
                shards,
                momenta,
                (gains, attn_bias, gain_moment, gain_square, bias_moment, bias_square),
            )
        )
        for i in (0, 4, 8):
            outs[i] = turn(outs[i])
        return (out_tokens, grad_tokens, *outs)
    weights = pack(weight_qkv, weight_out, weight_gate_up, weight_down)
    momenta = pack(momentum_qkv, momentum_out, momentum_gate_up, momentum_down)
    full = lax.all_gather(weights.astype(LOW), "fsdp", axis=0, tiled=False)
    aligned = attn_rows % 16 == 0 and ff_rows % 16 == 0
    pieces = offsets(attn_rows, ff_rows)
    if not aligned:
        full = jnp.concatenate(
            [full[:, s : s + n].reshape(1, fsdp * n, width) for s, n in pieces], axis=1
        )
    out_tokens, grad_tokens, grads, stats = layer(
        tokens, cotangent, lengths, variates, times, full, gains, attn_bias, ff, WIDE
    )
    if not aligned:
        wholes = offsets(attn_width, ff)
        grads = jnp.concatenate(
            [grads[0, s : s + n].reshape(fsdp, n // fsdp, width) for s, n in wholes], axis=1
        )
    summed = lax.psum_scatter(grads, "fsdp", scatter_dimension=0, tiled=False)
    grad_rows = lax.psum(summed.astype(LOW), "ns").astype(WIDE)
    bias_part = jnp.sum(stats[8:, :PAIR], axis=1).reshape(2, 8)[:, :heads]
    grad_gains, grad_bias = lax.psum((stats[:2], bias_part), ("fsdp", "ns"))

    new_momenta = MUON_MU * momenta + grad_rows
    advance = grad_rows + MUON_MU * new_momenta
    parts = [advance[s : s + n] for s, n in pieces]
    grams = jnp.stack(
        [
            lax.dot_general(
                y,
                y,
                (((0,), (0,)), ((), ())),
                precision=lax.Precision.HIGHEST,
                preferred_element_type=WIDE,
            )
            for y in parts
        ]
    )
    factor = newton_schulz(lax.psum(grams, "fsdp"))
    turned = jnp.concatenate(
        [
            (scale_attn if i < 4 else scale_ff)
            * jnp.dot(
                y, factor[i], precision=lax.Precision.HIGHEST, preferred_element_type=WIDE
            )
            for i, y in enumerate(parts)
        ],
        axis=0,
    )
    new_weights = weights * shrink - turned
    new_gain_moment, new_gain_square, new_gains = adam_step(
        gains, grad_gains, gain_moment, gain_square
    )
    new_bias_moment, new_bias_square, new_bias = adam_step(
        attn_bias, grad_bias, bias_moment, bias_square
    )
    return (
        out_tokens,
        grad_tokens,
        *unpack(grad_rows, attn_rows, ff_rows),
        *unpack(new_momenta, attn_rows, ff_rows),
        *unpack(new_weights, attn_rows, ff_rows),
        grad_gains,
        new_gain_moment,
        new_gain_square,
        new_gains,
        grad_bias,
        new_bias_moment,
        new_bias_square,
        new_bias,
    )


def solution(mesh):
    rows = P(("fsdp", "ns"), None)
    line = P(("fsdp", "ns"))
    matrices = (P(None, None, "fsdp"), P("fsdp", None), P(None, None, "fsdp"), P("fsdp", None))
    return jax.shard_map(
        body,
        mesh=mesh,
        in_specs=(rows, rows, line, rows, line, *matrices, *matrices, *([P()] * 6)),
        out_specs=(rows, rows, *matrices, *matrices, *matrices, *([P()] * 8)),
        check_vma=False,
    )
```

```python
import functools
import math

import jax
import jax.numpy as jnp
import numpy as np
from jax import lax
from jax.experimental import pallas as pl
from jax.experimental.pallas import tpu as pltpu
from jax.sharding import PartitionSpec as P

HEAD_DIM = 64
BUCKET = 64
TIME_SLOTS = 64
NS_ITERS = 5
STEP = 10

EPS_NORM = 1e-06
ROPE_BASE = 10000.0
NEG_FILL = -1000000000.0
COEF_A = 3.4445
COEF_B = -4.775
COEF_C = 2.0315
NS_EPS = 1e-07
MUON_MU = 0.95
MUON_RATE = 0.25
MUON_DECAY = 0.01
ADAM_RATE = 0.8
BETA_ONE = 0.9
BETA_TWO = 0.95
ADAM_EPS = 1e-08

LOW = jnp.bfloat16
WIDE = jnp.float32
BLOCK = 256
PAIR = 2 * BUCKET
LANES = 2 * HEAD_DIM
STATS = 24
WHOLE = pl.BlockSpec(memory_space=pltpu.VMEM)
SCALARS = pl.BlockSpec(memory_space=pltpu.SMEM)
ANYWHERE = pl.BlockSpec(memory_space=pl.ANY)


def mul_nn(left, right):
    return lax.dot_general(left, right, (((1,), (0,)), ((), ())), preferred_element_type=WIDE)


def mul_nt(left, right):
    return lax.dot_general(left, right, (((1,), (1,)), ((), ())), preferred_element_type=WIDE)


def mul_tn(left, right):
    return lax.dot_general(left, right, (((0,), (0,)), ((), ())), preferred_element_type=WIDE)


def offsets(attn_rows, ff_rows):
    counts = [attn_rows] * 4 + [ff_rows] * 3
    starts = [sum(counts[:i]) for i in range(7)]
    return list(zip(starts, counts))


def layer_kernel(
    pieces,
    lengths,
    bias,
    tok_ref,
    cot_ref,
    var_ref,
    time_ref,
    table_ref,
    gain_ref,
    w_ref,
    out_ref,
    gtok_ref,
    grad_ref,
    stat_ref,
    n1_s,
    n2_s,
    att_s,
    gml_s,
    hid_s,
    glow_s,
    gg_s,
    gu_s,
    gqkv_s,
):
    step = pl.program_id(0)
    rows, width = tok_ref.shape
    heads = bias.shape[1]
    here = pl.ds(pl.multiple_of(step * rows, rows), rows)

    def weight(first, last):
        parts = []
        for i in range(first, last):
            start, count = pieces[i]
            part = w_ref[:, start : start + count, :]
            parts.append(part.reshape(part.shape[0] * count, width))
        return parts[0] if len(parts) == 1 else jnp.concatenate(parts, axis=0)

    @pl.when(step == 0)
    def _():
        stat_ref[...] = jnp.zeros_like(stat_ref)

    lane = lax.broadcasted_iota(jnp.int32, (1, LANES), 1)
    low_head = lane < HEAD_DIM
    low_half = lane % HEAD_DIM < HEAD_DIM // 2
    per_block = rows // PAIR
    var_rows = var_ref[pl.ds(step * per_block, per_block), :]
    time_rows = time_ref[pl.ds(step * per_block, per_block), :]
    filler = jnp.zeros((8 - 2 * per_block, PAIR), WIDE)
    columns = jnp.concatenate([var_rows, time_rows, filler], axis=0).T
    slots = lax.broadcasted_iota(jnp.int32, (1, TIME_SLOTS), 1).astype(WIDE)
    hot = jnp.concatenate(
        [(columns[:, per_block + p : per_block + p + 1] == slots) for p in range(per_block)], axis=0
    ).astype(LOW)
    looked = mul_nn(hot, table_ref[0]) + mul_nn(hot, table_ref[1]) + mul_nn(hot, table_ref[2])
    cosine = looked[:, :LANES]
    sine = looked[:, LANES:]

    def swapped(values):
        half = HEAD_DIM // 2
        return jnp.where(
            low_half, pltpu.roll(values, LANES - half, 1), pltpu.roll(values, half, 1)
        )

    gain_one = gain_ref[0:1, :]
    gain_two = gain_ref[1:2, :]
    tokens = tok_ref[...].astype(WIDE)
    scale_one = lax.rsqrt(jnp.mean(tokens * tokens, axis=-1, keepdims=True) + EPS_NORM)
    unit_one = tokens * scale_one
    normed_one = (unit_one * gain_one).astype(LOW)
    n1_s[here, :] = normed_one
    qkv = mul_nt(normed_one, weight(0, 3))

    query_scale = HEAD_DIM ** (-0.5)
    units = []
    attended = []
    row_id = lax.broadcasted_iota(jnp.int32, (PAIR, 1), 0)
    lane_id = lax.broadcasted_iota(jnp.int32, (1, PAIR), 1)
    same_bucket = (row_id < BUCKET) == (lane_id < BUCKET)
    masks = []
    live_cols = []
    for p in range(per_block):
        first = lengths[(step * per_block + p) * 2]
        second = lengths[(step * per_block + p) * 2 + 1]
        live_key = lane_id % BUCKET < jnp.where(lane_id < BUCKET, first, second)
        live_cols.append(row_id % BUCKET < jnp.where(row_id < BUCKET, first, second))
        mask = same_bucket & live_key
        same_var = columns[:, p : p + 1] == var_rows[p : p + 1, :]
        masks.append((mask, same_var))

    for hp in range(heads // 2):
        cols = slice(hp * LANES, (hp + 1) * LANES)
        q = qkv[:, cols]
        k = qkv[:, width + hp * LANES : width + (hp + 1) * LANES]
        v = qkv[:, 2 * width + hp * LANES : 2 * width + (hp + 1) * LANES].astype(LOW)
        q = ((q * cosine + swapped(q) * sine) * query_scale).astype(LOW)
        k = (k * cosine + swapped(k) * sine).astype(LOW)
        q_first = jnp.where(low_head, q, jnp.zeros_like(q))
        q_second = jnp.where(low_head, jnp.zeros_like(q), q)
        att_pairs = []
        for p in range(per_block):
            part = slice(p * PAIR, (p + 1) * PAIR)
            mask, same_var = masks[p]
            q2 = jnp.concatenate([q_first[part], q_second[part]], axis=0)
            kp = k[part]
            vp = v[part]
            raw = mul_nt(q2, kp)
            halves = []
            for j in range(2):
                h = 2 * hp + j
                biased = raw[j * PAIR : (j + 1) * PAIR] + jnp.where(
                    same_var, bias[0, h], bias[1, h]
                )
                halves.append(jnp.where(mask, biased, NEG_FILL))
            scores = jnp.concatenate(halves, axis=0)
            top = jnp.max(scores, axis=-1, keepdims=True)
            exponent = jnp.exp(scores - top)
            probs = exponent / jnp.sum(exponent, axis=-1, keepdims=True)
            probs_low = probs.astype(LOW)
            both = mul_nn(probs_low, vp)
            att_pairs.append(jnp.where(low_head, both[:PAIR], both[PAIR:]))
            units.append((hp, p, q2, kp, vp, probs, probs_low))
        attended.append(jnp.concatenate(att_pairs, axis=0).astype(LOW))
    attended = jnp.concatenate(attended, axis=1)
    att_s[here, :] = attended
    w_out = weight(3, 4)
    mid = tokens + mul_nn(attended, w_out)
    scale_two = lax.rsqrt(jnp.mean(mid * mid, axis=-1, keepdims=True) + EPS_NORM)
    unit_two = mid * scale_two
    normed_two = (unit_two * gain_two).astype(LOW)
    n2_s[here, :] = normed_two
    w_gate = weight(4, 5)
    w_up = weight(5, 6)
    w_down = weight(6, 7)
    gate = mul_nt(normed_two, w_gate)
    up = mul_nt(normed_two, w_up)
    sig = 1.0 / (1.0 + jnp.exp(-gate))
    silu = gate * sig
    hidden = (silu * up).astype(LOW)
    hid_s[here, :] = hidden
    out_ref[...] = (mid + mul_nn(hidden, w_down)).astype(LOW)

    live_row = jnp.concatenate(live_cols, axis=0)
    g_out = jnp.where(live_row, cot_ref[...].astype(WIDE), 0.0)
    g_low = g_out.astype(LOW)
    glow_s[here, :] = g_low
    g_hidden = mul_nt(g_low, w_down)
    g_gate = (g_hidden * up * sig * (1.0 + gate * (1.0 - sig))).astype(LOW)
    g_up = (g_hidden * silu).astype(LOW)
    gg_s[here, :] = g_gate
    gu_s[here, :] = g_up
    e_two = mul_nn(g_gate, w_gate) + mul_nn(g_up, w_up)
    stat_ref[1:2, :] += jnp.sum(e_two * unit_two, axis=0, keepdims=True)
    scaled = e_two * gain_two
    g_mid = g_out + scale_two * (
        scaled - unit_two * jnp.mean(scaled * unit_two, axis=-1, keepdims=True)
    )
    g_mid_low = g_mid.astype(LOW)
    gml_s[here, :] = g_mid_low
    g_att = mul_nt(g_mid_low, w_out).astype(LOW)

    parts_q = [[None] * per_block for _ in range(heads // 2)]
    parts_k = [[None] * per_block for _ in range(heads // 2)]
    parts_v = [[None] * per_block for _ in range(heads // 2)]
    for hp, p, q2, kp, vp, probs, probs_low in units:
        part = slice(p * PAIR, (p + 1) * PAIR)
        mask, same_var = masks[p]
        ga = g_att[part, hp * LANES : (hp + 1) * LANES]
        ga2 = jnp.concatenate(
            [
                jnp.where(low_head, ga, jnp.zeros_like(ga)),
                jnp.where(low_head, jnp.zeros_like(ga), ga),
            ],
            axis=0,
        )
        g_probs = mul_nt(ga2, vp)
        row_dot = jnp.sum(probs * g_probs, axis=-1, keepdims=True)
        g_scores = probs * (g_probs - row_dot)
        for j in range(2):
            h = 2 * hp + j
            mine = g_scores[j * PAIR : (j + 1) * PAIR]
            stat_ref[8 + h : 9 + h, :PAIR] += jnp.sum(
                jnp.where(same_var, mine, 0.0), axis=0, keepdims=True
            )
            stat_ref[16 + h : 17 + h, :PAIR] += jnp.sum(
                jnp.where(same_var, 0.0, mine), axis=0, keepdims=True
            )
        low_scores = g_scores.astype(LOW)
        both = mul_nn(low_scores, kp)
        parts_q[hp][p] = jnp.where(low_head, both[:PAIR], both[PAIR:])
        parts_k[hp][p] = mul_tn(low_scores, q2)
        parts_v[hp][p] = mul_tn(probs_low, ga2)
    g_q = []
    g_k = []
    g_v = []
    for hp in range(heads // 2):
        dq = jnp.concatenate(parts_q[hp], axis=0)
        dk = jnp.concatenate(parts_k[hp], axis=0)
        g_q.append(((dq * cosine - swapped(dq) * sine) * query_scale).astype(LOW))
        g_k.append((dk * cosine - swapped(dk) * sine).astype(LOW))
        g_v.append(jnp.concatenate(parts_v[hp], axis=0).astype(LOW))
    g_qkv = jnp.concatenate(g_q + g_k + g_v, axis=1)
    gqkv_s[here, :] = g_qkv
    e_one = mul_nn(g_qkv, weight(0, 3))
    stat_ref[0:1, :] += jnp.sum(e_one * unit_one, axis=0, keepdims=True)
    scaled = e_one * gain_one
    gtok_ref[...] = (
        g_mid
        + scale_one * (scaled - unit_one * jnp.mean(scaled * unit_one, axis=-1, keepdims=True))
    ).astype(LOW)

    @pl.when(step == pl.num_programs(0) - 1)
    def _():
        def put(index, left, right):
            start, count = pieces[index]
            grad_ref[:, start : start + count, :] = (
                mul_tn(left, right)
                .reshape(grad_ref.shape[0], count, width)
                .astype(grad_ref.dtype)
            )

        for j in range(3):
            put(j, gqkv_s[:, j * width : (j + 1) * width], n1_s[...])
        put(3, att_s[...], gml_s[...])
        put(4, gg_s[...], n2_s[...])
        put(5, gu_s[...], n2_s[...])
        put(6, hid_s[...], glow_s[...])


def layer(tokens, cotangent, lengths, variates, times, packed, gains, attn_bias, ff, grad_type):
    rows, width = tokens.shape
    heads = attn_bias.shape[1]
    copies, shard_rows, _ = packed.shape
    pieces = offsets(heads * HEAD_DIM // copies, ff // copies)
    half = HEAD_DIM // 2
    frequency = ROPE_BASE ** (-2.0 * jnp.arange(half, dtype=WIDE) / HEAD_DIM)
    angles = jnp.arange(TIME_SLOTS, dtype=WIDE)[:, None] * frequency[None, :]
    cosine, sine = jnp.cos(angles), jnp.sin(angles)
    table = jnp.concatenate([cosine] * 4 + [-sine, sine, -sine, sine], axis=1)
    first = table.astype(LOW)
    rest = table - first.astype(WIDE)
    second = rest.astype(LOW)
    third = (rest - second.astype(WIDE)).astype(LOW)
    table = jnp.stack([first, second, third])
    grid = rows // BLOCK
    block = pl.BlockSpec((BLOCK, width), lambda i: (i, 0))
    low_scratch = lambda columns: pltpu.VMEM((rows, columns), LOW)
    return pl.pallas_call(
        functools.partial(layer_kernel, pieces),
        grid=(grid,),
        out_shape=(
            jax.ShapeDtypeStruct((rows, width), LOW),
            jax.ShapeDtypeStruct((rows, width), LOW),
            jax.ShapeDtypeStruct((copies, shard_rows, width), grad_type),
            jax.ShapeDtypeStruct((STATS, width), WIDE),
        ),
        in_specs=[SCALARS, SCALARS, block, block, WHOLE, WHOLE, WHOLE, WHOLE, WHOLE],
        out_specs=(block, block, WHOLE, WHOLE),
        scratch_shapes=[
            low_scratch(width),
            low_scratch(width),
            low_scratch(width),
            low_scratch(width),
            low_scratch(ff),
            low_scratch(width),
            low_scratch(ff),
            low_scratch(ff),
            low_scratch(3 * width),
        ],
        compiler_params=pltpu.CompilerParams(vmem_limit_bytes=58 << 20),
        name="layer",
    )(
        lengths,
        attn_bias,
        tokens,
        cotangent,
        variates.astype(WIDE).reshape(rows // PAIR, PAIR),
        times.astype(WIDE).reshape(rows // PAIR, PAIR),
        table,
        gains,
        packed,
    )


def pack(qkv, out, gate_up, down):
    width = out.shape[-1]
    return jnp.concatenate(
        [
            jnp.swapaxes(qkv, 1, 2).reshape(-1, width),
            out,
            jnp.swapaxes(gate_up, 1, 2).reshape(-1, width),
            down,
        ],
        axis=0,
    )


def unpack(packed, attn_rows, ff_rows):
    width = packed.shape[-1]
    qkv = jnp.swapaxes(packed[: 3 * attn_rows].reshape(3, attn_rows, width), 1, 2)
    out = packed[3 * attn_rows : 4 * attn_rows]
    ends = 4 * attn_rows + 2 * ff_rows
    gate_up = jnp.swapaxes(packed[4 * attn_rows : ends].reshape(2, ff_rows, width), 1, 2)
    return qkv, out, gate_up, packed[ends:]


def newton_schulz(gram_mat):
    def product(left, right):
        return jnp.einsum(
            "mde,mef->mdf",
            left,
            right,
            precision=lax.Precision.HIGHEST,
            preferred_element_type=WIDE,
        )

    norm_val = jnp.sqrt(jnp.trace(gram_mat, axis1=1, axis2=2))[:, None, None] + NS_EPS
    gram_mat = gram_mat / (norm_val * norm_val)
    unit = jnp.eye(gram_mat.shape[-1], dtype=WIDE)[None]
    chain = None
    for turn_idx in range(NS_ITERS):
        poly_mat = COEF_A * unit + COEF_B * gram_mat + COEF_C * product(gram_mat, gram_mat)
        chain = poly_mat if chain is None else product(poly_mat, chain)
        if turn_idx < NS_ITERS - 1:
            gram_mat = product(product(poly_mat, gram_mat), poly_mat)
    return chain / norm_val


def adam_step(param, grad, moment, square):
    new_moment = BETA_ONE * moment + (1.0 - BETA_ONE) * grad
    new_square = BETA_TWO * square + (1.0 - BETA_TWO) * grad * grad
    corrected = new_moment / (1.0 - BETA_ONE**STEP)
    scaled = jnp.sqrt(new_square / (1.0 - BETA_TWO**STEP)) + ADAM_EPS
    return (new_moment, new_square, param - ADAM_RATE * corrected / scaled)


DEPTH, ACROSS = 4, 2
SIDES, CORES = 2, 2
TURNS = (2, 1, 3, 0)
OWNERS = (
    (2, 0, 0, 0),
    (2, 1, 0, 1),
    (1, 1, 0, 0),
    (2, 1, 1, 0),
    (2, 0, 1, 1),
    (1, 0, 0, 1),
    (1, 1, 1, 0),
)


def place():
    f = lax.axis_index("fsdp")
    n = lax.axis_index("ns")
    return f // ACROSS, f % ACROSS, n // CORES, n % CORES


def device(z, x, y, c):
    return (z * ACROSS + x, y * CORES + c)


def remote(src, dst, send_sem, recv_sem, where):
    return pltpu.make_async_remote_copy(
        src_ref=src,
        dst_ref=dst,
        send_sem=send_sem,
        recv_sem=recv_sem,
        device_id=where,
        device_id_type=pl.DeviceIdType.MESH,
    )


def greet(where):
    pl.semaphore_signal(
        pltpu.get_barrier_semaphore(),
        inc=1,
        device_id=where,
        device_id_type=pl.DeviceIdType.MESH,
    )


def halves(value):
    high = value.astype(LOW)
    return high, (value - high.astype(WIDE)).astype(LOW)


def square_wide(value):
    high, low = halves(value)
    cross = mul_nn(high, low)
    return mul_nn(high, high) + (cross + cross.T)


def mul_wide(left, right):
    columns = right.shape[1]
    left_high, left_low = halves(left)
    right_high, right_low = halves(right)
    first = mul_nn(left_high, jnp.concatenate([right_high, right_low], axis=1))
    return first[:, :columns] + (first[:, columns:] + mul_nn(left_low, right_high))


def gram_wide(value):
    high, low = halves(value)
    cross = mul_tn(high, low)
    return mul_tn(high, high) + (cross + cross.T)


def whole_kernel(
    pieces,
    lengths,
    bias,
    tok_hbm,
    cot_hbm,
    var_ref,
    time_ref,
    table_ref,
    gain_ref,
    wqkv_ref,
    wout_ref,
    wgate_up_ref,
    wdown_ref,
    mqkv_hbm,
    mout_hbm,
    mgate_up_hbm,
    mdown_hbm,
    out_ref,
    gtok_ref,
    grows_ref,
    xrows_ref,
    total_ref,
    tok_ref,
    cot_ref,
    mqkv_ref,
    mout_ref,
    mgate_up_ref,
    mdown_ref,
    load_sem,
    w_s,
    grad_s,
    momenta,
    n1_s,
    n2_s,
    att_s,
    gml_s,
    glow_s,
    hid_s,
    gg_s,
    gu_s,
    low_s,
    gqkv_s,
    probs_s,
    mid_s,
    gmid_s,
    gatt_s,
    scale_s,
    rope_s,
    y_attn,
    y_ff,
    g_attn,
    g_ff,
    x_attn,
    x_ff,
    gram_s,
    chain_s,
    stat_s,
    stat_in,
    stat_acc,
    stat_line,
    stat_send,
    stat_recv,
    adv_recv,
    mom_recv,
    x_send,
    x_recv,
    fan_send,
    fan_recv,
    *per_part,
):
    z, x, y, c = place()
    shard = z * ACROSS + x
    rows, width = tok_ref.shape
    heads = bias.shape[1]
    sibling = device(z, x, y, 1 - c)
    facing = device(z, x, 1 - y, c)
    corner = device(z, x, 1 - y, 1 - c)
    beside = device(z, 1 - x, y, c)
    upper = device(z + 1, x, y, c)
    lower = device(z - 1, x, y, c)
    world = DEPTH * ACROSS * SIDES * CORES
    rank = shard * (SIDES * CORES) + y * CORES + c
    line = [lax.rem(z + k, DEPTH) for k in range(DEPTH)]
    part = 2 * c + y

    def hello(i, carry):
        other = lax.rem(rank + 1 + i, world)
        greet((other // (SIDES * CORES), lax.rem(other, SIDES * CORES)))
        return carry

    lax.fori_loop(0, world - 1, hello, 0)
    loads = [
        pltpu.make_async_copy(src, dst, load_sem.at[i])
        for i, (src, dst) in enumerate(
            (
                (tok_hbm, tok_ref),
                (cot_hbm, cot_ref),
                (mqkv_hbm, mqkv_ref),
                (mout_hbm, mout_ref),
                (mgate_up_hbm, mgate_up_ref),
                (mdown_hbm, mdown_ref),
            )
        )
    ]
    for one in loads:
        one.start()

    def put(index, value):
        start, count = pieces[index]
        w_s[shard, start : start + count, :] = value.astype(LOW)

    for j in range(3):
        put(j, wqkv_ref[j])
    put(3, wout_ref[...])
    put(4, wgate_up_ref[0].T)
    put(5, wgate_up_ref[1].T)
    put(6, wdown_ref[...])
    pl.semaphore_wait(pltpu.get_barrier_semaphore(), world - 1)

    has_up = z < DEPTH - 1
    has_down = z > 0

    def exists(rel):
        return (z + rel >= 0) & (z + rel < DEPTH)

    class Gather:
        def __init__(self, start, count, sems):
            self.start_row, self.half = start, count // 2
            (
                self.up_send,
                self.down_send,
                self.x_send,
                self.sib_send,
                self.below_recv,
                self.above_recv,
                self.x_recv,
                self.sib_recv,
            ) = sems

        def view(self, at, core):
            first = pl.multiple_of(self.start_row + core * self.half, 16)
            return w_s.at[at, pl.ds(first, self.half)]

        def mine(self, rel):
            return self.view(shard + rel * ACROSS, c)

        def others(self, rel):
            return self.view((z + rel) * ACROSS + 1 - x, c)

        def up(self, d):
            return remote(
                self.mine(-d), self.mine(-d), self.up_send.at[d], self.below_recv.at[d], upper
            )

        def down(self, d):
            return remote(
                self.mine(d), self.mine(d), self.down_send.at[d], self.above_recv.at[d], lower
            )

        def over(self, rel, where):
            return remote(
                self.mine(rel), where, self.x_send.at[rel + 3], self.x_recv.at[rel + 3], beside
            )

        def sib(self, kind, rel, src):
            return remote(
                src, src, self.sib_send.at[kind, rel + 3], self.sib_recv.at[kind, rel + 3], sibling
            )

        def start(self):
            @pl.when(has_up)
            def _():
                self.up(0).start()

            @pl.when(has_down)
            def _():
                self.down(0).start()

            self.over(0, self.mine(0)).start()

        def hop(self, d):
            @pl.when(exists(-d))
            def _():
                here = self.mine(-d)
                remote(
                    here, here, self.up_send.at[d], self.below_recv.at[d - 1], lower
                ).wait_recv()
                if d < DEPTH - 1:

                    @pl.when(has_up)
                    def _():
                        self.up(d).start()

                self.over(-d, here).start()
                self.sib(0, -d, here).start()

            @pl.when(exists(d))
            def _():
                here = self.mine(d)
                remote(
                    here, here, self.down_send.at[d], self.above_recv.at[d - 1], upper
                ).wait_recv()
                if d < DEPTH - 1:

                    @pl.when(has_down)
                    def _():
                        self.down(d).start()

                self.over(d, here).start()
                self.sib(0, d, here).start()

        def from_beside(self, d):
            for rel in (0,) if d == 0 else (-d, d):

                @pl.when(exists(rel))
                def _():
                    there = self.others(rel)
                    remote(
                        there, there, self.x_send.at[rel + 3], self.x_recv.at[rel + 3], beside
                    ).wait_recv()
                    self.sib(1, rel, there).start()

        def arrive(self):
            for rel in range(1 - DEPTH, DEPTH):

                @pl.when(exists(rel))
                def _():
                    if rel != 0:
                        self.sib(0, rel, self.view(shard + rel * ACROSS, 1 - c)).wait_recv()
                    self.sib(1, rel, self.view((z + rel) * ACROSS + 1 - x, 1 - c)).wait_recv()

        def sent(self):
            for rel in range(1 - DEPTH, DEPTH):

                @pl.when(exists(rel))
                def _():
                    if rel != 0:
                        self.sib(0, rel, self.mine(rel)).wait_send()
                    self.sib(1, rel, self.others(rel)).wait_send()
                    self.over(rel, self.mine(rel)).wait_send()

            for d in range(DEPTH - 1):

                @pl.when(exists(-d) & has_up)
                def _():
                    self.up(d).wait_send()

                @pl.when(exists(d) & has_down)
                def _():
                    self.down(d).wait_send()

    ff_row = pieces[4][0]
    last_row = pieces[6][0] + pieces[6][1]
    spans = ((0, ff_row), (ff_row, last_row - ff_row))
    each = len(per_part) // 2
    gathers = [Gather(*spans[i], per_part[i * each : i * each + 8]) for i in range(2)]
    attn_gather, ff_gather = gathers
    class Reduce:
        def __init__(self, start, count, refs):
            self.start_row, self.half, self.quarter = start, count // 2, count // 4
            (
                self.in_zero,
                self.acc_zero,
                self.in_one,
                self.acc_one,
                self.in_two,
                self.acc_two,
                self.in_three,
                self.send_zero,
                self.send_one,
                self.send_two,
                self.send_three,
                self.recv_zero,
                self.recv_one,
                self.recv_two,
                self.recv_three,
                self.mom_send,
                self.adv_send,
                self.row_send,
                self.row_recv,
            ) = refs
            self.keep_quarter = pl.ds(pl.multiple_of(y * self.quarter, 16), self.quarter)
            self.give_quarter = pl.ds(pl.multiple_of((1 - y) * self.quarter, 16), self.quarter)
            self.first_quarter = pl.ds(0, self.quarter)

        def half_of(self, core):
            return pl.ds(pl.multiple_of(self.start_row + core * self.half, 16), self.half)

        def rows_of(self, quarter):
            first = pl.multiple_of(self.start_row + quarter * self.quarter, 16)
            return pl.ds(first, self.quarter)

        def zero(self, k):
            return remote(
                grad_s.at[line[k], :, self.half_of(1 - c)],
                self.in_zero.at[k],
                self.send_zero.at[k],
                self.recv_zero.at[k],
                sibling,
            )

        def one(self, k, core):
            if core == 0:
                src, dst = self.acc_zero.at[k, :, self.give_quarter], self.in_one.at[
                    k, :, self.first_quarter
                ]
            else:
                src, dst = self.acc_zero.at[k, 1 - x], self.in_one.at[k, 0]
            where = facing if core == 0 else beside
            return remote(src, dst, self.send_one.at[k], self.recv_one.at[k], where)

        def two(self, k, core):
            if core == 0:
                src = self.acc_one.at[k, 1 - x, self.first_quarter]
            else:
                src = self.acc_one.at[k, 0, self.give_quarter]
            where = beside if core == 0 else facing
            return remote(src, self.in_two.at[k], self.send_two.at[k], self.recv_two.at[k], where)

        def three(self, k):
            return remote(
                self.acc_two.at[k],
                self.in_three.at[k],
                self.send_three.at[k],
                self.recv_three.at[k],
                device(line[k], x, y, c),
            )

        def start(self):
            for k in TURNS:
                self.zero(k).start()

        def add(self, left, right):
            return (left.astype(WIDE) + right.astype(WIDE)).astype(LOW)

        def first(self):
            for k in TURNS:
                self.zero(k).wait_recv()
                self.acc_zero[k] = self.add(grad_s[line[k], :, self.half_of(c)], self.in_zero[k])
                for core in range(2):

                    @pl.when(c == core)
                    def _():
                        self.one(k, core).start()

        def second(self, t):
            k, quarter = TURNS[t], self.quarter

            @pl.when(c == 0)
            def _():
                self.one(k, 0).wait_recv()
                self.acc_one[k, :, :quarter] = self.add(
                    self.acc_zero[k, :, self.keep_quarter], self.in_one[k, :, :quarter]
                )
                self.two(k, 0).start()

            @pl.when(c == 1)
            def _():
                self.one(k, 1).wait_recv()
                self.acc_one[k, 0] = self.add(self.acc_zero[k, x], self.in_one[k, 0])
                self.two(k, 1).start()

        def third(self, t):
            k, quarter = TURNS[t], self.quarter

            @pl.when(c == 0)
            def _():
                self.two(k, 0).wait_recv()
                self.acc_two[k] = self.add(self.acc_one[k, x, :quarter], self.in_two[k])

            @pl.when(c == 1)
            def _():
                self.two(k, 1).wait_recv()
                self.acc_two[k] = self.add(self.acc_one[k, 0, self.keep_quarter], self.in_two[k])

            if k != 0:
                self.three(k).start()

        def segments(self, index):
            found = []
            begin = self.start_row + index * self.quarter
            for m, (start, count) in enumerate(pieces):
                first, last = max(start, begin), min(start + count, begin + self.quarter)
                if first < last:
                    found.append((m, first - begin, first - start, last - first))
            return found

        def to_owner(self, kind, index, i, stays=False):
            m, first, to, count = self.segments(index)[i]
            begin = self.start_row + index * self.quarter + first
            source = (momenta, grows_ref)[kind].at[pl.ds(begin, count)]
            target = stage(kind, m).at[shard, pl.ds(to, count)]
            sent = (self.mom_send, self.adv_send)[kind].at[i]
            got = (mom_recv, adv_recv)[kind].at[0]
            if stays:
                return pltpu.make_async_copy(source, target, got)
            return remote(source, target, sent, got, device(*OWNERS[m]))

        def all_to_owners(self, kind):
            for index in range(4):
                for i, (m, _, _, _) in enumerate(self.segments(index)):

                    @pl.when((part == index) & jnp.logical_not(owned(m)))
                    def _():
                        self.to_owner(kind, index, i).start()

                    @pl.when((part == index) & owned(m))
                    def _():
                        self.to_owner(kind, index, i, stays=True).start()

        def send_momenta(self):
            self.all_to_owners(0)

        def row_copy(self, j, quarter, where):
            here = grows_ref.at[self.rows_of(quarter)]
            return remote(here, here, self.row_send.at[j], self.row_recv.at[j], where)

        def finish(self):
            total = self.acc_two[0].astype(WIDE)
            for k in range(1, DEPTH):
                self.three(k).wait_recv()
                total = total + self.in_three[k].astype(WIDE)
            grows_ref[self.rows_of(part), :] = total.astype(LOW)
            self.all_to_owners(1)
            for j, where in enumerate((sibling, facing, corner)):
                self.row_copy(j, part, where).start()

        def done(self):
            mates = ((sibling, 0, 1), (facing, 1, 0), (corner, 1, 1))
            for j, (where, dy, dc) in enumerate(mates):
                self.row_copy(j, 2 * (c ^ dc) + (y ^ dy), where).wait_recv()
                self.row_copy(j, part, where).wait_send()
            for index in range(4):
                for i, (m, _, _, _) in enumerate(self.segments(index)):

                    @pl.when((part == index) & jnp.logical_not(owned(m)))
                    def _():
                        for kind in range(2):
                            self.to_owner(kind, index, i).wait_send()

            for k in TURNS:
                self.zero(k).wait_send()
                if k != 0:
                    self.three(k).wait_send()
                for core in range(2):

                    @pl.when(c == core)
                    def _():
                        self.one(k, core).wait_send()
                        self.two(k, core).wait_send()

    def owned(m):
        oz, ox, oy, oc = OWNERS[m]
        return (z == oz) & (x == ox) & (y == oy) & (c == oc)

    def stage(kind, m):
        return ((y_attn, y_ff), (g_attn, g_ff))[kind][int(m >= 4)]

    reduces = [Reduce(*spans[i], per_part[i * each + 8 : (i + 1) * each]) for i in range(2)]
    attn_reduce, ff_reduce = reduces

    attn_gather.start()
    ff_gather.start()

    for one in loads:
        one.wait()
    for i, (value, turned) in enumerate(((mgate_up_ref[0], 4), (mgate_up_ref[1], 5))):
        start, count = pieces[turned]
        momenta[start : start + count, :] = value.T
    for j in range(3):
        start, count = pieces[j]
        momenta[start : start + count, :] = mqkv_ref[j]
    momenta[pieces[3][0] : pieces[3][0] + pieces[3][1], :] = mout_ref[...]
    momenta[pieces[6][0] : last_row, :] = mdown_ref[...]
    stat_s[...] = jnp.zeros_like(stat_s)

    lane = lax.broadcasted_iota(jnp.int32, (1, LANES), 1)
    low_head = lane < HEAD_DIM
    low_half = lane % HEAD_DIM < HEAD_DIM // 2
    row_id = lax.broadcasted_iota(jnp.int32, (PAIR, 1), 0)
    lane_id = lax.broadcasted_iota(jnp.int32, (1, PAIR), 1)
    same_bucket = (row_id < BUCKET) == (lane_id < BUCKET)
    slots = lax.broadcasted_iota(jnp.int32, (1, TIME_SLOTS), 1)
    query_scale = HEAD_DIM ** (-0.5)
    gain_one = gain_ref[0:1, :]
    gain_two = gain_ref[1:2, :]

    def column(row):
        return jnp.broadcast_to(row, (8, PAIR)).T[:, 0:1]

    def var_row(pair):
        two = var_ref[pl.ds(2 * pair, 2), :]
        return jnp.concatenate([two[0:1], two[1:2]], axis=1).astype(WIDE)

    def block_of(i, size):
        return pl.ds(pl.multiple_of(i * size, size), size)

    def prepare(i, carry):
        here = block_of(i, PAIR)
        times = column(time_ref[pl.ds(i, 1), :].astype(WIDE)).astype(jnp.int32)
        hot = (times == slots).astype(LOW)
        rope_s[here, :] = (
            mul_nn(hot, table_ref[0]) + mul_nn(hot, table_ref[1]) + mul_nn(hot, table_ref[2])
        )
        tokens = tok_ref[here, :].astype(WIDE)
        scale = lax.rsqrt(jnp.mean(tokens * tokens, axis=-1, keepdims=True) + EPS_NORM)
        scale_s[here, 0:1] = scale
        n1_s[here, :] = (tokens * scale * gain_one).astype(LOW)
        first, second = lengths[2 * i], lengths[2 * i + 1]
        live = row_id % BUCKET < jnp.where(row_id < BUCKET, first, second)
        glow_s[here, :] = jnp.where(live, cot_ref[here, :].astype(WIDE), 0.0).astype(LOW)
        return carry

    lax.fori_loop(0, rows // PAIR, prepare, 0)

    for d in range(1, DEPTH):
        attn_gather.hop(d)
        if d < DEPTH - 1:
            ff_gather.hop(d)
    for d in range(DEPTH):
        attn_gather.from_beside(d)
    attn_gather.arrive()

    def weight(first, last):
        parts = []
        for i in range(first, last):
            start, count = pieces[i]
            piece = w_s[:, start : start + count, :]
            parts.append(piece.reshape(piece.shape[0] * count, width))
        return parts[0] if len(parts) == 1 else jnp.concatenate(parts, axis=0)

    def swapped(values):
        half = HEAD_DIM // 2
        return jnp.where(
            low_half, pltpu.roll(values, LANES - half, 1), pltpu.roll(values, half, 1)
        )

    def two_heads(value):
        none = jnp.zeros_like(value)
        return jnp.concatenate(
            [jnp.where(low_head, value, none), jnp.where(low_head, none, value)], axis=0
        )

    per_block = BLOCK // PAIR

    def attend(i, carry):
        here = block_of(i, BLOCK)
        qkv = mul_nt(n1_s[here, :], weight(0, 3))
        cosine = rope_s[here, :LANES]
        sine = rope_s[here, LANES:]
        masks = []
        for p in range(per_block):
            pair = i * per_block + p
            first, second = lengths[2 * pair], lengths[2 * pair + 1]
            live_key = lane_id % BUCKET < jnp.where(lane_id < BUCKET, first, second)
            row = var_row(pair)
            masks.append((same_bucket & live_key, column(row) == row))
        attended = []
        for hp in range(heads // 2):
            first = hp * LANES
            q = qkv[:, first : first + LANES]
            k = qkv[:, width + first : width + first + LANES]
            v = qkv[:, 2 * width + first : 2 * width + first + LANES].astype(LOW)
            q = ((q * cosine + swapped(q) * sine) * query_scale).astype(LOW)
            k = (k * cosine + swapped(k) * sine).astype(LOW)
            low_s[here, first : first + LANES] = q
            low_s[here, width + first : width + first + LANES] = k
            low_s[here, 2 * width + first : 2 * width + first + LANES] = v
            pairs = []
            for p in range(per_block):
                span = slice(p * PAIR, (p + 1) * PAIR)
                mask, same_var = masks[p]
                raw = mul_nt(two_heads(q[span]), k[span])
                both = []
                for j in range(2):
                    h = 2 * hp + j
                    biased = raw[j * PAIR : (j + 1) * PAIR] + jnp.where(
                        same_var, bias[0, h], bias[1, h]
                    )
                    both.append(jnp.where(mask, biased, NEG_FILL))
                scores = jnp.concatenate(both, axis=0)
                exponent = jnp.exp(scores - jnp.max(scores, axis=-1, keepdims=True))
                probs = exponent / jnp.sum(exponent, axis=-1, keepdims=True)
                probs_s[i * per_block + p, hp] = probs
                both = mul_nn(probs.astype(LOW), v[span])
                pairs.append(jnp.where(low_head, both[:PAIR], both[PAIR:]))
            attended.append(jnp.concatenate(pairs, axis=0).astype(LOW))
        attended = jnp.concatenate(attended, axis=1)
        att_s[here, :] = attended
        mid = tok_ref[here, :].astype(WIDE) + mul_nn(attended, weight(3, 4))
        mid_s[here, :] = mid
        scale = lax.rsqrt(jnp.mean(mid * mid, axis=-1, keepdims=True) + EPS_NORM)
        scale_s[here, 1:2] = scale
        n2_s[here, :] = (mid * scale * gain_two).astype(LOW)
        @pl.when(i == 0)
        def _():
            ff_gather.hop(DEPTH - 1)
            ff_gather.from_beside(0)
            ff_gather.from_beside(1)

        for d in range(2, DEPTH):

            @pl.when(i == d - 1)
            def _():
                ff_gather.from_beside(d)

        return carry

    lax.fori_loop(0, rows // BLOCK, attend, 0)
    ff_gather.arrive()
    for one in reduces:
        one.send_momenta()

    def feed(i, carry):
        here = block_of(i, BLOCK)
        normed_two = n2_s[here, :]
        w_gate, w_up, w_down = weight(4, 5), weight(5, 6), weight(6, 7)
        gate = mul_nt(normed_two, w_gate)
        up = mul_nt(normed_two, w_up)
        sig = 1.0 / (1.0 + jnp.exp(-gate))
        silu = gate * sig
        hid_s[here, :] = (silu * up).astype(LOW)
        g_low = glow_s[here, :]
        g_hidden = mul_nt(g_low, w_down)
        g_gate = (g_hidden * up * sig * (1.0 + gate * (1.0 - sig))).astype(LOW)
        g_up = (g_hidden * silu).astype(LOW)
        gg_s[here, :] = g_gate
        gu_s[here, :] = g_up
        e_two = mul_nn(g_gate, w_gate) + mul_nn(g_up, w_up)
        scale = scale_s[here, 1:2]
        unit = mid_s[here, :] * scale
        stat_s[1:2, :] += jnp.sum(e_two * unit, axis=0, keepdims=True)
        scaled = e_two * gain_two
        g_mid = g_low.astype(WIDE) + scale * (
            scaled - unit * jnp.mean(scaled * unit, axis=-1, keepdims=True)
        )
        gmid_s[here, :] = g_mid
        g_mid_low = g_mid.astype(LOW)
        gml_s[here, :] = g_mid_low
        gatt_s[here, :] = mul_nt(g_mid_low, weight(3, 4)).astype(LOW)
        return carry

    lax.fori_loop(0, rows // BLOCK, feed, 0)

    def grad_put(index, left, right):
        start, count = pieces[index]
        grad_s[:, :, start : start + count, :] = (
            mul_tn(left, right).reshape(DEPTH, ACROSS, count, width).astype(LOW)
        )

    grad_put(4, gg_s[...], n2_s[...])
    grad_put(5, gu_s[...], n2_s[...])
    grad_put(6, hid_s[...], glow_s[...])
    ff_reduce.start()

    def attend_back(i, carry):
        here = block_of(i, PAIR)
        row = var_row(i)
        same_var = column(row) == row
        cosine = rope_s[here, :LANES]
        sine = rope_s[here, LANES:]
        for hp in range(heads // 2):
            first = hp * LANES
            q2 = two_heads(low_s[here, first : first + LANES])
            k = low_s[here, width + first : width + first + LANES]
            v = low_s[here, 2 * width + first : 2 * width + first + LANES]
            probs = probs_s[i, hp]
            ga2 = two_heads(gatt_s[here, first : first + LANES])
            g_probs = mul_nt(ga2, v)
            row_dot = jnp.sum(probs * g_probs, axis=-1, keepdims=True)
            g_scores = probs * (g_probs - row_dot)
            for j in range(2):
                h = 2 * hp + j
                mine = g_scores[j * PAIR : (j + 1) * PAIR]
                stat_s[8 + h : 9 + h, :PAIR] += jnp.sum(
                    jnp.where(same_var, mine, 0.0), axis=0, keepdims=True
                )
                stat_s[16 + h : 17 + h, :PAIR] += jnp.sum(
                    jnp.where(same_var, 0.0, mine), axis=0, keepdims=True
                )
            low_scores = g_scores.astype(LOW)
            both = mul_nn(low_scores, k)
            dq = jnp.where(low_head, both[:PAIR], both[PAIR:])
            dk = mul_tn(low_scores, q2)
            dv = mul_tn(probs.astype(LOW), ga2)
            gqkv_s[here, first : first + LANES] = (
                (dq * cosine - swapped(dq) * sine) * query_scale
            ).astype(LOW)
            gqkv_s[here, width + first : width + first + LANES] = (
                dk * cosine - swapped(dk) * sine
            ).astype(LOW)
            gqkv_s[here, 2 * width + first : 2 * width + first + LANES] = dv.astype(LOW)
        @pl.when(i == 0)
        def _():
            ff_reduce.first()

        for t in range(DEPTH):

            @pl.when(i == t + 2)
            def _():
                ff_reduce.second(t)

            @pl.when(i == t + 4)
            def _():
                ff_reduce.third(t)

        return carry

    lax.fori_loop(0, rows // PAIR, attend_back, 0)
    for j in range(3):
        grad_put(j, gqkv_s[:, j * width : (j + 1) * width], n1_s[...])
    grad_put(3, att_s[...], gml_s[...])
    attn_reduce.start()

    def last(i):
        here = block_of(i, 2 * BLOCK)
        e_one = mul_nn(gqkv_s[here, :], weight(0, 3))
        scale = scale_s[here, 0:1]
        unit = tok_ref[here, :].astype(WIDE) * scale
        stat_s[0:1, :] += jnp.sum(e_one * unit, axis=0, keepdims=True)
        scaled = e_one * gain_one
        gtok_ref[here, :] = (
            gmid_s[here, :]
            + scale * (scaled - unit * jnp.mean(scaled * unit, axis=-1, keepdims=True))
        ).astype(LOW)

    def outgoing(i):
        here = block_of(i, 2 * BLOCK)
        out_ref[here, :] = (mid_s[here, :] + mul_nn(hid_s[here, :], weight(6, 7))).astype(LOW)

    def stat_copy(step, src, where):
        return remote(src, stat_in.at[step], stat_send.at[step], stat_recv.at[step], where)

    attn_reduce.first()
    last(0)
    ff_reduce.finish()
    last(1)
    stat_copy(0, stat_s, sibling).start()
    attn_reduce.second(0)
    attn_reduce.second(1)
    attn_reduce.second(2)
    attn_reduce.third(0)
    attn_reduce.second(3)
    stat_copy(0, stat_s, sibling).wait()
    stat_acc[0] = stat_s[...] + stat_in[0]
    stat_copy(1, stat_acc.at[0], facing).start()
    for t in range(1, DEPTH):
        attn_reduce.third(t)
    stat_copy(1, stat_acc.at[0], facing).wait()
    stat_acc[1] = stat_acc[0] + stat_in[1]
    stat_copy(2, stat_acc.at[1], beside).start()
    attn_reduce.finish()
    stat_copy(2, stat_acc.at[1], beside).wait()
    stat_acc[2] = stat_acc[1] + stat_in[2]
    stat_line[z] = stat_acc[2]

    def stat_send_line(j):
        return remote(
            stat_acc.at[2],
            stat_line.at[z],
            stat_send.at[2 + j],
            stat_recv.at[2 + j],
            device(line[j], x, y, c),
        )

    for j in range(1, DEPTH):
        stat_send_line(j).start()

    attn_owner = functools.reduce(jnp.logical_or, [owned(m) for m in range(4)])
    ff_owner = functools.reduce(jnp.logical_or, [owned(m) for m in range(4, 7)])

    chips = DEPTH * ACROSS * SIDES

    def x_copy(m, i):
        start, count = pieces[m]
        source = x_attn if m < 4 else x_ff
        to = i // SIDES
        return remote(
            source.at[to],
            xrows_ref.at[pl.ds(start, count)],
            x_send.at[i],
            x_recv.at[m],
            (to, lax.rem(i, SIDES) * CORES + OWNERS[m][3]),
        )

    mine = shard * SIDES + y
    unit_mat = lax.broadcasted_iota(jnp.int32, (width, width), 0) == lax.broadcasted_iota(
        jnp.int32, (width, width), 1
    )
    diagonal = jnp.where(unit_mat, COEF_A, 0.0)

    def advance(y_buf, g_buf):
        pltpu.make_async_copy(y_buf, y_buf, mom_recv.at[0]).wait()
        pltpu.make_async_copy(g_buf, g_buf, adv_recv.at[0]).wait()
        grad = g_buf[...].astype(WIDE)
        return grad + MUON_MU * (MUON_MU * y_buf[...] + grad)

    def poly(value):
        return diagonal + COEF_B * value + COEF_C * square_wide(value)

    def send_x(m, first, count):
        def send(i, carry):
            @pl.when(i != mine)
            def _():
                x_copy(m, i).start()

            return carry

        lax.fori_loop(first, first + count, send, 0)

    def keep_x(m):
        start, count = pieces[m]
        source = x_attn if m < 4 else x_ff
        pltpu.make_async_copy(
            source.at[shard], xrows_ref.at[pl.ds(start, count)], x_recv.at[m]
        ).start()

    @pl.when(attn_owner)
    def _():
        value = advance(y_attn, g_attn).reshape(-1, width)
        total = jnp.sum(jnp.sum(value * value, axis=0, keepdims=True), axis=1, keepdims=True)
        chain_s[...] = value * (1.0 / (jnp.sqrt(total) + NS_EPS))

        def turn(i, carry):
            now = chain_s[...]
            chain_s[...] = mul_wide(now, poly(gram_wide(now)))
            return carry

        lax.fori_loop(0, NS_ITERS, turn, 0)
        x_attn[...] = chain_s[...].astype(LOW).reshape(x_attn.shape)
        for m in range(4):

            @pl.when(owned(m))
            def _():
                send_x(m, 0, chips)
                keep_x(m)

    @pl.when(ff_owner)
    def _():
        y_ff[...] = advance(y_ff, g_ff)
        gram_mat = gram_wide(y_ff[...].reshape(-1, width))
        trace = jnp.sum(jnp.where(unit_mat, gram_mat, 0.0), keepdims=True)
        inverse = 1.0 / (jnp.sqrt(trace) + NS_EPS)
        gram_mat = gram_mat * (inverse * inverse)
        step_mat = poly(gram_mat)
        gram_s[...] = mul_wide(mul_wide(gram_mat, step_mat), step_mat)
        chain_s[...] = step_mat * inverse

        def turn(i, carry):
            now = gram_s[...]
            step_now = poly(now)
            both = mul_wide(jnp.concatenate([now, chain_s[...]], axis=0), step_now)
            chain_s[...] = both[width:]
            gram_s[...] = mul_wide(both[:width], step_now)
            return carry

        lax.fori_loop(0, NS_ITERS - 2, turn, 0)
        chain_s[...] = mul_wide(chain_s[...], poly(gram_s[...]))

        def give(i, carry):
            at = lax.rem(z + 2 + i, DEPTH)
            these = pl.ds(at * ACROSS, ACROSS)
            value = y_ff[these].reshape(-1, width)
            x_ff[these] = mul_wide(value, chain_s[...]).astype(LOW).reshape(
                ACROSS, x_ff.shape[1], width
            )
            for m in range(4, 7):

                @pl.when(owned(m))
                def _():
                    send_x(m, at * (ACROSS * SIDES), ACROSS * SIDES)

            return carry

        lax.fori_loop(0, DEPTH, give, 0)
        for m in range(4, 7):

            @pl.when(owned(m))
            def _():
                keep_x(m)

    outgoing(0)
    outgoing(1)

    for j in range(1, DEPTH):
        remote(
            stat_acc.at[2],
            stat_line.at[lax.rem(z + DEPTH - j, DEPTH)],
            stat_send.at[2 + j],
            stat_recv.at[2 + j],
            device(line[j], x, y, c),
        ).wait()
    total_ref[...] = (stat_line[0] + stat_line[1]) + (stat_line[2] + stat_line[3])
    for one in gathers:
        one.sent()
    for one in reduces:
        one.done()

    def fan_copy(m):
        start, count = pieces[m]
        rows_m = xrows_ref.at[pl.ds(start, count)]
        return remote(rows_m, rows_m, fan_send.at[m], fan_recv.at[m], sibling)

    for m in range(7):
        start, count = pieces[m]

        @pl.when(c == OWNERS[m][3])
        def _():
            rows_m = xrows_ref.at[pl.ds(start, count)]
            pltpu.make_async_copy(rows_m, rows_m, x_recv.at[m]).wait()
            fan_copy(m).start()

    for m in range(7):

        @pl.when(c != OWNERS[m][3])
        def _():
            fan_copy(m).wait_recv()

        @pl.when(c == OWNERS[m][3])
        def _():
            fan_copy(m).wait_send()

        @pl.when(owned(m))
        def _():
            def sent(i, carry):
                x_copy(m, lax.rem(mine + i, chips)).wait_send()
                return carry

            lax.fori_loop(1, chips, sent, 0)


def rotary_table():
    half = HEAD_DIM // 2
    frequency = (ROPE_BASE ** (-2.0 * np.arange(half) / HEAD_DIM)).astype(np.float32)
    angles = np.arange(TIME_SLOTS, dtype=np.float32)[:, None] * frequency[None, :]
    cosine = np.cos(angles.astype(np.float64)).astype(np.float32)
    sine = np.sin(angles.astype(np.float64)).astype(np.float32)
    table = np.concatenate([cosine] * 4 + [-sine, sine, -sine, sine], axis=1)
    parts = []
    for _ in range(3):
        parts.append(table.astype(LOW))
        table = table - parts[-1].astype(np.float32)
    return np.stack(parts)


def whole_step(tokens, cotangent, lengths, variates, times, gains, attn_bias, weights, momenta):
    rows, width = tokens.shape
    heads = attn_bias.shape[1]
    attn_rows, ff_rows = weights[1].shape[0], weights[3].shape[0]
    pieces = offsets(attn_rows, ff_rows)
    ff = ff_rows * DEPTH * ACROSS
    shards = DEPTH * ACROSS
    shard_rows = 4 * attn_rows + 3 * ff_rows
    low = lambda *shape: pltpu.VMEM(shape, LOW)
    wide = lambda *shape: pltpu.VMEM(shape, WIDE)
    dma = lambda *shape: pltpu.SemaphoreType.DMA(shape)

    def part_scratch(count):
        half, quarter = count // 2, count // 4
        relative = 2 * DEPTH - 1
        return [
            dma(DEPTH),
            dma(DEPTH),
            dma(relative),
            dma(2, relative),
            dma(DEPTH),
            dma(DEPTH),
            dma(relative),
            dma(2, relative),
            low(DEPTH, ACROSS, half, width),
            low(DEPTH, ACROSS, half, width),
            low(DEPTH, ACROSS, half, width),
            low(DEPTH, ACROSS, half, width),
            low(DEPTH, quarter, width),
            low(DEPTH, quarter, width),
            low(DEPTH, quarter, width),
            *[dma(DEPTH) for _ in range(8)],
            dma(3),
            dma(3),
            dma(3),
            dma(3),
        ]

    return pl.pallas_call(
        functools.partial(whole_kernel, pieces),
        out_shape=(
            jax.ShapeDtypeStruct((rows, width), LOW),
            jax.ShapeDtypeStruct((rows, width), LOW),
            jax.ShapeDtypeStruct((shard_rows, width), LOW),
            jax.ShapeDtypeStruct((shard_rows, width), LOW),
            jax.ShapeDtypeStruct((STATS, width), WIDE),
        ),
        in_specs=[SCALARS] * 2 + [ANYWHERE] * 2 + [WHOLE] * 8 + [ANYWHERE] * 4,
        out_specs=(WHOLE,) * 5,
        scratch_shapes=[
            low(rows, width),
            low(rows, width),
            *[wide(*m.shape) for m in momenta],
            dma(6),
            low(shards, shard_rows, width),
            low(DEPTH, ACROSS, shard_rows, width),
            wide(shard_rows, width),
            low(rows, width),
            low(rows, width),
            low(rows, width),
            low(rows, width),
            low(rows, width),
            low(rows, ff),
            low(rows, ff),
            low(rows, ff),
            low(rows, 3 * width),
            low(rows, 3 * width),
            wide(rows // PAIR, heads // 2, 2 * PAIR, PAIR),
            wide(rows, width),
            wide(rows, width),
            low(rows, width),
            wide(rows, 2),
            wide(rows, 2 * LANES),
            wide(shards, attn_rows, width),
            wide(shards, ff_rows, width),
            low(shards, attn_rows, width),
            low(shards, ff_rows, width),
            low(shards, attn_rows, width),
            low(shards, ff_rows, width),
            wide(width, width),
            wide(width, width),
            wide(STATS, width),
            wide(3, STATS, width),
            wide(3, STATS, width),
            wide(DEPTH, STATS, width),
            dma(6),
            dma(6),
            dma(1),
            dma(1),
            dma(shards * SIDES),
            dma(7),
            dma(7),
            dma(7),
            *part_scratch(4 * attn_rows),
            *part_scratch(3 * ff_rows),
        ],
        compiler_params=pltpu.CompilerParams(
            vmem_limit_bytes=60 << 20, collective_id=0, has_side_effects=True
        ),
        name="whole",
    )(
        lengths,
        attn_bias,
        tokens,
        cotangent,
        variates,
        times.reshape(rows // PAIR, PAIR),
        jnp.asarray(rotary_table()),
        gains,
        *weights,
        *momenta,
    )


def update_kernel(
    pieces,
    factors,
    grow_ref,
    xrow_ref,
    stat_ref,
    w_qkv,
    w_out,
    w_gate_up,
    w_down,
    m_qkv,
    m_out,
    m_gate_up,
    m_down,
    gains,
    bias,
    gain_moment,
    gain_square,
    bias_moment,
    bias_square,
    out_in,
    gtok_in,
    g_qkv,
    g_out,
    g_gate_up,
    g_down,
    nm_qkv,
    nm_out,
    nm_gate_up,
    nm_down,
    nw_qkv,
    nw_out,
    nw_gate_up,
    nw_down,
    g_gains,
    n_gain_moment,
    n_gain_square,
    n_gains,
    g_bias,
    n_bias_moment,
    n_bias_square,
    n_bias,
    out_tokens,
    grad_tokens,
    sems,
):
    copies = (
        pltpu.make_async_copy(out_in, out_tokens, sems.at[0]),
        pltpu.make_async_copy(gtok_in, grad_tokens, sems.at[1]),
    )
    for one_copy in copies:
        one_copy.start()
    shrink = 1.0 - MUON_RATE * MUON_DECAY

    def one(index, turned, g, m, w, nm, nw):
        start, count = pieces[index]
        grad = grow_ref[start : start + count, :].astype(WIDE)
        ortho = xrow_ref[start : start + count, :].astype(WIDE)
        if turned:
            grad, ortho = grad.T, ortho.T
        g[...] = grad
        nm[...] = MUON_MU * m[...] + grad
        nw[...] = w[...] * shrink - factors[index] * ortho

    for j in range(3):
        one(j, False, *[r.at[j] for r in (g_qkv, m_qkv, w_qkv, nm_qkv, nw_qkv)])
    one(3, False, g_out, m_out, w_out, nm_out, nw_out)
    for j in range(2):
        refs = (g_gate_up, m_gate_up, w_gate_up, nm_gate_up, nw_gate_up)
        one(4 + j, True, *[r.at[j] for r in refs])
    one(6, False, g_down, m_down, w_down, nm_down, nw_down)

    grad = stat_ref[0:2, :]
    g_gains[...] = grad
    n_gain_moment[...], n_gain_square[...], n_gains[...] = adam_step(
        gains[...], grad, gain_moment[...], gain_square[...]
    )
    heads = bias.shape[1]
    sums = jnp.sum(stat_ref[8:24, :PAIR].T, axis=0, keepdims=True)
    grad = jnp.concatenate([sums[:, :heads], sums[:, 8 : 8 + heads]], axis=0)
    g_bias[...] = grad
    n_bias_moment[...], n_bias_square[...], n_bias[...] = adam_step(
        bias[...], grad, bias_moment[...], bias_square[...]
    )
    for one_copy in copies:
        one_copy.wait()


def update(factors, grad_rows, ortho_rows, stats, weights, momenta, small, rows):
    pieces = offsets(weights[1].shape[0], weights[3].shape[0])
    gains, bias = small[:2]
    like = lambda a: jax.ShapeDtypeStruct(a.shape, WIDE)
    outs = [like(a) for a in (*weights, *weights, *weights, *[gains] * 4, *[bias] * 4)]
    return pl.pallas_call(
        functools.partial(update_kernel, pieces, factors),
        out_shape=(*outs, *[jax.ShapeDtypeStruct(r.shape, r.dtype) for r in rows]),
        in_specs=[WHOLE] * 19,
        out_specs=(*[WHOLE] * len(outs), *[ANYWHERE] * 2),
        scratch_shapes=[pltpu.SemaphoreType.DMA((2,))],
        compiler_params=pltpu.CompilerParams(vmem_limit_bytes=58 << 20),
        name="update",
    )(grad_rows, ortho_rows, stats, *weights, *momenta, *small, *rows)


def body(
    tokens,
    cotangent,
    lengths,
    variates,
    times,
    weight_qkv,
    weight_out,
    weight_gate_up,
    weight_down,
    momentum_qkv,
    momentum_out,
    momentum_gate_up,
    momentum_down,
    gains,
    attn_bias,
    gain_moment,
    gain_square,
    bias_moment,
    bias_square,
):
    width = tokens.shape[1]
    heads = attn_bias.shape[1]
    attn_rows = weight_out.shape[0]
    ff_rows = weight_down.shape[0]
    fsdp = lax.axis_size("fsdp")
    ff = ff_rows * fsdp
    attn_width = attn_rows * fsdp
    shrink = 1.0 - MUON_RATE * MUON_DECAY
    scale_attn = MUON_RATE * 0.2 * math.sqrt(max(width, attn_width))
    scale_ff = MUON_RATE * 0.2 * math.sqrt(max(width, ff))
    sizes = (fsdp, lax.axis_size("ns"))
    if sizes == (DEPTH * ACROSS, SIDES * CORES) and attn_rows == 48 and ff_rows == 128:
        turn = lambda a: jnp.swapaxes(a, 1, 2)
        shards = (turn(weight_qkv), weight_out, weight_gate_up, weight_down)
        momenta = (turn(momentum_qkv), momentum_out, momentum_gate_up, momentum_down)
        out_tokens, grad_tokens, grad_rows, ortho_rows, stats = whole_step(
            tokens, cotangent, lengths, variates, times, gains, attn_bias, shards, momenta
        )
        outs = list(
            update(
                (scale_attn,) * 4 + (scale_ff,) * 3,
                grad_rows,
                ortho_rows,
                stats,
                shards,
                momenta,
                (gains, attn_bias, gain_moment, gain_square, bias_moment, bias_square),
                (out_tokens, grad_tokens),
            )
        )
        out_tokens, grad_tokens = outs[-2:]
        outs = outs[:-2]
        for i in (0, 4, 8):
            outs[i] = turn(outs[i])
        return (out_tokens, grad_tokens, *outs)
    weights = pack(weight_qkv, weight_out, weight_gate_up, weight_down)
    momenta = pack(momentum_qkv, momentum_out, momentum_gate_up, momentum_down)
    full = lax.all_gather(weights.astype(LOW), "fsdp", axis=0, tiled=False)
    aligned = attn_rows % 16 == 0 and ff_rows % 16 == 0
    pieces = offsets(attn_rows, ff_rows)
    if not aligned:
        full = jnp.concatenate(
            [full[:, s : s + n].reshape(1, fsdp * n, width) for s, n in pieces], axis=1
        )
    out_tokens, grad_tokens, grads, stats = layer(
        tokens, cotangent, lengths, variates, times, full, gains, attn_bias, ff, WIDE
    )
    if not aligned:
        wholes = offsets(attn_width, ff)
        grads = jnp.concatenate(
            [grads[0, s : s + n].reshape(fsdp, n // fsdp, width) for s, n in wholes], axis=1
        )
    summed = lax.psum_scatter(grads, "fsdp", scatter_dimension=0, tiled=False)
    grad_rows = lax.psum(summed.astype(LOW), "ns").astype(WIDE)
    bias_part = jnp.sum(stats[8:, :PAIR], axis=1).reshape(2, 8)[:, :heads]
    grad_gains, grad_bias = lax.psum((stats[:2], bias_part), ("fsdp", "ns"))

    new_momenta = MUON_MU * momenta + grad_rows
    advance = grad_rows + MUON_MU * new_momenta
    parts = [advance[s : s + n] for s, n in pieces]
    grams = jnp.stack(
        [
            lax.dot_general(
                y,
                y,
                (((0,), (0,)), ((), ())),
                precision=lax.Precision.HIGHEST,
                preferred_element_type=WIDE,
            )
            for y in parts
        ]
    )
    factor = newton_schulz(lax.psum(grams, "fsdp"))
    turned = jnp.concatenate(
        [
            (scale_attn if i < 4 else scale_ff)
            * jnp.dot(
                y, factor[i], precision=lax.Precision.HIGHEST, preferred_element_type=WIDE
            )
            for i, y in enumerate(parts)
        ],
        axis=0,
    )
    new_weights = weights * shrink - turned
    new_gain_moment, new_gain_square, new_gains = adam_step(
        gains, grad_gains, gain_moment, gain_square
    )
    new_bias_moment, new_bias_square, new_bias = adam_step(
        attn_bias, grad_bias, bias_moment, bias_square
    )
    return (
        out_tokens,
        grad_tokens,
        *unpack(grad_rows, attn_rows, ff_rows),
        *unpack(new_momenta, attn_rows, ff_rows),
        *unpack(new_weights, attn_rows, ff_rows),
        grad_gains,
        new_gain_moment,
        new_gain_square,
        new_gains,
        grad_bias,
        new_bias_moment,
        new_bias_square,
        new_bias,
    )


def solution(mesh):
    rows = P(("fsdp", "ns"), None)
    line = P(("fsdp", "ns"))
    matrices = (P(None, None, "fsdp"), P("fsdp", None), P(None, None, "fsdp"), P("fsdp", None))
    return jax.shard_map(
        body,
        mesh=mesh,
        in_specs=(rows, rows, line, rows, line, *matrices, *matrices, *([P()] * 6)),
        out_specs=(rows, rows, *matrices, *matrices, *matrices, *([P()] * 8)),
        check_vma=False,
    )
```

```python
import functools
import math

import jax
import jax.numpy as jnp
import numpy as np
from jax import lax
from jax.experimental import pallas as pl
from jax.experimental.pallas import tpu as pltpu
from jax.sharding import PartitionSpec as P

HEAD_DIM = 64
BUCKET = 64
TIME_SLOTS = 64
NS_ITERS = 5
STEP = 10

EPS_NORM = 1e-06
ROPE_BASE = 10000.0
NEG_FILL = -1000000000.0
COEF_A = 3.4445
COEF_B = -4.775
COEF_C = 2.0315
NS_EPS = 1e-07
MUON_MU = 0.95
MUON_RATE = 0.25
MUON_DECAY = 0.01
ADAM_RATE = 0.8
BETA_ONE = 0.9
BETA_TWO = 0.95
ADAM_EPS = 1e-08

LOW = jnp.bfloat16
WIDE = jnp.float32
BLOCK = 256
PAIR = 2 * BUCKET
LANES = 2 * HEAD_DIM
STATS = 24
WHOLE = pl.BlockSpec(memory_space=pltpu.VMEM)
SCALARS = pl.BlockSpec(memory_space=pltpu.SMEM)
ANYWHERE = pl.BlockSpec(memory_space=pl.ANY)


def mul_nn(left, right):
    return lax.dot_general(left, right, (((1,), (0,)), ((), ())), preferred_element_type=WIDE)


def mul_nt(left, right):
    return lax.dot_general(left, right, (((1,), (1,)), ((), ())), preferred_element_type=WIDE)


def mul_tn(left, right):
    return lax.dot_general(left, right, (((0,), (0,)), ((), ())), preferred_element_type=WIDE)


def offsets(attn_rows, ff_rows):
    counts = [attn_rows] * 4 + [ff_rows] * 3
    starts = [sum(counts[:i]) for i in range(7)]
    return list(zip(starts, counts))


def layer_kernel(
    pieces,
    lengths,
    bias,
    tok_ref,
    cot_ref,
    var_ref,
    time_ref,
    table_ref,
    gain_ref,
    w_ref,
    out_ref,
    gtok_ref,
    grad_ref,
    stat_ref,
    n1_s,
    n2_s,
    att_s,
    gml_s,
    hid_s,
    glow_s,
    gg_s,
    gu_s,
    gqkv_s,
):
    step = pl.program_id(0)
    rows, width = tok_ref.shape
    heads = bias.shape[1]
    here = pl.ds(pl.multiple_of(step * rows, rows), rows)

    def weight(first, last):
        parts = []
        for i in range(first, last):
            start, count = pieces[i]
            part = w_ref[:, start : start + count, :]
            parts.append(part.reshape(part.shape[0] * count, width))
        return parts[0] if len(parts) == 1 else jnp.concatenate(parts, axis=0)

    @pl.when(step == 0)
    def _():
        stat_ref[...] = jnp.zeros_like(stat_ref)

    lane = lax.broadcasted_iota(jnp.int32, (1, LANES), 1)
    low_head = lane < HEAD_DIM
    low_half = lane % HEAD_DIM < HEAD_DIM // 2
    per_block = rows // PAIR
    var_rows = var_ref[pl.ds(step * per_block, per_block), :]
    time_rows = time_ref[pl.ds(step * per_block, per_block), :]
    filler = jnp.zeros((8 - 2 * per_block, PAIR), WIDE)
    columns = jnp.concatenate([var_rows, time_rows, filler], axis=0).T
    slots = lax.broadcasted_iota(jnp.int32, (1, TIME_SLOTS), 1).astype(WIDE)
    hot = jnp.concatenate(
        [(columns[:, per_block + p : per_block + p + 1] == slots) for p in range(per_block)], axis=0
    ).astype(LOW)
    looked = mul_nn(hot, table_ref[0]) + mul_nn(hot, table_ref[1]) + mul_nn(hot, table_ref[2])
    cosine = looked[:, :LANES]
    sine = looked[:, LANES:]

    def swapped(values):
        half = HEAD_DIM // 2
        return jnp.where(
            low_half, pltpu.roll(values, LANES - half, 1), pltpu.roll(values, half, 1)
        )

    gain_one = gain_ref[0:1, :]
    gain_two = gain_ref[1:2, :]
    tokens = tok_ref[...].astype(WIDE)
    scale_one = lax.rsqrt(jnp.mean(tokens * tokens, axis=-1, keepdims=True) + EPS_NORM)
    unit_one = tokens * scale_one
    normed_one = (unit_one * gain_one).astype(LOW)
    n1_s[here, :] = normed_one
    qkv = mul_nt(normed_one, weight(0, 3))

    query_scale = HEAD_DIM ** (-0.5)
    units = []
    attended = []
    row_id = lax.broadcasted_iota(jnp.int32, (PAIR, 1), 0)
    lane_id = lax.broadcasted_iota(jnp.int32, (1, PAIR), 1)
    same_bucket = (row_id < BUCKET) == (lane_id < BUCKET)
    masks = []
    live_cols = []
    for p in range(per_block):
        first = lengths[(step * per_block + p) * 2]
        second = lengths[(step * per_block + p) * 2 + 1]
        live_key = lane_id % BUCKET < jnp.where(lane_id < BUCKET, first, second)
        live_cols.append(row_id % BUCKET < jnp.where(row_id < BUCKET, first, second))
        mask = same_bucket & live_key
        same_var = columns[:, p : p + 1] == var_rows[p : p + 1, :]
        masks.append((mask, same_var))

    for hp in range(heads // 2):
        cols = slice(hp * LANES, (hp + 1) * LANES)
        q = qkv[:, cols]
        k = qkv[:, width + hp * LANES : width + (hp + 1) * LANES]
        v = qkv[:, 2 * width + hp * LANES : 2 * width + (hp + 1) * LANES].astype(LOW)
        q = ((q * cosine + swapped(q) * sine) * query_scale).astype(LOW)
        k = (k * cosine + swapped(k) * sine).astype(LOW)
        q_first = jnp.where(low_head, q, jnp.zeros_like(q))
        q_second = jnp.where(low_head, jnp.zeros_like(q), q)
        att_pairs = []
        for p in range(per_block):
            part = slice(p * PAIR, (p + 1) * PAIR)
            mask, same_var = masks[p]
            q2 = jnp.concatenate([q_first[part], q_second[part]], axis=0)
            kp = k[part]
            vp = v[part]
            raw = mul_nt(q2, kp)
            halves = []
            for j in range(2):
                h = 2 * hp + j
                biased = raw[j * PAIR : (j + 1) * PAIR] + jnp.where(
                    same_var, bias[0, h], bias[1, h]
                )
                halves.append(jnp.where(mask, biased, NEG_FILL))
            scores = jnp.concatenate(halves, axis=0)
            top = jnp.max(scores, axis=-1, keepdims=True)
            exponent = jnp.exp(scores - top)
            probs = exponent / jnp.sum(exponent, axis=-1, keepdims=True)
            probs_low = probs.astype(LOW)
            both = mul_nn(probs_low, vp)
            att_pairs.append(jnp.where(low_head, both[:PAIR], both[PAIR:]))
            units.append((hp, p, q2, kp, vp, probs, probs_low))
        attended.append(jnp.concatenate(att_pairs, axis=0).astype(LOW))
    attended = jnp.concatenate(attended, axis=1)
    att_s[here, :] = attended
    w_out = weight(3, 4)
    mid = tokens + mul_nn(attended, w_out)
    scale_two = lax.rsqrt(jnp.mean(mid * mid, axis=-1, keepdims=True) + EPS_NORM)
    unit_two = mid * scale_two
    normed_two = (unit_two * gain_two).astype(LOW)
    n2_s[here, :] = normed_two
    w_gate = weight(4, 5)
    w_up = weight(5, 6)
    w_down = weight(6, 7)
    gate = mul_nt(normed_two, w_gate)
    up = mul_nt(normed_two, w_up)
    sig = 1.0 / (1.0 + jnp.exp(-gate))
    silu = gate * sig
    hidden = (silu * up).astype(LOW)
    hid_s[here, :] = hidden
    out_ref[...] = (mid + mul_nn(hidden, w_down)).astype(LOW)

    live_row = jnp.concatenate(live_cols, axis=0)
    g_out = jnp.where(live_row, cot_ref[...].astype(WIDE), 0.0)
    g_low = g_out.astype(LOW)
    glow_s[here, :] = g_low
    g_hidden = mul_nt(g_low, w_down)
    g_gate = (g_hidden * up * sig * (1.0 + gate * (1.0 - sig))).astype(LOW)
    g_up = (g_hidden * silu).astype(LOW)
    gg_s[here, :] = g_gate
    gu_s[here, :] = g_up
    e_two = mul_nn(g_gate, w_gate) + mul_nn(g_up, w_up)
    stat_ref[1:2, :] += jnp.sum(e_two * unit_two, axis=0, keepdims=True)
    scaled = e_two * gain_two
    g_mid = g_out + scale_two * (
        scaled - unit_two * jnp.mean(scaled * unit_two, axis=-1, keepdims=True)
    )
    g_mid_low = g_mid.astype(LOW)
    gml_s[here, :] = g_mid_low
    g_att = mul_nt(g_mid_low, w_out).astype(LOW)

    parts_q = [[None] * per_block for _ in range(heads // 2)]
    parts_k = [[None] * per_block for _ in range(heads // 2)]
    parts_v = [[None] * per_block for _ in range(heads // 2)]
    for hp, p, q2, kp, vp, probs, probs_low in units:
        part = slice(p * PAIR, (p + 1) * PAIR)
        mask, same_var = masks[p]
        ga = g_att[part, hp * LANES : (hp + 1) * LANES]
        ga2 = jnp.concatenate(
            [
                jnp.where(low_head, ga, jnp.zeros_like(ga)),
                jnp.where(low_head, jnp.zeros_like(ga), ga),
            ],
            axis=0,
        )
        g_probs = mul_nt(ga2, vp)
        row_dot = jnp.sum(probs * g_probs, axis=-1, keepdims=True)
        g_scores = probs * (g_probs - row_dot)
        for j in range(2):
            h = 2 * hp + j
            mine = g_scores[j * PAIR : (j + 1) * PAIR]
            stat_ref[8 + h : 9 + h, :PAIR] += jnp.sum(
                jnp.where(same_var, mine, 0.0), axis=0, keepdims=True
            )
            stat_ref[16 + h : 17 + h, :PAIR] += jnp.sum(
                jnp.where(same_var, 0.0, mine), axis=0, keepdims=True
            )
        low_scores = g_scores.astype(LOW)
        both = mul_nn(low_scores, kp)
        parts_q[hp][p] = jnp.where(low_head, both[:PAIR], both[PAIR:])
        parts_k[hp][p] = mul_tn(low_scores, q2)
        parts_v[hp][p] = mul_tn(probs_low, ga2)
    g_q = []
    g_k = []
    g_v = []
    for hp in range(heads // 2):
        dq = jnp.concatenate(parts_q[hp], axis=0)
        dk = jnp.concatenate(parts_k[hp], axis=0)
        g_q.append(((dq * cosine - swapped(dq) * sine) * query_scale).astype(LOW))
        g_k.append((dk * cosine - swapped(dk) * sine).astype(LOW))
        g_v.append(jnp.concatenate(parts_v[hp], axis=0).astype(LOW))
    g_qkv = jnp.concatenate(g_q + g_k + g_v, axis=1)
    gqkv_s[here, :] = g_qkv
    e_one = mul_nn(g_qkv, weight(0, 3))
    stat_ref[0:1, :] += jnp.sum(e_one * unit_one, axis=0, keepdims=True)
    scaled = e_one * gain_one
    gtok_ref[...] = (
        g_mid
        + scale_one * (scaled - unit_one * jnp.mean(scaled * unit_one, axis=-1, keepdims=True))
    ).astype(LOW)

    @pl.when(step == pl.num_programs(0) - 1)
    def _():
        def put(index, left, right):
            start, count = pieces[index]
            grad_ref[:, start : start + count, :] = (
                mul_tn(left, right)
                .reshape(grad_ref.shape[0], count, width)
                .astype(grad_ref.dtype)
            )

        for j in range(3):
            put(j, gqkv_s[:, j * width : (j + 1) * width], n1_s[...])
        put(3, att_s[...], gml_s[...])
        put(4, gg_s[...], n2_s[...])
        put(5, gu_s[...], n2_s[...])
        put(6, hid_s[...], glow_s[...])


def layer(tokens, cotangent, lengths, variates, times, packed, gains, attn_bias, ff, grad_type):
    rows, width = tokens.shape
    heads = attn_bias.shape[1]
    copies, shard_rows, _ = packed.shape
    pieces = offsets(heads * HEAD_DIM // copies, ff // copies)
    half = HEAD_DIM // 2
    frequency = ROPE_BASE ** (-2.0 * jnp.arange(half, dtype=WIDE) / HEAD_DIM)
    angles = jnp.arange(TIME_SLOTS, dtype=WIDE)[:, None] * frequency[None, :]
    cosine, sine = jnp.cos(angles), jnp.sin(angles)
    table = jnp.concatenate([cosine] * 4 + [-sine, sine, -sine, sine], axis=1)
    first = table.astype(LOW)
    rest = table - first.astype(WIDE)
    second = rest.astype(LOW)
    third = (rest - second.astype(WIDE)).astype(LOW)
    table = jnp.stack([first, second, third])
    grid = rows // BLOCK
    block = pl.BlockSpec((BLOCK, width), lambda i: (i, 0))
    low_scratch = lambda columns: pltpu.VMEM((rows, columns), LOW)
    return pl.pallas_call(
        functools.partial(layer_kernel, pieces),
        grid=(grid,),
        out_shape=(
            jax.ShapeDtypeStruct((rows, width), LOW),
            jax.ShapeDtypeStruct((rows, width), LOW),
            jax.ShapeDtypeStruct((copies, shard_rows, width), grad_type),
            jax.ShapeDtypeStruct((STATS, width), WIDE),
        ),
        in_specs=[SCALARS, SCALARS, block, block, WHOLE, WHOLE, WHOLE, WHOLE, WHOLE],
        out_specs=(block, block, WHOLE, WHOLE),
        scratch_shapes=[
            low_scratch(width),
            low_scratch(width),
            low_scratch(width),
            low_scratch(width),
            low_scratch(ff),
            low_scratch(width),
            low_scratch(ff),
            low_scratch(ff),
            low_scratch(3 * width),
        ],
        compiler_params=pltpu.CompilerParams(vmem_limit_bytes=58 << 20),
        name="layer",
    )(
        lengths,
        attn_bias,
        tokens,
        cotangent,
        variates.astype(WIDE).reshape(rows // PAIR, PAIR),
        times.astype(WIDE).reshape(rows // PAIR, PAIR),
        table,
        gains,
        packed,
    )


def pack(qkv, out, gate_up, down):
    width = out.shape[-1]
    return jnp.concatenate(
        [
            jnp.swapaxes(qkv, 1, 2).reshape(-1, width),
            out,
            jnp.swapaxes(gate_up, 1, 2).reshape(-1, width),
            down,
        ],
        axis=0,
    )


def unpack(packed, attn_rows, ff_rows):
    width = packed.shape[-1]
    qkv = jnp.swapaxes(packed[: 3 * attn_rows].reshape(3, attn_rows, width), 1, 2)
    out = packed[3 * attn_rows : 4 * attn_rows]
    ends = 4 * attn_rows + 2 * ff_rows
    gate_up = jnp.swapaxes(packed[4 * attn_rows : ends].reshape(2, ff_rows, width), 1, 2)
    return qkv, out, gate_up, packed[ends:]


def newton_schulz(gram_mat):
    def product(left, right):
        return jnp.einsum(
            "mde,mef->mdf",
            left,
            right,
            precision=lax.Precision.HIGHEST,
            preferred_element_type=WIDE,
        )

    norm_val = jnp.sqrt(jnp.trace(gram_mat, axis1=1, axis2=2))[:, None, None] + NS_EPS
    gram_mat = gram_mat / (norm_val * norm_val)
    unit = jnp.eye(gram_mat.shape[-1], dtype=WIDE)[None]
    chain = None
    for turn_idx in range(NS_ITERS):
        poly_mat = COEF_A * unit + COEF_B * gram_mat + COEF_C * product(gram_mat, gram_mat)
        chain = poly_mat if chain is None else product(poly_mat, chain)
        if turn_idx < NS_ITERS - 1:
            gram_mat = product(product(poly_mat, gram_mat), poly_mat)
    return chain / norm_val


def adam_step(param, grad, moment, square):
    new_moment = BETA_ONE * moment + (1.0 - BETA_ONE) * grad
    new_square = BETA_TWO * square + (1.0 - BETA_TWO) * grad * grad
    corrected = new_moment / (1.0 - BETA_ONE**STEP)
    scaled = jnp.sqrt(new_square / (1.0 - BETA_TWO**STEP)) + ADAM_EPS
    return (new_moment, new_square, param - ADAM_RATE * corrected / scaled)


DEPTH, ACROSS = 4, 2
SIDES, CORES = 2, 2
OWNERS = (
    (2, 0, 0, 0),
    (2, 1, 0, 1),
    (1, 1, 0, 0),
    (2, 1, 1, 0),
    (2, 0, 1, 1),
    (1, 0, 0, 1),
    (1, 1, 1, 0),
)


def place():
    f = lax.axis_index("fsdp")
    n = lax.axis_index("ns")
    return f // ACROSS, f % ACROSS, n // CORES, n % CORES


def device(z, x, y, c):
    return (z * ACROSS + x, y * CORES + c)


def remote(src, dst, send_sem, recv_sem, where):
    return pltpu.make_async_remote_copy(
        src_ref=src,
        dst_ref=dst,
        send_sem=send_sem,
        recv_sem=recv_sem,
        device_id=where,
        device_id_type=pl.DeviceIdType.MESH,
    )


def greet(where):
    pl.semaphore_signal(
        pltpu.get_barrier_semaphore(),
        inc=1,
        device_id=where,
        device_id_type=pl.DeviceIdType.MESH,
    )


def halves(value):
    high = value.astype(LOW)
    return high, (value - high.astype(WIDE)).astype(LOW)


def square_wide(value):
    high, low = halves(value)
    cross = mul_nn(high, low)
    return mul_nn(high, high) + (cross + cross.T)


def mul_wide(left, right):
    columns = right.shape[1]
    left_high, left_low = halves(left)
    right_high, right_low = halves(right)
    first = mul_nn(left_high, jnp.concatenate([right_high, right_low], axis=1))
    return first[:, :columns] + (first[:, columns:] + mul_nn(left_low, right_high))


def gram_wide(value):
    high, low = halves(value)
    cross = mul_tn(high, low)
    return mul_tn(high, high) + (cross + cross.T)


def whole_kernel(
    pieces,
    lengths,
    bias,
    tok_hbm,
    cot_hbm,
    var_ref,
    time_ref,
    table_ref,
    gain_ref,
    wqkv_ref,
    wout_ref,
    wgate_up_ref,
    wdown_ref,
    mqkv_hbm,
    mout_hbm,
    mgate_up_hbm,
    mdown_hbm,
    out_ref,
    gtok_ref,
    grows_ref,
    xrows_ref,
    total_ref,
    tok_ref,
    cot_ref,
    mqkv_ref,
    mout_ref,
    mgate_up_ref,
    mdown_ref,
    load_sem,
    w_s,
    grad_s,
    momenta,
    n1_s,
    n2_s,
    att_s,
    gml_s,
    glow_s,
    hid_s,
    gg_s,
    gu_s,
    low_s,
    gqkv_s,
    probs_s,
    mid_s,
    gmid_s,
    gatt_s,
    scale_s,
    rope_s,
    y_attn,
    y_ff,
    g_attn,
    g_ff,
    x_attn,
    x_ff,
    gram_s,
    chain_s,
    stat_s,
    stat_in,
    stat_acc,
    stat_line,
    stat_send,
    stat_recv,
    adv_recv,
    mom_recv,
    x_send,
    x_recv,
    fan_send,
    fan_recv,
    *per_part,
):
    z, x, y, c = place()
    shard = z * ACROSS + x
    rows, width = tok_ref.shape
    heads = bias.shape[1]
    sibling = device(z, x, y, 1 - c)
    facing = device(z, x, 1 - y, c)
    corner = device(z, x, 1 - y, 1 - c)
    beside = device(z, 1 - x, y, c)
    upper = device(z + 1, x, y, c)
    lower = device(z - 1, x, y, c)
    world = DEPTH * ACROSS * SIDES * CORES
    rank = shard * (SIDES * CORES) + y * CORES + c
    line = [lax.rem(z + k, DEPTH) for k in range(DEPTH)]

    def far_first(t):
        low_z = jnp.minimum(z, DEPTH - 1 - z)
        turn = DEPTH - 1 - t
        turn = low_z if turn == 0 else jnp.where(turn - 1 < low_z, turn - 1, turn)
        return jnp.where(z == low_z, turn, DEPTH - 1 - turn)
    part = 2 * c + y

    def hello(i, carry):
        other = lax.rem(rank + 1 + i, world)
        greet((other // (SIDES * CORES), lax.rem(other, SIDES * CORES)))
        return carry

    lax.fori_loop(0, world - 1, hello, 0)
    loads = [
        pltpu.make_async_copy(src, dst, load_sem.at[i])
        for i, (src, dst) in enumerate(
            (
                (tok_hbm, tok_ref),
                (cot_hbm, cot_ref),
                (mqkv_hbm, mqkv_ref),
                (mout_hbm, mout_ref),
                (mgate_up_hbm, mgate_up_ref),
                (mdown_hbm, mdown_ref),
            )
        )
    ]
    for one in loads:
        one.start()

    def put(index, value):
        start, count = pieces[index]
        w_s[shard, start : start + count, :] = value.astype(LOW)

    for j in range(3):
        put(j, wqkv_ref[j])
    put(3, wout_ref[...])
    put(4, wgate_up_ref[0].T)
    put(5, wgate_up_ref[1].T)
    put(6, wdown_ref[...])
    pl.semaphore_wait(pltpu.get_barrier_semaphore(), world - 1)

    has_up = z < DEPTH - 1
    has_down = z > 0

    def exists(rel):
        return (z + rel >= 0) & (z + rel < DEPTH)

    class Gather:
        def __init__(self, start, count, sems):
            self.start_row, self.half = start, count // 2
            (
                self.up_send,
                self.down_send,
                self.x_send,
                self.sib_send,
                self.below_recv,
                self.above_recv,
                self.x_recv,
                self.sib_recv,
            ) = sems

        def view(self, at, core):
            first = pl.multiple_of(self.start_row + core * self.half, 16)
            return w_s.at[at, pl.ds(first, self.half)]

        def mine(self, rel):
            return self.view(shard + rel * ACROSS, c)

        def others(self, rel):
            return self.view((z + rel) * ACROSS + 1 - x, c)

        def up(self, d):
            return remote(
                self.mine(-d), self.mine(-d), self.up_send.at[d], self.below_recv.at[d], upper
            )

        def down(self, d):
            return remote(
                self.mine(d), self.mine(d), self.down_send.at[d], self.above_recv.at[d], lower
            )

        def over(self, rel, where):
            return remote(
                self.mine(rel), where, self.x_send.at[rel + 3], self.x_recv.at[rel + 3], beside
            )

        def sib(self, kind, rel, src):
            return remote(
                src, src, self.sib_send.at[kind, rel + 3], self.sib_recv.at[kind, rel + 3], sibling
            )

        def start(self):
            @pl.when(has_up)
            def _():
                self.up(0).start()

            @pl.when(has_down)
            def _():
                self.down(0).start()

            self.over(0, self.mine(0)).start()

        def hop(self, d):
            @pl.when(exists(-d))
            def _():
                here = self.mine(-d)
                remote(
                    here, here, self.up_send.at[d], self.below_recv.at[d - 1], lower
                ).wait_recv()
                if d < DEPTH - 1:

                    @pl.when(has_up)
                    def _():
                        self.up(d).start()

                self.over(-d, here).start()
                self.sib(0, -d, here).start()

            @pl.when(exists(d))
            def _():
                here = self.mine(d)
                remote(
                    here, here, self.down_send.at[d], self.above_recv.at[d - 1], upper
                ).wait_recv()
                if d < DEPTH - 1:

                    @pl.when(has_down)
                    def _():
                        self.down(d).start()

                self.over(d, here).start()
                self.sib(0, d, here).start()

        def from_beside(self, d):
            for rel in (0,) if d == 0 else (-d, d):

                @pl.when(exists(rel))
                def _():
                    there = self.others(rel)
                    remote(
                        there, there, self.x_send.at[rel + 3], self.x_recv.at[rel + 3], beside
                    ).wait_recv()
                    self.sib(1, rel, there).start()

        def arrive(self):
            for rel in range(1 - DEPTH, DEPTH):

                @pl.when(exists(rel))
                def _():
                    if rel != 0:
                        self.sib(0, rel, self.view(shard + rel * ACROSS, 1 - c)).wait_recv()
                    self.sib(1, rel, self.view((z + rel) * ACROSS + 1 - x, 1 - c)).wait_recv()

        def sent(self):
            for rel in range(1 - DEPTH, DEPTH):

                @pl.when(exists(rel))
                def _():
                    if rel != 0:
                        self.sib(0, rel, self.mine(rel)).wait_send()
                    self.sib(1, rel, self.others(rel)).wait_send()
                    self.over(rel, self.mine(rel)).wait_send()

            for d in range(DEPTH - 1):

                @pl.when(exists(-d) & has_up)
                def _():
                    self.up(d).wait_send()

                @pl.when(exists(d) & has_down)
                def _():
                    self.down(d).wait_send()

    ff_row = pieces[4][0]
    last_row = pieces[6][0] + pieces[6][1]
    spans = ((0, ff_row), (ff_row, last_row - ff_row))
    each = len(per_part) // 2
    gathers = [Gather(*spans[i], per_part[i * each : i * each + 8]) for i in range(2)]
    attn_gather, ff_gather = gathers
    class Reduce:
        def __init__(self, start, count, refs):
            self.order, self.own = far_first, DEPTH - 1
            self.start_row, self.half, self.quarter = start, count // 2, count // 4
            (
                self.in_zero,
                self.acc_zero,
                self.in_one,
                self.acc_one,
                self.in_two,
                self.acc_two,
                self.in_three,
                self.send_zero,
                self.send_one,
                self.send_two,
                self.send_three,
                self.recv_zero,
                self.recv_one,
                self.recv_two,
                self.recv_three,
                self.mom_send,
                self.adv_send,
                self.row_send,
                self.row_recv,
            ) = refs
            self.keep_quarter = pl.ds(pl.multiple_of(y * self.quarter, 16), self.quarter)
            self.give_quarter = pl.ds(pl.multiple_of((1 - y) * self.quarter, 16), self.quarter)
            self.first_quarter = pl.ds(0, self.quarter)

        def half_of(self, core):
            return pl.ds(pl.multiple_of(self.start_row + core * self.half, 16), self.half)

        def rows_of(self, quarter):
            first = pl.multiple_of(self.start_row + quarter * self.quarter, 16)
            return pl.ds(first, self.quarter)

        def zero(self, t):
            return remote(
                grad_s.at[self.order(t), :, self.half_of(1 - c)],
                self.in_zero.at[t],
                self.send_zero.at[t],
                self.recv_zero.at[t],
                sibling,
            )

        def crosses(self, t, way):
            return (c + t) % 2 == way

        def one(self, k, core):
            if core == 0:
                src, dst = self.acc_zero.at[k, :, self.give_quarter], self.in_one.at[
                    k, :, self.first_quarter
                ]
            else:
                src, dst = self.acc_zero.at[k, 1 - x], self.in_one.at[k, 0]
            where = facing if core == 0 else beside
            return remote(src, dst, self.send_one.at[k], self.recv_one.at[k], where)

        def two(self, k, core):
            if core == 0:
                src = self.acc_one.at[k, 1 - x, self.first_quarter]
            else:
                src = self.acc_one.at[k, 0, self.give_quarter]
            where = beside if core == 0 else facing
            return remote(src, self.in_two.at[k], self.send_two.at[k], self.recv_two.at[k], where)

        def three(self, t):
            return remote(
                self.acc_two.at[t],
                self.in_three.at[z],
                self.send_three.at[t],
                self.recv_three.at[z],
                device(self.order(t), x, y, c),
            )

        def add(self, left, right):
            return (left.astype(WIDE) + right.astype(WIDE)).astype(LOW)

        def start(self):
            for t in range(DEPTH):
                self.zero(t).start()

        def first(self, t):
            self.zero(t).wait_recv()
            kept = grad_s[self.order(t), :, self.half_of(c)]
            self.acc_zero[t] = self.add(kept, self.in_zero[t])
            for core in range(2):

                @pl.when(self.crosses(t, core))
                def _():
                    self.one(t, core).start()

        def second(self, t):
            quarter = self.quarter

            @pl.when(self.crosses(t, 0))
            def _():
                self.one(t, 0).wait_recv()
                self.acc_one[t, :, :quarter] = self.add(
                    self.acc_zero[t, :, self.keep_quarter], self.in_one[t, :, :quarter]
                )
                self.two(t, 0).start()

            @pl.when(self.crosses(t, 1))
            def _():
                self.one(t, 1).wait_recv()
                self.acc_one[t, 0] = self.add(self.acc_zero[t, x], self.in_one[t, 0])
                self.two(t, 1).start()

        def third(self, t):
            quarter = self.quarter

            @pl.when(self.crosses(t, 0))
            def _():
                self.two(t, 0).wait_recv()
                self.acc_two[t] = self.add(self.acc_one[t, x, :quarter], self.in_two[t])

            @pl.when(self.crosses(t, 1))
            def _():
                self.two(t, 1).wait_recv()
                self.acc_two[t] = self.add(self.acc_one[t, 0, self.keep_quarter], self.in_two[t])

            @pl.when(self.order(t) != z)
            def _():
                self.three(t).start()

        def segments(self, index):
            found = []
            begin = self.start_row + index * self.quarter
            for m, (start, count) in enumerate(pieces):
                first, last = max(start, begin), min(start + count, begin + self.quarter)
                if first < last:
                    found.append((m, first - begin, first - start, last - first))
            return found

        def to_owner(self, kind, index, i, stays=False):
            m, first, to, count = self.segments(index)[i]
            begin = self.start_row + index * self.quarter + first
            source = (momenta, grows_ref)[kind].at[pl.ds(begin, count)]
            target = stage(kind, m).at[shard, pl.ds(to, count)]
            sent = (self.mom_send, self.adv_send)[kind].at[i]
            got = (mom_recv, adv_recv)[kind].at[0]
            if stays:
                return pltpu.make_async_copy(source, target, got)
            return remote(source, target, sent, got, device(*OWNERS[m]))

        def all_to_owners(self, kind):
            for index in range(4):
                for i, (m, _, _, _) in enumerate(self.segments(index)):

                    @pl.when((part == index) & jnp.logical_not(owned(m)))
                    def _():
                        self.to_owner(kind, index, i).start()

                    @pl.when((part == index) & owned(m))
                    def _():
                        self.to_owner(kind, index, i, stays=True).start()

        def send_momenta(self):
            self.all_to_owners(0)

        def row_copy(self, j, quarter, where):
            here = grows_ref.at[self.rows_of(quarter)]
            return remote(here, here, self.row_send.at[j], self.row_recv.at[j], where)

        def finish(self):
            total = self.acc_two[self.own].astype(WIDE)
            for j in range(1, DEPTH):
                there = self.in_three.at[line[j]]
                remote(
                    there, there, self.send_three.at[0], self.recv_three.at[line[j]], sibling
                ).wait_recv()
                total = total + self.in_three[line[j]].astype(WIDE)
            grows_ref[self.rows_of(part), :] = total.astype(LOW)
            self.all_to_owners(1)
            for j, where in enumerate((sibling, facing, corner)):
                self.row_copy(j, part, where).start()

        def done(self):
            mates = ((sibling, 0, 1), (facing, 1, 0), (corner, 1, 1))
            for j, (where, dy, dc) in enumerate(mates):
                self.row_copy(j, 2 * (c ^ dc) + (y ^ dy), where).wait_recv()
                self.row_copy(j, part, where).wait_send()
            for index in range(4):
                for i, (m, _, _, _) in enumerate(self.segments(index)):

                    @pl.when((part == index) & jnp.logical_not(owned(m)))
                    def _():
                        for kind in range(2):
                            self.to_owner(kind, index, i).wait_send()

            for t in range(DEPTH):
                self.zero(t).wait_send()

                @pl.when(self.order(t) != z)
                def _():
                    self.three(t).wait_send()

                for core in range(2):

                    @pl.when(self.crosses(t, core))
                    def _():
                        self.one(t, core).wait_send()
                        self.two(t, core).wait_send()

    def owned(m):
        oz, ox, oy, oc = OWNERS[m]
        return (z == oz) & (x == ox) & (y == oy) & (c == oc)

    def stage(kind, m):
        return ((y_attn, y_ff), (g_attn, g_ff))[kind][int(m >= 4)]

    reduces = [Reduce(*spans[i], per_part[i * each + 8 : (i + 1) * each]) for i in range(2)]
    attn_reduce, ff_reduce = reduces

    attn_gather.start()
    ff_gather.start()

    for one in loads:
        one.wait()
    for i, (value, turned) in enumerate(((mgate_up_ref[0], 4), (mgate_up_ref[1], 5))):
        start, count = pieces[turned]
        momenta[start : start + count, :] = value.T
    for j in range(3):
        start, count = pieces[j]
        momenta[start : start + count, :] = mqkv_ref[j]
    momenta[pieces[3][0] : pieces[3][0] + pieces[3][1], :] = mout_ref[...]
    momenta[pieces[6][0] : last_row, :] = mdown_ref[...]
    stat_s[...] = jnp.zeros_like(stat_s)

    lane = lax.broadcasted_iota(jnp.int32, (1, LANES), 1)
    low_head = lane < HEAD_DIM
    low_half = lane % HEAD_DIM < HEAD_DIM // 2
    row_id = lax.broadcasted_iota(jnp.int32, (PAIR, 1), 0)
    lane_id = lax.broadcasted_iota(jnp.int32, (1, PAIR), 1)
    same_bucket = (row_id < BUCKET) == (lane_id < BUCKET)
    slots = lax.broadcasted_iota(jnp.int32, (1, TIME_SLOTS), 1)
    query_scale = HEAD_DIM ** (-0.5)
    gain_one = gain_ref[0:1, :]
    gain_two = gain_ref[1:2, :]

    def column(row):
        return jnp.broadcast_to(row, (8, PAIR)).T[:, 0:1]

    def var_row(pair):
        two = var_ref[pl.ds(2 * pair, 2), :]
        return jnp.concatenate([two[0:1], two[1:2]], axis=1).astype(WIDE)

    def block_of(i, size):
        return pl.ds(pl.multiple_of(i * size, size), size)

    def prepare(i, carry):
        here = block_of(i, PAIR)
        times = column(time_ref[pl.ds(i, 1), :].astype(WIDE)).astype(jnp.int32)
        hot = (times == slots).astype(LOW)
        rope_s[here, :] = (
            mul_nn(hot, table_ref[0]) + mul_nn(hot, table_ref[1]) + mul_nn(hot, table_ref[2])
        )
        tokens = tok_ref[here, :].astype(WIDE)
        scale = lax.rsqrt(jnp.mean(tokens * tokens, axis=-1, keepdims=True) + EPS_NORM)
        scale_s[here, 0:1] = scale
        n1_s[here, :] = (tokens * scale * gain_one).astype(LOW)
        first, second = lengths[2 * i], lengths[2 * i + 1]
        live = row_id % BUCKET < jnp.where(row_id < BUCKET, first, second)
        glow_s[here, :] = jnp.where(live, cot_ref[here, :].astype(WIDE), 0.0).astype(LOW)
        return carry

    lax.fori_loop(0, rows // PAIR, prepare, 0)

    for d in range(1, DEPTH):
        attn_gather.hop(d)
        if d < DEPTH - 1:
            ff_gather.hop(d)
    for d in range(DEPTH):
        attn_gather.from_beside(d)
    attn_gather.arrive()

    def weight(first, last):
        parts = []
        for i in range(first, last):
            start, count = pieces[i]
            piece = w_s[:, start : start + count, :]
            parts.append(piece.reshape(piece.shape[0] * count, width))
        return parts[0] if len(parts) == 1 else jnp.concatenate(parts, axis=0)

    def swapped(values):
        half = HEAD_DIM // 2
        return jnp.where(
            low_half, pltpu.roll(values, LANES - half, 1), pltpu.roll(values, half, 1)
        )

    def two_heads(value):
        none = jnp.zeros_like(value)
        return jnp.concatenate(
            [jnp.where(low_head, value, none), jnp.where(low_head, none, value)], axis=0
        )

    per_block = BLOCK // PAIR

    def attend(i, carry):
        here = block_of(i, BLOCK)
        qkv = mul_nt(n1_s[here, :], weight(0, 3))
        cosine = rope_s[here, :LANES]
        sine = rope_s[here, LANES:]
        masks = []
        for p in range(per_block):
            pair = i * per_block + p
            first, second = lengths[2 * pair], lengths[2 * pair + 1]
            live_key = lane_id % BUCKET < jnp.where(lane_id < BUCKET, first, second)
            row = var_row(pair)
            masks.append((same_bucket & live_key, column(row) == row))
        attended = []
        for hp in range(heads // 2):
            first = hp * LANES
            q = qkv[:, first : first + LANES]
            k = qkv[:, width + first : width + first + LANES]
            v = qkv[:, 2 * width + first : 2 * width + first + LANES].astype(LOW)
            q = ((q * cosine + swapped(q) * sine) * query_scale).astype(LOW)
            k = (k * cosine + swapped(k) * sine).astype(LOW)
            low_s[here, first : first + LANES] = q
            low_s[here, width + first : width + first + LANES] = k
            low_s[here, 2 * width + first : 2 * width + first + LANES] = v
            pairs = []
            for p in range(per_block):
                span = slice(p * PAIR, (p + 1) * PAIR)
                mask, same_var = masks[p]
                raw = mul_nt(two_heads(q[span]), k[span])
                both = []
                for j in range(2):
                    h = 2 * hp + j
                    biased = raw[j * PAIR : (j + 1) * PAIR] + jnp.where(
                        same_var, bias[0, h], bias[1, h]
                    )
                    both.append(jnp.where(mask, biased, NEG_FILL))
                scores = jnp.concatenate(both, axis=0)
                exponent = jnp.exp(scores - jnp.max(scores, axis=-1, keepdims=True))
                probs = exponent / jnp.sum(exponent, axis=-1, keepdims=True)
                probs_s[i * per_block + p, hp] = probs
                both = mul_nn(probs.astype(LOW), v[span])
                pairs.append(jnp.where(low_head, both[:PAIR], both[PAIR:]))
            attended.append(jnp.concatenate(pairs, axis=0).astype(LOW))
        attended = jnp.concatenate(attended, axis=1)
        att_s[here, :] = attended
        mid = tok_ref[here, :].astype(WIDE) + mul_nn(attended, weight(3, 4))
        mid_s[here, :] = mid
        scale = lax.rsqrt(jnp.mean(mid * mid, axis=-1, keepdims=True) + EPS_NORM)
        scale_s[here, 1:2] = scale
        n2_s[here, :] = (mid * scale * gain_two).astype(LOW)
        @pl.when(i == 0)
        def _():
            ff_gather.hop(DEPTH - 1)
            ff_gather.from_beside(0)
            ff_gather.from_beside(1)

        for d in range(2, DEPTH):

            @pl.when(i == d - 1)
            def _():
                ff_gather.from_beside(d)

        return carry

    lax.fori_loop(0, rows // BLOCK, attend, 0)
    ff_gather.arrive()
    for one in reduces:
        one.send_momenta()

    def feed(i, carry):
        here = block_of(i, BLOCK)
        normed_two = n2_s[here, :]
        w_gate, w_up, w_down = weight(4, 5), weight(5, 6), weight(6, 7)
        gate = mul_nt(normed_two, w_gate)
        up = mul_nt(normed_two, w_up)
        sig = 1.0 / (1.0 + jnp.exp(-gate))
        silu = gate * sig
        hid_s[here, :] = (silu * up).astype(LOW)
        g_low = glow_s[here, :]
        g_hidden = mul_nt(g_low, w_down)
        g_gate = (g_hidden * up * sig * (1.0 + gate * (1.0 - sig))).astype(LOW)
        g_up = (g_hidden * silu).astype(LOW)
        gg_s[here, :] = g_gate
        gu_s[here, :] = g_up
        e_two = mul_nn(g_gate, w_gate) + mul_nn(g_up, w_up)
        scale = scale_s[here, 1:2]
        unit = mid_s[here, :] * scale
        stat_s[1:2, :] += jnp.sum(e_two * unit, axis=0, keepdims=True)
        scaled = e_two * gain_two
        g_mid = g_low.astype(WIDE) + scale * (
            scaled - unit * jnp.mean(scaled * unit, axis=-1, keepdims=True)
        )
        gmid_s[here, :] = g_mid
        g_mid_low = g_mid.astype(LOW)
        gml_s[here, :] = g_mid_low
        gatt_s[here, :] = mul_nt(g_mid_low, weight(3, 4)).astype(LOW)
        return carry

    lax.fori_loop(0, rows // BLOCK, feed, 0)

    def grad_put(index, left, right):
        start, count = pieces[index]
        grad_s[:, :, start : start + count, :] = (
            mul_tn(left, right).reshape(DEPTH, ACROSS, count, width).astype(LOW)
        )

    grad_put(4, gg_s[...], n2_s[...])
    grad_put(5, gu_s[...], n2_s[...])
    grad_put(6, hid_s[...], glow_s[...])
    ff_reduce.start()
    grad_put(3, att_s[...], gml_s[...])

    def attend_back(i, carry):
        here = block_of(i, PAIR)
        row = var_row(i)
        same_var = column(row) == row
        cosine = rope_s[here, :LANES]
        sine = rope_s[here, LANES:]
        for hp in range(heads // 2):
            first = hp * LANES
            q2 = two_heads(low_s[here, first : first + LANES])
            k = low_s[here, width + first : width + first + LANES]
            v = low_s[here, 2 * width + first : 2 * width + first + LANES]
            probs = probs_s[i, hp]
            ga2 = two_heads(gatt_s[here, first : first + LANES])
            g_probs = mul_nt(ga2, v)
            row_dot = jnp.sum(probs * g_probs, axis=-1, keepdims=True)
            g_scores = probs * (g_probs - row_dot)
            for j in range(2):
                h = 2 * hp + j
                mine = g_scores[j * PAIR : (j + 1) * PAIR]
                stat_s[8 + h : 9 + h, :PAIR] += jnp.sum(
                    jnp.where(same_var, mine, 0.0), axis=0, keepdims=True
                )
                stat_s[16 + h : 17 + h, :PAIR] += jnp.sum(
                    jnp.where(same_var, 0.0, mine), axis=0, keepdims=True
                )
            low_scores = g_scores.astype(LOW)
            both = mul_nn(low_scores, k)
            dq = jnp.where(low_head, both[:PAIR], both[PAIR:])
            dk = mul_tn(low_scores, q2)
            dv = mul_tn(probs.astype(LOW), ga2)
            gqkv_s[here, first : first + LANES] = (
                (dq * cosine - swapped(dq) * sine) * query_scale
            ).astype(LOW)
            gqkv_s[here, width + first : width + first + LANES] = (
                dk * cosine - swapped(dk) * sine
            ).astype(LOW)
            gqkv_s[here, 2 * width + first : 2 * width + first + LANES] = dv.astype(LOW)
        @pl.when(i == 0)
        def _():
            for t in range(DEPTH):
                ff_reduce.first(t)

        @pl.when(i == 4)
        def _():
            ff_reduce.second(0)
            ff_reduce.second(1)

        @pl.when(i == 6)
        def _():
            ff_reduce.third(0)
            ff_reduce.third(1)
            ff_reduce.second(2)
            ff_reduce.second(3)

        return carry

    lax.fori_loop(0, rows // PAIR, attend_back, 0)
    for j in range(3):
        grad_put(j, gqkv_s[:, j * width : (j + 1) * width], n1_s[...])
    attn_reduce.start()
    ff_reduce.third(2)
    ff_reduce.third(3)

    def last(i):
        here = block_of(i, 2 * BLOCK)
        e_one = mul_nn(gqkv_s[here, :], weight(0, 3))
        scale = scale_s[here, 0:1]
        unit = tok_ref[here, :].astype(WIDE) * scale
        stat_s[0:1, :] += jnp.sum(e_one * unit, axis=0, keepdims=True)
        scaled = e_one * gain_one
        gtok_ref[here, :] = (
            gmid_s[here, :]
            + scale * (scaled - unit * jnp.mean(scaled * unit, axis=-1, keepdims=True))
        ).astype(LOW)

    def outgoing(i):
        here = block_of(i, 2 * BLOCK)
        out_ref[here, :] = (mid_s[here, :] + mul_nn(hid_s[here, :], weight(6, 7))).astype(LOW)

    def stat_copy(step, src, where):
        return remote(src, stat_in.at[step], stat_send.at[step], stat_recv.at[step], where)

    for t in range(DEPTH):
        attn_reduce.first(t)
    last(0)
    last(1)
    stat_copy(0, stat_s, sibling).start()
    ff_reduce.finish()
    attn_reduce.second(0)
    attn_reduce.second(1)
    stat_copy(0, stat_s, sibling).wait()
    stat_acc[0] = stat_s[...] + stat_in[0]
    stat_copy(1, stat_acc.at[0], facing).start()
    attn_reduce.second(2)
    attn_reduce.second(3)
    for t in range(DEPTH):
        attn_reduce.third(t)
    stat_copy(1, stat_acc.at[0], facing).wait()
    stat_acc[1] = stat_acc[0] + stat_in[1]
    stat_copy(2, stat_acc.at[1], beside).start()
    attn_owner = functools.reduce(jnp.logical_or, [owned(m) for m in range(4)])
    ff_owner = functools.reduce(jnp.logical_or, [owned(m) for m in range(4, 7)])

    chips = DEPTH * ACROSS * SIDES

    def x_copy(m, i):
        start, count = pieces[m]
        source = x_attn if m < 4 else x_ff
        to = i // SIDES
        return remote(
            source.at[to],
            xrows_ref.at[pl.ds(start, count)],
            x_send.at[i],
            x_recv.at[m],
            (to, lax.rem(i, SIDES) * CORES + OWNERS[m][3]),
        )

    mine = shard * SIDES + y
    unit_mat = lax.broadcasted_iota(jnp.int32, (width, width), 0) == lax.broadcasted_iota(
        jnp.int32, (width, width), 1
    )
    diagonal = jnp.where(unit_mat, COEF_A, 0.0)

    def advance(y_buf, g_buf):
        pltpu.make_async_copy(y_buf, y_buf, mom_recv.at[0]).wait()
        pltpu.make_async_copy(g_buf, g_buf, adv_recv.at[0]).wait()
        grad = g_buf[...].astype(WIDE)
        return grad + MUON_MU * (MUON_MU * y_buf[...] + grad)

    def poly(value):
        return diagonal + COEF_B * value + COEF_C * square_wide(value)

    @pl.when(ff_owner)
    def _():
        y_ff[...] = advance(y_ff, g_ff)
        gram_mat = gram_wide(y_ff[...].reshape(-1, width))
        trace = jnp.sum(jnp.where(unit_mat, gram_mat, 0.0), keepdims=True)
        inverse = 1.0 / (jnp.sqrt(trace) + NS_EPS)
        gram_mat = gram_mat * (inverse * inverse)
        step_mat = poly(gram_mat)
        gram_s[...] = mul_wide(mul_wide(gram_mat, step_mat), step_mat)
        chain_s[...] = step_mat * inverse

    attn_reduce.finish()
    stat_copy(2, stat_acc.at[1], beside).wait()
    stat_acc[2] = stat_acc[1] + stat_in[2]
    stat_line[z] = stat_acc[2]

    def stat_send_line(j):
        return remote(
            stat_acc.at[2],
            stat_line.at[z],
            stat_send.at[2 + j],
            stat_recv.at[2 + j],
            device(line[j], x, y, c),
        )

    for j in range(1, DEPTH):
        stat_send_line(j).start()

    def send_x(m, first, count):
        def send(i, carry):
            @pl.when(i != mine)
            def _():
                x_copy(m, i).start()

            return carry

        lax.fori_loop(first, first + count, send, 0)

    def keep_x(m):
        start, count = pieces[m]
        source = x_attn if m < 4 else x_ff
        pltpu.make_async_copy(
            source.at[shard], xrows_ref.at[pl.ds(start, count)], x_recv.at[m]
        ).start()

    @pl.when(attn_owner)
    def _():
        value = advance(y_attn, g_attn).reshape(-1, width)
        total = jnp.sum(jnp.sum(value * value, axis=0, keepdims=True), axis=1, keepdims=True)
        chain_s[...] = value * (1.0 / (jnp.sqrt(total) + NS_EPS))

        def turn(i, carry):
            now = chain_s[...]
            chain_s[...] = mul_wide(now, poly(gram_wide(now)))
            return carry

        lax.fori_loop(0, NS_ITERS, turn, 0)
        x_attn[...] = chain_s[...].astype(LOW).reshape(x_attn.shape)
        for m in range(4):

            @pl.when(owned(m))
            def _():
                send_x(m, 0, chips)
                keep_x(m)

    @pl.when(ff_owner)
    def _():
        def turn(i, carry):
            now = gram_s[...]
            step_now = poly(now)
            both = mul_wide(jnp.concatenate([now, chain_s[...]], axis=0), step_now)
            chain_s[...] = both[width:]
            gram_s[...] = mul_wide(both[:width], step_now)
            return carry

        lax.fori_loop(0, NS_ITERS - 2, turn, 0)
        chain_s[...] = mul_wide(chain_s[...], poly(gram_s[...]))

        def give(i, carry):
            at = lax.rem(z + 2 + i, DEPTH)
            these = pl.ds(at * ACROSS, ACROSS)
            value = y_ff[these].reshape(-1, width)
            x_ff[these] = mul_wide(value, chain_s[...]).astype(LOW).reshape(
                ACROSS, x_ff.shape[1], width
            )
            for m in range(4, 7):

                @pl.when(owned(m))
                def _():
                    send_x(m, at * (ACROSS * SIDES), ACROSS * SIDES)

            return carry

        lax.fori_loop(0, DEPTH, give, 0)
        for m in range(4, 7):

            @pl.when(owned(m))
            def _():
                keep_x(m)

    outgoing(0)
    outgoing(1)

    for j in range(1, DEPTH):
        remote(
            stat_acc.at[2],
            stat_line.at[lax.rem(z + DEPTH - j, DEPTH)],
            stat_send.at[2 + j],
            stat_recv.at[2 + j],
            device(line[j], x, y, c),
        ).wait()
    total_ref[...] = (stat_line[0] + stat_line[1]) + (stat_line[2] + stat_line[3])
    for one in gathers:
        one.sent()
    for one in reduces:
        one.done()

    def fan_copy(m):
        start, count = pieces[m]
        rows_m = xrows_ref.at[pl.ds(start, count)]
        return remote(rows_m, rows_m, fan_send.at[m], fan_recv.at[m], sibling)

    for m in range(7):
        start, count = pieces[m]

        @pl.when(c == OWNERS[m][3])
        def _():
            rows_m = xrows_ref.at[pl.ds(start, count)]
            pltpu.make_async_copy(rows_m, rows_m, x_recv.at[m]).wait()
            fan_copy(m).start()

    for m in range(7):

        @pl.when(c != OWNERS[m][3])
        def _():
            fan_copy(m).wait_recv()

        @pl.when(c == OWNERS[m][3])
        def _():
            fan_copy(m).wait_send()

        @pl.when(owned(m))
        def _():
            def sent(i, carry):
                x_copy(m, lax.rem(mine + i, chips)).wait_send()
                return carry

            lax.fori_loop(1, chips, sent, 0)


def rotary_table():
    half = HEAD_DIM // 2
    frequency = (ROPE_BASE ** (-2.0 * np.arange(half) / HEAD_DIM)).astype(np.float32)
    angles = np.arange(TIME_SLOTS, dtype=np.float32)[:, None] * frequency[None, :]
    cosine = np.cos(angles.astype(np.float64)).astype(np.float32)
    sine = np.sin(angles.astype(np.float64)).astype(np.float32)
    table = np.concatenate([cosine] * 4 + [-sine, sine, -sine, sine], axis=1)
    parts = []
    for _ in range(3):
        parts.append(table.astype(LOW))
        table = table - parts[-1].astype(np.float32)
    return np.stack(parts)


def whole_step(tokens, cotangent, lengths, variates, times, gains, attn_bias, weights, momenta):
    rows, width = tokens.shape
    heads = attn_bias.shape[1]
    attn_rows, ff_rows = weights[1].shape[0], weights[3].shape[0]
    pieces = offsets(attn_rows, ff_rows)
    ff = ff_rows * DEPTH * ACROSS
    shards = DEPTH * ACROSS
    shard_rows = 4 * attn_rows + 3 * ff_rows
    low = lambda *shape: pltpu.VMEM(shape, LOW)
    wide = lambda *shape: pltpu.VMEM(shape, WIDE)
    dma = lambda *shape: pltpu.SemaphoreType.DMA(shape)

    def part_scratch(count):
        half, quarter = count // 2, count // 4
        relative = 2 * DEPTH - 1
        return [
            dma(DEPTH),
            dma(DEPTH),
            dma(relative),
            dma(2, relative),
            dma(DEPTH),
            dma(DEPTH),
            dma(relative),
            dma(2, relative),
            low(DEPTH, ACROSS, half, width),
            low(DEPTH, ACROSS, half, width),
            low(DEPTH, ACROSS, half, width),
            low(DEPTH, ACROSS, half, width),
            low(DEPTH, quarter, width),
            low(DEPTH, quarter, width),
            low(DEPTH, quarter, width),
            *[dma(DEPTH) for _ in range(8)],
            dma(3),
            dma(3),
            dma(3),
            dma(3),
        ]

    return pl.pallas_call(
        functools.partial(whole_kernel, pieces),
        out_shape=(
            jax.ShapeDtypeStruct((rows, width), LOW),
            jax.ShapeDtypeStruct((rows, width), LOW),
            jax.ShapeDtypeStruct((shard_rows, width), LOW),
            jax.ShapeDtypeStruct((shard_rows, width), LOW),
            jax.ShapeDtypeStruct((STATS, width), WIDE),
        ),
        in_specs=[SCALARS] * 2 + [ANYWHERE] * 2 + [WHOLE] * 8 + [ANYWHERE] * 4,
        out_specs=(WHOLE,) * 5,
        scratch_shapes=[
            low(rows, width),
            low(rows, width),
            *[wide(*m.shape) for m in momenta],
            dma(6),
            low(shards, shard_rows, width),
            low(DEPTH, ACROSS, shard_rows, width),
            wide(shard_rows, width),
            low(rows, width),
            low(rows, width),
            low(rows, width),
            low(rows, width),
            low(rows, width),
            low(rows, ff),
            low(rows, ff),
            low(rows, ff),
            low(rows, 3 * width),
            low(rows, 3 * width),
            wide(rows // PAIR, heads // 2, 2 * PAIR, PAIR),
            wide(rows, width),
            wide(rows, width),
            low(rows, width),
            wide(rows, 2),
            wide(rows, 2 * LANES),
            wide(shards, attn_rows, width),
            wide(shards, ff_rows, width),
            low(shards, attn_rows, width),
            low(shards, ff_rows, width),
            low(shards, attn_rows, width),
            low(shards, ff_rows, width),
            wide(width, width),
            wide(width, width),
            wide(STATS, width),
            wide(3, STATS, width),
            wide(3, STATS, width),
            wide(DEPTH, STATS, width),
            dma(6),
            dma(6),
            dma(1),
            dma(1),
            dma(shards * SIDES),
            dma(7),
            dma(7),
            dma(7),
            *part_scratch(4 * attn_rows),
            *part_scratch(3 * ff_rows),
        ],
        compiler_params=pltpu.CompilerParams(
            vmem_limit_bytes=60 << 20, collective_id=0, has_side_effects=True
        ),
        name="whole",
    )(
        lengths,
        attn_bias,
        tokens,
        cotangent,
        variates,
        times.reshape(rows // PAIR, PAIR),
        jnp.asarray(rotary_table()),
        gains,
        *weights,
        *momenta,
    )


def update_kernel(
    pieces,
    factors,
    grow_ref,
    xrow_ref,
    stat_ref,
    w_qkv,
    w_out,
    w_gate_up,
    w_down,
    m_qkv,
    m_out,
    m_gate_up,
    m_down,
    gains,
    bias,
    gain_moment,
    gain_square,
    bias_moment,
    bias_square,
    out_in,
    gtok_in,
    g_qkv,
    g_out,
    g_gate_up,
    g_down,
    nm_qkv,
    nm_out,
    nm_gate_up,
    nm_down,
    nw_qkv,
    nw_out,
    nw_gate_up,
    nw_down,
    g_gains,
    n_gain_moment,
    n_gain_square,
    n_gains,
    g_bias,
    n_bias_moment,
    n_bias_square,
    n_bias,
    out_tokens,
    grad_tokens,
    sems,
):
    copies = (
        pltpu.make_async_copy(out_in, out_tokens, sems.at[0]),
        pltpu.make_async_copy(gtok_in, grad_tokens, sems.at[1]),
    )
    for one_copy in copies:
        one_copy.start()
    shrink = 1.0 - MUON_RATE * MUON_DECAY

    def one(index, turned, g, m, w, nm, nw):
        start, count = pieces[index]
        grad = grow_ref[start : start + count, :].astype(WIDE)
        ortho = xrow_ref[start : start + count, :].astype(WIDE)
        if turned:
            grad, ortho = grad.T, ortho.T
        g[...] = grad
        nm[...] = MUON_MU * m[...] + grad
        nw[...] = w[...] * shrink - factors[index] * ortho

    for j in range(3):
        one(j, False, *[r.at[j] for r in (g_qkv, m_qkv, w_qkv, nm_qkv, nw_qkv)])
    one(3, False, g_out, m_out, w_out, nm_out, nw_out)
    for j in range(2):
        refs = (g_gate_up, m_gate_up, w_gate_up, nm_gate_up, nw_gate_up)
        one(4 + j, True, *[r.at[j] for r in refs])
    one(6, False, g_down, m_down, w_down, nm_down, nw_down)

    grad = stat_ref[0:2, :]
    g_gains[...] = grad
    n_gain_moment[...], n_gain_square[...], n_gains[...] = adam_step(
        gains[...], grad, gain_moment[...], gain_square[...]
    )
    heads = bias.shape[1]
    sums = jnp.sum(stat_ref[8:24, :PAIR].T, axis=0, keepdims=True)
    grad = jnp.concatenate([sums[:, :heads], sums[:, 8 : 8 + heads]], axis=0)
    g_bias[...] = grad
    n_bias_moment[...], n_bias_square[...], n_bias[...] = adam_step(
        bias[...], grad, bias_moment[...], bias_square[...]
    )
    for one_copy in copies:
        one_copy.wait()


def update(factors, grad_rows, ortho_rows, stats, weights, momenta, small, rows):
    pieces = offsets(weights[1].shape[0], weights[3].shape[0])
    gains, bias = small[:2]
    like = lambda a: jax.ShapeDtypeStruct(a.shape, WIDE)
    outs = [like(a) for a in (*weights, *weights, *weights, *[gains] * 4, *[bias] * 4)]
    return pl.pallas_call(
        functools.partial(update_kernel, pieces, factors),
        out_shape=(*outs, *[jax.ShapeDtypeStruct(r.shape, r.dtype) for r in rows]),
        in_specs=[WHOLE] * 19,
        out_specs=(*[WHOLE] * len(outs), *[ANYWHERE] * 2),
        scratch_shapes=[pltpu.SemaphoreType.DMA((2,))],
        compiler_params=pltpu.CompilerParams(vmem_limit_bytes=58 << 20),
        name="update",
    )(grad_rows, ortho_rows, stats, *weights, *momenta, *small, *rows)


def body(
    tokens,
    cotangent,
    lengths,
    variates,
    times,
    weight_qkv,
    weight_out,
    weight_gate_up,
    weight_down,
    momentum_qkv,
    momentum_out,
    momentum_gate_up,
    momentum_down,
    gains,
    attn_bias,
    gain_moment,
    gain_square,
    bias_moment,
    bias_square,
):
    width = tokens.shape[1]
    heads = attn_bias.shape[1]
    attn_rows = weight_out.shape[0]
    ff_rows = weight_down.shape[0]
    fsdp = lax.axis_size("fsdp")
    ff = ff_rows * fsdp
    attn_width = attn_rows * fsdp
    shrink = 1.0 - MUON_RATE * MUON_DECAY
    scale_attn = MUON_RATE * 0.2 * math.sqrt(max(width, attn_width))
    scale_ff = MUON_RATE * 0.2 * math.sqrt(max(width, ff))
    sizes = (fsdp, lax.axis_size("ns"))
    if sizes == (DEPTH * ACROSS, SIDES * CORES) and attn_rows == 48 and ff_rows == 128:
        turn = lambda a: jnp.swapaxes(a, 1, 2)
        shards = (turn(weight_qkv), weight_out, weight_gate_up, weight_down)
        momenta = (turn(momentum_qkv), momentum_out, momentum_gate_up, momentum_down)
        out_tokens, grad_tokens, grad_rows, ortho_rows, stats = whole_step(
            tokens, cotangent, lengths, variates, times, gains, attn_bias, shards, momenta
        )
        outs = list(
            update(
                (scale_attn,) * 4 + (scale_ff,) * 3,
                grad_rows,
                ortho_rows,
                stats,
                shards,
                momenta,
                (gains, attn_bias, gain_moment, gain_square, bias_moment, bias_square),
                (out_tokens, grad_tokens),
            )
        )
        out_tokens, grad_tokens = outs[-2:]
        outs = outs[:-2]
        for i in (0, 4, 8):
            outs[i] = turn(outs[i])
        return (out_tokens, grad_tokens, *outs)
    weights = pack(weight_qkv, weight_out, weight_gate_up, weight_down)
    momenta = pack(momentum_qkv, momentum_out, momentum_gate_up, momentum_down)
    full = lax.all_gather(weights.astype(LOW), "fsdp", axis=0, tiled=False)
    aligned = attn_rows % 16 == 0 and ff_rows % 16 == 0
    pieces = offsets(attn_rows, ff_rows)
    if not aligned:
        full = jnp.concatenate(
            [full[:, s : s + n].reshape(1, fsdp * n, width) for s, n in pieces], axis=1
        )
    out_tokens, grad_tokens, grads, stats = layer(
        tokens, cotangent, lengths, variates, times, full, gains, attn_bias, ff, WIDE
    )
    if not aligned:
        wholes = offsets(attn_width, ff)
        grads = jnp.concatenate(
            [grads[0, s : s + n].reshape(fsdp, n // fsdp, width) for s, n in wholes], axis=1
        )
    summed = lax.psum_scatter(grads, "fsdp", scatter_dimension=0, tiled=False)
    grad_rows = lax.psum(summed.astype(LOW), "ns").astype(WIDE)
    bias_part = jnp.sum(stats[8:, :PAIR], axis=1).reshape(2, 8)[:, :heads]
    grad_gains, grad_bias = lax.psum((stats[:2], bias_part), ("fsdp", "ns"))

    new_momenta = MUON_MU * momenta + grad_rows
    advance = grad_rows + MUON_MU * new_momenta
    parts = [advance[s : s + n] for s, n in pieces]
    grams = jnp.stack(
        [
            lax.dot_general(
                y,
                y,
                (((0,), (0,)), ((), ())),
                precision=lax.Precision.HIGHEST,
                preferred_element_type=WIDE,
            )
            for y in parts
        ]
    )
    factor = newton_schulz(lax.psum(grams, "fsdp"))
    turned = jnp.concatenate(
        [
            (scale_attn if i < 4 else scale_ff)
            * jnp.dot(
                y, factor[i], precision=lax.Precision.HIGHEST, preferred_element_type=WIDE
            )
            for i, y in enumerate(parts)
        ],
        axis=0,
    )
    new_weights = weights * shrink - turned
    new_gain_moment, new_gain_square, new_gains = adam_step(
        gains, grad_gains, gain_moment, gain_square
    )
    new_bias_moment, new_bias_square, new_bias = adam_step(
        attn_bias, grad_bias, bias_moment, bias_square
    )
    return (
        out_tokens,
        grad_tokens,
        *unpack(grad_rows, attn_rows, ff_rows),
        *unpack(new_momenta, attn_rows, ff_rows),
        *unpack(new_weights, attn_rows, ff_rows),
        grad_gains,
        new_gain_moment,
        new_gain_square,
        new_gains,
        grad_bias,
        new_bias_moment,
        new_bias_square,
        new_bias,
    )


def solution(mesh):
    rows = P(("fsdp", "ns"), None)
    line = P(("fsdp", "ns"))
    matrices = (P(None, None, "fsdp"), P("fsdp", None), P(None, None, "fsdp"), P("fsdp", None))
    return jax.shard_map(
        body,
        mesh=mesh,
        in_specs=(rows, rows, line, rows, line, *matrices, *matrices, *([P()] * 6)),
        out_specs=(rows, rows, *matrices, *matrices, *matrices, *([P()] * 8)),
        check_vma=False,
    )
```

```python
import functools
import math

import jax
import jax.numpy as jnp
import numpy as np
from jax import lax
from jax.experimental import pallas as pl
from jax.experimental.pallas import tpu as pltpu
from jax.sharding import PartitionSpec as P

HEAD_DIM = 64
BUCKET = 64
TIME_SLOTS = 64
NS_ITERS = 5
STEP = 10

EPS_NORM = 1e-06
ROPE_BASE = 10000.0
NEG_FILL = -1000000000.0
COEF_A = 3.4445
COEF_B = -4.775
COEF_C = 2.0315
NS_EPS = 1e-07
MUON_MU = 0.95
MUON_RATE = 0.25
MUON_DECAY = 0.01
ADAM_RATE = 0.8
BETA_ONE = 0.9
BETA_TWO = 0.95
ADAM_EPS = 1e-08

LOW = jnp.bfloat16
WIDE = jnp.float32
BLOCK = 256
PAIR = 2 * BUCKET
LANES = 2 * HEAD_DIM
STATS = 24
WHOLE = pl.BlockSpec(memory_space=pltpu.VMEM)
SCALARS = pl.BlockSpec(memory_space=pltpu.SMEM)
ANYWHERE = pl.BlockSpec(memory_space=pl.ANY)


def mul_nn(left, right):
    return lax.dot_general(left, right, (((1,), (0,)), ((), ())), preferred_element_type=WIDE)


def mul_nt(left, right):
    return lax.dot_general(left, right, (((1,), (1,)), ((), ())), preferred_element_type=WIDE)


def mul_tn(left, right):
    return lax.dot_general(left, right, (((0,), (0,)), ((), ())), preferred_element_type=WIDE)


def offsets(attn_rows, ff_rows):
    counts = [attn_rows] * 4 + [ff_rows] * 3
    starts = [sum(counts[:i]) for i in range(7)]
    return list(zip(starts, counts))


def layer_kernel(
    pieces,
    lengths,
    bias,
    tok_ref,
    cot_ref,
    var_ref,
    time_ref,
    table_ref,
    gain_ref,
    w_ref,
    out_ref,
    gtok_ref,
    grad_ref,
    stat_ref,
    n1_s,
    n2_s,
    att_s,
    gml_s,
    hid_s,
    glow_s,
    gg_s,
    gu_s,
    gqkv_s,
):
    step = pl.program_id(0)
    rows, width = tok_ref.shape
    heads = bias.shape[1]
    here = pl.ds(pl.multiple_of(step * rows, rows), rows)

    def weight(first, last):
        parts = []
        for i in range(first, last):
            start, count = pieces[i]
            part = w_ref[:, start : start + count, :]
            parts.append(part.reshape(part.shape[0] * count, width))
        return parts[0] if len(parts) == 1 else jnp.concatenate(parts, axis=0)

    @pl.when(step == 0)
    def _():
        stat_ref[...] = jnp.zeros_like(stat_ref)

    lane = lax.broadcasted_iota(jnp.int32, (1, LANES), 1)
    low_head = lane < HEAD_DIM
    low_half = lane % HEAD_DIM < HEAD_DIM // 2
    per_block = rows // PAIR
    var_rows = var_ref[pl.ds(step * per_block, per_block), :]
    time_rows = time_ref[pl.ds(step * per_block, per_block), :]
    filler = jnp.zeros((8 - 2 * per_block, PAIR), WIDE)
    columns = jnp.concatenate([var_rows, time_rows, filler], axis=0).T
    slots = lax.broadcasted_iota(jnp.int32, (1, TIME_SLOTS), 1).astype(WIDE)
    hot = jnp.concatenate(
        [(columns[:, per_block + p : per_block + p + 1] == slots) for p in range(per_block)], axis=0
    ).astype(LOW)
    looked = mul_nn(hot, table_ref[0]) + mul_nn(hot, table_ref[1]) + mul_nn(hot, table_ref[2])
    cosine = looked[:, :LANES]
    sine = looked[:, LANES:]

    def swapped(values):
        half = HEAD_DIM // 2
        return jnp.where(
            low_half, pltpu.roll(values, LANES - half, 1), pltpu.roll(values, half, 1)
        )

    gain_one = gain_ref[0:1, :]
    gain_two = gain_ref[1:2, :]
    tokens = tok_ref[...].astype(WIDE)
    scale_one = lax.rsqrt(jnp.mean(tokens * tokens, axis=-1, keepdims=True) + EPS_NORM)
    unit_one = tokens * scale_one
    normed_one = (unit_one * gain_one).astype(LOW)
    n1_s[here, :] = normed_one
    qkv = mul_nt(normed_one, weight(0, 3))

    query_scale = HEAD_DIM ** (-0.5)
    units = []
    attended = []
    row_id = lax.broadcasted_iota(jnp.int32, (PAIR, 1), 0)
    lane_id = lax.broadcasted_iota(jnp.int32, (1, PAIR), 1)
    same_bucket = (row_id < BUCKET) == (lane_id < BUCKET)
    masks = []
    live_cols = []
    for p in range(per_block):
        first = lengths[(step * per_block + p) * 2]
        second = lengths[(step * per_block + p) * 2 + 1]
        live_key = lane_id % BUCKET < jnp.where(lane_id < BUCKET, first, second)
        live_cols.append(row_id % BUCKET < jnp.where(row_id < BUCKET, first, second))
        mask = same_bucket & live_key
        same_var = columns[:, p : p + 1] == var_rows[p : p + 1, :]
        masks.append((mask, same_var))

    for hp in range(heads // 2):
        cols = slice(hp * LANES, (hp + 1) * LANES)
        q = qkv[:, cols]
        k = qkv[:, width + hp * LANES : width + (hp + 1) * LANES]
        v = qkv[:, 2 * width + hp * LANES : 2 * width + (hp + 1) * LANES].astype(LOW)
        q = ((q * cosine + swapped(q) * sine) * query_scale).astype(LOW)
        k = (k * cosine + swapped(k) * sine).astype(LOW)
        q_first = jnp.where(low_head, q, jnp.zeros_like(q))
        q_second = jnp.where(low_head, jnp.zeros_like(q), q)
        att_pairs = []
        for p in range(per_block):
            part = slice(p * PAIR, (p + 1) * PAIR)
            mask, same_var = masks[p]
            q2 = jnp.concatenate([q_first[part], q_second[part]], axis=0)
            kp = k[part]
            vp = v[part]
            raw = mul_nt(q2, kp)
            halves = []
            for j in range(2):
                h = 2 * hp + j
                biased = raw[j * PAIR : (j + 1) * PAIR] + jnp.where(
                    same_var, bias[0, h], bias[1, h]
                )
                halves.append(jnp.where(mask, biased, NEG_FILL))
            scores = jnp.concatenate(halves, axis=0)
            top = jnp.max(scores, axis=-1, keepdims=True)
            exponent = jnp.exp(scores - top)
            probs = exponent / jnp.sum(exponent, axis=-1, keepdims=True)
            probs_low = probs.astype(LOW)
            both = mul_nn(probs_low, vp)
            att_pairs.append(jnp.where(low_head, both[:PAIR], both[PAIR:]))
            units.append((hp, p, q2, kp, vp, probs, probs_low))
        attended.append(jnp.concatenate(att_pairs, axis=0).astype(LOW))
    attended = jnp.concatenate(attended, axis=1)
    att_s[here, :] = attended
    w_out = weight(3, 4)
    mid = tokens + mul_nn(attended, w_out)
    scale_two = lax.rsqrt(jnp.mean(mid * mid, axis=-1, keepdims=True) + EPS_NORM)
    unit_two = mid * scale_two
    normed_two = (unit_two * gain_two).astype(LOW)
    n2_s[here, :] = normed_two
    w_gate = weight(4, 5)
    w_up = weight(5, 6)
    w_down = weight(6, 7)
    gate = mul_nt(normed_two, w_gate)
    up = mul_nt(normed_two, w_up)
    sig = 1.0 / (1.0 + jnp.exp(-gate))
    silu = gate * sig
    hidden = (silu * up).astype(LOW)
    hid_s[here, :] = hidden
    out_ref[...] = (mid + mul_nn(hidden, w_down)).astype(LOW)

    live_row = jnp.concatenate(live_cols, axis=0)
    g_out = jnp.where(live_row, cot_ref[...].astype(WIDE), 0.0)
    g_low = g_out.astype(LOW)
    glow_s[here, :] = g_low
    g_hidden = mul_nt(g_low, w_down)
    g_gate = (g_hidden * up * sig * (1.0 + gate * (1.0 - sig))).astype(LOW)
    g_up = (g_hidden * silu).astype(LOW)
    gg_s[here, :] = g_gate
    gu_s[here, :] = g_up
    e_two = mul_nn(g_gate, w_gate) + mul_nn(g_up, w_up)
    stat_ref[1:2, :] += jnp.sum(e_two * unit_two, axis=0, keepdims=True)
    scaled = e_two * gain_two
    g_mid = g_out + scale_two * (
        scaled - unit_two * jnp.mean(scaled * unit_two, axis=-1, keepdims=True)
    )
    g_mid_low = g_mid.astype(LOW)
    gml_s[here, :] = g_mid_low
    g_att = mul_nt(g_mid_low, w_out).astype(LOW)

    parts_q = [[None] * per_block for _ in range(heads // 2)]
    parts_k = [[None] * per_block for _ in range(heads // 2)]
    parts_v = [[None] * per_block for _ in range(heads // 2)]
    for hp, p, q2, kp, vp, probs, probs_low in units:
        part = slice(p * PAIR, (p + 1) * PAIR)
        mask, same_var = masks[p]
        ga = g_att[part, hp * LANES : (hp + 1) * LANES]
        ga2 = jnp.concatenate(
            [
                jnp.where(low_head, ga, jnp.zeros_like(ga)),
                jnp.where(low_head, jnp.zeros_like(ga), ga),
            ],
            axis=0,
        )
        g_probs = mul_nt(ga2, vp)
        row_dot = jnp.sum(probs * g_probs, axis=-1, keepdims=True)
        g_scores = probs * (g_probs - row_dot)
        for j in range(2):
            h = 2 * hp + j
            mine = g_scores[j * PAIR : (j + 1) * PAIR]
            stat_ref[8 + h : 9 + h, :PAIR] += jnp.sum(
                jnp.where(same_var, mine, 0.0), axis=0, keepdims=True
            )
            stat_ref[16 + h : 17 + h, :PAIR] += jnp.sum(
                jnp.where(same_var, 0.0, mine), axis=0, keepdims=True
            )
        low_scores = g_scores.astype(LOW)
        both = mul_nn(low_scores, kp)
        parts_q[hp][p] = jnp.where(low_head, both[:PAIR], both[PAIR:])
        parts_k[hp][p] = mul_tn(low_scores, q2)
        parts_v[hp][p] = mul_tn(probs_low, ga2)
    g_q = []
    g_k = []
    g_v = []
    for hp in range(heads // 2):
        dq = jnp.concatenate(parts_q[hp], axis=0)
        dk = jnp.concatenate(parts_k[hp], axis=0)
        g_q.append(((dq * cosine - swapped(dq) * sine) * query_scale).astype(LOW))
        g_k.append((dk * cosine - swapped(dk) * sine).astype(LOW))
        g_v.append(jnp.concatenate(parts_v[hp], axis=0).astype(LOW))
    g_qkv = jnp.concatenate(g_q + g_k + g_v, axis=1)
    gqkv_s[here, :] = g_qkv
    e_one = mul_nn(g_qkv, weight(0, 3))
    stat_ref[0:1, :] += jnp.sum(e_one * unit_one, axis=0, keepdims=True)
    scaled = e_one * gain_one
    gtok_ref[...] = (
        g_mid
        + scale_one * (scaled - unit_one * jnp.mean(scaled * unit_one, axis=-1, keepdims=True))
    ).astype(LOW)

    @pl.when(step == pl.num_programs(0) - 1)
    def _():
        def put(index, left, right):
            start, count = pieces[index]
            grad_ref[:, start : start + count, :] = (
                mul_tn(left, right)
                .reshape(grad_ref.shape[0], count, width)
                .astype(grad_ref.dtype)
            )

        for j in range(3):
            put(j, gqkv_s[:, j * width : (j + 1) * width], n1_s[...])
        put(3, att_s[...], gml_s[...])
        put(4, gg_s[...], n2_s[...])
        put(5, gu_s[...], n2_s[...])
        put(6, hid_s[...], glow_s[...])


def layer(tokens, cotangent, lengths, variates, times, packed, gains, attn_bias, ff, grad_type):
    rows, width = tokens.shape
    heads = attn_bias.shape[1]
    copies, shard_rows, _ = packed.shape
    pieces = offsets(heads * HEAD_DIM // copies, ff // copies)
    half = HEAD_DIM // 2
    frequency = ROPE_BASE ** (-2.0 * jnp.arange(half, dtype=WIDE) / HEAD_DIM)
    angles = jnp.arange(TIME_SLOTS, dtype=WIDE)[:, None] * frequency[None, :]
    cosine, sine = jnp.cos(angles), jnp.sin(angles)
    table = jnp.concatenate([cosine] * 4 + [-sine, sine, -sine, sine], axis=1)
    first = table.astype(LOW)
    rest = table - first.astype(WIDE)
    second = rest.astype(LOW)
    third = (rest - second.astype(WIDE)).astype(LOW)
    table = jnp.stack([first, second, third])
    grid = rows // BLOCK
    block = pl.BlockSpec((BLOCK, width), lambda i: (i, 0))
    low_scratch = lambda columns: pltpu.VMEM((rows, columns), LOW)
    return pl.pallas_call(
        functools.partial(layer_kernel, pieces),
        grid=(grid,),
        out_shape=(
            jax.ShapeDtypeStruct((rows, width), LOW),
            jax.ShapeDtypeStruct((rows, width), LOW),
            jax.ShapeDtypeStruct((copies, shard_rows, width), grad_type),
            jax.ShapeDtypeStruct((STATS, width), WIDE),
        ),
        in_specs=[SCALARS, SCALARS, block, block, WHOLE, WHOLE, WHOLE, WHOLE, WHOLE],
        out_specs=(block, block, WHOLE, WHOLE),
        scratch_shapes=[
            low_scratch(width),
            low_scratch(width),
            low_scratch(width),
            low_scratch(width),
            low_scratch(ff),
            low_scratch(width),
            low_scratch(ff),
            low_scratch(ff),
            low_scratch(3 * width),
        ],
        compiler_params=pltpu.CompilerParams(vmem_limit_bytes=58 << 20),
        name="layer",
    )(
        lengths,
        attn_bias,
        tokens,
        cotangent,
        variates.astype(WIDE).reshape(rows // PAIR, PAIR),
        times.astype(WIDE).reshape(rows // PAIR, PAIR),
        table,
        gains,
        packed,
    )


def pack(qkv, out, gate_up, down):
    width = out.shape[-1]
    return jnp.concatenate(
        [
            jnp.swapaxes(qkv, 1, 2).reshape(-1, width),
            out,
            jnp.swapaxes(gate_up, 1, 2).reshape(-1, width),
            down,
        ],
        axis=0,
    )


def unpack(packed, attn_rows, ff_rows):
    width = packed.shape[-1]
    qkv = jnp.swapaxes(packed[: 3 * attn_rows].reshape(3, attn_rows, width), 1, 2)
    out = packed[3 * attn_rows : 4 * attn_rows]
    ends = 4 * attn_rows + 2 * ff_rows
    gate_up = jnp.swapaxes(packed[4 * attn_rows : ends].reshape(2, ff_rows, width), 1, 2)
    return qkv, out, gate_up, packed[ends:]


def newton_schulz(gram_mat):
    def product(left, right):
        return jnp.einsum(
            "mde,mef->mdf",
            left,
            right,
            precision=lax.Precision.HIGHEST,
            preferred_element_type=WIDE,
        )

    norm_val = jnp.sqrt(jnp.trace(gram_mat, axis1=1, axis2=2))[:, None, None] + NS_EPS
    gram_mat = gram_mat / (norm_val * norm_val)
    unit = jnp.eye(gram_mat.shape[-1], dtype=WIDE)[None]
    chain = None
    for turn_idx in range(NS_ITERS):
        poly_mat = COEF_A * unit + COEF_B * gram_mat + COEF_C * product(gram_mat, gram_mat)
        chain = poly_mat if chain is None else product(poly_mat, chain)
        if turn_idx < NS_ITERS - 1:
            gram_mat = product(product(poly_mat, gram_mat), poly_mat)
    return chain / norm_val


def adam_step(param, grad, moment, square):
    new_moment = BETA_ONE * moment + (1.0 - BETA_ONE) * grad
    new_square = BETA_TWO * square + (1.0 - BETA_TWO) * grad * grad
    corrected = new_moment / (1.0 - BETA_ONE**STEP)
    scaled = jnp.sqrt(new_square / (1.0 - BETA_TWO**STEP)) + ADAM_EPS
    return (new_moment, new_square, param - ADAM_RATE * corrected / scaled)


DEPTH, ACROSS = 4, 2
SIDES, CORES = 2, 2
OWNERS = (
    (2, 0, 0, 0),
    (2, 1, 0, 1),
    (1, 1, 0, 0),
    (2, 1, 1, 0),
    (2, 0, 1, 1),
    (1, 0, 0, 1),
    (1, 1, 1, 0),
)


def place():
    f = lax.axis_index("fsdp")
    n = lax.axis_index("ns")
    return f // ACROSS, f % ACROSS, n // CORES, n % CORES


def device(z, x, y, c):
    return (z * ACROSS + x, y * CORES + c)


def remote(src, dst, send_sem, recv_sem, where):
    return pltpu.make_async_remote_copy(
        src_ref=src,
        dst_ref=dst,
        send_sem=send_sem,
        recv_sem=recv_sem,
        device_id=where,
        device_id_type=pl.DeviceIdType.MESH,
    )


def greet(where):
    pl.semaphore_signal(
        pltpu.get_barrier_semaphore(),
        inc=1,
        device_id=where,
        device_id_type=pl.DeviceIdType.MESH,
    )


def halves(value):
    high = value.astype(LOW)
    return high, (value - high.astype(WIDE)).astype(LOW)


def square_wide(value):
    high, low = halves(value)
    cross = mul_nn(high, low)
    return mul_nn(high, high) + (cross + cross.T)


def mul_wide(left, right):
    columns = right.shape[1]
    left_high, left_low = halves(left)
    right_high, right_low = halves(right)
    first = mul_nn(left_high, jnp.concatenate([right_high, right_low], axis=1))
    return first[:, :columns] + (first[:, columns:] + mul_nn(left_low, right_high))


def gram_wide(value):
    high, low = halves(value)
    cross = mul_tn(high, low)
    return mul_tn(high, high) + (cross + cross.T)


def whole_kernel(
    pieces,
    lengths,
    bias,
    tok_hbm,
    cot_hbm,
    var_ref,
    time_ref,
    table_ref,
    gain_ref,
    wqkv_ref,
    wout_ref,
    wgate_up_ref,
    wdown_ref,
    mqkv_hbm,
    mout_hbm,
    mgate_up_hbm,
    mdown_hbm,
    out_hbm,
    gtok_hbm,
    grows_ref,
    xrows_ref,
    total_ref,
    tok_ref,
    cot_ref,
    mqkv_ref,
    mout_ref,
    mgate_up_ref,
    mdown_ref,
    load_sem,
    out_ref,
    gtok_ref,
    out_sem,
    w_s,
    grad_s,
    momenta,
    n1_s,
    n2_s,
    att_s,
    gml_s,
    glow_s,
    hid_s,
    gg_s,
    gu_s,
    low_s,
    gqkv_s,
    probs_s,
    mid_s,
    gmid_s,
    gatt_s,
    scale_s,
    rope_s,
    y_attn,
    y_ff,
    g_attn,
    g_ff,
    x_attn,
    x_ff,
    gram_s,
    chain_s,
    stat_s,
    stat_in,
    stat_acc,
    stat_line,
    stat_send,
    stat_recv,
    adv_recv,
    mom_recv,
    x_send,
    x_recv,
    fan_send,
    fan_recv,
    *per_part,
):
    z, x, y, c = place()
    shard = z * ACROSS + x
    rows, width = tok_ref.shape
    heads = bias.shape[1]
    sibling = device(z, x, y, 1 - c)
    facing = device(z, x, 1 - y, c)
    corner = device(z, x, 1 - y, 1 - c)
    beside = device(z, 1 - x, y, c)
    upper = device(z + 1, x, y, c)
    lower = device(z - 1, x, y, c)
    world = DEPTH * ACROSS * SIDES * CORES
    rank = shard * (SIDES * CORES) + y * CORES + c
    line = [lax.rem(z + k, DEPTH) for k in range(DEPTH)]

    def far_first(t):
        low_z = jnp.minimum(z, DEPTH - 1 - z)
        turn = DEPTH - 1 - t
        turn = low_z if turn == 0 else jnp.where(turn - 1 < low_z, turn - 1, turn)
        return jnp.where(z == low_z, turn, DEPTH - 1 - turn)
    part = 2 * c + y

    def hello(i, carry):
        other = lax.rem(rank + 1 + i, world)
        greet((other // (SIDES * CORES), lax.rem(other, SIDES * CORES)))
        return carry

    lax.fori_loop(0, world - 1, hello, 0)
    loads = [
        pltpu.make_async_copy(src, dst, load_sem.at[i])
        for i, (src, dst) in enumerate(
            (
                (tok_hbm, tok_ref),
                (cot_hbm, cot_ref),
                (mqkv_hbm, mqkv_ref),
                (mout_hbm, mout_ref),
                (mgate_up_hbm, mgate_up_ref),
                (mdown_hbm, mdown_ref),
            )
        )
    ]
    for one in loads:
        one.start()

    def put(index, value):
        start, count = pieces[index]
        w_s[shard, start : start + count, :] = value.astype(LOW)

    for j in range(3):
        put(j, wqkv_ref[j])
    put(3, wout_ref[...])
    put(4, wgate_up_ref[0].T)
    put(5, wgate_up_ref[1].T)
    put(6, wdown_ref[...])
    pl.semaphore_wait(pltpu.get_barrier_semaphore(), world - 1)

    has_up = z < DEPTH - 1
    has_down = z > 0

    def exists(rel):
        return (z + rel >= 0) & (z + rel < DEPTH)

    class Gather:
        def __init__(self, start, count, sems):
            self.start_row, self.half = start, count // 2
            (
                self.up_send,
                self.down_send,
                self.x_send,
                self.sib_send,
                self.below_recv,
                self.above_recv,
                self.x_recv,
                self.sib_recv,
            ) = sems

        def view(self, at, core):
            first = pl.multiple_of(self.start_row + core * self.half, 16)
            return w_s.at[at, pl.ds(first, self.half)]

        def mine(self, rel):
            return self.view(shard + rel * ACROSS, c)

        def others(self, rel):
            return self.view((z + rel) * ACROSS + 1 - x, c)

        def up(self, d):
            return remote(
                self.mine(-d), self.mine(-d), self.up_send.at[d], self.below_recv.at[d], upper
            )

        def down(self, d):
            return remote(
                self.mine(d), self.mine(d), self.down_send.at[d], self.above_recv.at[d], lower
            )

        def over(self, rel, where):
            return remote(
                self.mine(rel), where, self.x_send.at[rel + 3], self.x_recv.at[rel + 3], beside
            )

        def sib(self, kind, rel, src):
            return remote(
                src, src, self.sib_send.at[kind, rel + 3], self.sib_recv.at[kind, rel + 3], sibling
            )

        def start(self):
            @pl.when(has_up)
            def _():
                self.up(0).start()

            @pl.when(has_down)
            def _():
                self.down(0).start()

            self.over(0, self.mine(0)).start()

        def hop(self, d):
            @pl.when(exists(-d))
            def _():
                here = self.mine(-d)
                remote(
                    here, here, self.up_send.at[d], self.below_recv.at[d - 1], lower
                ).wait_recv()
                if d < DEPTH - 1:

                    @pl.when(has_up)
                    def _():
                        self.up(d).start()

                self.over(-d, here).start()
                self.sib(0, -d, here).start()

            @pl.when(exists(d))
            def _():
                here = self.mine(d)
                remote(
                    here, here, self.down_send.at[d], self.above_recv.at[d - 1], upper
                ).wait_recv()
                if d < DEPTH - 1:

                    @pl.when(has_down)
                    def _():
                        self.down(d).start()

                self.over(d, here).start()
                self.sib(0, d, here).start()

        def from_beside(self, d):
            for rel in (0,) if d == 0 else (-d, d):

                @pl.when(exists(rel))
                def _():
                    there = self.others(rel)
                    remote(
                        there, there, self.x_send.at[rel + 3], self.x_recv.at[rel + 3], beside
                    ).wait_recv()
                    self.sib(1, rel, there).start()

        def arrive(self):
            for rel in range(1 - DEPTH, DEPTH):

                @pl.when(exists(rel))
                def _():
                    if rel != 0:
                        self.sib(0, rel, self.view(shard + rel * ACROSS, 1 - c)).wait_recv()
                    self.sib(1, rel, self.view((z + rel) * ACROSS + 1 - x, 1 - c)).wait_recv()

        def sent(self):
            for rel in range(1 - DEPTH, DEPTH):

                @pl.when(exists(rel))
                def _():
                    if rel != 0:
                        self.sib(0, rel, self.mine(rel)).wait_send()
                    self.sib(1, rel, self.others(rel)).wait_send()
                    self.over(rel, self.mine(rel)).wait_send()

            for d in range(DEPTH - 1):

                @pl.when(exists(-d) & has_up)
                def _():
                    self.up(d).wait_send()

                @pl.when(exists(d) & has_down)
                def _():
                    self.down(d).wait_send()

    ff_row = pieces[4][0]
    last_row = pieces[6][0] + pieces[6][1]
    spans = ((0, ff_row), (ff_row, last_row - ff_row))
    each = len(per_part) // 2
    gathers = [Gather(*spans[i], per_part[i * each : i * each + 8]) for i in range(2)]
    attn_gather, ff_gather = gathers
    class Reduce:
        def __init__(self, start, count, refs):
            self.order, self.own = far_first, DEPTH - 1
            self.start_row, self.half, self.quarter = start, count // 2, count // 4
            (
                self.in_zero,
                self.acc_zero,
                self.in_one,
                self.acc_one,
                self.in_two,
                self.acc_two,
                self.in_three,
                self.send_zero,
                self.send_one,
                self.send_two,
                self.send_three,
                self.recv_zero,
                self.recv_one,
                self.recv_two,
                self.recv_three,
                self.mom_send,
                self.adv_send,
                self.row_send,
                self.row_recv,
            ) = refs
            self.keep_quarter = pl.ds(pl.multiple_of(y * self.quarter, 16), self.quarter)
            self.give_quarter = pl.ds(pl.multiple_of((1 - y) * self.quarter, 16), self.quarter)
            self.first_quarter = pl.ds(0, self.quarter)

        def half_of(self, core):
            return pl.ds(pl.multiple_of(self.start_row + core * self.half, 16), self.half)

        def rows_of(self, quarter):
            first = pl.multiple_of(self.start_row + quarter * self.quarter, 16)
            return pl.ds(first, self.quarter)

        def zero(self, t):
            return remote(
                grad_s.at[self.order(t), :, self.half_of(1 - c)],
                self.in_zero.at[t],
                self.send_zero.at[t],
                self.recv_zero.at[t],
                sibling,
            )

        def crosses(self, t, way):
            return (c + t) % 2 == way

        def one(self, k, core):
            if core == 0:
                src, dst = self.acc_zero.at[k, :, self.give_quarter], self.in_one.at[
                    k, :, self.first_quarter
                ]
            else:
                src, dst = self.acc_zero.at[k, 1 - x], self.in_one.at[k, 0]
            where = facing if core == 0 else beside
            return remote(src, dst, self.send_one.at[k], self.recv_one.at[k], where)

        def two(self, k, core):
            if core == 0:
                src = self.acc_one.at[k, 1 - x, self.first_quarter]
            else:
                src = self.acc_one.at[k, 0, self.give_quarter]
            where = beside if core == 0 else facing
            return remote(src, self.in_two.at[k], self.send_two.at[k], self.recv_two.at[k], where)

        def three(self, t):
            return remote(
                self.acc_two.at[t],
                self.in_three.at[z],
                self.send_three.at[t],
                self.recv_three.at[z],
                device(self.order(t), x, y, c),
            )

        def add(self, left, right):
            return (left.astype(WIDE) + right.astype(WIDE)).astype(LOW)

        def start(self):
            for t in range(DEPTH):
                self.zero(t).start()

        def first(self, t):
            self.zero(t).wait_recv()
            kept = grad_s[self.order(t), :, self.half_of(c)]
            self.acc_zero[t] = self.add(kept, self.in_zero[t])
            for core in range(2):

                @pl.when(self.crosses(t, core))
                def _():
                    self.one(t, core).start()

        def second(self, t):
            quarter = self.quarter

            @pl.when(self.crosses(t, 0))
            def _():
                self.one(t, 0).wait_recv()
                self.acc_one[t, :, :quarter] = self.add(
                    self.acc_zero[t, :, self.keep_quarter], self.in_one[t, :, :quarter]
                )
                self.two(t, 0).start()

            @pl.when(self.crosses(t, 1))
            def _():
                self.one(t, 1).wait_recv()
                self.acc_one[t, 0] = self.add(self.acc_zero[t, x], self.in_one[t, 0])
                self.two(t, 1).start()

        def third(self, t):
            quarter = self.quarter

            @pl.when(self.crosses(t, 0))
            def _():
                self.two(t, 0).wait_recv()
                self.acc_two[t] = self.add(self.acc_one[t, x, :quarter], self.in_two[t])

            @pl.when(self.crosses(t, 1))
            def _():
                self.two(t, 1).wait_recv()
                self.acc_two[t] = self.add(self.acc_one[t, 0, self.keep_quarter], self.in_two[t])

            @pl.when(self.order(t) != z)
            def _():
                self.three(t).start()

        def segments(self, index):
            found = []
            begin = self.start_row + index * self.quarter
            for m, (start, count) in enumerate(pieces):
                first, last = max(start, begin), min(start + count, begin + self.quarter)
                if first < last:
                    found.append((m, first - begin, first - start, last - first))
            return found

        def to_owner(self, kind, index, i, stays=False):
            m, first, to, count = self.segments(index)[i]
            begin = self.start_row + index * self.quarter + first
            source = (momenta, grows_ref)[kind].at[pl.ds(begin, count)]
            target = stage(kind, m).at[shard, pl.ds(to, count)]
            sent = (self.mom_send, self.adv_send)[kind].at[i]
            got = (mom_recv, adv_recv)[kind].at[0]
            if stays:
                return pltpu.make_async_copy(source, target, got)
            return remote(source, target, sent, got, device(*OWNERS[m]))

        def all_to_owners(self, kind):
            for index in range(4):
                for i, (m, _, _, _) in enumerate(self.segments(index)):

                    @pl.when((part == index) & jnp.logical_not(owned(m)))
                    def _():
                        self.to_owner(kind, index, i).start()

                    @pl.when((part == index) & owned(m))
                    def _():
                        self.to_owner(kind, index, i, stays=True).start()

        def send_momenta(self):
            self.all_to_owners(0)

        def row_copy(self, j, quarter, where):
            here = grows_ref.at[self.rows_of(quarter)]
            return remote(here, here, self.row_send.at[j], self.row_recv.at[j], where)

        def finish(self):
            total = self.acc_two[self.own].astype(WIDE)
            for j in range(1, DEPTH):
                there = self.in_three.at[line[j]]
                remote(
                    there, there, self.send_three.at[0], self.recv_three.at[line[j]], sibling
                ).wait_recv()
                total = total + self.in_three[line[j]].astype(WIDE)
            grows_ref[self.rows_of(part), :] = total.astype(LOW)
            self.all_to_owners(1)

        def give_rows(self):
            for j, where in enumerate((sibling, facing, corner)):
                self.row_copy(j, part, where).start()

        def done(self):
            mates = ((sibling, 0, 1), (facing, 1, 0), (corner, 1, 1))
            for j, (where, dy, dc) in enumerate(mates):
                self.row_copy(j, 2 * (c ^ dc) + (y ^ dy), where).wait_recv()
                self.row_copy(j, part, where).wait_send()
            for index in range(4):
                for i, (m, _, _, _) in enumerate(self.segments(index)):

                    @pl.when((part == index) & jnp.logical_not(owned(m)))
                    def _():
                        for kind in range(2):
                            self.to_owner(kind, index, i).wait_send()

            for t in range(DEPTH):
                self.zero(t).wait_send()

                @pl.when(self.order(t) != z)
                def _():
                    self.three(t).wait_send()

                for core in range(2):

                    @pl.when(self.crosses(t, core))
                    def _():
                        self.one(t, core).wait_send()
                        self.two(t, core).wait_send()

    def owned(m):
        oz, ox, oy, oc = OWNERS[m]
        return (z == oz) & (x == ox) & (y == oy) & (c == oc)

    def stage(kind, m):
        return ((y_attn, y_ff), (g_attn, g_ff))[kind][int(m >= 4)]

    reduces = [Reduce(*spans[i], per_part[i * each + 8 : (i + 1) * each]) for i in range(2)]
    attn_reduce, ff_reduce = reduces

    attn_gather.start()
    ff_gather.start()

    for one in loads:
        one.wait()
    for i, (value, turned) in enumerate(((mgate_up_ref[0], 4), (mgate_up_ref[1], 5))):
        start, count = pieces[turned]
        momenta[start : start + count, :] = value.T
    for j in range(3):
        start, count = pieces[j]
        momenta[start : start + count, :] = mqkv_ref[j]
    momenta[pieces[3][0] : pieces[3][0] + pieces[3][1], :] = mout_ref[...]
    momenta[pieces[6][0] : last_row, :] = mdown_ref[...]
    stat_s[...] = jnp.zeros_like(stat_s)

    lane = lax.broadcasted_iota(jnp.int32, (1, LANES), 1)
    low_head = lane < HEAD_DIM
    low_half = lane % HEAD_DIM < HEAD_DIM // 2
    row_id = lax.broadcasted_iota(jnp.int32, (PAIR, 1), 0)
    lane_id = lax.broadcasted_iota(jnp.int32, (1, PAIR), 1)
    same_bucket = (row_id < BUCKET) == (lane_id < BUCKET)
    slots = lax.broadcasted_iota(jnp.int32, (1, TIME_SLOTS), 1)
    query_scale = HEAD_DIM ** (-0.5)
    gain_one = gain_ref[0:1, :]
    gain_two = gain_ref[1:2, :]

    def column(row):
        return jnp.broadcast_to(row, (8, PAIR)).T[:, 0:1]

    def var_row(pair):
        two = var_ref[pl.ds(2 * pair, 2), :]
        return jnp.concatenate([two[0:1], two[1:2]], axis=1).astype(WIDE)

    def block_of(i, size):
        return pl.ds(pl.multiple_of(i * size, size), size)

    def prepare(i, carry):
        here = block_of(i, PAIR)
        times = column(time_ref[pl.ds(i, 1), :].astype(WIDE)).astype(jnp.int32)
        hot = (times == slots).astype(LOW)
        rope_s[here, :] = (
            mul_nn(hot, table_ref[0]) + mul_nn(hot, table_ref[1]) + mul_nn(hot, table_ref[2])
        )
        tokens = tok_ref[here, :].astype(WIDE)
        scale = lax.rsqrt(jnp.mean(tokens * tokens, axis=-1, keepdims=True) + EPS_NORM)
        scale_s[here, 0:1] = scale
        n1_s[here, :] = (tokens * scale * gain_one).astype(LOW)
        first, second = lengths[2 * i], lengths[2 * i + 1]
        live = row_id % BUCKET < jnp.where(row_id < BUCKET, first, second)
        glow_s[here, :] = jnp.where(live, cot_ref[here, :].astype(WIDE), 0.0).astype(LOW)
        return carry

    lax.fori_loop(0, rows // PAIR, prepare, 0)

    for d in range(1, DEPTH):
        attn_gather.hop(d)
        if d < DEPTH - 1:
            ff_gather.hop(d)
    for d in range(DEPTH):
        attn_gather.from_beside(d)
    attn_gather.arrive()

    def weight(first, last):
        parts = []
        for i in range(first, last):
            start, count = pieces[i]
            piece = w_s[:, start : start + count, :]
            parts.append(piece.reshape(piece.shape[0] * count, width))
        return parts[0] if len(parts) == 1 else jnp.concatenate(parts, axis=0)

    def swapped(values):
        half = HEAD_DIM // 2
        return jnp.where(
            low_half, pltpu.roll(values, LANES - half, 1), pltpu.roll(values, half, 1)
        )

    def two_heads(value):
        none = jnp.zeros_like(value)
        return jnp.concatenate(
            [jnp.where(low_head, value, none), jnp.where(low_head, none, value)], axis=0
        )

    per_block = BLOCK // PAIR

    def attend(i, carry):
        here = block_of(i, BLOCK)
        qkv = mul_nt(n1_s[here, :], weight(0, 3))
        cosine = rope_s[here, :LANES]
        sine = rope_s[here, LANES:]
        masks = []
        for p in range(per_block):
            pair = i * per_block + p
            first, second = lengths[2 * pair], lengths[2 * pair + 1]
            live_key = lane_id % BUCKET < jnp.where(lane_id < BUCKET, first, second)
            row = var_row(pair)
            masks.append((same_bucket & live_key, column(row) == row))
        attended = []
        for hp in range(heads // 2):
            first = hp * LANES
            q = qkv[:, first : first + LANES]
            k = qkv[:, width + first : width + first + LANES]
            v = qkv[:, 2 * width + first : 2 * width + first + LANES].astype(LOW)
            q = ((q * cosine + swapped(q) * sine) * query_scale).astype(LOW)
            k = (k * cosine + swapped(k) * sine).astype(LOW)
            low_s[here, first : first + LANES] = q
            low_s[here, width + first : width + first + LANES] = k
            low_s[here, 2 * width + first : 2 * width + first + LANES] = v
            pairs = []
            for p in range(per_block):
                span = slice(p * PAIR, (p + 1) * PAIR)
                mask, same_var = masks[p]
                raw = mul_nt(two_heads(q[span]), k[span])
                both = []
                for j in range(2):
                    h = 2 * hp + j
                    biased = raw[j * PAIR : (j + 1) * PAIR] + jnp.where(
                        same_var, bias[0, h], bias[1, h]
                    )
                    both.append(jnp.where(mask, biased, NEG_FILL))
                scores = jnp.concatenate(both, axis=0)
                exponent = jnp.exp(scores - jnp.max(scores, axis=-1, keepdims=True))
                probs = exponent / jnp.sum(exponent, axis=-1, keepdims=True)
                probs_s[i * per_block + p, hp] = probs
                both = mul_nn(probs.astype(LOW), v[span])
                pairs.append(jnp.where(low_head, both[:PAIR], both[PAIR:]))
            attended.append(jnp.concatenate(pairs, axis=0).astype(LOW))
        attended = jnp.concatenate(attended, axis=1)
        att_s[here, :] = attended
        mid = tok_ref[here, :].astype(WIDE) + mul_nn(attended, weight(3, 4))
        mid_s[here, :] = mid
        scale = lax.rsqrt(jnp.mean(mid * mid, axis=-1, keepdims=True) + EPS_NORM)
        scale_s[here, 1:2] = scale
        n2_s[here, :] = (mid * scale * gain_two).astype(LOW)
        @pl.when(i == 0)
        def _():
            ff_gather.hop(DEPTH - 1)
            ff_gather.from_beside(0)
            ff_gather.from_beside(1)

        for d in range(2, DEPTH):

            @pl.when(i == d - 1)
            def _():
                ff_gather.from_beside(d)

        return carry

    lax.fori_loop(0, rows // BLOCK, attend, 0)
    ff_gather.arrive()
    for one in reduces:
        one.send_momenta()

    def feed(i, carry):
        here = block_of(i, 2 * BLOCK)
        normed_two = n2_s[here, :]
        w_gate, w_up, w_down = weight(4, 5), weight(5, 6), weight(6, 7)
        gate = mul_nt(normed_two, w_gate)
        up = mul_nt(normed_two, w_up)
        sig = 1.0 / (1.0 + jnp.exp(-gate))
        silu = gate * sig
        hid_s[here, :] = (silu * up).astype(LOW)
        g_low = glow_s[here, :]
        g_hidden = mul_nt(g_low, w_down)
        g_gate = (g_hidden * up * sig * (1.0 + gate * (1.0 - sig))).astype(LOW)
        g_up = (g_hidden * silu).astype(LOW)
        gg_s[here, :] = g_gate
        gu_s[here, :] = g_up
        e_two = mul_nn(g_gate, w_gate) + mul_nn(g_up, w_up)
        scale = scale_s[here, 1:2]
        unit = mid_s[here, :] * scale
        stat_s[1:2, :] += jnp.sum(e_two * unit, axis=0, keepdims=True)
        scaled = e_two * gain_two
        g_mid = g_low.astype(WIDE) + scale * (
            scaled - unit * jnp.mean(scaled * unit, axis=-1, keepdims=True)
        )
        gmid_s[here, :] = g_mid
        g_mid_low = g_mid.astype(LOW)
        gml_s[here, :] = g_mid_low
        gatt_s[here, :] = mul_nt(g_mid_low, weight(3, 4)).astype(LOW)
        return carry

    lax.fori_loop(0, rows // (2 * BLOCK), feed, 0)

    def grad_put(index, left, right):
        start, count = pieces[index]
        grad_s[:, :, start : start + count, :] = (
            mul_tn(left, right).reshape(DEPTH, ACROSS, count, width).astype(LOW)
        )

    grad_put(4, gg_s[...], n2_s[...])
    grad_put(5, gu_s[...], n2_s[...])
    grad_put(6, hid_s[...], glow_s[...])
    ff_reduce.start()
    grad_put(3, att_s[...], gml_s[...])

    def attend_back(i, carry):
        here = block_of(i, PAIR)
        row = var_row(i)
        same_var = column(row) == row
        cosine = rope_s[here, :LANES]
        sine = rope_s[here, LANES:]
        for hp in range(heads // 2):
            first = hp * LANES
            q2 = two_heads(low_s[here, first : first + LANES])
            k = low_s[here, width + first : width + first + LANES]
            v = low_s[here, 2 * width + first : 2 * width + first + LANES]
            probs = probs_s[i, hp]
            ga2 = two_heads(gatt_s[here, first : first + LANES])
            g_probs = mul_nt(ga2, v)
            row_dot = jnp.sum(probs * g_probs, axis=-1, keepdims=True)
            g_scores = probs * (g_probs - row_dot)
            for j in range(2):
                h = 2 * hp + j
                mine = g_scores[j * PAIR : (j + 1) * PAIR]
                stat_s[8 + h : 9 + h, :PAIR] += jnp.sum(
                    jnp.where(same_var, mine, 0.0), axis=0, keepdims=True
                )
                stat_s[16 + h : 17 + h, :PAIR] += jnp.sum(
                    jnp.where(same_var, 0.0, mine), axis=0, keepdims=True
                )
            low_scores = g_scores.astype(LOW)
            both = mul_nn(low_scores, k)
            dq = jnp.where(low_head, both[:PAIR], both[PAIR:])
            dk = mul_tn(low_scores, q2)
            dv = mul_tn(probs.astype(LOW), ga2)
            gqkv_s[here, first : first + LANES] = (
                (dq * cosine - swapped(dq) * sine) * query_scale
            ).astype(LOW)
            gqkv_s[here, width + first : width + first + LANES] = (
                dk * cosine - swapped(dk) * sine
            ).astype(LOW)
            gqkv_s[here, 2 * width + first : 2 * width + first + LANES] = dv.astype(LOW)
        @pl.when(i == 0)
        def _():
            for t in range(DEPTH):
                ff_reduce.first(t)

        @pl.when(i == 4)
        def _():
            ff_reduce.second(0)
            ff_reduce.second(1)

        @pl.when(i == 6)
        def _():
            ff_reduce.third(0)
            ff_reduce.third(1)
            ff_reduce.second(2)
            ff_reduce.second(3)

        return carry

    lax.fori_loop(0, rows // PAIR, attend_back, 0)
    for j in range(3):
        grad_put(j, gqkv_s[:, j * width : (j + 1) * width], n1_s[...])
    attn_reduce.start()
    ff_reduce.third(2)
    ff_reduce.third(3)

    def last(i):
        here = block_of(i, 2 * BLOCK)
        e_one = mul_nn(gqkv_s[here, :], weight(0, 3))
        scale = scale_s[here, 0:1]
        unit = tok_ref[here, :].astype(WIDE) * scale
        stat_s[0:1, :] += jnp.sum(e_one * unit, axis=0, keepdims=True)
        scaled = e_one * gain_one
        gtok_ref[here, :] = (
            gmid_s[here, :]
            + scale * (scaled - unit * jnp.mean(scaled * unit, axis=-1, keepdims=True))
        ).astype(LOW)

    def outgoing(i):
        here = block_of(i, 2 * BLOCK)
        out_ref[here, :] = (mid_s[here, :] + mul_nn(hid_s[here, :], weight(6, 7))).astype(LOW)

    def stat_copy(step, src, where):
        return remote(src, stat_in.at[step], stat_send.at[step], stat_recv.at[step], where)

    for t in range(DEPTH):
        attn_reduce.first(t)
    last(0)
    last(1)
    leave = [
        pltpu.make_async_copy(gtok_ref, gtok_hbm, out_sem.at[0]),
        pltpu.make_async_copy(out_ref, out_hbm, out_sem.at[1]),
    ]
    leave[0].start()
    stat_copy(0, stat_s, sibling).start()
    ff_reduce.finish()
    attn_reduce.second(0)
    attn_reduce.second(1)
    stat_copy(0, stat_s, sibling).wait()
    stat_acc[0] = stat_s[...] + stat_in[0]
    stat_copy(1, stat_acc.at[0], facing).start()
    attn_reduce.second(2)
    attn_reduce.second(3)
    for t in range(DEPTH):
        attn_reduce.third(t)
    stat_copy(1, stat_acc.at[0], facing).wait()
    stat_acc[1] = stat_acc[0] + stat_in[1]
    stat_copy(2, stat_acc.at[1], beside).start()
    attn_owner = functools.reduce(jnp.logical_or, [owned(m) for m in range(4)])
    ff_owner = functools.reduce(jnp.logical_or, [owned(m) for m in range(4, 7)])

    chips = DEPTH * ACROSS * SIDES

    def x_copy(m, i):
        start, count = pieces[m]
        source = x_attn if m < 4 else x_ff
        to = i // SIDES
        return remote(
            source.at[to],
            xrows_ref.at[pl.ds(start, count)],
            x_send.at[i],
            x_recv.at[m],
            (to, lax.rem(i, SIDES) * CORES + OWNERS[m][3]),
        )

    mine = shard * SIDES + y
    unit_mat = lax.broadcasted_iota(jnp.int32, (width, width), 0) == lax.broadcasted_iota(
        jnp.int32, (width, width), 1
    )
    diagonal = jnp.where(unit_mat, COEF_A, 0.0)

    def advance(y_buf, g_buf):
        pltpu.make_async_copy(y_buf, y_buf, mom_recv.at[0]).wait()
        pltpu.make_async_copy(g_buf, g_buf, adv_recv.at[0]).wait()
        grad = g_buf[...].astype(WIDE)
        return grad + MUON_MU * (MUON_MU * y_buf[...] + grad)

    def poly(value):
        return diagonal + COEF_B * value + COEF_C * square_wide(value)

    @pl.when(ff_owner)
    def _():
        y_ff[...] = advance(y_ff, g_ff)
        gram_mat = gram_wide(y_ff[...].reshape(-1, width))
        trace = jnp.sum(jnp.where(unit_mat, gram_mat, 0.0), keepdims=True)
        inverse = 1.0 / (jnp.sqrt(trace) + NS_EPS)
        gram_mat = gram_mat * (inverse * inverse)
        step_mat = poly(gram_mat)
        gram_s[...] = mul_wide(mul_wide(gram_mat, step_mat), step_mat)
        chain_s[...] = step_mat * inverse

    attn_reduce.finish()
    for one in reduces:
        one.give_rows()
    stat_copy(2, stat_acc.at[1], beside).wait()
    stat_acc[2] = stat_acc[1] + stat_in[2]
    stat_line[z] = stat_acc[2]

    def stat_send_line(j):
        return remote(
            stat_acc.at[2],
            stat_line.at[z],
            stat_send.at[2 + j],
            stat_recv.at[2 + j],
            device(line[j], x, y, c),
        )

    for j in range(1, DEPTH):
        stat_send_line(j).start()

    def send_x(m, first, count):
        def send(i, carry):
            @pl.when(i != mine)
            def _():
                x_copy(m, i).start()

            return carry

        lax.fori_loop(first, first + count, send, 0)

    def keep_x(m):
        start, count = pieces[m]
        source = x_attn if m < 4 else x_ff
        pltpu.make_async_copy(
            source.at[shard], xrows_ref.at[pl.ds(start, count)], x_recv.at[m]
        ).start()

    @pl.when(attn_owner)
    def _():
        value = advance(y_attn, g_attn).reshape(-1, width)
        total = jnp.sum(jnp.sum(value * value, axis=0, keepdims=True), axis=1, keepdims=True)
        chain_s[...] = value * (1.0 / (jnp.sqrt(total) + NS_EPS))

        def turn(i, carry):
            now = chain_s[...]
            chain_s[...] = mul_wide(now, poly(gram_wide(now)))
            return carry

        lax.fori_loop(0, NS_ITERS, turn, 0)
        x_attn[...] = chain_s[...].astype(LOW).reshape(x_attn.shape)
        for m in range(4):

            @pl.when(owned(m))
            def _():
                send_x(m, 0, chips)
                keep_x(m)

    @pl.when(ff_owner)
    def _():
        def turn(i, carry):
            now = gram_s[...]
            step_now = poly(now)
            both = mul_wide(jnp.concatenate([now, chain_s[...]], axis=0), step_now)
            chain_s[...] = both[width:]
            gram_s[...] = mul_wide(both[:width], step_now)
            return carry

        lax.fori_loop(0, NS_ITERS - 2, turn, 0)
        chain_s[...] = mul_wide(chain_s[...], poly(gram_s[...]))

        def give(i, carry):
            at = lax.rem(z + 2 + i, DEPTH)
            these = pl.ds(at * ACROSS, ACROSS)
            value = y_ff[these].reshape(-1, width)
            x_ff[these] = mul_wide(value, chain_s[...]).astype(LOW).reshape(
                ACROSS, x_ff.shape[1], width
            )
            for m in range(4, 7):

                @pl.when(owned(m))
                def _():
                    send_x(m, at * (ACROSS * SIDES), ACROSS * SIDES)

            return carry

        lax.fori_loop(0, DEPTH, give, 0)
        for m in range(4, 7):

            @pl.when(owned(m))
            def _():
                keep_x(m)

    outgoing(0)
    outgoing(1)
    leave[1].start()

    for j in range(1, DEPTH):
        remote(
            stat_acc.at[2],
            stat_line.at[lax.rem(z + DEPTH - j, DEPTH)],
            stat_send.at[2 + j],
            stat_recv.at[2 + j],
            device(line[j], x, y, c),
        ).wait()
    total_ref[...] = (stat_line[0] + stat_line[1]) + (stat_line[2] + stat_line[3])
    for one in gathers:
        one.sent()
    for one in reduces:
        one.done()

    def fan_copy(m):
        start, count = pieces[m]
        rows_m = xrows_ref.at[pl.ds(start, count)]
        return remote(rows_m, rows_m, fan_send.at[m], fan_recv.at[m], sibling)

    for m in range(7):
        start, count = pieces[m]

        @pl.when(c == OWNERS[m][3])
        def _():
            rows_m = xrows_ref.at[pl.ds(start, count)]
            pltpu.make_async_copy(rows_m, rows_m, x_recv.at[m]).wait()
            fan_copy(m).start()

    for m in range(7):

        @pl.when(c != OWNERS[m][3])
        def _():
            fan_copy(m).wait_recv()

        @pl.when(c == OWNERS[m][3])
        def _():
            fan_copy(m).wait_send()

        @pl.when(owned(m))
        def _():
            def sent(i, carry):
                x_copy(m, lax.rem(mine + i, chips)).wait_send()
                return carry

            lax.fori_loop(1, chips, sent, 0)

    for one in leave:
        one.wait()


def rotary_table():
    half = HEAD_DIM // 2
    frequency = (ROPE_BASE ** (-2.0 * np.arange(half) / HEAD_DIM)).astype(np.float32)
    angles = np.arange(TIME_SLOTS, dtype=np.float32)[:, None] * frequency[None, :]
    cosine = np.cos(angles.astype(np.float64)).astype(np.float32)
    sine = np.sin(angles.astype(np.float64)).astype(np.float32)
    table = np.concatenate([cosine] * 4 + [-sine, sine, -sine, sine], axis=1)
    parts = []
    for _ in range(3):
        parts.append(table.astype(LOW))
        table = table - parts[-1].astype(np.float32)
    return np.stack(parts)


def whole_step(tokens, cotangent, lengths, variates, times, gains, attn_bias, weights, momenta):
    rows, width = tokens.shape
    heads = attn_bias.shape[1]
    attn_rows, ff_rows = weights[1].shape[0], weights[3].shape[0]
    pieces = offsets(attn_rows, ff_rows)
    ff = ff_rows * DEPTH * ACROSS
    shards = DEPTH * ACROSS
    shard_rows = 4 * attn_rows + 3 * ff_rows
    low = lambda *shape: pltpu.VMEM(shape, LOW)
    wide = lambda *shape: pltpu.VMEM(shape, WIDE)
    dma = lambda *shape: pltpu.SemaphoreType.DMA(shape)

    def part_scratch(count):
        half, quarter = count // 2, count // 4
        relative = 2 * DEPTH - 1
        return [
            dma(DEPTH),
            dma(DEPTH),
            dma(relative),
            dma(2, relative),
            dma(DEPTH),
            dma(DEPTH),
            dma(relative),
            dma(2, relative),
            low(DEPTH, ACROSS, half, width),
            low(DEPTH, ACROSS, half, width),
            low(DEPTH, ACROSS, half, width),
            low(DEPTH, ACROSS, half, width),
            low(DEPTH, quarter, width),
            low(DEPTH, quarter, width),
            low(DEPTH, quarter, width),
            *[dma(DEPTH) for _ in range(8)],
            dma(3),
            dma(3),
            dma(3),
            dma(3),
        ]

    return pl.pallas_call(
        functools.partial(whole_kernel, pieces),
        out_shape=(
            jax.ShapeDtypeStruct((rows, width), LOW),
            jax.ShapeDtypeStruct((rows, width), LOW),
            jax.ShapeDtypeStruct((shard_rows, width), LOW),
            jax.ShapeDtypeStruct((shard_rows, width), LOW),
            jax.ShapeDtypeStruct((STATS, width), WIDE),
        ),
        in_specs=[SCALARS] * 2 + [ANYWHERE] * 2 + [WHOLE] * 8 + [ANYWHERE] * 4,
        out_specs=(ANYWHERE, ANYWHERE, WHOLE, WHOLE, WHOLE),
        scratch_shapes=[
            low(rows, width),
            low(rows, width),
            *[wide(*m.shape) for m in momenta],
            dma(6),
            low(rows, width),
            low(rows, width),
            dma(2),
            low(shards, shard_rows, width),
            low(DEPTH, ACROSS, shard_rows, width),
            wide(shard_rows, width),
            low(rows, width),
            low(rows, width),
            low(rows, width),
            low(rows, width),
            low(rows, width),
            low(rows, ff),
            low(rows, ff),
            low(rows, ff),
            low(rows, 3 * width),
            low(rows, 3 * width),
            wide(rows // PAIR, heads // 2, 2 * PAIR, PAIR),
            wide(rows, width),
            wide(rows, width),
            low(rows, width),
            wide(rows, 2),
            wide(rows, 2 * LANES),
            wide(shards, attn_rows, width),
            wide(shards, ff_rows, width),
            low(shards, attn_rows, width),
            low(shards, ff_rows, width),
            low(shards, attn_rows, width),
            low(shards, ff_rows, width),
            wide(width, width),
            wide(width, width),
            wide(STATS, width),
            wide(3, STATS, width),
            wide(3, STATS, width),
            wide(DEPTH, STATS, width),
            dma(6),
            dma(6),
            dma(1),
            dma(1),
            dma(shards * SIDES),
            dma(7),
            dma(7),
            dma(7),
            *part_scratch(4 * attn_rows),
            *part_scratch(3 * ff_rows),
        ],
        compiler_params=pltpu.CompilerParams(
            vmem_limit_bytes=60 << 20, collective_id=0, has_side_effects=True
        ),
        name="whole",
    )(
        lengths,
        attn_bias,
        tokens,
        cotangent,
        variates,
        times.reshape(rows // PAIR, PAIR),
        jnp.asarray(rotary_table()),
        gains,
        *weights,
        *momenta,
    )


def update_kernel(
    pieces,
    factors,
    grow_ref,
    xrow_ref,
    stat_ref,
    w_qkv,
    w_out,
    w_gate_up,
    w_down,
    m_qkv,
    m_out,
    m_gate_up,
    m_down,
    gains,
    bias,
    gain_moment,
    gain_square,
    bias_moment,
    bias_square,
    out_in,
    gtok_in,
    g_qkv,
    g_out,
    g_gate_up,
    g_down,
    nm_qkv,
    nm_out,
    nm_gate_up,
    nm_down,
    nw_qkv,
    nw_out,
    nw_gate_up,
    nw_down,
    g_gains,
    n_gain_moment,
    n_gain_square,
    n_gains,
    g_bias,
    n_bias_moment,
    n_bias_square,
    n_bias,
    out_tokens,
    grad_tokens,
    sems,
):
    copies = (
        pltpu.make_async_copy(out_in, out_tokens, sems.at[0]),
        pltpu.make_async_copy(gtok_in, grad_tokens, sems.at[1]),
    )
    for one_copy in copies:
        one_copy.start()
    shrink = 1.0 - MUON_RATE * MUON_DECAY

    def one(index, turned, g, m, w, nm, nw):
        start, count = pieces[index]
        grad = grow_ref[start : start + count, :].astype(WIDE)
        ortho = xrow_ref[start : start + count, :].astype(WIDE)
        if turned:
            grad, ortho = grad.T, ortho.T
        g[...] = grad
        nm[...] = MUON_MU * m[...] + grad
        nw[...] = w[...] * shrink - factors[index] * ortho

    for j in range(3):
        one(j, False, *[r.at[j] for r in (g_qkv, m_qkv, w_qkv, nm_qkv, nw_qkv)])
    one(3, False, g_out, m_out, w_out, nm_out, nw_out)
    for j in range(2):
        refs = (g_gate_up, m_gate_up, w_gate_up, nm_gate_up, nw_gate_up)
        one(4 + j, True, *[r.at[j] for r in refs])
    one(6, False, g_down, m_down, w_down, nm_down, nw_down)

    grad = stat_ref[0:2, :]
    g_gains[...] = grad
    n_gain_moment[...], n_gain_square[...], n_gains[...] = adam_step(
        gains[...], grad, gain_moment[...], gain_square[...]
    )
    heads = bias.shape[1]
    sums = jnp.sum(stat_ref[8:24, :PAIR].T, axis=0, keepdims=True)
    grad = jnp.concatenate([sums[:, :heads], sums[:, 8 : 8 + heads]], axis=0)
    g_bias[...] = grad
    n_bias_moment[...], n_bias_square[...], n_bias[...] = adam_step(
        bias[...], grad, bias_moment[...], bias_square[...]
    )
    for one_copy in copies:
        one_copy.wait()


def update(factors, grad_rows, ortho_rows, stats, weights, momenta, small, rows):
    pieces = offsets(weights[1].shape[0], weights[3].shape[0])
    gains, bias = small[:2]
    like = lambda a: jax.ShapeDtypeStruct(a.shape, WIDE)
    outs = [like(a) for a in (*weights, *weights, *weights, *[gains] * 4, *[bias] * 4)]
    return pl.pallas_call(
        functools.partial(update_kernel, pieces, factors),
        out_shape=(*outs, *[jax.ShapeDtypeStruct(r.shape, r.dtype) for r in rows]),
        in_specs=[WHOLE] * 19,
        out_specs=(*[WHOLE] * len(outs), *[ANYWHERE] * 2),
        scratch_shapes=[pltpu.SemaphoreType.DMA((2,))],
        compiler_params=pltpu.CompilerParams(vmem_limit_bytes=58 << 20),
        name="update",
    )(grad_rows, ortho_rows, stats, *weights, *momenta, *small, *rows)


def body(
    tokens,
    cotangent,
    lengths,
    variates,
    times,
    weight_qkv,
    weight_out,
    weight_gate_up,
    weight_down,
    momentum_qkv,
    momentum_out,
    momentum_gate_up,
    momentum_down,
    gains,
    attn_bias,
    gain_moment,
    gain_square,
    bias_moment,
    bias_square,
):
    width = tokens.shape[1]
    heads = attn_bias.shape[1]
    attn_rows = weight_out.shape[0]
    ff_rows = weight_down.shape[0]
    fsdp = lax.axis_size("fsdp")
    ff = ff_rows * fsdp
    attn_width = attn_rows * fsdp
    shrink = 1.0 - MUON_RATE * MUON_DECAY
    scale_attn = MUON_RATE * 0.2 * math.sqrt(max(width, attn_width))
    scale_ff = MUON_RATE * 0.2 * math.sqrt(max(width, ff))
    sizes = (fsdp, lax.axis_size("ns"))
    if sizes == (DEPTH * ACROSS, SIDES * CORES) and attn_rows == 48 and ff_rows == 128:
        turn = lambda a: jnp.swapaxes(a, 1, 2)
        shards = (turn(weight_qkv), weight_out, weight_gate_up, weight_down)
        momenta = (turn(momentum_qkv), momentum_out, momentum_gate_up, momentum_down)
        out_tokens, grad_tokens, grad_rows, ortho_rows, stats = whole_step(
            tokens, cotangent, lengths, variates, times, gains, attn_bias, shards, momenta
        )
        outs = list(
            update(
                (scale_attn,) * 4 + (scale_ff,) * 3,
                grad_rows,
                ortho_rows,
                stats,
                shards,
                momenta,
                (gains, attn_bias, gain_moment, gain_square, bias_moment, bias_square),
                (out_tokens, grad_tokens),
            )
        )
        out_tokens, grad_tokens = outs[-2:]
        outs = outs[:-2]
        for i in (0, 4, 8):
            outs[i] = turn(outs[i])
        return (out_tokens, grad_tokens, *outs)
    weights = pack(weight_qkv, weight_out, weight_gate_up, weight_down)
    momenta = pack(momentum_qkv, momentum_out, momentum_gate_up, momentum_down)
    full = lax.all_gather(weights.astype(LOW), "fsdp", axis=0, tiled=False)
    aligned = attn_rows % 16 == 0 and ff_rows % 16 == 0
    pieces = offsets(attn_rows, ff_rows)
    if not aligned:
        full = jnp.concatenate(
            [full[:, s : s + n].reshape(1, fsdp * n, width) for s, n in pieces], axis=1
        )
    out_tokens, grad_tokens, grads, stats = layer(
        tokens, cotangent, lengths, variates, times, full, gains, attn_bias, ff, WIDE
    )
    if not aligned:
        wholes = offsets(attn_width, ff)
        grads = jnp.concatenate(
            [grads[0, s : s + n].reshape(fsdp, n // fsdp, width) for s, n in wholes], axis=1
        )
    summed = lax.psum_scatter(grads, "fsdp", scatter_dimension=0, tiled=False)
    grad_rows = lax.psum(summed.astype(LOW), "ns").astype(WIDE)
    bias_part = jnp.sum(stats[8:, :PAIR], axis=1).reshape(2, 8)[:, :heads]
    grad_gains, grad_bias = lax.psum((stats[:2], bias_part), ("fsdp", "ns"))

    new_momenta = MUON_MU * momenta + grad_rows
    advance = grad_rows + MUON_MU * new_momenta
    parts = [advance[s : s + n] for s, n in pieces]
    grams = jnp.stack(
        [
            lax.dot_general(
                y,
                y,
                (((0,), (0,)), ((), ())),
                precision=lax.Precision.HIGHEST,
                preferred_element_type=WIDE,
            )
            for y in parts
        ]
    )
    factor = newton_schulz(lax.psum(grams, "fsdp"))
    turned = jnp.concatenate(
        [
            (scale_attn if i < 4 else scale_ff)
            * jnp.dot(
                y, factor[i], precision=lax.Precision.HIGHEST, preferred_element_type=WIDE
            )
            for i, y in enumerate(parts)
        ],
        axis=0,
    )
    new_weights = weights * shrink - turned
    new_gain_moment, new_gain_square, new_gains = adam_step(
        gains, grad_gains, gain_moment, gain_square
    )
    new_bias_moment, new_bias_square, new_bias = adam_step(
        attn_bias, grad_bias, bias_moment, bias_square
    )
    return (
        out_tokens,
        grad_tokens,
        *unpack(grad_rows, attn_rows, ff_rows),
        *unpack(new_momenta, attn_rows, ff_rows),
        *unpack(new_weights, attn_rows, ff_rows),
        grad_gains,
        new_gain_moment,
        new_gain_square,
        new_gains,
        grad_bias,
        new_bias_moment,
        new_bias_square,
        new_bias,
    )


def solution(mesh):
    rows = P(("fsdp", "ns"), None)
    line = P(("fsdp", "ns"))
    matrices = (P(None, None, "fsdp"), P("fsdp", None), P(None, None, "fsdp"), P("fsdp", None))
    return jax.shard_map(
        body,
        mesh=mesh,
        in_specs=(rows, rows, line, rows, line, *matrices, *matrices, *([P()] * 6)),
        out_specs=(rows, rows, *matrices, *matrices, *matrices, *([P()] * 8)),
        check_vma=False,
    )
```

```python
import functools
import math

import jax
import jax.numpy as jnp
import numpy as np
from jax import lax
from jax.experimental import pallas as pl
from jax.experimental.pallas import tpu as pltpu
from jax.sharding import PartitionSpec as P

HEAD_DIM = 64
BUCKET = 64
TIME_SLOTS = 64
NS_ITERS = 5
STEP = 10

EPS_NORM = 1e-06
ROPE_BASE = 10000.0
NEG_FILL = -1000000000.0
COEF_A = 3.4445
COEF_B = -4.775
COEF_C = 2.0315
NS_EPS = 1e-07
MUON_MU = 0.95
MUON_RATE = 0.25
MUON_DECAY = 0.01
ADAM_RATE = 0.8
BETA_ONE = 0.9
BETA_TWO = 0.95
ADAM_EPS = 1e-08

LOW = jnp.bfloat16
WIDE = jnp.float32
BLOCK = 256
PAIR = 2 * BUCKET
LANES = 2 * HEAD_DIM
STATS = 24
WHOLE = pl.BlockSpec(memory_space=pltpu.VMEM)
SCALARS = pl.BlockSpec(memory_space=pltpu.SMEM)
ANYWHERE = pl.BlockSpec(memory_space=pl.ANY)


def mul_nn(left, right):
    return lax.dot_general(left, right, (((1,), (0,)), ((), ())), preferred_element_type=WIDE)


def mul_nt(left, right):
    return lax.dot_general(left, right, (((1,), (1,)), ((), ())), preferred_element_type=WIDE)


def mul_tn(left, right):
    return lax.dot_general(left, right, (((0,), (0,)), ((), ())), preferred_element_type=WIDE)


def offsets(attn_rows, ff_rows):
    counts = [attn_rows] * 4 + [ff_rows] * 3
    starts = [sum(counts[:i]) for i in range(7)]
    return list(zip(starts, counts))


def layer_kernel(
    pieces,
    lengths,
    bias,
    tok_ref,
    cot_ref,
    var_ref,
    time_ref,
    table_ref,
    gain_ref,
    w_ref,
    out_ref,
    gtok_ref,
    grad_ref,
    stat_ref,
    n1_s,
    n2_s,
    att_s,
    gml_s,
    hid_s,
    glow_s,
    gg_s,
    gu_s,
    gqkv_s,
):
    step = pl.program_id(0)
    rows, width = tok_ref.shape
    heads = bias.shape[1]
    here = pl.ds(pl.multiple_of(step * rows, rows), rows)

    def weight(first, last):
        parts = []
        for i in range(first, last):
            start, count = pieces[i]
            part = w_ref[:, start : start + count, :]
            parts.append(part.reshape(part.shape[0] * count, width))
        return parts[0] if len(parts) == 1 else jnp.concatenate(parts, axis=0)

    @pl.when(step == 0)
    def _():
        stat_ref[...] = jnp.zeros_like(stat_ref)

    lane = lax.broadcasted_iota(jnp.int32, (1, LANES), 1)
    low_head = lane < HEAD_DIM
    low_half = lane % HEAD_DIM < HEAD_DIM // 2
    per_block = rows // PAIR
    var_rows = var_ref[pl.ds(step * per_block, per_block), :]
    time_rows = time_ref[pl.ds(step * per_block, per_block), :]
    filler = jnp.zeros((8 - 2 * per_block, PAIR), WIDE)
    columns = jnp.concatenate([var_rows, time_rows, filler], axis=0).T
    slots = lax.broadcasted_iota(jnp.int32, (1, TIME_SLOTS), 1).astype(WIDE)
    hot = jnp.concatenate(
        [(columns[:, per_block + p : per_block + p + 1] == slots) for p in range(per_block)], axis=0
    ).astype(LOW)
    looked = mul_nn(hot, table_ref[0]) + mul_nn(hot, table_ref[1]) + mul_nn(hot, table_ref[2])
    cosine = looked[:, :LANES]
    sine = looked[:, LANES:]

    def swapped(values):
        half = HEAD_DIM // 2
        return jnp.where(
            low_half, pltpu.roll(values, LANES - half, 1), pltpu.roll(values, half, 1)
        )

    gain_one = gain_ref[0:1, :]
    gain_two = gain_ref[1:2, :]
    tokens = tok_ref[...].astype(WIDE)
    scale_one = lax.rsqrt(jnp.mean(tokens * tokens, axis=-1, keepdims=True) + EPS_NORM)
    unit_one = tokens * scale_one
    normed_one = (unit_one * gain_one).astype(LOW)
    n1_s[here, :] = normed_one
    qkv = mul_nt(normed_one, weight(0, 3))

    query_scale = HEAD_DIM ** (-0.5)
    units = []
    attended = []
    row_id = lax.broadcasted_iota(jnp.int32, (PAIR, 1), 0)
    lane_id = lax.broadcasted_iota(jnp.int32, (1, PAIR), 1)
    same_bucket = (row_id < BUCKET) == (lane_id < BUCKET)
    masks = []
    live_cols = []
    for p in range(per_block):
        first = lengths[(step * per_block + p) * 2]
        second = lengths[(step * per_block + p) * 2 + 1]
        live_key = lane_id % BUCKET < jnp.where(lane_id < BUCKET, first, second)
        live_cols.append(row_id % BUCKET < jnp.where(row_id < BUCKET, first, second))
        mask = same_bucket & live_key
        same_var = columns[:, p : p + 1] == var_rows[p : p + 1, :]
        masks.append((mask, same_var))

    for hp in range(heads // 2):
        cols = slice(hp * LANES, (hp + 1) * LANES)
        q = qkv[:, cols]
        k = qkv[:, width + hp * LANES : width + (hp + 1) * LANES]
        v = qkv[:, 2 * width + hp * LANES : 2 * width + (hp + 1) * LANES].astype(LOW)
        q = ((q * cosine + swapped(q) * sine) * query_scale).astype(LOW)
        k = (k * cosine + swapped(k) * sine).astype(LOW)
        q_first = jnp.where(low_head, q, jnp.zeros_like(q))
        q_second = jnp.where(low_head, jnp.zeros_like(q), q)
        att_pairs = []
        for p in range(per_block):
            part = slice(p * PAIR, (p + 1) * PAIR)
            mask, same_var = masks[p]
            q2 = jnp.concatenate([q_first[part], q_second[part]], axis=0)
            kp = k[part]
            vp = v[part]
            raw = mul_nt(q2, kp)
            halves = []
            for j in range(2):
                h = 2 * hp + j
                biased = raw[j * PAIR : (j + 1) * PAIR] + jnp.where(
                    same_var, bias[0, h], bias[1, h]
                )
                halves.append(jnp.where(mask, biased, NEG_FILL))
            scores = jnp.concatenate(halves, axis=0)
            top = jnp.max(scores, axis=-1, keepdims=True)
            exponent = jnp.exp(scores - top)
            probs = exponent / jnp.sum(exponent, axis=-1, keepdims=True)
            probs_low = probs.astype(LOW)
            both = mul_nn(probs_low, vp)
            att_pairs.append(jnp.where(low_head, both[:PAIR], both[PAIR:]))
            units.append((hp, p, q2, kp, vp, probs, probs_low))
        attended.append(jnp.concatenate(att_pairs, axis=0).astype(LOW))
    attended = jnp.concatenate(attended, axis=1)
    att_s[here, :] = attended
    w_out = weight(3, 4)
    mid = tokens + mul_nn(attended, w_out)
    scale_two = lax.rsqrt(jnp.mean(mid * mid, axis=-1, keepdims=True) + EPS_NORM)
    unit_two = mid * scale_two
    normed_two = (unit_two * gain_two).astype(LOW)
    n2_s[here, :] = normed_two
    w_gate = weight(4, 5)
    w_up = weight(5, 6)
    w_down = weight(6, 7)
    gate = mul_nt(normed_two, w_gate)
    up = mul_nt(normed_two, w_up)
    sig = 1.0 / (1.0 + jnp.exp(-gate))
    silu = gate * sig
    hidden = (silu * up).astype(LOW)
    hid_s[here, :] = hidden
    out_ref[...] = (mid + mul_nn(hidden, w_down)).astype(LOW)

    live_row = jnp.concatenate(live_cols, axis=0)
    g_out = jnp.where(live_row, cot_ref[...].astype(WIDE), 0.0)
    g_low = g_out.astype(LOW)
    glow_s[here, :] = g_low
    g_hidden = mul_nt(g_low, w_down)
    g_gate = (g_hidden * up * sig * (1.0 + gate * (1.0 - sig))).astype(LOW)
    g_up = (g_hidden * silu).astype(LOW)
    gg_s[here, :] = g_gate
    gu_s[here, :] = g_up
    e_two = mul_nn(g_gate, w_gate) + mul_nn(g_up, w_up)
    stat_ref[1:2, :] += jnp.sum(e_two * unit_two, axis=0, keepdims=True)
    scaled = e_two * gain_two
    g_mid = g_out + scale_two * (
        scaled - unit_two * jnp.mean(scaled * unit_two, axis=-1, keepdims=True)
    )
    g_mid_low = g_mid.astype(LOW)
    gml_s[here, :] = g_mid_low
    g_att = mul_nt(g_mid_low, w_out).astype(LOW)

    parts_q = [[None] * per_block for _ in range(heads // 2)]
    parts_k = [[None] * per_block for _ in range(heads // 2)]
    parts_v = [[None] * per_block for _ in range(heads // 2)]
    for hp, p, q2, kp, vp, probs, probs_low in units:
        part = slice(p * PAIR, (p + 1) * PAIR)
        mask, same_var = masks[p]
        ga = g_att[part, hp * LANES : (hp + 1) * LANES]
        ga2 = jnp.concatenate(
            [
                jnp.where(low_head, ga, jnp.zeros_like(ga)),
                jnp.where(low_head, jnp.zeros_like(ga), ga),
            ],
            axis=0,
        )
        g_probs = mul_nt(ga2, vp)
        row_dot = jnp.sum(probs * g_probs, axis=-1, keepdims=True)
        g_scores = probs * (g_probs - row_dot)
        for j in range(2):
            h = 2 * hp + j
            mine = g_scores[j * PAIR : (j + 1) * PAIR]
            stat_ref[8 + h : 9 + h, :PAIR] += jnp.sum(
                jnp.where(same_var, mine, 0.0), axis=0, keepdims=True
            )
            stat_ref[16 + h : 17 + h, :PAIR] += jnp.sum(
                jnp.where(same_var, 0.0, mine), axis=0, keepdims=True
            )
        low_scores = g_scores.astype(LOW)
        both = mul_nn(low_scores, kp)
        parts_q[hp][p] = jnp.where(low_head, both[:PAIR], both[PAIR:])
        parts_k[hp][p] = mul_tn(low_scores, q2)
        parts_v[hp][p] = mul_tn(probs_low, ga2)
    g_q = []
    g_k = []
    g_v = []
    for hp in range(heads // 2):
        dq = jnp.concatenate(parts_q[hp], axis=0)
        dk = jnp.concatenate(parts_k[hp], axis=0)
        g_q.append(((dq * cosine - swapped(dq) * sine) * query_scale).astype(LOW))
        g_k.append((dk * cosine - swapped(dk) * sine).astype(LOW))
        g_v.append(jnp.concatenate(parts_v[hp], axis=0).astype(LOW))
    g_qkv = jnp.concatenate(g_q + g_k + g_v, axis=1)
    gqkv_s[here, :] = g_qkv
    e_one = mul_nn(g_qkv, weight(0, 3))
    stat_ref[0:1, :] += jnp.sum(e_one * unit_one, axis=0, keepdims=True)
    scaled = e_one * gain_one
    gtok_ref[...] = (
        g_mid
        + scale_one * (scaled - unit_one * jnp.mean(scaled * unit_one, axis=-1, keepdims=True))
    ).astype(LOW)

    @pl.when(step == pl.num_programs(0) - 1)
    def _():
        def put(index, left, right):
            start, count = pieces[index]
            grad_ref[:, start : start + count, :] = (
                mul_tn(left, right)
                .reshape(grad_ref.shape[0], count, width)
                .astype(grad_ref.dtype)
            )

        for j in range(3):
            put(j, gqkv_s[:, j * width : (j + 1) * width], n1_s[...])
        put(3, att_s[...], gml_s[...])
        put(4, gg_s[...], n2_s[...])
        put(5, gu_s[...], n2_s[...])
        put(6, hid_s[...], glow_s[...])


def layer(tokens, cotangent, lengths, variates, times, packed, gains, attn_bias, ff, grad_type):
    rows, width = tokens.shape
    heads = attn_bias.shape[1]
    copies, shard_rows, _ = packed.shape
    pieces = offsets(heads * HEAD_DIM // copies, ff // copies)
    half = HEAD_DIM // 2
    frequency = ROPE_BASE ** (-2.0 * jnp.arange(half, dtype=WIDE) / HEAD_DIM)
    angles = jnp.arange(TIME_SLOTS, dtype=WIDE)[:, None] * frequency[None, :]
    cosine, sine = jnp.cos(angles), jnp.sin(angles)
    table = jnp.concatenate([cosine] * 4 + [-sine, sine, -sine, sine], axis=1)
    first = table.astype(LOW)
    rest = table - first.astype(WIDE)
    second = rest.astype(LOW)
    third = (rest - second.astype(WIDE)).astype(LOW)
    table = jnp.stack([first, second, third])
    grid = rows // BLOCK
    block = pl.BlockSpec((BLOCK, width), lambda i: (i, 0))
    low_scratch = lambda columns: pltpu.VMEM((rows, columns), LOW)
    return pl.pallas_call(
        functools.partial(layer_kernel, pieces),
        grid=(grid,),
        out_shape=(
            jax.ShapeDtypeStruct((rows, width), LOW),
            jax.ShapeDtypeStruct((rows, width), LOW),
            jax.ShapeDtypeStruct((copies, shard_rows, width), grad_type),
            jax.ShapeDtypeStruct((STATS, width), WIDE),
        ),
        in_specs=[SCALARS, SCALARS, block, block, WHOLE, WHOLE, WHOLE, WHOLE, WHOLE],
        out_specs=(block, block, WHOLE, WHOLE),
        scratch_shapes=[
            low_scratch(width),
            low_scratch(width),
            low_scratch(width),
            low_scratch(width),
            low_scratch(ff),
            low_scratch(width),
            low_scratch(ff),
            low_scratch(ff),
            low_scratch(3 * width),
        ],
        compiler_params=pltpu.CompilerParams(vmem_limit_bytes=58 << 20),
        name="layer",
    )(
        lengths,
        attn_bias,
        tokens,
        cotangent,
        variates.astype(WIDE).reshape(rows // PAIR, PAIR),
        times.astype(WIDE).reshape(rows // PAIR, PAIR),
        table,
        gains,
        packed,
    )


def pack(qkv, out, gate_up, down):
    width = out.shape[-1]
    return jnp.concatenate(
        [
            jnp.swapaxes(qkv, 1, 2).reshape(-1, width),
            out,
            jnp.swapaxes(gate_up, 1, 2).reshape(-1, width),
            down,
        ],
        axis=0,
    )


def unpack(packed, attn_rows, ff_rows):
    width = packed.shape[-1]
    qkv = jnp.swapaxes(packed[: 3 * attn_rows].reshape(3, attn_rows, width), 1, 2)
    out = packed[3 * attn_rows : 4 * attn_rows]
    ends = 4 * attn_rows + 2 * ff_rows
    gate_up = jnp.swapaxes(packed[4 * attn_rows : ends].reshape(2, ff_rows, width), 1, 2)
    return qkv, out, gate_up, packed[ends:]


def newton_schulz(gram_mat):
    def product(left, right):
        return jnp.einsum(
            "mde,mef->mdf",
            left,
            right,
            precision=lax.Precision.HIGHEST,
            preferred_element_type=WIDE,
        )

    norm_val = jnp.sqrt(jnp.trace(gram_mat, axis1=1, axis2=2))[:, None, None] + NS_EPS
    gram_mat = gram_mat / (norm_val * norm_val)
    unit = jnp.eye(gram_mat.shape[-1], dtype=WIDE)[None]
    chain = None
    for turn_idx in range(NS_ITERS):
        poly_mat = COEF_A * unit + COEF_B * gram_mat + COEF_C * product(gram_mat, gram_mat)
        chain = poly_mat if chain is None else product(poly_mat, chain)
        if turn_idx < NS_ITERS - 1:
            gram_mat = product(product(poly_mat, gram_mat), poly_mat)
    return chain / norm_val


def adam_step(param, grad, moment, square):
    new_moment = BETA_ONE * moment + (1.0 - BETA_ONE) * grad
    new_square = BETA_TWO * square + (1.0 - BETA_TWO) * grad * grad
    corrected = new_moment / (1.0 - BETA_ONE**STEP)
    scaled = jnp.sqrt(new_square / (1.0 - BETA_TWO**STEP)) + ADAM_EPS
    return (new_moment, new_square, param - ADAM_RATE * corrected / scaled)


DEPTH, ACROSS = 4, 2
SIDES, CORES = 2, 2
OWNERS = (
    (2, 0, 0, 0),
    (2, 1, 1, 0),
    (1, 1, 0, 1),
    (1, 0, 1, 1),
    (1, 0, 0, 0),
    (2, 0, 1, 0),
    (1, 1, 1, 1),
)


def place():
    f = lax.axis_index("fsdp")
    n = lax.axis_index("ns")
    return f // ACROSS, f % ACROSS, n // CORES, n % CORES


def device(z, x, y, c):
    return (z * ACROSS + x, y * CORES + c)


def remote(src, dst, send_sem, recv_sem, where):
    return pltpu.make_async_remote_copy(
        src_ref=src,
        dst_ref=dst,
        send_sem=send_sem,
        recv_sem=recv_sem,
        device_id=where,
        device_id_type=pl.DeviceIdType.MESH,
    )


def greet(where):
    pl.semaphore_signal(
        pltpu.get_barrier_semaphore(),
        inc=1,
        device_id=where,
        device_id_type=pl.DeviceIdType.MESH,
    )


def halves(value):
    high = value.astype(LOW)
    return high, (value - high.astype(WIDE)).astype(LOW)


def square_wide(value):
    high, low = halves(value)
    cross = mul_nn(high, low)
    return mul_nn(high, high) + (cross + cross.T)


def mul_wide(left, right):
    columns = right.shape[1]
    left_high, left_low = halves(left)
    right_high, right_low = halves(right)
    first = mul_nn(left_high, jnp.concatenate([right_high, right_low], axis=1))
    return first[:, :columns] + (first[:, columns:] + mul_nn(left_low, right_high))


def gram_wide(value):
    high, low = halves(value)
    cross = mul_tn(high, low)
    return mul_tn(high, high) + (cross + cross.T)


def whole_kernel(
    pieces,
    lengths,
    bias,
    tok_hbm,
    cot_hbm,
    var_ref,
    time_ref,
    table_ref,
    gain_ref,
    wqkv_ref,
    wout_ref,
    wgate_up_ref,
    wdown_ref,
    mqkv_hbm,
    mout_hbm,
    mgate_up_hbm,
    mdown_hbm,
    out_hbm,
    gtok_hbm,
    grows_ref,
    xrows_ref,
    total_ref,
    tok_ref,
    cot_ref,
    mqkv_ref,
    mout_ref,
    mgate_up_ref,
    mdown_ref,
    load_sem,
    out_ref,
    gtok_ref,
    out_sem,
    w_s,
    grad_s,
    momenta,
    n1_s,
    n2_s,
    att_s,
    gml_s,
    glow_s,
    hid_s,
    gg_s,
    gu_s,
    low_s,
    gqkv_s,
    probs_s,
    mid_s,
    gmid_s,
    gatt_s,
    scale_s,
    rope_s,
    y_attn,
    y_ff,
    g_attn,
    g_ff,
    x_attn,
    x_ff,
    gram_s,
    chain_s,
    stat_s,
    stat_in,
    stat_acc,
    stat_line,
    stat_send,
    stat_recv,
    adv_recv,
    mom_recv,
    x_send,
    x_recv,
    fan_send,
    fan_recv,
    *per_part,
):
    z, x, y, c = place()
    shard = z * ACROSS + x
    rows, width = tok_ref.shape
    heads = bias.shape[1]
    sibling = device(z, x, y, 1 - c)
    facing = device(z, x, 1 - y, c)
    corner = device(z, x, 1 - y, 1 - c)
    beside = device(z, 1 - x, y, c)
    upper = device(z + 1, x, y, c)
    lower = device(z - 1, x, y, c)
    world = DEPTH * ACROSS * SIDES * CORES
    rank = shard * (SIDES * CORES) + y * CORES + c
    line = [lax.rem(z + k, DEPTH) for k in range(DEPTH)]

    def far_first(t):
        low_z = jnp.minimum(z, DEPTH - 1 - z)
        turn = DEPTH - 1 - t
        turn = low_z if turn == 0 else jnp.where(turn - 1 < low_z, turn - 1, turn)
        return jnp.where(z == low_z, turn, DEPTH - 1 - turn)
    part = 2 * c + y

    def hello(i, carry):
        other = lax.rem(rank + 1 + i, world)
        greet((other // (SIDES * CORES), lax.rem(other, SIDES * CORES)))
        return carry

    lax.fori_loop(0, world - 1, hello, 0)
    loads = [
        pltpu.make_async_copy(src, dst, load_sem.at[i])
        for i, (src, dst) in enumerate(
            (
                (tok_hbm, tok_ref),
                (cot_hbm, cot_ref),
                (mqkv_hbm, mqkv_ref),
                (mout_hbm, mout_ref),
                (mgate_up_hbm, mgate_up_ref),
                (mdown_hbm, mdown_ref),
            )
        )
    ]
    for one in loads:
        one.start()

    def put(index, value):
        start, count = pieces[index]
        w_s[shard, start : start + count, :] = value.astype(LOW)

    for j in range(3):
        put(j, wqkv_ref[j])
    put(3, wout_ref[...])
    put(4, wgate_up_ref[0].T)
    put(5, wgate_up_ref[1].T)
    put(6, wdown_ref[...])
    pl.semaphore_wait(pltpu.get_barrier_semaphore(), world - 1)

    has_up = z < DEPTH - 1
    has_down = z > 0

    def exists(rel):
        return (z + rel >= 0) & (z + rel < DEPTH)

    class Gather:
        def __init__(self, start, count, sems):
            self.start_row, self.half = start, count // 2
            (
                self.up_send,
                self.down_send,
                self.x_send,
                self.sib_send,
                self.below_recv,
                self.above_recv,
                self.x_recv,
                self.sib_recv,
            ) = sems

        def view(self, at, core):
            first = pl.multiple_of(self.start_row + core * self.half, 16)
            return w_s.at[at, pl.ds(first, self.half)]

        def mine(self, rel):
            return self.view(shard + rel * ACROSS, c)

        def others(self, rel):
            return self.view((z + rel) * ACROSS + 1 - x, c)

        def up(self, d):
            return remote(
                self.mine(-d), self.mine(-d), self.up_send.at[d], self.below_recv.at[d], upper
            )

        def down(self, d):
            return remote(
                self.mine(d), self.mine(d), self.down_send.at[d], self.above_recv.at[d], lower
            )

        def over(self, rel, where):
            return remote(
                self.mine(rel), where, self.x_send.at[rel + 3], self.x_recv.at[rel + 3], beside
            )

        def sib(self, kind, rel, src):
            return remote(
                src, src, self.sib_send.at[kind, rel + 3], self.sib_recv.at[kind, rel + 3], sibling
            )

        def start(self):
            @pl.when(has_up)
            def _():
                self.up(0).start()

            @pl.when(has_down)
            def _():
                self.down(0).start()

            self.over(0, self.mine(0)).start()

        def hop(self, d):
            @pl.when(exists(-d))
            def _():
                here = self.mine(-d)
                remote(
                    here, here, self.up_send.at[d], self.below_recv.at[d - 1], lower
                ).wait_recv()
                if d < DEPTH - 1:

                    @pl.when(has_up)
                    def _():
                        self.up(d).start()

                self.over(-d, here).start()
                self.sib(0, -d, here).start()

            @pl.when(exists(d))
            def _():
                here = self.mine(d)
                remote(
                    here, here, self.down_send.at[d], self.above_recv.at[d - 1], upper
                ).wait_recv()
                if d < DEPTH - 1:

                    @pl.when(has_down)
                    def _():
                        self.down(d).start()

                self.over(d, here).start()
                self.sib(0, d, here).start()

        def from_beside(self, d):
            for rel in (0,) if d == 0 else (-d, d):

                @pl.when(exists(rel))
                def _():
                    there = self.others(rel)
                    remote(
                        there, there, self.x_send.at[rel + 3], self.x_recv.at[rel + 3], beside
                    ).wait_recv()
                    self.sib(1, rel, there).start()

        def arrive(self):
            for rel in range(1 - DEPTH, DEPTH):

                @pl.when(exists(rel))
                def _():
                    if rel != 0:
                        self.sib(0, rel, self.view(shard + rel * ACROSS, 1 - c)).wait_recv()
                    self.sib(1, rel, self.view((z + rel) * ACROSS + 1 - x, 1 - c)).wait_recv()

        def sent(self):
            for rel in range(1 - DEPTH, DEPTH):

                @pl.when(exists(rel))
                def _():
                    if rel != 0:
                        self.sib(0, rel, self.mine(rel)).wait_send()
                    self.sib(1, rel, self.others(rel)).wait_send()
                    self.over(rel, self.mine(rel)).wait_send()

            for d in range(DEPTH - 1):

                @pl.when(exists(-d) & has_up)
                def _():
                    self.up(d).wait_send()

                @pl.when(exists(d) & has_down)
                def _():
                    self.down(d).wait_send()

    ff_row = pieces[4][0]
    last_row = pieces[6][0] + pieces[6][1]
    spans = ((0, ff_row), (ff_row, last_row - ff_row))
    each = len(per_part) // 2
    gathers = [Gather(*spans[i], per_part[i * each : i * each + 8]) for i in range(2)]
    attn_gather, ff_gather = gathers
    class Reduce:
        def __init__(self, start, count, refs):
            self.order, self.own = far_first, DEPTH - 1
            self.start_row, self.half, self.quarter = start, count // 2, count // 4
            (
                self.in_zero,
                self.acc_zero,
                self.in_one,
                self.acc_one,
                self.in_two,
                self.acc_two,
                self.in_three,
                self.send_zero,
                self.send_one,
                self.send_two,
                self.send_three,
                self.recv_zero,
                self.recv_one,
                self.recv_two,
                self.recv_three,
                self.mom_send,
                self.adv_send,
                self.row_send,
                self.row_recv,
            ) = refs
            self.keep_quarter = pl.ds(pl.multiple_of(y * self.quarter, 16), self.quarter)
            self.give_quarter = pl.ds(pl.multiple_of((1 - y) * self.quarter, 16), self.quarter)
            self.first_quarter = pl.ds(0, self.quarter)

        def half_of(self, core):
            return pl.ds(pl.multiple_of(self.start_row + core * self.half, 16), self.half)

        def rows_of(self, quarter):
            first = pl.multiple_of(self.start_row + quarter * self.quarter, 16)
            return pl.ds(first, self.quarter)

        def zero(self, t):
            return remote(
                grad_s.at[self.order(t), :, self.half_of(1 - c)],
                self.in_zero.at[t],
                self.send_zero.at[t],
                self.recv_zero.at[t],
                sibling,
            )

        def crosses(self, t, way):
            return (c + t) % 2 == way

        def one(self, k, core):
            if core == 0:
                src, dst = self.acc_zero.at[k, :, self.give_quarter], self.in_one.at[
                    k, :, self.first_quarter
                ]
            else:
                src, dst = self.acc_zero.at[k, 1 - x], self.in_one.at[k, 0]
            where = facing if core == 0 else beside
            return remote(src, dst, self.send_one.at[k], self.recv_one.at[k], where)

        def two(self, k, core):
            if core == 0:
                src = self.acc_one.at[k, 1 - x, self.first_quarter]
            else:
                src = self.acc_one.at[k, 0, self.give_quarter]
            where = beside if core == 0 else facing
            return remote(src, self.in_two.at[k], self.send_two.at[k], self.recv_two.at[k], where)

        def three(self, t):
            return remote(
                self.acc_two.at[t],
                self.in_three.at[z],
                self.send_three.at[t],
                self.recv_three.at[z],
                device(self.order(t), x, y, c),
            )

        def add(self, left, right):
            return (left.astype(WIDE) + right.astype(WIDE)).astype(LOW)

        def start(self):
            for t in range(DEPTH):
                self.zero(t).start()

        def first(self, t):
            self.zero(t).wait_recv()
            kept = grad_s[self.order(t), :, self.half_of(c)]
            self.acc_zero[t] = self.add(kept, self.in_zero[t])
            for core in range(2):

                @pl.when(self.crosses(t, core))
                def _():
                    self.one(t, core).start()

        def second(self, t):
            quarter = self.quarter

            @pl.when(self.crosses(t, 0))
            def _():
                self.one(t, 0).wait_recv()
                self.acc_one[t, :, :quarter] = self.add(
                    self.acc_zero[t, :, self.keep_quarter], self.in_one[t, :, :quarter]
                )
                self.two(t, 0).start()

            @pl.when(self.crosses(t, 1))
            def _():
                self.one(t, 1).wait_recv()
                self.acc_one[t, 0] = self.add(self.acc_zero[t, x], self.in_one[t, 0])
                self.two(t, 1).start()

        def third(self, t):
            quarter = self.quarter

            @pl.when(self.crosses(t, 0))
            def _():
                self.two(t, 0).wait_recv()
                self.acc_two[t] = self.add(self.acc_one[t, x, :quarter], self.in_two[t])

            @pl.when(self.crosses(t, 1))
            def _():
                self.two(t, 1).wait_recv()
                self.acc_two[t] = self.add(self.acc_one[t, 0, self.keep_quarter], self.in_two[t])

            @pl.when(self.order(t) != z)
            def _():
                self.three(t).start()

        def segments(self, index):
            found = []
            begin = self.start_row + index * self.quarter
            for m, (start, count) in enumerate(pieces):
                first, last = max(start, begin), min(start + count, begin + self.quarter)
                if first < last:
                    found.append((m, first - begin, first - start, last - first))
            return found

        def to_owner(self, kind, index, i, stays=False):
            m, first, to, count = self.segments(index)[i]
            begin = self.start_row + index * self.quarter + first
            source = (momenta, grows_ref)[kind].at[pl.ds(begin, count)]
            target = stage(kind, m).at[shard, pl.ds(to, count)]
            sent = (self.mom_send, self.adv_send)[kind].at[i]
            got = (mom_recv, adv_recv)[kind].at[0]
            if stays:
                return pltpu.make_async_copy(source, target, got)
            return remote(source, target, sent, got, device(*OWNERS[m]))

        def all_to_owners(self, kind):
            for index in range(4):
                for i, (m, _, _, _) in enumerate(self.segments(index)):

                    @pl.when((part == index) & jnp.logical_not(owned(m)))
                    def _():
                        self.to_owner(kind, index, i).start()

                    @pl.when((part == index) & owned(m))
                    def _():
                        self.to_owner(kind, index, i, stays=True).start()

        def send_momenta(self):
            self.all_to_owners(0)

        def row_copy(self, j, quarter, where):
            here = grows_ref.at[self.rows_of(quarter)]
            return remote(here, here, self.row_send.at[j], self.row_recv.at[j], where)

        def finish(self):
            total = self.acc_two[self.own].astype(WIDE)
            for j in range(1, DEPTH):
                there = self.in_three.at[line[j]]
                remote(
                    there, there, self.send_three.at[0], self.recv_three.at[line[j]], sibling
                ).wait_recv()
                total = total + self.in_three[line[j]].astype(WIDE)
            grows_ref[self.rows_of(part), :] = total.astype(LOW)
            self.all_to_owners(1)

        def give_rows(self):
            for j, where in enumerate((sibling, facing, corner)):
                self.row_copy(j, part, where).start()

        def done(self):
            mates = ((sibling, 0, 1), (facing, 1, 0), (corner, 1, 1))
            for j, (where, dy, dc) in enumerate(mates):
                self.row_copy(j, 2 * (c ^ dc) + (y ^ dy), where).wait_recv()
                self.row_copy(j, part, where).wait_send()
            for index in range(4):
                for i, (m, _, _, _) in enumerate(self.segments(index)):

                    @pl.when((part == index) & jnp.logical_not(owned(m)))
                    def _():
                        for kind in range(2):
                            self.to_owner(kind, index, i).wait_send()

            for t in range(DEPTH):
                self.zero(t).wait_send()

                @pl.when(self.order(t) != z)
                def _():
                    self.three(t).wait_send()

                for core in range(2):

                    @pl.when(self.crosses(t, core))
                    def _():
                        self.one(t, core).wait_send()
                        self.two(t, core).wait_send()

    def owned(m):
        oz, ox, oy, oc = OWNERS[m]
        return (z == oz) & (x == ox) & (y == oy) & (c == oc)

    def stage(kind, m):
        return ((y_attn, y_ff), (g_attn, g_ff))[kind][int(m >= 4)]

    reduces = [Reduce(*spans[i], per_part[i * each + 8 : (i + 1) * each]) for i in range(2)]
    attn_reduce, ff_reduce = reduces

    attn_gather.start()
    ff_gather.start()

    for one in loads:
        one.wait()
    for i, (value, turned) in enumerate(((mgate_up_ref[0], 4), (mgate_up_ref[1], 5))):
        start, count = pieces[turned]
        momenta[start : start + count, :] = value.T
    for j in range(3):
        start, count = pieces[j]
        momenta[start : start + count, :] = mqkv_ref[j]
    momenta[pieces[3][0] : pieces[3][0] + pieces[3][1], :] = mout_ref[...]
    momenta[pieces[6][0] : last_row, :] = mdown_ref[...]
    stat_s[...] = jnp.zeros_like(stat_s)

    lane = lax.broadcasted_iota(jnp.int32, (1, LANES), 1)
    low_head = lane < HEAD_DIM
    low_half = lane % HEAD_DIM < HEAD_DIM // 2
    row_id = lax.broadcasted_iota(jnp.int32, (PAIR, 1), 0)
    lane_id = lax.broadcasted_iota(jnp.int32, (1, PAIR), 1)
    same_bucket = (row_id < BUCKET) == (lane_id < BUCKET)
    slots = lax.broadcasted_iota(jnp.int32, (1, TIME_SLOTS), 1)
    query_scale = HEAD_DIM ** (-0.5)
    gain_one = gain_ref[0:1, :]
    gain_two = gain_ref[1:2, :]

    def column(row):
        return jnp.broadcast_to(row, (8, PAIR)).T[:, 0:1]

    def var_row(pair):
        two = var_ref[pl.ds(2 * pair, 2), :]
        return jnp.concatenate([two[0:1], two[1:2]], axis=1).astype(WIDE)

    def block_of(i, size):
        return pl.ds(pl.multiple_of(i * size, size), size)

    def prepare(i, carry):
        here = block_of(i, PAIR)
        times = column(time_ref[pl.ds(i, 1), :].astype(WIDE)).astype(jnp.int32)
        hot = (times == slots).astype(LOW)
        rope_s[here, :] = (
            mul_nn(hot, table_ref[0]) + mul_nn(hot, table_ref[1]) + mul_nn(hot, table_ref[2])
        )
        tokens = tok_ref[here, :].astype(WIDE)
        scale = lax.rsqrt(jnp.mean(tokens * tokens, axis=-1, keepdims=True) + EPS_NORM)
        scale_s[here, 0:1] = scale
        n1_s[here, :] = (tokens * scale * gain_one).astype(LOW)
        first, second = lengths[2 * i], lengths[2 * i + 1]
        live = row_id % BUCKET < jnp.where(row_id < BUCKET, first, second)
        glow_s[here, :] = jnp.where(live, cot_ref[here, :].astype(WIDE), 0.0).astype(LOW)
        return carry

    lax.fori_loop(0, rows // PAIR, prepare, 0)

    for d in range(1, DEPTH):
        attn_gather.hop(d)
        if d < DEPTH - 1:
            ff_gather.hop(d)
    for d in range(DEPTH):
        attn_gather.from_beside(d)
    attn_gather.arrive()

    def weight(first, last):
        parts = []
        for i in range(first, last):
            start, count = pieces[i]
            piece = w_s[:, start : start + count, :]
            parts.append(piece.reshape(piece.shape[0] * count, width))
        return parts[0] if len(parts) == 1 else jnp.concatenate(parts, axis=0)

    def swapped(values):
        half = HEAD_DIM // 2
        return jnp.where(
            low_half, pltpu.roll(values, LANES - half, 1), pltpu.roll(values, half, 1)
        )

    def two_heads(value):
        none = jnp.zeros_like(value)
        return jnp.concatenate(
            [jnp.where(low_head, value, none), jnp.where(low_head, none, value)], axis=0
        )

    per_block = BLOCK // PAIR

    def attend(i, carry):
        here = block_of(i, BLOCK)
        qkv = mul_nt(n1_s[here, :], weight(0, 3))
        cosine = rope_s[here, :LANES]
        sine = rope_s[here, LANES:]
        masks = []
        for p in range(per_block):
            pair = i * per_block + p
            first, second = lengths[2 * pair], lengths[2 * pair + 1]
            live_key = lane_id % BUCKET < jnp.where(lane_id < BUCKET, first, second)
            row = var_row(pair)
            masks.append((same_bucket & live_key, column(row) == row))
        attended = []
        for hp in range(heads // 2):
            first = hp * LANES
            q = qkv[:, first : first + LANES]
            k = qkv[:, width + first : width + first + LANES]
            v = qkv[:, 2 * width + first : 2 * width + first + LANES].astype(LOW)
            q = ((q * cosine + swapped(q) * sine) * query_scale).astype(LOW)
            k = (k * cosine + swapped(k) * sine).astype(LOW)
            low_s[here, first : first + LANES] = q
            low_s[here, width + first : width + first + LANES] = k
            low_s[here, 2 * width + first : 2 * width + first + LANES] = v
            pairs = []
            for p in range(per_block):
                span = slice(p * PAIR, (p + 1) * PAIR)
                mask, same_var = masks[p]
                raw = mul_nt(two_heads(q[span]), k[span])
                both = []
                for j in range(2):
                    h = 2 * hp + j
                    biased = raw[j * PAIR : (j + 1) * PAIR] + jnp.where(
                        same_var, bias[0, h], bias[1, h]
                    )
                    both.append(jnp.where(mask, biased, NEG_FILL))
                scores = jnp.concatenate(both, axis=0)
                exponent = jnp.exp(scores - jnp.max(scores, axis=-1, keepdims=True))
                probs = exponent / jnp.sum(exponent, axis=-1, keepdims=True)
                probs_s[i * per_block + p, hp] = probs
                both = mul_nn(probs.astype(LOW), v[span])
                pairs.append(jnp.where(low_head, both[:PAIR], both[PAIR:]))
            attended.append(jnp.concatenate(pairs, axis=0).astype(LOW))
        attended = jnp.concatenate(attended, axis=1)
        att_s[here, :] = attended
        mid = tok_ref[here, :].astype(WIDE) + mul_nn(attended, weight(3, 4))
        mid_s[here, :] = mid
        scale = lax.rsqrt(jnp.mean(mid * mid, axis=-1, keepdims=True) + EPS_NORM)
        scale_s[here, 1:2] = scale
        n2_s[here, :] = (mid * scale * gain_two).astype(LOW)
        @pl.when(i == 0)
        def _():
            ff_gather.hop(DEPTH - 1)
            ff_gather.from_beside(0)
            ff_gather.from_beside(1)

        for d in range(2, DEPTH):

            @pl.when(i == d - 1)
            def _():
                ff_gather.from_beside(d)

        return carry

    lax.fori_loop(0, rows // BLOCK, attend, 0)
    ff_gather.arrive()
    for one in reduces:
        one.send_momenta()

    def feed(i, carry):
        here = block_of(i, 2 * BLOCK)
        normed_two = n2_s[here, :]
        w_gate, w_up, w_down = weight(4, 5), weight(5, 6), weight(6, 7)
        gate = mul_nt(normed_two, w_gate)
        up = mul_nt(normed_two, w_up)
        sig = 1.0 / (1.0 + jnp.exp(-gate))
        silu = gate * sig
        hid_s[here, :] = (silu * up).astype(LOW)
        g_low = glow_s[here, :]
        g_hidden = mul_nt(g_low, w_down)
        g_gate = (g_hidden * up * sig * (1.0 + gate * (1.0 - sig))).astype(LOW)
        g_up = (g_hidden * silu).astype(LOW)
        gg_s[here, :] = g_gate
        gu_s[here, :] = g_up
        e_two = mul_nn(g_gate, w_gate) + mul_nn(g_up, w_up)
        scale = scale_s[here, 1:2]
        unit = mid_s[here, :] * scale
        stat_s[1:2, :] += jnp.sum(e_two * unit, axis=0, keepdims=True)
        scaled = e_two * gain_two
        g_mid = g_low.astype(WIDE) + scale * (
            scaled - unit * jnp.mean(scaled * unit, axis=-1, keepdims=True)
        )
        gmid_s[here, :] = g_mid
        g_mid_low = g_mid.astype(LOW)
        gml_s[here, :] = g_mid_low
        gatt_s[here, :] = mul_nt(g_mid_low, weight(3, 4)).astype(LOW)
        return carry

    lax.fori_loop(0, rows // (2 * BLOCK), feed, 0)

    def grad_put(index, left, right):
        start, count = pieces[index]
        grad_s[:, :, start : start + count, :] = (
            mul_tn(left, right).reshape(DEPTH, ACROSS, count, width).astype(LOW)
        )

    grad_put(4, gg_s[...], n2_s[...])
    grad_put(5, gu_s[...], n2_s[...])
    grad_put(6, hid_s[...], glow_s[...])
    ff_reduce.start()
    grad_put(3, att_s[...], gml_s[...])

    def attend_back(i, carry):
        here = block_of(i, PAIR)
        row = var_row(i)
        same_var = column(row) == row
        cosine = rope_s[here, :LANES]
        sine = rope_s[here, LANES:]
        for hp in range(heads // 2):
            first = hp * LANES
            q2 = two_heads(low_s[here, first : first + LANES])
            k = low_s[here, width + first : width + first + LANES]
            v = low_s[here, 2 * width + first : 2 * width + first + LANES]
            probs = probs_s[i, hp]
            ga2 = two_heads(gatt_s[here, first : first + LANES])
            g_probs = mul_nt(ga2, v)
            row_dot = jnp.sum(probs * g_probs, axis=-1, keepdims=True)
            g_scores = probs * (g_probs - row_dot)
            for j in range(2):
                h = 2 * hp + j
                mine = g_scores[j * PAIR : (j + 1) * PAIR]
                stat_s[8 + h : 9 + h, :PAIR] += jnp.sum(
                    jnp.where(same_var, mine, 0.0), axis=0, keepdims=True
                )
                stat_s[16 + h : 17 + h, :PAIR] += jnp.sum(
                    jnp.where(same_var, 0.0, mine), axis=0, keepdims=True
                )
            low_scores = g_scores.astype(LOW)
            both = mul_nn(low_scores, k)
            dq = jnp.where(low_head, both[:PAIR], both[PAIR:])
            dk = mul_tn(low_scores, q2)
            dv = mul_tn(probs.astype(LOW), ga2)
            gqkv_s[here, first : first + LANES] = (
                (dq * cosine - swapped(dq) * sine) * query_scale
            ).astype(LOW)
            gqkv_s[here, width + first : width + first + LANES] = (
                dk * cosine - swapped(dk) * sine
            ).astype(LOW)
            gqkv_s[here, 2 * width + first : 2 * width + first + LANES] = dv.astype(LOW)
        @pl.when(i == 0)
        def _():
            for t in range(DEPTH):
                ff_reduce.first(t)

        @pl.when(i == 4)
        def _():
            ff_reduce.second(0)
            ff_reduce.second(1)

        @pl.when(i == 6)
        def _():
            ff_reduce.third(0)
            ff_reduce.third(1)
            ff_reduce.second(2)
            ff_reduce.second(3)

        return carry

    lax.fori_loop(0, rows // PAIR, attend_back, 0)
    for j in range(3):
        grad_put(j, gqkv_s[:, j * width : (j + 1) * width], n1_s[...])
    attn_reduce.start()
    ff_reduce.third(2)
    ff_reduce.third(3)

    def last(i):
        here = block_of(i, 2 * BLOCK)
        e_one = mul_nn(gqkv_s[here, :], weight(0, 3))
        scale = scale_s[here, 0:1]
        unit = tok_ref[here, :].astype(WIDE) * scale
        stat_s[0:1, :] += jnp.sum(e_one * unit, axis=0, keepdims=True)
        scaled = e_one * gain_one
        gtok_ref[here, :] = (
            gmid_s[here, :]
            + scale * (scaled - unit * jnp.mean(scaled * unit, axis=-1, keepdims=True))
        ).astype(LOW)

    def outgoing(i):
        here = block_of(i, 2 * BLOCK)
        out_ref[here, :] = (mid_s[here, :] + mul_nn(hid_s[here, :], weight(6, 7))).astype(LOW)

    def stat_copy(step, src, where):
        return remote(src, stat_in.at[step], stat_send.at[step], stat_recv.at[step], where)

    for t in range(DEPTH):
        attn_reduce.first(t)
    last(0)
    last(1)
    leave = [
        pltpu.make_async_copy(gtok_ref, gtok_hbm, out_sem.at[0]),
        pltpu.make_async_copy(out_ref, out_hbm, out_sem.at[1]),
    ]
    leave[0].start()
    stat_copy(0, stat_s, sibling).start()
    ff_reduce.finish()
    attn_reduce.second(0)
    attn_reduce.second(1)
    stat_copy(0, stat_s, sibling).wait()
    stat_acc[0] = stat_s[...] + stat_in[0]
    stat_copy(1, stat_acc.at[0], facing).start()
    attn_reduce.second(2)
    attn_reduce.second(3)
    for t in range(DEPTH):
        attn_reduce.third(t)
    stat_copy(1, stat_acc.at[0], facing).wait()
    stat_acc[1] = stat_acc[0] + stat_in[1]
    stat_copy(2, stat_acc.at[1], beside).start()
    attn_owner = functools.reduce(jnp.logical_or, [owned(m) for m in range(4)])
    ff_owner = functools.reduce(jnp.logical_or, [owned(m) for m in range(4, 7)])

    chips = DEPTH * ACROSS * SIDES

    def x_copy(m, i):
        start, count = pieces[m]
        source = x_attn if m < 4 else x_ff
        to = i // SIDES
        return remote(
            source.at[to],
            xrows_ref.at[pl.ds(start, count)],
            x_send.at[i],
            x_recv.at[m],
            (to, lax.rem(i, SIDES) * CORES + OWNERS[m][3]),
        )

    mine = shard * SIDES + y
    unit_mat = lax.broadcasted_iota(jnp.int32, (width, width), 0) == lax.broadcasted_iota(
        jnp.int32, (width, width), 1
    )
    diagonal = jnp.where(unit_mat, COEF_A, 0.0)

    def advance(y_buf, g_buf):
        pltpu.make_async_copy(y_buf, y_buf, mom_recv.at[0]).wait()
        pltpu.make_async_copy(g_buf, g_buf, adv_recv.at[0]).wait()
        grad = g_buf[...].astype(WIDE)
        return grad + MUON_MU * (MUON_MU * y_buf[...] + grad)

    def poly(value):
        return diagonal + COEF_B * value + COEF_C * square_wide(value)

    @pl.when(ff_owner)
    def _():
        y_ff[...] = advance(y_ff, g_ff)
        gram_mat = gram_wide(y_ff[...].reshape(-1, width))
        trace = jnp.sum(jnp.where(unit_mat, gram_mat, 0.0), keepdims=True)
        inverse = 1.0 / (jnp.sqrt(trace) + NS_EPS)
        gram_mat = gram_mat * (inverse * inverse)
        step_mat = poly(gram_mat)
        gram_s[...] = mul_wide(mul_wide(gram_mat, step_mat), step_mat)
        chain_s[...] = step_mat * inverse

    attn_reduce.finish()
    for one in reduces:
        one.give_rows()
    stat_copy(2, stat_acc.at[1], beside).wait()
    stat_acc[2] = stat_acc[1] + stat_in[2]
    stat_line[z] = stat_acc[2]

    def stat_send_line(j):
        return remote(
            stat_acc.at[2],
            stat_line.at[z],
            stat_send.at[2 + j],
            stat_recv.at[2 + j],
            device(line[j], x, y, c),
        )

    for j in range(1, DEPTH):
        stat_send_line(j).start()

    def send_x(m, first, count):
        def send(i, carry):
            @pl.when(i != mine)
            def _():
                x_copy(m, i).start()

            return carry

        lax.fori_loop(first, first + count, send, 0)

    def keep_x(m):
        start, count = pieces[m]
        source = x_attn if m < 4 else x_ff
        pltpu.make_async_copy(
            source.at[shard], xrows_ref.at[pl.ds(start, count)], x_recv.at[m]
        ).start()

    @pl.when(attn_owner)
    def _():
        value = advance(y_attn, g_attn).reshape(-1, width)
        total = jnp.sum(jnp.sum(value * value, axis=0, keepdims=True), axis=1, keepdims=True)
        chain_s[...] = value * (1.0 / (jnp.sqrt(total) + NS_EPS))

        def turn(i, carry):
            now = chain_s[...]
            chain_s[...] = mul_wide(now, poly(gram_wide(now)))
            return carry

        lax.fori_loop(0, NS_ITERS, turn, 0)
        x_attn[...] = chain_s[...].astype(LOW).reshape(x_attn.shape)
        for m in range(4):

            @pl.when(owned(m))
            def _():
                send_x(m, 0, chips)
                keep_x(m)

    @pl.when(ff_owner)
    def _():
        def turn(i, carry):
            now = gram_s[...]
            step_now = poly(now)
            both = mul_wide(jnp.concatenate([now, chain_s[...]], axis=0), step_now)
            chain_s[...] = both[width:]
            gram_s[...] = mul_wide(both[:width], step_now)
            return carry

        lax.fori_loop(0, NS_ITERS - 2, turn, 0)
        chain_s[...] = mul_wide(chain_s[...], poly(gram_s[...]))

        def give(i, carry):
            at = lax.rem(z + 2 + i, DEPTH)
            these = pl.ds(at * ACROSS, ACROSS)
            value = y_ff[these].reshape(-1, width)
            x_ff[these] = mul_wide(value, chain_s[...]).astype(LOW).reshape(
                ACROSS, x_ff.shape[1], width
            )
            for m in range(4, 7):

                @pl.when(owned(m))
                def _():
                    send_x(m, at * (ACROSS * SIDES), ACROSS * SIDES)

            return carry

        lax.fori_loop(0, DEPTH, give, 0)
        for m in range(4, 7):

            @pl.when(owned(m))
            def _():
                keep_x(m)

    outgoing(0)
    outgoing(1)
    leave[1].start()

    for j in range(1, DEPTH):
        remote(
            stat_acc.at[2],
            stat_line.at[lax.rem(z + DEPTH - j, DEPTH)],
            stat_send.at[2 + j],
            stat_recv.at[2 + j],
            device(line[j], x, y, c),
        ).wait()
    total_ref[...] = (stat_line[0] + stat_line[1]) + (stat_line[2] + stat_line[3])
    for one in gathers:
        one.sent()
    for one in reduces:
        one.done()

    def fan_copy(m):
        start, count = pieces[m]
        rows_m = xrows_ref.at[pl.ds(start, count)]
        return remote(rows_m, rows_m, fan_send.at[m], fan_recv.at[m], sibling)

    for m in range(7):
        start, count = pieces[m]

        @pl.when(c == OWNERS[m][3])
        def _():
            rows_m = xrows_ref.at[pl.ds(start, count)]
            pltpu.make_async_copy(rows_m, rows_m, x_recv.at[m]).wait()
            fan_copy(m).start()

    for m in range(7):

        @pl.when(c != OWNERS[m][3])
        def _():
            fan_copy(m).wait_recv()

        @pl.when(c == OWNERS[m][3])
        def _():
            fan_copy(m).wait_send()

        @pl.when(owned(m))
        def _():
            def sent(i, carry):
                x_copy(m, lax.rem(mine + i, chips)).wait_send()
                return carry

            lax.fori_loop(1, chips, sent, 0)

    for one in leave:
        one.wait()


def rotary_table():
    half = HEAD_DIM // 2
    frequency = (ROPE_BASE ** (-2.0 * np.arange(half) / HEAD_DIM)).astype(np.float32)
    angles = np.arange(TIME_SLOTS, dtype=np.float32)[:, None] * frequency[None, :]
    cosine = np.cos(angles.astype(np.float64)).astype(np.float32)
    sine = np.sin(angles.astype(np.float64)).astype(np.float32)
    table = np.concatenate([cosine] * 4 + [-sine, sine, -sine, sine], axis=1)
    parts = []
    for _ in range(3):
        parts.append(table.astype(LOW))
        table = table - parts[-1].astype(np.float32)
    return np.stack(parts)


def whole_step(tokens, cotangent, lengths, variates, times, gains, attn_bias, weights, momenta):
    rows, width = tokens.shape
    heads = attn_bias.shape[1]
    attn_rows, ff_rows = weights[1].shape[0], weights[3].shape[0]
    pieces = offsets(attn_rows, ff_rows)
    ff = ff_rows * DEPTH * ACROSS
    shards = DEPTH * ACROSS
    shard_rows = 4 * attn_rows + 3 * ff_rows
    low = lambda *shape: pltpu.VMEM(shape, LOW)
    wide = lambda *shape: pltpu.VMEM(shape, WIDE)
    dma = lambda *shape: pltpu.SemaphoreType.DMA(shape)

    def part_scratch(count):
        half, quarter = count // 2, count // 4
        relative = 2 * DEPTH - 1
        return [
            dma(DEPTH),
            dma(DEPTH),
            dma(relative),
            dma(2, relative),
            dma(DEPTH),
            dma(DEPTH),
            dma(relative),
            dma(2, relative),
            low(DEPTH, ACROSS, half, width),
            low(DEPTH, ACROSS, half, width),
            low(DEPTH, ACROSS, half, width),
            low(DEPTH, ACROSS, half, width),
            low(DEPTH, quarter, width),
            low(DEPTH, quarter, width),
            low(DEPTH, quarter, width),
            *[dma(DEPTH) for _ in range(8)],
            dma(3),
            dma(3),
            dma(3),
            dma(3),
        ]

    return pl.pallas_call(
        functools.partial(whole_kernel, pieces),
        out_shape=(
            jax.ShapeDtypeStruct((rows, width), LOW),
            jax.ShapeDtypeStruct((rows, width), LOW),
            jax.ShapeDtypeStruct((shard_rows, width), LOW),
            jax.ShapeDtypeStruct((shard_rows, width), LOW),
            jax.ShapeDtypeStruct((STATS, width), WIDE),
        ),
        in_specs=[SCALARS] * 2 + [ANYWHERE] * 2 + [WHOLE] * 8 + [ANYWHERE] * 4,
        out_specs=(ANYWHERE, ANYWHERE, WHOLE, WHOLE, WHOLE),
        scratch_shapes=[
            low(rows, width),
            low(rows, width),
            *[wide(*m.shape) for m in momenta],
            dma(6),
            low(rows, width),
            low(rows, width),
            dma(2),
            low(shards, shard_rows, width),
            low(DEPTH, ACROSS, shard_rows, width),
            wide(shard_rows, width),
            low(rows, width),
            low(rows, width),
            low(rows, width),
            low(rows, width),
            low(rows, width),
            low(rows, ff),
            low(rows, ff),
            low(rows, ff),
            low(rows, 3 * width),
            low(rows, 3 * width),
            wide(rows // PAIR, heads // 2, 2 * PAIR, PAIR),
            wide(rows, width),
            wide(rows, width),
            low(rows, width),
            wide(rows, 2),
            wide(rows, 2 * LANES),
            wide(shards, attn_rows, width),
            wide(shards, ff_rows, width),
            low(shards, attn_rows, width),
            low(shards, ff_rows, width),
            low(shards, attn_rows, width),
            low(shards, ff_rows, width),
            wide(width, width),
            wide(width, width),
            wide(STATS, width),
            wide(3, STATS, width),
            wide(3, STATS, width),
            wide(DEPTH, STATS, width),
            dma(6),
            dma(6),
            dma(1),
            dma(1),
            dma(shards * SIDES),
            dma(7),
            dma(7),
            dma(7),
            *part_scratch(4 * attn_rows),
            *part_scratch(3 * ff_rows),
        ],
        compiler_params=pltpu.CompilerParams(
            vmem_limit_bytes=60 << 20, collective_id=0, has_side_effects=True
        ),
        name="whole",
    )(
        lengths,
        attn_bias,
        tokens,
        cotangent,
        variates,
        times.reshape(rows // PAIR, PAIR),
        jnp.asarray(rotary_table()),
        gains,
        *weights,
        *momenta,
    )


def update_kernel(
    pieces,
    factors,
    grow_ref,
    xrow_ref,
    stat_ref,
    w_qkv,
    w_out,
    w_gate_up,
    w_down,
    m_qkv,
    m_out,
    m_gate_up,
    m_down,
    gains,
    bias,
    gain_moment,
    gain_square,
    bias_moment,
    bias_square,
    out_in,
    gtok_in,
    g_qkv,
    g_out,
    g_gate_up,
    g_down,
    nm_qkv,
    nm_out,
    nm_gate_up,
    nm_down,
    nw_qkv,
    nw_out,
    nw_gate_up,
    nw_down,
    g_gains,
    n_gain_moment,
    n_gain_square,
    n_gains,
    g_bias,
    n_bias_moment,
    n_bias_square,
    n_bias,
    out_tokens,
    grad_tokens,
    sems,
):
    copies = (
        pltpu.make_async_copy(out_in, out_tokens, sems.at[0]),
        pltpu.make_async_copy(gtok_in, grad_tokens, sems.at[1]),
    )
    for one_copy in copies:
        one_copy.start()
    shrink = 1.0 - MUON_RATE * MUON_DECAY

    def one(index, turned, g, m, w, nm, nw):
        start, count = pieces[index]
        grad = grow_ref[start : start + count, :].astype(WIDE)
        ortho = xrow_ref[start : start + count, :].astype(WIDE)
        if turned:
            grad, ortho = grad.T, ortho.T
        g[...] = grad
        nm[...] = MUON_MU * m[...] + grad
        nw[...] = w[...] * shrink - factors[index] * ortho

    for j in range(3):
        one(j, False, *[r.at[j] for r in (g_qkv, m_qkv, w_qkv, nm_qkv, nw_qkv)])
    one(3, False, g_out, m_out, w_out, nm_out, nw_out)
    for j in range(2):
        refs = (g_gate_up, m_gate_up, w_gate_up, nm_gate_up, nw_gate_up)
        one(4 + j, True, *[r.at[j] for r in refs])
    one(6, False, g_down, m_down, w_down, nm_down, nw_down)

    grad = stat_ref[0:2, :]
    g_gains[...] = grad
    n_gain_moment[...], n_gain_square[...], n_gains[...] = adam_step(
        gains[...], grad, gain_moment[...], gain_square[...]
    )
    heads = bias.shape[1]
    sums = jnp.sum(stat_ref[8:24, :PAIR].T, axis=0, keepdims=True)
    grad = jnp.concatenate([sums[:, :heads], sums[:, 8 : 8 + heads]], axis=0)
    g_bias[...] = grad
    n_bias_moment[...], n_bias_square[...], n_bias[...] = adam_step(
        bias[...], grad, bias_moment[...], bias_square[...]
    )
    for one_copy in copies:
        one_copy.wait()


def update(factors, grad_rows, ortho_rows, stats, weights, momenta, small, rows):
    pieces = offsets(weights[1].shape[0], weights[3].shape[0])
    gains, bias = small[:2]
    like = lambda a: jax.ShapeDtypeStruct(a.shape, WIDE)
    outs = [like(a) for a in (*weights, *weights, *weights, *[gains] * 4, *[bias] * 4)]
    return pl.pallas_call(
        functools.partial(update_kernel, pieces, factors),
        out_shape=(*outs, *[jax.ShapeDtypeStruct(r.shape, r.dtype) for r in rows]),
        in_specs=[WHOLE] * 19,
        out_specs=(*[WHOLE] * len(outs), *[ANYWHERE] * 2),
        scratch_shapes=[pltpu.SemaphoreType.DMA((2,))],
        compiler_params=pltpu.CompilerParams(vmem_limit_bytes=58 << 20),
        name="update",
    )(grad_rows, ortho_rows, stats, *weights, *momenta, *small, *rows)


def body(
    tokens,
    cotangent,
    lengths,
    variates,
    times,
    weight_qkv,
    weight_out,
    weight_gate_up,
    weight_down,
    momentum_qkv,
    momentum_out,
    momentum_gate_up,
    momentum_down,
    gains,
    attn_bias,
    gain_moment,
    gain_square,
    bias_moment,
    bias_square,
):
    width = tokens.shape[1]
    heads = attn_bias.shape[1]
    attn_rows = weight_out.shape[0]
    ff_rows = weight_down.shape[0]
    fsdp = lax.axis_size("fsdp")
    ff = ff_rows * fsdp
    attn_width = attn_rows * fsdp
    shrink = 1.0 - MUON_RATE * MUON_DECAY
    scale_attn = MUON_RATE * 0.2 * math.sqrt(max(width, attn_width))
    scale_ff = MUON_RATE * 0.2 * math.sqrt(max(width, ff))
    sizes = (fsdp, lax.axis_size("ns"))
    if sizes == (DEPTH * ACROSS, SIDES * CORES) and attn_rows == 48 and ff_rows == 128:
        turn = lambda a: jnp.swapaxes(a, 1, 2)
        shards = (turn(weight_qkv), weight_out, weight_gate_up, weight_down)
        momenta = (turn(momentum_qkv), momentum_out, momentum_gate_up, momentum_down)
        out_tokens, grad_tokens, grad_rows, ortho_rows, stats = whole_step(
            tokens, cotangent, lengths, variates, times, gains, attn_bias, shards, momenta
        )
        outs = list(
            update(
                (scale_attn,) * 4 + (scale_ff,) * 3,
                grad_rows,
                ortho_rows,
                stats,
                shards,
                momenta,
                (gains, attn_bias, gain_moment, gain_square, bias_moment, bias_square),
                (out_tokens, grad_tokens),
            )
        )
        out_tokens, grad_tokens = outs[-2:]
        outs = outs[:-2]
        for i in (0, 4, 8):
            outs[i] = turn(outs[i])
        return (out_tokens, grad_tokens, *outs)
    weights = pack(weight_qkv, weight_out, weight_gate_up, weight_down)
    momenta = pack(momentum_qkv, momentum_out, momentum_gate_up, momentum_down)
    full = lax.all_gather(weights.astype(LOW), "fsdp", axis=0, tiled=False)
    aligned = attn_rows % 16 == 0 and ff_rows % 16 == 0
    pieces = offsets(attn_rows, ff_rows)
    if not aligned:
        full = jnp.concatenate(
            [full[:, s : s + n].reshape(1, fsdp * n, width) for s, n in pieces], axis=1
        )
    out_tokens, grad_tokens, grads, stats = layer(
        tokens, cotangent, lengths, variates, times, full, gains, attn_bias, ff, WIDE
    )
    if not aligned:
        wholes = offsets(attn_width, ff)
        grads = jnp.concatenate(
            [grads[0, s : s + n].reshape(fsdp, n // fsdp, width) for s, n in wholes], axis=1
        )
    summed = lax.psum_scatter(grads, "fsdp", scatter_dimension=0, tiled=False)
    grad_rows = lax.psum(summed.astype(LOW), "ns").astype(WIDE)
    bias_part = jnp.sum(stats[8:, :PAIR], axis=1).reshape(2, 8)[:, :heads]
    grad_gains, grad_bias = lax.psum((stats[:2], bias_part), ("fsdp", "ns"))

    new_momenta = MUON_MU * momenta + grad_rows
    advance = grad_rows + MUON_MU * new_momenta
    parts = [advance[s : s + n] for s, n in pieces]
    grams = jnp.stack(
        [
            lax.dot_general(
                y,
                y,
                (((0,), (0,)), ((), ())),
                precision=lax.Precision.HIGHEST,
                preferred_element_type=WIDE,
            )
            for y in parts
        ]
    )
    factor = newton_schulz(lax.psum(grams, "fsdp"))
    turned = jnp.concatenate(
        [
            (scale_attn if i < 4 else scale_ff)
            * jnp.dot(
                y, factor[i], precision=lax.Precision.HIGHEST, preferred_element_type=WIDE
            )
            for i, y in enumerate(parts)
        ],
        axis=0,
    )
    new_weights = weights * shrink - turned
    new_gain_moment, new_gain_square, new_gains = adam_step(
        gains, grad_gains, gain_moment, gain_square
    )
    new_bias_moment, new_bias_square, new_bias = adam_step(
        attn_bias, grad_bias, bias_moment, bias_square
    )
    return (
        out_tokens,
        grad_tokens,
        *unpack(grad_rows, attn_rows, ff_rows),
        *unpack(new_momenta, attn_rows, ff_rows),
        *unpack(new_weights, attn_rows, ff_rows),
        grad_gains,
        new_gain_moment,
        new_gain_square,
        new_gains,
        grad_bias,
        new_bias_moment,
        new_bias_square,
        new_bias,
    )


def solution(mesh):
    rows = P(("fsdp", "ns"), None)
    line = P(("fsdp", "ns"))
    matrices = (P(None, None, "fsdp"), P("fsdp", None), P(None, None, "fsdp"), P("fsdp", None))
    return jax.shard_map(
        body,
        mesh=mesh,
        in_specs=(rows, rows, line, rows, line, *matrices, *matrices, *([P()] * 6)),
        out_specs=(rows, rows, *matrices, *matrices, *matrices, *([P()] * 8)),
        check_vma=False,
    )
```

```python
import functools
import math

import jax
import jax.numpy as jnp
import numpy as np
from jax import lax
from jax.experimental import pallas as pl
from jax.experimental.pallas import tpu as pltpu
from jax.sharding import PartitionSpec as P

HEAD_DIM = 64
BUCKET = 64
TIME_SLOTS = 64
NS_ITERS = 5
STEP = 10

EPS_NORM = 1e-06
ROPE_BASE = 10000.0
NEG_FILL = -1000000000.0
COEF_A = 3.4445
COEF_B = -4.775
COEF_C = 2.0315
NS_EPS = 1e-07
MUON_MU = 0.95
MUON_RATE = 0.25
MUON_DECAY = 0.01
ADAM_RATE = 0.8
BETA_ONE = 0.9
BETA_TWO = 0.95
ADAM_EPS = 1e-08

LOW = jnp.bfloat16
WIDE = jnp.float32
BLOCK = 256
PAIR = 2 * BUCKET
LANES = 2 * HEAD_DIM
STATS = 24
WHOLE = pl.BlockSpec(memory_space=pltpu.VMEM)
SCALARS = pl.BlockSpec(memory_space=pltpu.SMEM)
ANYWHERE = pl.BlockSpec(memory_space=pl.ANY)


def mul_nn(left, right):
    return lax.dot_general(left, right, (((1,), (0,)), ((), ())), preferred_element_type=WIDE)


def mul_nt(left, right):
    return lax.dot_general(left, right, (((1,), (1,)), ((), ())), preferred_element_type=WIDE)


def mul_tn(left, right):
    return lax.dot_general(left, right, (((0,), (0,)), ((), ())), preferred_element_type=WIDE)


def offsets(attn_rows, ff_rows):
    counts = [attn_rows] * 4 + [ff_rows] * 3
    starts = [sum(counts[:i]) for i in range(7)]
    return list(zip(starts, counts))


def layer_kernel(
    pieces,
    lengths,
    bias,
    tok_ref,
    cot_ref,
    var_ref,
    time_ref,
    table_ref,
    gain_ref,
    w_ref,
    out_ref,
    gtok_ref,
    grad_ref,
    stat_ref,
    n1_s,
    n2_s,
    att_s,
    gml_s,
    hid_s,
    glow_s,
    gg_s,
    gu_s,
    gqkv_s,
):
    step = pl.program_id(0)
    rows, width = tok_ref.shape
    heads = bias.shape[1]
    here = pl.ds(pl.multiple_of(step * rows, rows), rows)

    def weight(first, last):
        parts = []
        for i in range(first, last):
            start, count = pieces[i]
            part = w_ref[:, start : start + count, :]
            parts.append(part.reshape(part.shape[0] * count, width))
        return parts[0] if len(parts) == 1 else jnp.concatenate(parts, axis=0)

    @pl.when(step == 0)
    def _():
        stat_ref[...] = jnp.zeros_like(stat_ref)

    lane = lax.broadcasted_iota(jnp.int32, (1, LANES), 1)
    low_head = lane < HEAD_DIM
    low_half = lane % HEAD_DIM < HEAD_DIM // 2
    per_block = rows // PAIR
    var_rows = var_ref[pl.ds(step * per_block, per_block), :]
    time_rows = time_ref[pl.ds(step * per_block, per_block), :]
    filler = jnp.zeros((8 - 2 * per_block, PAIR), WIDE)
    columns = jnp.concatenate([var_rows, time_rows, filler], axis=0).T
    slots = lax.broadcasted_iota(jnp.int32, (1, TIME_SLOTS), 1).astype(WIDE)
    hot = jnp.concatenate(
        [(columns[:, per_block + p : per_block + p + 1] == slots) for p in range(per_block)], axis=0
    ).astype(LOW)
    looked = mul_nn(hot, table_ref[0]) + mul_nn(hot, table_ref[1]) + mul_nn(hot, table_ref[2])
    cosine = looked[:, :LANES]
    sine = looked[:, LANES:]

    def swapped(values):
        half = HEAD_DIM // 2
        return jnp.where(
            low_half, pltpu.roll(values, LANES - half, 1), pltpu.roll(values, half, 1)
        )

    gain_one = gain_ref[0:1, :]
    gain_two = gain_ref[1:2, :]
    tokens = tok_ref[...].astype(WIDE)
    scale_one = lax.rsqrt(jnp.mean(tokens * tokens, axis=-1, keepdims=True) + EPS_NORM)
    unit_one = tokens * scale_one
    normed_one = (unit_one * gain_one).astype(LOW)
    n1_s[here, :] = normed_one
    qkv = mul_nt(normed_one, weight(0, 3))

    query_scale = HEAD_DIM ** (-0.5)
    units = []
    attended = []
    row_id = lax.broadcasted_iota(jnp.int32, (PAIR, 1), 0)
    lane_id = lax.broadcasted_iota(jnp.int32, (1, PAIR), 1)
    same_bucket = (row_id < BUCKET) == (lane_id < BUCKET)
    masks = []
    live_cols = []
    for p in range(per_block):
        first = lengths[(step * per_block + p) * 2]
        second = lengths[(step * per_block + p) * 2 + 1]
        live_key = lane_id % BUCKET < jnp.where(lane_id < BUCKET, first, second)
        live_cols.append(row_id % BUCKET < jnp.where(row_id < BUCKET, first, second))
        mask = same_bucket & live_key
        same_var = columns[:, p : p + 1] == var_rows[p : p + 1, :]
        masks.append((mask, same_var))

    for hp in range(heads // 2):
        cols = slice(hp * LANES, (hp + 1) * LANES)
        q = qkv[:, cols]
        k = qkv[:, width + hp * LANES : width + (hp + 1) * LANES]
        v = qkv[:, 2 * width + hp * LANES : 2 * width + (hp + 1) * LANES].astype(LOW)
        q = ((q * cosine + swapped(q) * sine) * query_scale).astype(LOW)
        k = (k * cosine + swapped(k) * sine).astype(LOW)
        q_first = jnp.where(low_head, q, jnp.zeros_like(q))
        q_second = jnp.where(low_head, jnp.zeros_like(q), q)
        att_pairs = []
        for p in range(per_block):
            part = slice(p * PAIR, (p + 1) * PAIR)
            mask, same_var = masks[p]
            q2 = jnp.concatenate([q_first[part], q_second[part]], axis=0)
            kp = k[part]
            vp = v[part]
            raw = mul_nt(q2, kp)
            halves = []
            for j in range(2):
                h = 2 * hp + j
                biased = raw[j * PAIR : (j + 1) * PAIR] + jnp.where(
                    same_var, bias[0, h], bias[1, h]
                )
                halves.append(jnp.where(mask, biased, NEG_FILL))
            scores = jnp.concatenate(halves, axis=0)
            top = jnp.max(scores, axis=-1, keepdims=True)
            exponent = jnp.exp(scores - top)
            probs = exponent / jnp.sum(exponent, axis=-1, keepdims=True)
            probs_low = probs.astype(LOW)
            both = mul_nn(probs_low, vp)
            att_pairs.append(jnp.where(low_head, both[:PAIR], both[PAIR:]))
            units.append((hp, p, q2, kp, vp, probs, probs_low))
        attended.append(jnp.concatenate(att_pairs, axis=0).astype(LOW))
    attended = jnp.concatenate(attended, axis=1)
    att_s[here, :] = attended
    w_out = weight(3, 4)
    mid = tokens + mul_nn(attended, w_out)
    scale_two = lax.rsqrt(jnp.mean(mid * mid, axis=-1, keepdims=True) + EPS_NORM)
    unit_two = mid * scale_two
    normed_two = (unit_two * gain_two).astype(LOW)
    n2_s[here, :] = normed_two
    w_gate = weight(4, 5)
    w_up = weight(5, 6)
    w_down = weight(6, 7)
    gate = mul_nt(normed_two, w_gate)
    up = mul_nt(normed_two, w_up)
    sig = 1.0 / (1.0 + jnp.exp(-gate))
    silu = gate * sig
    hidden = (silu * up).astype(LOW)
    hid_s[here, :] = hidden
    out_ref[...] = (mid + mul_nn(hidden, w_down)).astype(LOW)

    live_row = jnp.concatenate(live_cols, axis=0)
    g_out = jnp.where(live_row, cot_ref[...].astype(WIDE), 0.0)
    g_low = g_out.astype(LOW)
    glow_s[here, :] = g_low
    g_hidden = mul_nt(g_low, w_down)
    g_gate = (g_hidden * up * sig * (1.0 + gate * (1.0 - sig))).astype(LOW)
    g_up = (g_hidden * silu).astype(LOW)
    gg_s[here, :] = g_gate
    gu_s[here, :] = g_up
    e_two = mul_nn(g_gate, w_gate) + mul_nn(g_up, w_up)
    stat_ref[1:2, :] += jnp.sum(e_two * unit_two, axis=0, keepdims=True)
    scaled = e_two * gain_two
    g_mid = g_out + scale_two * (
        scaled - unit_two * jnp.mean(scaled * unit_two, axis=-1, keepdims=True)
    )
    g_mid_low = g_mid.astype(LOW)
    gml_s[here, :] = g_mid_low
    g_att = mul_nt(g_mid_low, w_out).astype(LOW)

    parts_q = [[None] * per_block for _ in range(heads // 2)]
    parts_k = [[None] * per_block for _ in range(heads // 2)]
    parts_v = [[None] * per_block for _ in range(heads // 2)]
    for hp, p, q2, kp, vp, probs, probs_low in units:
        part = slice(p * PAIR, (p + 1) * PAIR)
        mask, same_var = masks[p]
        ga = g_att[part, hp * LANES : (hp + 1) * LANES]
        ga2 = jnp.concatenate(
            [
                jnp.where(low_head, ga, jnp.zeros_like(ga)),
                jnp.where(low_head, jnp.zeros_like(ga), ga),
            ],
            axis=0,
        )
        g_probs = mul_nt(ga2, vp)
        row_dot = jnp.sum(probs * g_probs, axis=-1, keepdims=True)
        g_scores = probs * (g_probs - row_dot)
        for j in range(2):
            h = 2 * hp + j
            mine = g_scores[j * PAIR : (j + 1) * PAIR]
            stat_ref[8 + h : 9 + h, :PAIR] += jnp.sum(
                jnp.where(same_var, mine, 0.0), axis=0, keepdims=True
            )
            stat_ref[16 + h : 17 + h, :PAIR] += jnp.sum(
                jnp.where(same_var, 0.0, mine), axis=0, keepdims=True
            )
        low_scores = g_scores.astype(LOW)
        both = mul_nn(low_scores, kp)
        parts_q[hp][p] = jnp.where(low_head, both[:PAIR], both[PAIR:])
        parts_k[hp][p] = mul_tn(low_scores, q2)
        parts_v[hp][p] = mul_tn(probs_low, ga2)
    g_q = []
    g_k = []
    g_v = []
    for hp in range(heads // 2):
        dq = jnp.concatenate(parts_q[hp], axis=0)
        dk = jnp.concatenate(parts_k[hp], axis=0)
        g_q.append(((dq * cosine - swapped(dq) * sine) * query_scale).astype(LOW))
        g_k.append((dk * cosine - swapped(dk) * sine).astype(LOW))
        g_v.append(jnp.concatenate(parts_v[hp], axis=0).astype(LOW))
    g_qkv = jnp.concatenate(g_q + g_k + g_v, axis=1)
    gqkv_s[here, :] = g_qkv
    e_one = mul_nn(g_qkv, weight(0, 3))
    stat_ref[0:1, :] += jnp.sum(e_one * unit_one, axis=0, keepdims=True)
    scaled = e_one * gain_one
    gtok_ref[...] = (
        g_mid
        + scale_one * (scaled - unit_one * jnp.mean(scaled * unit_one, axis=-1, keepdims=True))
    ).astype(LOW)

    @pl.when(step == pl.num_programs(0) - 1)
    def _():
        def put(index, left, right):
            start, count = pieces[index]
            grad_ref[:, start : start + count, :] = (
                mul_tn(left, right)
                .reshape(grad_ref.shape[0], count, width)
                .astype(grad_ref.dtype)
            )

        for j in range(3):
            put(j, gqkv_s[:, j * width : (j + 1) * width], n1_s[...])
        put(3, att_s[...], gml_s[...])
        put(4, gg_s[...], n2_s[...])
        put(5, gu_s[...], n2_s[...])
        put(6, hid_s[...], glow_s[...])


def layer(tokens, cotangent, lengths, variates, times, packed, gains, attn_bias, ff, grad_type):
    rows, width = tokens.shape
    heads = attn_bias.shape[1]
    copies, shard_rows, _ = packed.shape
    pieces = offsets(heads * HEAD_DIM // copies, ff // copies)
    half = HEAD_DIM // 2
    frequency = ROPE_BASE ** (-2.0 * jnp.arange(half, dtype=WIDE) / HEAD_DIM)
    angles = jnp.arange(TIME_SLOTS, dtype=WIDE)[:, None] * frequency[None, :]
    cosine, sine = jnp.cos(angles), jnp.sin(angles)
    table = jnp.concatenate([cosine] * 4 + [-sine, sine, -sine, sine], axis=1)
    first = table.astype(LOW)
    rest = table - first.astype(WIDE)
    second = rest.astype(LOW)
    third = (rest - second.astype(WIDE)).astype(LOW)
    table = jnp.stack([first, second, third])
    grid = rows // BLOCK
    block = pl.BlockSpec((BLOCK, width), lambda i: (i, 0))
    low_scratch = lambda columns: pltpu.VMEM((rows, columns), LOW)
    return pl.pallas_call(
        functools.partial(layer_kernel, pieces),
        grid=(grid,),
        out_shape=(
            jax.ShapeDtypeStruct((rows, width), LOW),
            jax.ShapeDtypeStruct((rows, width), LOW),
            jax.ShapeDtypeStruct((copies, shard_rows, width), grad_type),
            jax.ShapeDtypeStruct((STATS, width), WIDE),
        ),
        in_specs=[SCALARS, SCALARS, block, block, WHOLE, WHOLE, WHOLE, WHOLE, WHOLE],
        out_specs=(block, block, WHOLE, WHOLE),
        scratch_shapes=[
            low_scratch(width),
            low_scratch(width),
            low_scratch(width),
            low_scratch(width),
            low_scratch(ff),
            low_scratch(width),
            low_scratch(ff),
            low_scratch(ff),
            low_scratch(3 * width),
        ],
        compiler_params=pltpu.CompilerParams(vmem_limit_bytes=58 << 20),
        name="layer",
    )(
        lengths,
        attn_bias,
        tokens,
        cotangent,
        variates.astype(WIDE).reshape(rows // PAIR, PAIR),
        times.astype(WIDE).reshape(rows // PAIR, PAIR),
        table,
        gains,
        packed,
    )


def pack(qkv, out, gate_up, down):
    width = out.shape[-1]
    return jnp.concatenate(
        [
            jnp.swapaxes(qkv, 1, 2).reshape(-1, width),
            out,
            jnp.swapaxes(gate_up, 1, 2).reshape(-1, width),
            down,
        ],
        axis=0,
    )


def unpack(packed, attn_rows, ff_rows):
    width = packed.shape[-1]
    qkv = jnp.swapaxes(packed[: 3 * attn_rows].reshape(3, attn_rows, width), 1, 2)
    out = packed[3 * attn_rows : 4 * attn_rows]
    ends = 4 * attn_rows + 2 * ff_rows
    gate_up = jnp.swapaxes(packed[4 * attn_rows : ends].reshape(2, ff_rows, width), 1, 2)
    return qkv, out, gate_up, packed[ends:]


def newton_schulz(gram_mat):
    def product(left, right):
        return jnp.einsum(
            "mde,mef->mdf",
            left,
            right,
            precision=lax.Precision.HIGHEST,
            preferred_element_type=WIDE,
        )

    norm_val = jnp.sqrt(jnp.trace(gram_mat, axis1=1, axis2=2))[:, None, None] + NS_EPS
    gram_mat = gram_mat / (norm_val * norm_val)
    unit = jnp.eye(gram_mat.shape[-1], dtype=WIDE)[None]
    chain = None
    for turn_idx in range(NS_ITERS):
        poly_mat = COEF_A * unit + COEF_B * gram_mat + COEF_C * product(gram_mat, gram_mat)
        chain = poly_mat if chain is None else product(poly_mat, chain)
        if turn_idx < NS_ITERS - 1:
            gram_mat = product(product(poly_mat, gram_mat), poly_mat)
    return chain / norm_val


def adam_step(param, grad, moment, square):
    new_moment = BETA_ONE * moment + (1.0 - BETA_ONE) * grad
    new_square = BETA_TWO * square + (1.0 - BETA_TWO) * grad * grad
    corrected = new_moment / (1.0 - BETA_ONE**STEP)
    scaled = jnp.sqrt(new_square / (1.0 - BETA_TWO**STEP)) + ADAM_EPS
    return (new_moment, new_square, param - ADAM_RATE * corrected / scaled)


DEPTH, ACROSS = 4, 2
SIDES, CORES = 2, 2
OWNERS = (
    (2, 0, 0, 0),
    (2, 1, 1, 0),
    (1, 1, 0, 1),
    (1, 0, 1, 1),
    (1, 0, 0, 0),
    (2, 0, 1, 0),
    (1, 1, 1, 1),
)


def place():
    f = lax.axis_index("fsdp")
    n = lax.axis_index("ns")
    return f // ACROSS, f % ACROSS, n // CORES, n % CORES


def device(z, x, y, c):
    return (z * ACROSS + x, y * CORES + c)


def remote(src, dst, send_sem, recv_sem, where):
    return pltpu.make_async_remote_copy(
        src_ref=src,
        dst_ref=dst,
        send_sem=send_sem,
        recv_sem=recv_sem,
        device_id=where,
        device_id_type=pl.DeviceIdType.MESH,
    )


def greet(where):
    pl.semaphore_signal(
        pltpu.get_barrier_semaphore(),
        inc=1,
        device_id=where,
        device_id_type=pl.DeviceIdType.MESH,
    )


def halves(value):
    high = value.astype(LOW)
    return high, (value - high.astype(WIDE)).astype(LOW)


def square_wide(value):
    high, low = halves(value)
    cross = mul_nn(high, low)
    return mul_nn(high, high) + (cross + cross.T)


def square_low(value):
    low = value.astype(LOW)
    return mul_nn(low, low)


def mul_wide(left, right):
    columns = right.shape[1]
    left_high, left_low = halves(left)
    right_high, right_low = halves(right)
    first = mul_nn(left_high, jnp.concatenate([right_high, right_low], axis=1))
    return first[:, :columns] + (first[:, columns:] + mul_nn(left_low, right_high))


def gram_wide(value):
    high, low = halves(value)
    cross = mul_tn(high, low)
    return mul_tn(high, high) + (cross + cross.T)


def whole_kernel(
    pieces,
    lengths,
    bias,
    tok_hbm,
    cot_hbm,
    var_ref,
    time_ref,
    table_ref,
    gain_ref,
    wqkv_ref,
    wout_ref,
    wgate_up_ref,
    wdown_ref,
    mqkv_hbm,
    mout_hbm,
    mgate_up_hbm,
    mdown_hbm,
    out_hbm,
    gtok_hbm,
    grows_ref,
    xrows_ref,
    total_ref,
    tok_ref,
    cot_ref,
    mqkv_ref,
    mout_ref,
    mgate_up_ref,
    mdown_ref,
    load_sem,
    out_ref,
    gtok_ref,
    out_sem,
    w_s,
    grad_s,
    momenta,
    n1_s,
    n2_s,
    att_s,
    gml_s,
    glow_s,
    hid_s,
    gg_s,
    gu_s,
    low_s,
    gqkv_s,
    probs_s,
    mid_s,
    gmid_s,
    gatt_s,
    scale_s,
    rope_s,
    y_attn,
    y_ff,
    g_attn,
    g_ff,
    x_attn,
    x_ff,
    gram_s,
    chain_s,
    stat_s,
    stat_in,
    stat_acc,
    stat_line,
    stat_send,
    stat_recv,
    adv_recv,
    mom_recv,
    x_send,
    x_recv,
    fan_send,
    fan_recv,
    *per_part,
):
    z, x, y, c = place()
    shard = z * ACROSS + x
    rows, width = tok_ref.shape
    heads = bias.shape[1]
    sibling = device(z, x, y, 1 - c)
    facing = device(z, x, 1 - y, c)
    corner = device(z, x, 1 - y, 1 - c)
    beside = device(z, 1 - x, y, c)
    upper = device(z + 1, x, y, c)
    lower = device(z - 1, x, y, c)
    world = DEPTH * ACROSS * SIDES * CORES
    rank = shard * (SIDES * CORES) + y * CORES + c
    line = [lax.rem(z + k, DEPTH) for k in range(DEPTH)]

    def far_first(t):
        low_z = jnp.minimum(z, DEPTH - 1 - z)
        turn = DEPTH - 1 - t
        turn = low_z if turn == 0 else jnp.where(turn - 1 < low_z, turn - 1, turn)
        return jnp.where(z == low_z, turn, DEPTH - 1 - turn)
    part = 2 * c + y

    for i in range(DEPTH * ACROSS):
        for j in range(SIDES * CORES):
            if i + j:
                greet(
                    (
                        lax.rem(shard + i, DEPTH * ACROSS),
                        lax.rem(y * CORES + c + j, SIDES * CORES),
                    )
                )

    loads = [
        pltpu.make_async_copy(src, dst, load_sem.at[i])
        for i, (src, dst) in enumerate(
            (
                (tok_hbm, tok_ref),
                (cot_hbm, cot_ref),
                (mqkv_hbm, mqkv_ref),
                (mout_hbm, mout_ref),
                (mgate_up_hbm, mgate_up_ref),
                (mdown_hbm, mdown_ref),
            )
        )
    ]
    for one in loads:
        one.start()

    def put(index, value):
        start, count = pieces[index]
        w_s[shard, start : start + count, :] = value.astype(LOW)

    for j in range(3):
        put(j, wqkv_ref[j])
    put(3, wout_ref[...])
    put(4, wgate_up_ref[0].T)
    put(5, wgate_up_ref[1].T)
    put(6, wdown_ref[...])
    pl.semaphore_wait(pltpu.get_barrier_semaphore(), world - 1)

    has_up = z < DEPTH - 1
    has_down = z > 0

    def exists(rel):
        return (z + rel >= 0) & (z + rel < DEPTH)

    class Gather:
        def __init__(self, start, count, sems):
            self.start_row, self.half = start, count // 2
            (
                self.up_send,
                self.down_send,
                self.x_send,
                self.sib_send,
                self.below_recv,
                self.above_recv,
                self.x_recv,
                self.sib_recv,
            ) = sems

        def view(self, at, core):
            first = pl.multiple_of(self.start_row + core * self.half, 16)
            return w_s.at[at, pl.ds(first, self.half)]

        def mine(self, rel):
            return self.view(shard + rel * ACROSS, c)

        def others(self, rel):
            return self.view((z + rel) * ACROSS + 1 - x, c)

        def up(self, d):
            return remote(
                self.mine(-d), self.mine(-d), self.up_send.at[d], self.below_recv.at[d], upper
            )

        def down(self, d):
            return remote(
                self.mine(d), self.mine(d), self.down_send.at[d], self.above_recv.at[d], lower
            )

        def over(self, rel, where):
            return remote(
                self.mine(rel), where, self.x_send.at[rel + 3], self.x_recv.at[rel + 3], beside
            )

        def sib(self, kind, rel, src):
            return remote(
                src, src, self.sib_send.at[kind, rel + 3], self.sib_recv.at[kind, rel + 3], sibling
            )

        def start(self):
            @pl.when(has_up)
            def _():
                self.up(0).start()

            @pl.when(has_down)
            def _():
                self.down(0).start()

            self.over(0, self.mine(0)).start()

        def hop(self, d):
            @pl.when(exists(-d))
            def _():
                here = self.mine(-d)
                remote(
                    here, here, self.up_send.at[d], self.below_recv.at[d - 1], lower
                ).wait_recv()
                if d < DEPTH - 1:

                    @pl.when(has_up)
                    def _():
                        self.up(d).start()

                self.over(-d, here).start()
                self.sib(0, -d, here).start()

            @pl.when(exists(d))
            def _():
                here = self.mine(d)
                remote(
                    here, here, self.down_send.at[d], self.above_recv.at[d - 1], upper
                ).wait_recv()
                if d < DEPTH - 1:

                    @pl.when(has_down)
                    def _():
                        self.down(d).start()

                self.over(d, here).start()
                self.sib(0, d, here).start()

        def from_beside(self, d):
            for rel in (0,) if d == 0 else (-d, d):

                @pl.when(exists(rel))
                def _():
                    there = self.others(rel)
                    remote(
                        there, there, self.x_send.at[rel + 3], self.x_recv.at[rel + 3], beside
                    ).wait_recv()
                    self.sib(1, rel, there).start()

        def arrive(self):
            for rel in range(1 - DEPTH, DEPTH):

                @pl.when(exists(rel))
                def _():
                    if rel != 0:
                        self.sib(0, rel, self.view(shard + rel * ACROSS, 1 - c)).wait_recv()
                    self.sib(1, rel, self.view((z + rel) * ACROSS + 1 - x, 1 - c)).wait_recv()

        def sent(self):
            for rel in range(1 - DEPTH, DEPTH):

                @pl.when(exists(rel))
                def _():
                    if rel != 0:
                        self.sib(0, rel, self.mine(rel)).wait_send()
                    self.sib(1, rel, self.others(rel)).wait_send()
                    self.over(rel, self.mine(rel)).wait_send()

            for d in range(DEPTH - 1):

                @pl.when(exists(-d) & has_up)
                def _():
                    self.up(d).wait_send()

                @pl.when(exists(d) & has_down)
                def _():
                    self.down(d).wait_send()

    ff_row = pieces[4][0]
    last_row = pieces[6][0] + pieces[6][1]
    spans = ((0, ff_row), (ff_row, last_row - ff_row))
    each = len(per_part) // 2
    gathers = [Gather(*spans[i], per_part[i * each : i * each + 8]) for i in range(2)]
    attn_gather, ff_gather = gathers
    class Reduce:
        def __init__(self, start, count, refs):
            self.order, self.own = far_first, DEPTH - 1
            self.start_row, self.half, self.quarter = start, count // 2, count // 4
            (
                self.in_zero,
                self.acc_zero,
                self.in_one,
                self.acc_one,
                self.in_two,
                self.acc_two,
                self.in_three,
                self.send_zero,
                self.send_one,
                self.send_two,
                self.send_three,
                self.recv_zero,
                self.recv_one,
                self.recv_two,
                self.recv_three,
                self.mom_send,
                self.adv_send,
                self.row_send,
                self.row_recv,
            ) = refs
            self.keep_quarter = pl.ds(pl.multiple_of(y * self.quarter, 16), self.quarter)
            self.give_quarter = pl.ds(pl.multiple_of((1 - y) * self.quarter, 16), self.quarter)
            self.first_quarter = pl.ds(0, self.quarter)

        def half_of(self, core):
            return pl.ds(pl.multiple_of(self.start_row + core * self.half, 16), self.half)

        def rows_of(self, quarter):
            first = pl.multiple_of(self.start_row + quarter * self.quarter, 16)
            return pl.ds(first, self.quarter)

        def zero(self, t):
            return remote(
                grad_s.at[self.order(t), :, self.half_of(1 - c)],
                self.in_zero.at[t],
                self.send_zero.at[t],
                self.recv_zero.at[t],
                sibling,
            )

        def crosses(self, t, way):
            return (c + t) % 2 == way

        def one(self, k, core):
            if core == 0:
                src, dst = self.acc_zero.at[k, :, self.give_quarter], self.in_one.at[
                    k, :, self.first_quarter
                ]
            else:
                src, dst = self.acc_zero.at[k, 1 - x], self.in_one.at[k, 0]
            where = facing if core == 0 else beside
            return remote(src, dst, self.send_one.at[k], self.recv_one.at[k], where)

        def two(self, k, core):
            if core == 0:
                src = self.acc_one.at[k, 1 - x, self.first_quarter]
            else:
                src = self.acc_one.at[k, 0, self.give_quarter]
            where = beside if core == 0 else facing
            return remote(src, self.in_two.at[k], self.send_two.at[k], self.recv_two.at[k], where)

        def three(self, t):
            return remote(
                self.acc_two.at[t],
                self.in_three.at[z],
                self.send_three.at[t],
                self.recv_three.at[z],
                device(self.order(t), x, y, c),
            )

        def add(self, left, right):
            return (left.astype(WIDE) + right.astype(WIDE)).astype(LOW)

        def start(self):
            for t in range(DEPTH):
                self.zero(t).start()

        def first(self, t):
            self.zero(t).wait_recv()
            kept = grad_s[self.order(t), :, self.half_of(c)]
            self.acc_zero[t] = self.add(kept, self.in_zero[t])
            for core in range(2):

                @pl.when(self.crosses(t, core))
                def _():
                    self.one(t, core).start()

        def second(self, t):
            quarter = self.quarter

            @pl.when(self.crosses(t, 0))
            def _():
                self.one(t, 0).wait_recv()
                self.acc_one[t, :, :quarter] = self.add(
                    self.acc_zero[t, :, self.keep_quarter], self.in_one[t, :, :quarter]
                )
                self.two(t, 0).start()

            @pl.when(self.crosses(t, 1))
            def _():
                self.one(t, 1).wait_recv()
                self.acc_one[t, 0] = self.add(self.acc_zero[t, x], self.in_one[t, 0])
                self.two(t, 1).start()

        def third(self, t):
            quarter = self.quarter

            @pl.when(self.crosses(t, 0))
            def _():
                self.two(t, 0).wait_recv()
                self.acc_two[t] = self.add(self.acc_one[t, x, :quarter], self.in_two[t])

            @pl.when(self.crosses(t, 1))
            def _():
                self.two(t, 1).wait_recv()
                self.acc_two[t] = self.add(self.acc_one[t, 0, self.keep_quarter], self.in_two[t])

            @pl.when(self.order(t) != z)
            def _():
                self.three(t).start()

        def segments(self, index):
            found = []
            begin = self.start_row + index * self.quarter
            for m, (start, count) in enumerate(pieces):
                first, last = max(start, begin), min(start + count, begin + self.quarter)
                if first < last:
                    found.append((m, first - begin, first - start, last - first))
            return found

        def to_owner(self, kind, index, i, stays=False):
            m, first, to, count = self.segments(index)[i]
            begin = self.start_row + index * self.quarter + first
            source = (momenta, grows_ref)[kind].at[pl.ds(begin, count)]
            target = stage(kind, m).at[shard, pl.ds(to, count)]
            sent = (self.mom_send, self.adv_send)[kind].at[i]
            got = (mom_recv, adv_recv)[kind].at[0]
            if stays:
                return pltpu.make_async_copy(source, target, got)
            return remote(source, target, sent, got, device(*OWNERS[m]))

        def all_to_owners(self, kind):
            for index in range(4):
                for i, (m, _, _, _) in enumerate(self.segments(index)):

                    @pl.when((part == index) & jnp.logical_not(owned(m)))
                    def _():
                        self.to_owner(kind, index, i).start()

                    @pl.when((part == index) & owned(m))
                    def _():
                        self.to_owner(kind, index, i, stays=True).start()

        def send_momenta(self):
            self.all_to_owners(0)

        def row_copy(self, j, quarter, where):
            here = grows_ref.at[self.rows_of(quarter)]
            return remote(here, here, self.row_send.at[j], self.row_recv.at[j], where)

        def finish(self):
            total = self.acc_two[self.own].astype(WIDE)
            for j in range(1, DEPTH):
                there = self.in_three.at[line[j]]
                remote(
                    there, there, self.send_three.at[0], self.recv_three.at[line[j]], sibling
                ).wait_recv()
                total = total + self.in_three[line[j]].astype(WIDE)
            grows_ref[self.rows_of(part), :] = total.astype(LOW)
            self.all_to_owners(1)

        def give_rows(self):
            for j, where in enumerate((sibling, facing, corner)):
                self.row_copy(j, part, where).start()

        def done(self):
            mates = ((sibling, 0, 1), (facing, 1, 0), (corner, 1, 1))
            for j, (where, dy, dc) in enumerate(mates):
                self.row_copy(j, 2 * (c ^ dc) + (y ^ dy), where).wait_recv()
                self.row_copy(j, part, where).wait_send()
            for index in range(4):
                for i, (m, _, _, _) in enumerate(self.segments(index)):

                    @pl.when((part == index) & jnp.logical_not(owned(m)))
                    def _():
                        for kind in range(2):
                            self.to_owner(kind, index, i).wait_send()

            for t in range(DEPTH):
                self.zero(t).wait_send()

                @pl.when(self.order(t) != z)
                def _():
                    self.three(t).wait_send()

                for core in range(2):

                    @pl.when(self.crosses(t, core))
                    def _():
                        self.one(t, core).wait_send()
                        self.two(t, core).wait_send()

    def owned(m):
        oz, ox, oy, oc = OWNERS[m]
        return (z == oz) & (x == ox) & (y == oy) & (c == oc)

    def stage(kind, m):
        return ((y_attn, y_ff), (g_attn, g_ff))[kind][int(m >= 4)]

    reduces = [Reduce(*spans[i], per_part[i * each + 8 : (i + 1) * each]) for i in range(2)]
    attn_reduce, ff_reduce = reduces

    attn_gather.start()
    ff_gather.start()

    for one in loads:
        one.wait()
    for i, (value, turned) in enumerate(((mgate_up_ref[0], 4), (mgate_up_ref[1], 5))):
        start, count = pieces[turned]
        momenta[start : start + count, :] = value.T
    for j in range(3):
        start, count = pieces[j]
        momenta[start : start + count, :] = mqkv_ref[j]
    momenta[pieces[3][0] : pieces[3][0] + pieces[3][1], :] = mout_ref[...]
    momenta[pieces[6][0] : last_row, :] = mdown_ref[...]
    stat_s[...] = jnp.zeros_like(stat_s)

    lane = lax.broadcasted_iota(jnp.int32, (1, LANES), 1)
    low_head = lane < HEAD_DIM
    low_half = lane % HEAD_DIM < HEAD_DIM // 2
    row_id = lax.broadcasted_iota(jnp.int32, (PAIR, 1), 0)
    lane_id = lax.broadcasted_iota(jnp.int32, (1, PAIR), 1)
    same_bucket = (row_id < BUCKET) == (lane_id < BUCKET)
    slots = lax.broadcasted_iota(jnp.int32, (1, TIME_SLOTS), 1)
    query_scale = HEAD_DIM ** (-0.5)
    gain_one = gain_ref[0:1, :]
    gain_two = gain_ref[1:2, :]

    def column(row):
        return jnp.broadcast_to(row, (8, PAIR)).T[:, 0:1]

    def var_row(pair):
        two = var_ref[pl.ds(2 * pair, 2), :]
        return jnp.concatenate([two[0:1], two[1:2]], axis=1).astype(WIDE)

    def block_of(i, size):
        return pl.ds(pl.multiple_of(i * size, size), size)

    def prepare(i, carry):
        here = block_of(i, PAIR)
        times = column(time_ref[pl.ds(i, 1), :].astype(WIDE)).astype(jnp.int32)
        hot = (times == slots).astype(LOW)
        rope_s[here, :] = (
            mul_nn(hot, table_ref[0]) + mul_nn(hot, table_ref[1]) + mul_nn(hot, table_ref[2])
        )
        tokens = tok_ref[here, :].astype(WIDE)
        scale = lax.rsqrt(jnp.mean(tokens * tokens, axis=-1, keepdims=True) + EPS_NORM)
        scale_s[here, 0:1] = scale
        n1_s[here, :] = (tokens * scale * gain_one).astype(LOW)
        first, second = lengths[2 * i], lengths[2 * i + 1]
        live = row_id % BUCKET < jnp.where(row_id < BUCKET, first, second)
        glow_s[here, :] = jnp.where(live, cot_ref[here, :].astype(WIDE), 0.0).astype(LOW)
        return carry

    lax.fori_loop(0, rows // PAIR, prepare, 0)

    for d in range(1, DEPTH):
        attn_gather.hop(d)
        if d < DEPTH - 1:
            ff_gather.hop(d)
    for d in range(DEPTH):
        attn_gather.from_beside(d)
    attn_gather.arrive()

    def weight(first, last):
        parts = []
        for i in range(first, last):
            start, count = pieces[i]
            piece = w_s[:, start : start + count, :]
            parts.append(piece.reshape(piece.shape[0] * count, width))
        return parts[0] if len(parts) == 1 else jnp.concatenate(parts, axis=0)

    def swapped(values):
        half = HEAD_DIM // 2
        return jnp.where(
            low_half, pltpu.roll(values, LANES - half, 1), pltpu.roll(values, half, 1)
        )

    def two_heads(value):
        none = jnp.zeros_like(value)
        return jnp.concatenate(
            [jnp.where(low_head, value, none), jnp.where(low_head, none, value)], axis=0
        )

    per_block = BLOCK // PAIR

    def attend(i, carry):
        here = block_of(i, BLOCK)
        qkv = mul_nt(n1_s[here, :], weight(0, 3))
        cosine = rope_s[here, :LANES]
        sine = rope_s[here, LANES:]
        masks = []
        for p in range(per_block):
            pair = i * per_block + p
            first, second = lengths[2 * pair], lengths[2 * pair + 1]
            live_key = lane_id % BUCKET < jnp.where(lane_id < BUCKET, first, second)
            row = var_row(pair)
            masks.append((same_bucket & live_key, column(row) == row))
        attended = []
        for hp in range(heads // 2):
            first = hp * LANES
            q = qkv[:, first : first + LANES]
            k = qkv[:, width + first : width + first + LANES]
            v = qkv[:, 2 * width + first : 2 * width + first + LANES].astype(LOW)
            q = ((q * cosine + swapped(q) * sine) * query_scale).astype(LOW)
            k = (k * cosine + swapped(k) * sine).astype(LOW)
            low_s[here, first : first + LANES] = q
            low_s[here, width + first : width + first + LANES] = k
            low_s[here, 2 * width + first : 2 * width + first + LANES] = v
            pairs = []
            for p in range(per_block):
                span = slice(p * PAIR, (p + 1) * PAIR)
                mask, same_var = masks[p]
                raw = mul_nt(two_heads(q[span]), k[span])
                both = []
                for j in range(2):
                    h = 2 * hp + j
                    biased = raw[j * PAIR : (j + 1) * PAIR] + jnp.where(
                        same_var, bias[0, h], bias[1, h]
                    )
                    both.append(jnp.where(mask, biased, NEG_FILL))
                scores = jnp.concatenate(both, axis=0)
                exponent = jnp.exp(scores - jnp.max(scores, axis=-1, keepdims=True))
                probs = exponent / jnp.sum(exponent, axis=-1, keepdims=True)
                probs_s[i * per_block + p, hp] = probs
                both = mul_nn(probs.astype(LOW), v[span])
                pairs.append(jnp.where(low_head, both[:PAIR], both[PAIR:]))
            attended.append(jnp.concatenate(pairs, axis=0).astype(LOW))
        attended = jnp.concatenate(attended, axis=1)
        att_s[here, :] = attended
        mid = tok_ref[here, :].astype(WIDE) + mul_nn(attended, weight(3, 4))
        mid_s[here, :] = mid
        scale = lax.rsqrt(jnp.mean(mid * mid, axis=-1, keepdims=True) + EPS_NORM)
        scale_s[here, 1:2] = scale
        n2_s[here, :] = (mid * scale * gain_two).astype(LOW)
        @pl.when(i == 0)
        def _():
            ff_gather.hop(DEPTH - 1)
            ff_gather.from_beside(0)
            ff_gather.from_beside(1)

        for d in range(2, DEPTH):

            @pl.when(i == d - 1)
            def _():
                ff_gather.from_beside(d)

        return carry

    lax.fori_loop(0, rows // BLOCK, attend, 0)
    ff_gather.arrive()
    for one in reduces:
        one.send_momenta()

    def feed(i, carry):
        here = block_of(i, 2 * BLOCK)
        normed_two = n2_s[here, :]
        w_gate, w_up, w_down = weight(4, 5), weight(5, 6), weight(6, 7)
        gate = mul_nt(normed_two, w_gate)
        up = mul_nt(normed_two, w_up)
        sig = 1.0 / (1.0 + jnp.exp(-gate))
        silu = gate * sig
        hid_s[here, :] = (silu * up).astype(LOW)
        g_low = glow_s[here, :]
        g_hidden = mul_nt(g_low, w_down)
        g_gate = (g_hidden * up * sig * (1.0 + gate * (1.0 - sig))).astype(LOW)
        g_up = (g_hidden * silu).astype(LOW)
        gg_s[here, :] = g_gate
        gu_s[here, :] = g_up
        e_two = mul_nn(g_gate, w_gate) + mul_nn(g_up, w_up)
        scale = scale_s[here, 1:2]
        unit = mid_s[here, :] * scale
        stat_s[1:2, :] += jnp.sum(e_two * unit, axis=0, keepdims=True)
        scaled = e_two * gain_two
        g_mid = g_low.astype(WIDE) + scale * (
            scaled - unit * jnp.mean(scaled * unit, axis=-1, keepdims=True)
        )
        gmid_s[here, :] = g_mid
        g_mid_low = g_mid.astype(LOW)
        gml_s[here, :] = g_mid_low
        gatt_s[here, :] = mul_nt(g_mid_low, weight(3, 4)).astype(LOW)
        return carry

    lax.fori_loop(0, rows // (2 * BLOCK), feed, 0)

    def grad_put(index, left, right):
        start, count = pieces[index]
        grad_s[:, :, start : start + count, :] = (
            mul_tn(left, right).reshape(DEPTH, ACROSS, count, width).astype(LOW)
        )

    grad_put(4, gg_s[...], n2_s[...])
    grad_put(5, gu_s[...], n2_s[...])
    grad_put(6, hid_s[...], glow_s[...])
    ff_reduce.start()
    grad_put(3, att_s[...], gml_s[...])

    def attend_back(i, carry):
        here = block_of(i, PAIR)
        row = var_row(i)
        same_var = column(row) == row
        cosine = rope_s[here, :LANES]
        sine = rope_s[here, LANES:]
        for hp in range(heads // 2):
            first = hp * LANES
            q2 = two_heads(low_s[here, first : first + LANES])
            k = low_s[here, width + first : width + first + LANES]
            v = low_s[here, 2 * width + first : 2 * width + first + LANES]
            probs = probs_s[i, hp]
            ga2 = two_heads(gatt_s[here, first : first + LANES])
            g_probs = mul_nt(ga2, v)
            row_dot = jnp.sum(probs * g_probs, axis=-1, keepdims=True)
            g_scores = probs * (g_probs - row_dot)
            for j in range(2):
                h = 2 * hp + j
                mine = g_scores[j * PAIR : (j + 1) * PAIR]
                stat_s[8 + h : 9 + h, :PAIR] += jnp.sum(
                    jnp.where(same_var, mine, 0.0), axis=0, keepdims=True
                )
                stat_s[16 + h : 17 + h, :PAIR] += jnp.sum(
                    jnp.where(same_var, 0.0, mine), axis=0, keepdims=True
                )
            low_scores = g_scores.astype(LOW)
            both = mul_nn(low_scores, k)
            dq = jnp.where(low_head, both[:PAIR], both[PAIR:])
            dk = mul_tn(low_scores, q2)
            dv = mul_tn(probs.astype(LOW), ga2)
            gqkv_s[here, first : first + LANES] = (
                (dq * cosine - swapped(dq) * sine) * query_scale
            ).astype(LOW)
            gqkv_s[here, width + first : width + first + LANES] = (
                dk * cosine - swapped(dk) * sine
            ).astype(LOW)
            gqkv_s[here, 2 * width + first : 2 * width + first + LANES] = dv.astype(LOW)
        @pl.when(i == 0)
        def _():
            for t in range(DEPTH):
                ff_reduce.first(t)

        @pl.when(i == 4)
        def _():
            ff_reduce.second(0)
            ff_reduce.second(1)

        @pl.when(i == 6)
        def _():
            ff_reduce.third(0)
            ff_reduce.third(1)
            ff_reduce.second(2)
            ff_reduce.second(3)

        return carry

    lax.fori_loop(0, rows // PAIR, attend_back, 0)
    for j in range(3):
        grad_put(j, gqkv_s[:, j * width : (j + 1) * width], n1_s[...])
    attn_reduce.start()
    ff_reduce.third(2)
    ff_reduce.third(3)

    def last(i):
        here = block_of(i, 2 * BLOCK)
        e_one = mul_nn(gqkv_s[here, :], weight(0, 3))
        scale = scale_s[here, 0:1]
        unit = tok_ref[here, :].astype(WIDE) * scale
        stat_s[0:1, :] += jnp.sum(e_one * unit, axis=0, keepdims=True)
        scaled = e_one * gain_one
        gtok_ref[here, :] = (
            gmid_s[here, :]
            + scale * (scaled - unit * jnp.mean(scaled * unit, axis=-1, keepdims=True))
        ).astype(LOW)

    def outgoing(i):
        here = block_of(i, 2 * BLOCK)
        out_ref[here, :] = (mid_s[here, :] + mul_nn(hid_s[here, :], weight(6, 7))).astype(LOW)

    def stat_copy(step, src, where):
        return remote(src, stat_in.at[step], stat_send.at[step], stat_recv.at[step], where)

    for t in range(DEPTH):
        attn_reduce.first(t)
    last(0)
    last(1)
    leave = [
        pltpu.make_async_copy(gtok_ref, gtok_hbm, out_sem.at[0]),
        pltpu.make_async_copy(out_ref, out_hbm, out_sem.at[1]),
    ]
    leave[0].start()
    stat_copy(0, stat_s, sibling).start()
    ff_reduce.finish()
    attn_reduce.second(0)
    attn_reduce.second(1)
    stat_copy(0, stat_s, sibling).wait()
    stat_acc[0] = stat_s[...] + stat_in[0]
    stat_copy(1, stat_acc.at[0], facing).start()
    attn_reduce.second(2)
    attn_reduce.second(3)
    for t in range(DEPTH):
        attn_reduce.third(t)
    stat_copy(1, stat_acc.at[0], facing).wait()
    stat_acc[1] = stat_acc[0] + stat_in[1]
    stat_copy(2, stat_acc.at[1], beside).start()
    attn_owner = functools.reduce(jnp.logical_or, [owned(m) for m in range(4)])
    ff_owner = functools.reduce(jnp.logical_or, [owned(m) for m in range(4, 7)])

    chips = DEPTH * ACROSS * SIDES

    def x_copy(m, i):
        start, count = pieces[m]
        source = x_attn if m < 4 else x_ff
        to = i // SIDES
        return remote(
            source.at[to],
            xrows_ref.at[pl.ds(start, count)],
            x_send.at[i],
            x_recv.at[m],
            (to, lax.rem(i, SIDES) * CORES + OWNERS[m][3]),
        )

    mine = shard * SIDES + y
    unit_mat = lax.broadcasted_iota(jnp.int32, (width, width), 0) == lax.broadcasted_iota(
        jnp.int32, (width, width), 1
    )
    diagonal = jnp.where(unit_mat, COEF_A, 0.0)

    def advance(y_buf, g_buf):
        pltpu.make_async_copy(y_buf, y_buf, mom_recv.at[0]).wait()
        pltpu.make_async_copy(g_buf, g_buf, adv_recv.at[0]).wait()
        grad = g_buf[...].astype(WIDE)
        return grad + MUON_MU * (MUON_MU * y_buf[...] + grad)

    def poly(value):
        return diagonal + COEF_B * value + COEF_C * square_wide(value)

    @pl.when(ff_owner)
    def _():
        y_ff[...] = advance(y_ff, g_ff)
        gram_mat = gram_wide(y_ff[...].reshape(-1, width))
        trace = jnp.sum(jnp.where(unit_mat, gram_mat, 0.0), keepdims=True)
        inverse = 1.0 / (jnp.sqrt(trace) + NS_EPS)
        gram_mat = gram_mat * (inverse * inverse)
        step_mat = poly(gram_mat)
        gram_s[...] = mul_wide(mul_wide(gram_mat, step_mat), step_mat)
        chain_s[...] = step_mat * inverse

    attn_reduce.finish()
    for one in reduces:
        one.give_rows()
    stat_copy(2, stat_acc.at[1], beside).wait()
    stat_acc[2] = stat_acc[1] + stat_in[2]
    stat_line[z] = stat_acc[2]

    def stat_send_line(j):
        return remote(
            stat_acc.at[2],
            stat_line.at[z],
            stat_send.at[2 + j],
            stat_recv.at[2 + j],
            device(line[j], x, y, c),
        )

    for j in range(1, DEPTH):
        stat_send_line(j).start()

    def send_x(m, first, count):
        def send(i, carry):
            @pl.when(i != mine)
            def _():
                x_copy(m, i).start()

            return carry

        lax.fori_loop(first, first + count, send, 0)

    def keep_x(m):
        start, count = pieces[m]
        source = x_attn if m < 4 else x_ff
        pltpu.make_async_copy(
            source.at[shard], xrows_ref.at[pl.ds(start, count)], x_recv.at[m]
        ).start()

    @pl.when(attn_owner)
    def _():
        value = advance(y_attn, g_attn).reshape(-1, width)
        total = jnp.sum(jnp.sum(value * value, axis=0, keepdims=True), axis=1, keepdims=True)
        chain_s[...] = value * (1.0 / (jnp.sqrt(total) + NS_EPS))

        def turn(i, carry):
            now = chain_s[...]
            chain_s[...] = mul_wide(now, poly(gram_wide(now)))
            return carry

        lax.fori_loop(0, NS_ITERS - 1, turn, 0)
        now = chain_s[...]
        now_low = now.astype(LOW)
        gram_mat = mul_tn(now_low, now_low)
        rest = COEF_B * gram_mat + COEF_C * square_low(gram_mat)
        last_x = COEF_A * now + mul_nn(now_low, rest.astype(LOW))
        x_attn[...] = last_x.astype(LOW).reshape(x_attn.shape)
        for m in range(4):

            @pl.when(owned(m))
            def _():
                send_x(m, 0, chips)
                keep_x(m)

    @pl.when(ff_owner)
    def _():
        def turn(i, carry):
            now = gram_s[...]
            step_now = poly(now)
            both = mul_wide(jnp.concatenate([now, chain_s[...]], axis=0), step_now)
            chain_s[...] = both[width:]
            gram_s[...] = mul_wide(both[:width], step_now)
            return carry

        lax.fori_loop(0, NS_ITERS - 2, turn, 0)
        gram_mat = gram_s[...]
        rest = (COEF_B * gram_mat + COEF_C * square_low(gram_mat)).astype(LOW)
        now = chain_s[...]
        high, small = halves(now)
        chain_s[...] = COEF_A * now + (mul_nn(high, rest) + mul_nn(small, rest))

        def give(i, carry):
            at = lax.rem(z + 2 + i, DEPTH)
            these = pl.ds(at * ACROSS, ACROSS)
            value = y_ff[these].reshape(-1, width)
            x_ff[these] = mul_wide(value, chain_s[...]).astype(LOW).reshape(
                ACROSS, x_ff.shape[1], width
            )
            for m in range(4, 7):

                @pl.when(owned(m))
                def _():
                    send_x(m, at * (ACROSS * SIDES), ACROSS * SIDES)

            return carry

        lax.fori_loop(0, DEPTH, give, 0)
        for m in range(4, 7):

            @pl.when(owned(m))
            def _():
                keep_x(m)

    outgoing(0)
    outgoing(1)
    leave[1].start()

    for j in range(1, DEPTH):
        remote(
            stat_acc.at[2],
            stat_line.at[lax.rem(z + DEPTH - j, DEPTH)],
            stat_send.at[2 + j],
            stat_recv.at[2 + j],
            device(line[j], x, y, c),
        ).wait()
    total_ref[...] = (stat_line[0] + stat_line[1]) + (stat_line[2] + stat_line[3])
    for one in gathers:
        one.sent()
    for one in reduces:
        one.done()

    def fan_copy(m):
        start, count = pieces[m]
        rows_m = xrows_ref.at[pl.ds(start, count)]
        return remote(rows_m, rows_m, fan_send.at[m], fan_recv.at[m], sibling)

    for m in range(7):
        start, count = pieces[m]

        @pl.when(c == OWNERS[m][3])
        def _():
            rows_m = xrows_ref.at[pl.ds(start, count)]
            pltpu.make_async_copy(rows_m, rows_m, x_recv.at[m]).wait()
            fan_copy(m).start()

    for m in range(7):

        @pl.when(c != OWNERS[m][3])
        def _():
            fan_copy(m).wait_recv()

        @pl.when(c == OWNERS[m][3])
        def _():
            fan_copy(m).wait_send()

        @pl.when(owned(m))
        def _():
            def sent(i, carry):
                x_copy(m, lax.rem(mine + i, chips)).wait_send()
                return carry

            lax.fori_loop(1, chips, sent, 0)

    for one in leave:
        one.wait()


def rotary_table():
    half = HEAD_DIM // 2
    frequency = (ROPE_BASE ** (-2.0 * np.arange(half) / HEAD_DIM)).astype(np.float32)
    angles = np.arange(TIME_SLOTS, dtype=np.float32)[:, None] * frequency[None, :]
    cosine = np.cos(angles.astype(np.float64)).astype(np.float32)
    sine = np.sin(angles.astype(np.float64)).astype(np.float32)
    table = np.concatenate([cosine] * 4 + [-sine, sine, -sine, sine], axis=1)
    parts = []
    for _ in range(3):
        parts.append(table.astype(LOW))
        table = table - parts[-1].astype(np.float32)
    return np.stack(parts)


def whole_step(tokens, cotangent, lengths, variates, times, gains, attn_bias, weights, momenta):
    rows, width = tokens.shape
    heads = attn_bias.shape[1]
    attn_rows, ff_rows = weights[1].shape[0], weights[3].shape[0]
    pieces = offsets(attn_rows, ff_rows)
    ff = ff_rows * DEPTH * ACROSS
    shards = DEPTH * ACROSS
    shard_rows = 4 * attn_rows + 3 * ff_rows
    low = lambda *shape: pltpu.VMEM(shape, LOW)
    wide = lambda *shape: pltpu.VMEM(shape, WIDE)
    dma = lambda *shape: pltpu.SemaphoreType.DMA(shape)

    def part_scratch(count):
        half, quarter = count // 2, count // 4
        relative = 2 * DEPTH - 1
        return [
            dma(DEPTH),
            dma(DEPTH),
            dma(relative),
            dma(2, relative),
            dma(DEPTH),
            dma(DEPTH),
            dma(relative),
            dma(2, relative),
            low(DEPTH, ACROSS, half, width),
            low(DEPTH, ACROSS, half, width),
            low(DEPTH, ACROSS, half, width),
            low(DEPTH, ACROSS, half, width),
            low(DEPTH, quarter, width),
            low(DEPTH, quarter, width),
            low(DEPTH, quarter, width),
            *[dma(DEPTH) for _ in range(8)],
            dma(3),
            dma(3),
            dma(3),
            dma(3),
        ]

    return pl.pallas_call(
        functools.partial(whole_kernel, pieces),
        out_shape=(
            jax.ShapeDtypeStruct((rows, width), LOW),
            jax.ShapeDtypeStruct((rows, width), LOW),
            jax.ShapeDtypeStruct((shard_rows, width), LOW),
            jax.ShapeDtypeStruct((shard_rows, width), LOW),
            jax.ShapeDtypeStruct((STATS, width), WIDE),
        ),
        in_specs=[SCALARS] * 2 + [ANYWHERE] * 2 + [WHOLE] * 8 + [ANYWHERE] * 4,
        out_specs=(ANYWHERE, ANYWHERE, WHOLE, WHOLE, WHOLE),
        scratch_shapes=[
            low(rows, width),
            low(rows, width),
            *[wide(*m.shape) for m in momenta],
            dma(6),
            low(rows, width),
            low(rows, width),
            dma(2),
            low(shards, shard_rows, width),
            low(DEPTH, ACROSS, shard_rows, width),
            wide(shard_rows, width),
            low(rows, width),
            low(rows, width),
            low(rows, width),
            low(rows, width),
            low(rows, width),
            low(rows, ff),
            low(rows, ff),
            low(rows, ff),
            low(rows, 3 * width),
            low(rows, 3 * width),
            wide(rows // PAIR, heads // 2, 2 * PAIR, PAIR),
            wide(rows, width),
            wide(rows, width),
            low(rows, width),
            wide(rows, 2),
            wide(rows, 2 * LANES),
            wide(shards, attn_rows, width),
            wide(shards, ff_rows, width),
            low(shards, attn_rows, width),
            low(shards, ff_rows, width),
            low(shards, attn_rows, width),
            low(shards, ff_rows, width),
            wide(width, width),
            wide(width, width),
            wide(STATS, width),
            wide(3, STATS, width),
            wide(3, STATS, width),
            wide(DEPTH, STATS, width),
            dma(6),
            dma(6),
            dma(1),
            dma(1),
            dma(shards * SIDES),
            dma(7),
            dma(7),
            dma(7),
            *part_scratch(4 * attn_rows),
            *part_scratch(3 * ff_rows),
        ],
        compiler_params=pltpu.CompilerParams(
            vmem_limit_bytes=60 << 20, collective_id=0, has_side_effects=True
        ),
        name="whole",
    )(
        lengths,
        attn_bias,
        tokens,
        cotangent,
        variates,
        times.reshape(rows // PAIR, PAIR),
        jnp.asarray(rotary_table()),
        gains,
        *weights,
        *momenta,
    )


def update_kernel(
    pieces,
    factors,
    grow_ref,
    xrow_ref,
    stat_ref,
    w_qkv,
    w_out,
    w_gate_up,
    w_down,
    m_qkv,
    m_out,
    m_gate_up,
    m_down,
    gains,
    bias,
    gain_moment,
    gain_square,
    bias_moment,
    bias_square,
    out_in,
    gtok_in,
    g_qkv,
    g_out,
    g_gate_up,
    g_down,
    nm_qkv,
    nm_out,
    nm_gate_up,
    nm_down,
    nw_qkv,
    nw_out,
    nw_gate_up,
    nw_down,
    g_gains,
    n_gain_moment,
    n_gain_square,
    n_gains,
    g_bias,
    n_bias_moment,
    n_bias_square,
    n_bias,
    out_tokens,
    grad_tokens,
    sems,
):
    copies = (
        pltpu.make_async_copy(out_in, out_tokens, sems.at[0]),
        pltpu.make_async_copy(gtok_in, grad_tokens, sems.at[1]),
    )
    for one_copy in copies:
        one_copy.start()
    shrink = 1.0 - MUON_RATE * MUON_DECAY

    def one(index, turned, g, m, w, nm, nw):
        start, count = pieces[index]
        grad = grow_ref[start : start + count, :].astype(WIDE)
        ortho = xrow_ref[start : start + count, :].astype(WIDE)
        if turned:
            grad, ortho = grad.T, ortho.T
        g[...] = grad
        nm[...] = MUON_MU * m[...] + grad
        nw[...] = w[...] * shrink - factors[index] * ortho

    for j in range(3):
        one(j, False, *[r.at[j] for r in (g_qkv, m_qkv, w_qkv, nm_qkv, nw_qkv)])
    one(3, False, g_out, m_out, w_out, nm_out, nw_out)
    for j in range(2):
        refs = (g_gate_up, m_gate_up, w_gate_up, nm_gate_up, nw_gate_up)
        one(4 + j, True, *[r.at[j] for r in refs])
    one(6, False, g_down, m_down, w_down, nm_down, nw_down)

    grad = stat_ref[0:2, :]
    g_gains[...] = grad
    n_gain_moment[...], n_gain_square[...], n_gains[...] = adam_step(
        gains[...], grad, gain_moment[...], gain_square[...]
    )
    heads = bias.shape[1]
    sums = jnp.sum(stat_ref[8:24, :PAIR].T, axis=0, keepdims=True)
    grad = jnp.concatenate([sums[:, :heads], sums[:, 8 : 8 + heads]], axis=0)
    g_bias[...] = grad
    n_bias_moment[...], n_bias_square[...], n_bias[...] = adam_step(
        bias[...], grad, bias_moment[...], bias_square[...]
    )
    for one_copy in copies:
        one_copy.wait()


def update(factors, grad_rows, ortho_rows, stats, weights, momenta, small, rows):
    pieces = offsets(weights[1].shape[0], weights[3].shape[0])
    gains, bias = small[:2]
    like = lambda a: jax.ShapeDtypeStruct(a.shape, WIDE)
    outs = [like(a) for a in (*weights, *weights, *weights, *[gains] * 4, *[bias] * 4)]
    return pl.pallas_call(
        functools.partial(update_kernel, pieces, factors),
        out_shape=(*outs, *[jax.ShapeDtypeStruct(r.shape, r.dtype) for r in rows]),
        in_specs=[WHOLE] * 19,
        out_specs=(*[WHOLE] * len(outs), *[ANYWHERE] * 2),
        scratch_shapes=[pltpu.SemaphoreType.DMA((2,))],
        compiler_params=pltpu.CompilerParams(vmem_limit_bytes=58 << 20),
        name="update",
    )(grad_rows, ortho_rows, stats, *weights, *momenta, *small, *rows)


def body(
    tokens,
    cotangent,
    lengths,
    variates,
    times,
    weight_qkv,
    weight_out,
    weight_gate_up,
    weight_down,
    momentum_qkv,
    momentum_out,
    momentum_gate_up,
    momentum_down,
    gains,
    attn_bias,
    gain_moment,
    gain_square,
    bias_moment,
    bias_square,
):
    width = tokens.shape[1]
    heads = attn_bias.shape[1]
    attn_rows = weight_out.shape[0]
    ff_rows = weight_down.shape[0]
    fsdp = lax.axis_size("fsdp")
    ff = ff_rows * fsdp
    attn_width = attn_rows * fsdp
    shrink = 1.0 - MUON_RATE * MUON_DECAY
    scale_attn = MUON_RATE * 0.2 * math.sqrt(max(width, attn_width))
    scale_ff = MUON_RATE * 0.2 * math.sqrt(max(width, ff))
    sizes = (fsdp, lax.axis_size("ns"))
    if sizes == (DEPTH * ACROSS, SIDES * CORES) and attn_rows == 48 and ff_rows == 128:
        turn = lambda a: jnp.swapaxes(a, 1, 2)
        shards = (turn(weight_qkv), weight_out, weight_gate_up, weight_down)
        momenta = (turn(momentum_qkv), momentum_out, momentum_gate_up, momentum_down)
        out_tokens, grad_tokens, grad_rows, ortho_rows, stats = whole_step(
            tokens, cotangent, lengths, variates, times, gains, attn_bias, shards, momenta
        )
        outs = list(
            update(
                (scale_attn,) * 4 + (scale_ff,) * 3,
                grad_rows,
                ortho_rows,
                stats,
                shards,
                momenta,
                (gains, attn_bias, gain_moment, gain_square, bias_moment, bias_square),
                (out_tokens, grad_tokens),
            )
        )
        out_tokens, grad_tokens = outs[-2:]
        outs = outs[:-2]
        for i in (0, 4, 8):
            outs[i] = turn(outs[i])
        return (out_tokens, grad_tokens, *outs)
    weights = pack(weight_qkv, weight_out, weight_gate_up, weight_down)
    momenta = pack(momentum_qkv, momentum_out, momentum_gate_up, momentum_down)
    full = lax.all_gather(weights.astype(LOW), "fsdp", axis=0, tiled=False)
    aligned = attn_rows % 16 == 0 and ff_rows % 16 == 0
    pieces = offsets(attn_rows, ff_rows)
    if not aligned:
        full = jnp.concatenate(
            [full[:, s : s + n].reshape(1, fsdp * n, width) for s, n in pieces], axis=1
        )
    out_tokens, grad_tokens, grads, stats = layer(
        tokens, cotangent, lengths, variates, times, full, gains, attn_bias, ff, WIDE
    )
    if not aligned:
        wholes = offsets(attn_width, ff)
        grads = jnp.concatenate(
            [grads[0, s : s + n].reshape(fsdp, n // fsdp, width) for s, n in wholes], axis=1
        )
    summed = lax.psum_scatter(grads, "fsdp", scatter_dimension=0, tiled=False)
    grad_rows = lax.psum(summed.astype(LOW), "ns").astype(WIDE)
    bias_part = jnp.sum(stats[8:, :PAIR], axis=1).reshape(2, 8)[:, :heads]
    grad_gains, grad_bias = lax.psum((stats[:2], bias_part), ("fsdp", "ns"))

    new_momenta = MUON_MU * momenta + grad_rows
    advance = grad_rows + MUON_MU * new_momenta
    parts = [advance[s : s + n] for s, n in pieces]
    grams = jnp.stack(
        [
            lax.dot_general(
                y,
                y,
                (((0,), (0,)), ((), ())),
                precision=lax.Precision.HIGHEST,
                preferred_element_type=WIDE,
            )
            for y in parts
        ]
    )
    factor = newton_schulz(lax.psum(grams, "fsdp"))
    turned = jnp.concatenate(
        [
            (scale_attn if i < 4 else scale_ff)
            * jnp.dot(
                y, factor[i], precision=lax.Precision.HIGHEST, preferred_element_type=WIDE
            )
            for i, y in enumerate(parts)
        ],
        axis=0,
    )
    new_weights = weights * shrink - turned
    new_gain_moment, new_gain_square, new_gains = adam_step(
        gains, grad_gains, gain_moment, gain_square
    )
    new_bias_moment, new_bias_square, new_bias = adam_step(
        attn_bias, grad_bias, bias_moment, bias_square
    )
    return (
        out_tokens,
        grad_tokens,
        *unpack(grad_rows, attn_rows, ff_rows),
        *unpack(new_momenta, attn_rows, ff_rows),
        *unpack(new_weights, attn_rows, ff_rows),
        grad_gains,
        new_gain_moment,
        new_gain_square,
        new_gains,
        grad_bias,
        new_bias_moment,
        new_bias_square,
        new_bias,
    )


def solution(mesh):
    rows = P(("fsdp", "ns"), None)
    line = P(("fsdp", "ns"))
    matrices = (P(None, None, "fsdp"), P("fsdp", None), P(None, None, "fsdp"), P("fsdp", None))
    return jax.shard_map(
        body,
        mesh=mesh,
        in_specs=(rows, rows, line, rows, line, *matrices, *matrices, *([P()] * 6)),
        out_specs=(rows, rows, *matrices, *matrices, *matrices, *([P()] * 8)),
        check_vma=False,
    )
```
